32 devices in a mesh: seq: 2 (over core), rows: 16 (over z, y, x).
Axes of the slice: x: 2, y: 2, z: 4, core: 2. Of those that a mesh axis runs over, the one named last changes fastest.
Arguments:
- tokens: bfloat16 [48, 1024, 768], P('rows', 'seq'), may hold values from -6 to 6
- segment_ids: int32 [48, 1024], P('rows', 'seq'), may hold values from 0 to 5, never falling along the last dimension, each value on 1 to 512 neighbouring positions
- cotangent: bfloat16 [48, 1024, 768], P('rows', 'seq'), may hold values from -6 to 6
- ln1_gain: bfloat16 [768], P(('seq', 'rows')), may hold values from 0.5 to 1.5
- ln1_bias: bfloat16 [768], P(('seq', 'rows')), may hold values from -1.75 to 1.75
- qkv_weight: bfloat16 [768, 2304], P(('seq', 'rows')), may hold values from -0.21875 to 0.21875
- qv_bias: bfloat16 [1536], P(('seq', 'rows')), may hold values from -0.625 to 0.625
- out_weight: bfloat16 [768, 768], P(('seq', 'rows')), may hold values from -0.875 to 0.875
- out_bias: bfloat16 [768], P(('seq', 'rows')), may hold values from -1.75 to 1.75
- ln2_gain: bfloat16 [768], P(('seq', 'rows')), may hold values from 0.5 to 1.5
- ln2_bias: bfloat16 [768], P(('seq', 'rows')), may hold values from -1.75 to 1.75
- up_weight: bfloat16 [768, 3072], P(('seq', 'rows')), may hold values from -0.21875 to 0.21875
- up_bias: bfloat16 [3072], P(('seq', 'rows')), may hold values from -1.75 to 1.75
- down_weight: bfloat16 [3072, 768], P(('seq', 'rows')), may hold values from -0.109375 to 0.109375
- down_bias: bfloat16 [768], P(('seq', 'rows')), may hold values from -1.75 to 1.75
- avg_qkv: float32 [768, 2304], P(('seq', 'rows')), may hold values from -0.21875 to 0.21875
- avg_out: float32 [768, 768], P(('seq', 'rows')), may hold values from -0.875 to 0.875
- avg_up: float32 [768, 3072], P(('seq', 'rows')), may hold values from -0.21875 to 0.21875
- avg_down: float32 [3072, 768], P(('seq', 'rows')), may hold values from -0.109375 to 0.109375
Outputs:
- out_tokens: bfloat16 [48, 1024, 768], P('rows', 'seq')
- grad_input: float32 [48, 1024, 768], P('rows', 'seq')
- grad_ln1_gain: float32 [768], P(('seq', 'rows'))
- grad_ln1_bias: float32 [768], P(('seq', 'rows'))
- grad_qkv_weight: float32 [768, 2304], P(('seq', 'rows'))
- grad_qv_bias: float32 [1536], P(('seq', 'rows'))
- grad_out_weight: float32 [768, 768], P(('seq', 'rows'))
- grad_out_bias: float32 [768], P(('seq', 'rows'))
- grad_ln2_gain: float32 [768], P(('seq', 'rows'))
- grad_ln2_bias: float32 [768], P(('seq', 'rows'))
- grad_up_weight: float32 [768, 3072], P(('seq', 'rows'))
- grad_up_bias: float32 [3072], P(('seq', 'rows'))
- grad_down_weight: float32 [3072, 768], P(('seq', 'rows'))
- grad_down_bias: float32 [768], P(('seq', 'rows'))
- new_avg_qkv: float32 [768, 2304], P(('seq', 'rows'))
- new_avg_out: float32 [768, 768], P(('seq', 'rows'))
- new_avg_up: float32 [768, 3072], P(('seq', 'rows'))
- new_avg_down: float32 [3072, 768], P(('seq', 'rows'))
The draws below stay inside these ranges and needn't reach their ends.
Inputs may be any that keep to these rules, and one draw needn't show every extreme that they name: `segment_ids`: along each row the ids never fall and every id from 0 to 5 appears; id 5 marks the padding at the end of the row; each id covers 1 to 512 positions of a row, and some id covers exactly 512 positions.
All inputs are finite; a program needn't handle non-finite values.
Results may differ from the reference program's by a relative error of at most 0.011.
Values may be sent and summed in bfloat16 or wider, within the bound.
No kernel may reach another device: no remote copies, remote signals or barrier semaphores. Data moves between devices by JAX's collectives and lax.ppermute only.
A program may use at most 320 MiB of HBM per device.

```python
import math
import jax
import jax.numpy as jnp
import numpy as np
from jax import lax

D = 768
HEADS = 12
HEAD_DIM = 64
FF = 3072
LEN = 1024
CLIPS = 6
ROWS = 48


def block_scale(stream_key, shape, split, smallest, largest):
    def one(dim, parts):
        heights = jax.random.uniform(jax.random.fold_in(jax.random.fold_in(stream_key, 6), dim), (parts,), jnp.float32, smallest / len(split), largest / len(split))
        return jnp.repeat(jnp.exp(heights), shape[dim] // parts).reshape((-1,) + (1,) * (len(shape) - dim - 1))

    level = one(*split[0])
    for cut in split[1:]:
        level = level * one(*cut)
    return level


def split_up(count, total, limit, lean):
    weights = [(1 << 20) // math.isqrt(standing ** lean) + 1 for standing in range(2, count + 1)]
    spare, holding = total - limit - (count - 1), [1] * (count - 1)
    while spare > 0:
        candidates = [i for i in range(count - 1) if holding[i] < limit]
        mass, budget = sum([weights[i] for i in candidates]), spare
        for i in candidates:
            addition = min(limit - holding[i], max(1, budget * weights[i] // mass), spare)
            holding[i] = holding[i] + addition
            spare = spare - addition
    return np.array([limit] + holding)


def ragged(key, amount, total, bound, skew):
    if amount == 2:
        one = jax.random.randint(key, (), max(1, total - bound), min(bound, total - 1) + 1)
        return jnp.stack([one, total - one])
    lengths = jnp.asarray(split_up(amount, total, bound, skew), jnp.int32)
    twos = (amount - 1) // 2
    source_of, sink = lengths[1:1 + 2 * twos:2], lengths[2:2 + 2 * twos:2]
    margin = jnp.minimum(source_of - 1, bound - sink)
    moved = jax.random.randint(jax.random.fold_in(key, 1), (twos,), 0, 1 << 20) % (margin + 1)
    lengths = lengths.at[1:1 + 2 * twos:2].set(source_of - moved).at[2:2 + 2 * twos:2].set(sink + moved)
    return lengths[jax.random.permutation(jax.random.fold_in(key, 2), amount)]


def bell_draw(rng, shape, width, reach, pieces=(), held_as=jnp.bfloat16):
    values = jax.random.normal(rng, shape, jnp.float32) * width
    if len(pieces) > 0:
        values = block_scale(rng, shape, pieces, -0.22, 0.18) * values
    return jnp.clip(values, min=-reach, max=reach).astype(held_as)


def setup_inputs(seed: int = 0) -> dict:
    keys = jax.random.split(jax.random.key(seed), 20)
    return {
        "tokens": bell_draw(keys[0], (ROWS, LEN, D), 1.0, 6.0, ((0, 16), (1, 2))),
        "segment_ids": jax.vmap(lambda own: jnp.searchsorted(jnp.cumsum(ragged(own, CLIPS, LEN, LEN // 2, 1)), jnp.arange(LEN), side="right"))(jax.random.split(keys[1], ROWS)).reshape((ROWS, LEN)).astype(jnp.int32),
        "cotangent": bell_draw(keys[2], (ROWS, LEN, D), 1.0, 6.0, ((0, 16), (1, 2))),
        "ln1_gain": jnp.clip(1.0 + 0.1 * jax.random.normal(keys[3], (D,), jnp.float32), 0.5, 1.5).astype(jnp.bfloat16),
        "ln1_bias": bell_draw(keys[4], (D,), 0.3, 1.75, ((0, 32),)),
        "qkv_weight": bell_draw(keys[5], (D, 3 * D), D ** -0.5, 0.21875, ((0, 32),)),
        "qv_bias": bell_draw(keys[6], (2 * D,), 0.1, 0.625, ((0, 32),)),
        "out_weight": bell_draw(keys[7], (D, D), (D // 16) ** -0.5, 0.875, ((0, 32),)),
        "out_bias": bell_draw(keys[8], (D,), 0.3, 1.75, ((0, 32),)),
        "ln2_gain": jnp.clip(1.0 + 0.1 * jax.random.normal(keys[9], (D,), jnp.float32), 0.5, 1.5).astype(jnp.bfloat16),
        "ln2_bias": bell_draw(keys[10], (D,), 0.3, 1.75, ((0, 32),)),
        "up_weight": bell_draw(keys[11], (D, FF), D ** -0.5, 0.21875, ((0, 32),)),
        "up_bias": bell_draw(keys[12], (FF,), 0.3, 1.75, ((0, 32),)),
        "down_weight": bell_draw(keys[13], (FF, D), FF ** -0.5, 0.109375, ((0, 32),)),
        "down_bias": bell_draw(keys[14], (D,), 0.3, 1.75, ((0, 32),)),
        "avg_qkv": bell_draw(keys[15], (D, 3 * D), D ** -0.5, 0.21875, ((0, 32),), jnp.float32),
        "avg_out": bell_draw(keys[16], (D, D), (D // 16) ** -0.5, 0.875, ((0, 32),), jnp.float32),
        "avg_up": bell_draw(keys[17], (D, FF), D ** -0.5, 0.21875, ((0, 32),), jnp.float32),
        "avg_down": bell_draw(keys[18], (FF, D), FF ** -0.5, 0.109375, ((0, 32),), jnp.float32),
    }


@jax.custom_vjp
def low(v):
    return lax.optimization_barrier(v.astype(jnp.bfloat16)).astype(jnp.float32)

@jax.custom_vjp
def low_back(v):
    return v

def low_keep(v):
    return (low(v), None)

def low_pass(kept, grad):
    return (grad,)

def back_keep(v):
    return (v, None)

def back_low(kept, grad):
    return (low(grad),)
low.defvjp(low_keep, low_pass)
low_back.defvjp(back_keep, back_low)

def layer_norm(value, gain, bias):
    middle = lax.optimization_barrier(jnp.mean(value, axis=-1, keepdims=True))
    centred = value - middle
    spread = lax.optimization_barrier(jnp.mean(centred * centred, axis=-1, keepdims=True))
    return centred * lax.rsqrt(spread + 1e-06) * gain + bias

def project(left, weight):
    return jnp.einsum('gtd,de->gte', left, weight, precision=lax.Precision.HIGHEST)

def attend(packed):
    query_rows, key_rows, value_rows, seg_row = packed
    query_heads = query_rows.reshape(LEN, HEADS, HEAD_DIM)
    key_heads = key_rows.reshape(LEN, HEADS, HEAD_DIM)
    value_heads = value_rows.reshape(LEN, HEADS, HEAD_DIM)
    scaled = low_back(0.125 * jnp.einsum('qhe,khe->qhk', query_heads, key_heads, precision=lax.Precision.HIGHEST))
    places = jnp.arange(LEN, dtype=jnp.int32)
    allowed = (seg_row[:, None] == seg_row[None, :]) & ((seg_row[None, :] != CLIPS - 1) | (places[:, None] == places[None, :]))
    allowed = allowed[:, None, :]
    expo = jnp.where(allowed, jnp.exp(jnp.where(allowed, scaled, 0.0)), 0.0)
    totals = low_back(lax.optimization_barrier(jnp.sum(expo, axis=-1)))
    weighted = low_back(jnp.einsum('qhk,khe->qhe', low(expo), value_heads, precision=lax.Precision.HIGHEST))
    return (weighted / totals[:, :, None]).reshape(LEN, HEADS * HEAD_DIM)

def layer_block(residual, seg_rows, params):
    gain_one, bias_one, w_qkv, b_qv, w_out, b_out, gain_two, bias_two, w_up, b_up, w_down, b_down = params
    normed = low(layer_norm(residual, gain_one, bias_one))
    mixed = project(normed, w_qkv)
    queries = low(low_back(mixed[..., :D] + b_qv[:D]))
    keys_all = low(low_back(mixed[..., D:2 * D]))
    values_all = low(low_back(mixed[..., 2 * D:] + b_qv[D:]))
    attended = lax.map(jax.checkpoint(attend), (queries, keys_all, values_all, seg_rows))
    attn_in = low(attended)
    middle = residual + low_back(project(attn_in, w_out) + b_out)
    normed_two = low(layer_norm(middle, gain_two, bias_two))
    hidden = low(jax.nn.gelu(low_back(project(normed_two, w_up) + b_up), approximate=False))
    return middle + low_back(project(hidden, w_down) + b_down)

def add_pair(first_term, second_term):
    return first_term + second_term

def reference(tokens, segment_ids, cotangent, ln1_gain, ln1_bias, qkv_weight, qv_bias, out_weight, out_bias, ln2_gain, ln2_bias, up_weight, up_bias, down_weight, down_bias, avg_qkv, avg_out, avg_up, avg_down):
    params = tuple((member.astype(jnp.float32) for member in (ln1_gain, ln1_bias, qkv_weight, qv_bias, out_weight, out_bias, ln2_gain, ln2_bias, up_weight, up_bias, down_weight, down_bias)))
    total_rows = tokens.shape[0]
    per_step = 4 if total_rows % 4 == 0 else 1
    count_steps = total_rows // per_step
    token_groups = tokens.astype(jnp.float32).reshape(count_steps, per_step, LEN, D)
    seg_groups = segment_ids.reshape(count_steps, per_step, LEN)
    cot_groups = cotangent.astype(jnp.float32).reshape(count_steps, per_step, LEN, D)

    def advance(carry, item):
        token_block, seg_block, cot_block = item

        def forward(inputs, weights):
            return layer_block(inputs, seg_block, weights)
        result, pull = jax.vjp(forward, token_block, params)
        grad_tokens, grad_params = pull(cot_block)
        carry = jax.tree.map(add_pair, carry, grad_params)
        return (carry, (result.astype(jnp.bfloat16), grad_tokens))
    start = tuple((jnp.zeros_like(member) for member in params))
    grads, (results, grad_tok) = lax.scan(advance, start, (token_groups, seg_groups, cot_groups))
    out_tokens = results.reshape(total_rows, LEN, D)
    grad_input = grad_tok.reshape(total_rows, LEN, D)
    new_qkv = 0.9 * avg_qkv + 0.1 * params[2]
    new_out = 0.9 * avg_out + 0.1 * params[4]
    new_up = 0.9 * avg_up + 0.1 * params[8]
    new_down = 0.9 * avg_down + 0.1 * params[10]
    return (out_tokens, grad_input, grads[0], grads[1], grads[2], grads[3], grads[4], grads[5], grads[6], grads[7], grads[8], grads[9], grads[10], grads[11], new_qkv, new_out, new_up, new_down)
```

```python
import functools

import jax
import jax.numpy as jnp
from jax import lax
from jax.experimental import pallas as pl
from jax.experimental.pallas import tpu as pltpu
from jax.sharding import Mesh
from jax.sharding import PartitionSpec as P

HEADS = 12
HEAD_DIM = 64
CLIPS = 6


def layer_norm(value, gain, bias):
    middle = jnp.mean(value, axis=-1, keepdims=True)
    centred = value - middle
    spread = jnp.mean(centred * centred, axis=-1, keepdims=True)
    return centred * lax.rsqrt(spread + 1e-06) * gain + bias


def exact_gelu(value):
    return jax.nn.gelu(value, approximate=False)


def permitted(seg_query, seg_key, pos_query, pos_key):
    same_clip = seg_query[:, :, None] == seg_key[:, None, :]
    open_key = (seg_key != CLIPS - 1)[:, None, :]
    diagonal = (pos_query[:, None] == pos_key[None, :])[None]
    return (same_clip & (open_key | diagonal))[:, :, None, :]


def scores(query_part, key_part):
    return 0.125 * jnp.einsum(
        "rqhe,rkhe->rqhk", query_part, key_part, preferred_element_type=jnp.float32
    )


def exponent(score_vals, allowed):
    return jnp.where(allowed, jnp.exp(jnp.where(allowed, score_vals, 0.0)), 0.0)


def on_device(
    tokens,
    segment_ids,
    cotangent,
    ln1_gain,
    ln1_bias,
    qkv_weight,
    qv_bias,
    out_weight,
    out_bias,
    ln2_gain,
    ln2_bias,
    up_weight,
    up_bias,
    down_weight,
    down_bias,
    avg_qkv,
    avg_out,
    avg_up,
    avg_down,
):
    f32 = jnp.float32
    bf16 = jnp.bfloat16
    rows_here, shard_len, width = tokens.shape
    count_rows = rows_here * shard_len
    own_pos = lax.axis_index("seq") * shard_len + jnp.arange(shard_len, dtype=jnp.int32)
    head_shape = (rows_here, shard_len, HEADS, HEAD_DIM)
    gain_one, bias_one, w_qkv, b_qv, w_out, b_out = (
        lax.all_gather(ln1_gain, ("seq", "rows"), axis=0, tiled=True),
        lax.all_gather(ln1_bias, ("seq", "rows"), axis=0, tiled=True),
        lax.all_gather(qkv_weight, ("seq", "rows"), axis=0, tiled=True),
        lax.all_gather(qv_bias, ("seq", "rows"), axis=0, tiled=True),
        lax.all_gather(out_weight, ("seq", "rows"), axis=0, tiled=True),
        lax.all_gather(out_bias, ("seq", "rows"), axis=0, tiled=True),
    )
    residual = tokens.astype(f32).reshape(count_rows, width)
    normed, norm_one_pull = jax.vjp(
        layer_norm, residual, gain_one.astype(f32), bias_one.astype(f32)
    )
    normed_low = normed.astype(bf16)
    mixed = jnp.dot(normed_low, w_qkv, preferred_element_type=f32)
    bias_qv = b_qv.astype(f32)
    query_heads = (mixed[:, :width] + bias_qv[:width]).astype(bf16).reshape(head_shape)
    key_heads = mixed[:, width : 2 * width].astype(bf16).reshape(head_shape)
    value_heads = (mixed[:, 2 * width :] + bias_qv[width:]).astype(bf16).reshape(head_shape)
    start_state = (jnp.zeros((rows_here, shard_len, HEADS), f32), jnp.zeros(head_shape, f32))
    piece_keys = lax.all_gather(key_heads, "seq", axis=1, tiled=True)
    piece_values = lax.all_gather(value_heads, "seq", axis=1, tiled=True)
    piece_seg = lax.all_gather(segment_ids, "seq", axis=1, tiled=True)
    piece_len = piece_keys.shape[1]
    block_len = min(piece_len, shard_len)

    def forward_advance(turn, state):
        totals, weighted = state
        offset = turn * block_len
        key_block = lax.dynamic_slice_in_dim(piece_keys, offset, block_len, 1)
        value_block = lax.dynamic_slice_in_dim(piece_values, offset, block_len, 1)
        seg_block = lax.dynamic_slice_in_dim(piece_seg, offset, block_len, 1)
        key_pos = offset + jnp.arange(block_len, dtype=jnp.int32)
        allowed = permitted(segment_ids, seg_block, own_pos, key_pos)
        expo = exponent(scores(query_heads, key_block), allowed)
        totals = totals + jnp.sum(expo, axis=-1)
        weighted = weighted + jnp.einsum(
            "rqhk,rkhe->rqhe", expo.astype(bf16), value_block, preferred_element_type=f32
        )
        return (totals, weighted)

    totals, weighted = lax.fori_loop(0, piece_len // block_len, forward_advance, start_state)
    attended = weighted / totals[..., None]
    attn_in = attended.reshape(count_rows, width).astype(bf16)
    middle = residual + jnp.dot(attn_in, w_out, preferred_element_type=f32) + b_out.astype(f32)
    gain_two, bias_two, w_up, b_up, w_down, b_down = (
        lax.all_gather(ln2_gain, ("seq", "rows"), axis=0, tiled=True),
        lax.all_gather(ln2_bias, ("seq", "rows"), axis=0, tiled=True),
        lax.all_gather(up_weight, ("seq", "rows"), axis=0, tiled=True),
        lax.all_gather(up_bias, ("seq", "rows"), axis=0, tiled=True),
        lax.all_gather(down_weight, ("seq", "rows"), axis=0, tiled=True),
        lax.all_gather(down_bias, ("seq", "rows"), axis=0, tiled=True),
    )
    normed_two, norm_two_pull = jax.vjp(
        layer_norm, middle, gain_two.astype(f32), bias_two.astype(f32)
    )
    normed_two_low = normed_two.astype(bf16)
    hidden_pre = jnp.dot(normed_two_low, w_up, preferred_element_type=f32) + b_up.astype(f32)
    hidden, gelu_pull = jax.vjp(exact_gelu, hidden_pre)
    hidden_low = hidden.astype(bf16)
    final = middle + jnp.dot(hidden_low, w_down, preferred_element_type=f32) + b_down.astype(f32)
    out_tokens = final.astype(bf16).reshape(tokens.shape)
    w_up_back, w_down_back = (
        lax.all_gather(up_weight, ("seq", "rows"), axis=0, tiled=True),
        lax.all_gather(down_weight, ("seq", "rows"), axis=0, tiled=True),
    )
    grad_out = cotangent.astype(f32).reshape(count_rows, width)
    grad_low = grad_out.astype(bf16)
    grad_down = jnp.einsum("nf,nd->fd", hidden_low, grad_low, preferred_element_type=f32)
    grad_down_b = jnp.sum(grad_low, axis=0, dtype=f32)
    grad_hidden = jnp.einsum("nd,fd->nf", grad_low, w_down_back, preferred_element_type=f32)
    (grad_pre,) = gelu_pull(grad_hidden)
    grad_pre_low = grad_pre.astype(bf16)
    grad_up = jnp.einsum("nd,nf->df", normed_two_low, grad_pre_low, preferred_element_type=f32)
    grad_up_b = jnp.sum(grad_pre_low, axis=0, dtype=f32)
    grad_normed_two = jnp.einsum("nf,df->nd", grad_pre_low, w_up_back, preferred_element_type=f32)
    grad_mid_norm, grad_gain_two, grad_bias_two = norm_two_pull(grad_normed_two)
    grad_mid = grad_out + grad_mid_norm
    mlp_sums = (
        lax.psum_scatter(grad_gain_two, ("seq", "rows"), scatter_dimension=0, tiled=True),
        lax.psum_scatter(grad_bias_two, ("seq", "rows"), scatter_dimension=0, tiled=True),
        lax.psum_scatter(grad_up, ("seq", "rows"), scatter_dimension=0, tiled=True),
        lax.psum_scatter(grad_up_b, ("seq", "rows"), scatter_dimension=0, tiled=True),
        lax.psum_scatter(grad_down, ("seq", "rows"), scatter_dimension=0, tiled=True),
        lax.psum_scatter(grad_down_b, ("seq", "rows"), scatter_dimension=0, tiled=True),
    )
    w_qkv_back, w_out_back = (
        lax.all_gather(qkv_weight, ("seq", "rows"), axis=0, tiled=True),
        lax.all_gather(out_weight, ("seq", "rows"), axis=0, tiled=True),
    )
    grad_mid_low = grad_mid.astype(bf16)
    grad_wout = jnp.einsum("nd,ne->de", attn_in, grad_mid_low, preferred_element_type=f32)
    grad_bout = jnp.sum(grad_mid_low, axis=0, dtype=f32)
    grad_att = jnp.einsum(
        "ne,de->nd", grad_mid_low, w_out_back, preferred_element_type=f32
    ).reshape(head_shape)
    grad_acc = (grad_att / totals[..., None]).astype(bf16)
    shift_low = (jnp.sum(grad_att * attended, axis=-1) / totals).astype(bf16)
    shift_wide = shift_low.astype(f32)
    query_piece_keys = lax.all_gather(key_heads, "seq", axis=1, tiled=True)
    query_piece_values = lax.all_gather(value_heads, "seq", axis=1, tiled=True)
    query_piece_seg = lax.all_gather(segment_ids, "seq", axis=1, tiled=True)
    piece_len = query_piece_keys.shape[1]
    query_block_len = min(piece_len, shard_len)

    def query_advance(turn, grad_query):
        offset = turn * query_block_len
        key_block = lax.dynamic_slice_in_dim(query_piece_keys, offset, query_block_len, 1)
        value_block = lax.dynamic_slice_in_dim(query_piece_values, offset, query_block_len, 1)
        seg_block = lax.dynamic_slice_in_dim(query_piece_seg, offset, query_block_len, 1)
        key_pos = offset + jnp.arange(query_block_len, dtype=jnp.int32)
        allowed = permitted(segment_ids, seg_block, own_pos, key_pos)
        expo = exponent(scores(query_heads, key_block), allowed)
        inner = jnp.einsum("rqhe,rkhe->rqhk", grad_acc, value_block, preferred_element_type=f32)
        grad_score = (expo * (inner - shift_wide[..., None])).astype(bf16)
        return grad_query + jnp.einsum(
            "rqhk,rkhe->rqhe", grad_score, key_block, preferred_element_type=f32
        )

    grad_query = lax.fori_loop(
        0, piece_len // query_block_len, query_advance, jnp.zeros(head_shape, f32)
    )
    key_start = (jnp.zeros(head_shape, f32), jnp.zeros(head_shape, f32))
    piece_queries = lax.all_gather(query_heads, "seq", axis=1, tiled=True)
    piece_grads = lax.all_gather(grad_acc, "seq", axis=1, tiled=True)
    key_piece_seg = lax.all_gather(segment_ids, "seq", axis=1, tiled=True)
    piece_shift = lax.all_gather(shift_low, "seq", axis=1, tiled=True)
    piece_len = piece_queries.shape[1]
    key_block_len = min(piece_len, shard_len)

    def key_advance(turn, state):
        grad_key, grad_value = state
        offset = turn * key_block_len
        query_block = lax.dynamic_slice_in_dim(piece_queries, offset, key_block_len, 1)
        grad_block = lax.dynamic_slice_in_dim(piece_grads, offset, key_block_len, 1)
        seg_block = lax.dynamic_slice_in_dim(key_piece_seg, offset, key_block_len, 1)
        shift_block = lax.dynamic_slice_in_dim(piece_shift, offset, key_block_len, 1).astype(f32)
        query_pos = offset + jnp.arange(key_block_len, dtype=jnp.int32)
        allowed = permitted(seg_block, segment_ids, query_pos, own_pos)
        expo = exponent(scores(query_block, key_heads), allowed)
        inner = jnp.einsum("rqhe,rkhe->rqhk", grad_block, value_heads, preferred_element_type=f32)
        grad_score = (expo * (inner - shift_block[..., None])).astype(bf16)
        grad_key = grad_key + jnp.einsum(
            "rqhk,rqhe->rkhe", grad_score, query_block, preferred_element_type=f32
        )
        grad_value = grad_value + jnp.einsum(
            "rqhk,rqhe->rkhe", expo.astype(bf16), grad_block, preferred_element_type=f32
        )
        return (grad_key, grad_value)

    grad_key, grad_value = lax.fori_loop(0, piece_len // key_block_len, key_advance, key_start)
    grad_q_low = (0.125 * grad_query).astype(bf16).reshape(count_rows, width)
    grad_k_low = (0.125 * grad_key).astype(bf16).reshape(count_rows, width)
    grad_v_low = grad_value.astype(bf16).reshape(count_rows, width)
    grad_mixed = jnp.concatenate([grad_q_low, grad_k_low, grad_v_low], axis=1)
    grad_wqkv = jnp.einsum("nd,ne->de", normed_low, grad_mixed, preferred_element_type=f32)
    grad_bqv = jnp.concatenate(
        [jnp.sum(grad_q_low, axis=0, dtype=f32), jnp.sum(grad_v_low, axis=0, dtype=f32)], axis=0
    )
    grad_normed = jnp.einsum("ne,de->nd", grad_mixed, w_qkv_back, preferred_element_type=f32)
    grad_res_norm, grad_gain_one, grad_bias_one = norm_one_pull(grad_normed)
    grad_input = (grad_mid + grad_res_norm).reshape(tokens.shape)
    attn_sums = (
        lax.psum_scatter(grad_gain_one, ("seq", "rows"), scatter_dimension=0, tiled=True),
        lax.psum_scatter(grad_bias_one, ("seq", "rows"), scatter_dimension=0, tiled=True),
        lax.psum_scatter(grad_wqkv, ("seq", "rows"), scatter_dimension=0, tiled=True),
        lax.psum_scatter(grad_bqv, ("seq", "rows"), scatter_dimension=0, tiled=True),
        lax.psum_scatter(grad_wout, ("seq", "rows"), scatter_dimension=0, tiled=True),
        lax.psum_scatter(grad_bout, ("seq", "rows"), scatter_dimension=0, tiled=True),
    )
    new_qkv = 0.9 * avg_qkv + 0.1 * qkv_weight.astype(f32)
    new_out = 0.9 * avg_out + 0.1 * out_weight.astype(f32)
    new_up = 0.9 * avg_up + 0.1 * up_weight.astype(f32)
    new_down = 0.9 * avg_down + 0.1 * down_weight.astype(f32)
    return (
        out_tokens,
        grad_input,
        attn_sums[0],
        attn_sums[1],
        attn_sums[2],
        attn_sums[3],
        attn_sums[4],
        attn_sums[5],
        mlp_sums[0],
        mlp_sums[1],
        mlp_sums[2],
        mlp_sums[3],
        mlp_sums[4],
        mlp_sums[5],
        new_qkv,
        new_out,
        new_up,
        new_down,
    )


f32 = jnp.float32
bf16 = jnp.bfloat16
NT = (((1,), (1,)), ((), ()))
LOG2E = 1.4426950408889634
SCORE = 0.125 * LOG2E
BIG = 16384.0
VMEM_BYTES = 60 * 1024 * 1024
TQ_F, TK_F = 256, 256
TK_B, TQ_B = 128, 256
LANE_LOG = 41
LANE_PAD = 44


def kernel_params(flops, bytes_accessed, transcendentals=0, order=("arbitrary",)):
    return dict(
        compiler_params=pltpu.CompilerParams(
            vmem_limit_bytes=VMEM_BYTES, dimension_semantics=order
        ),
        cost_estimate=pl.CostEstimate(
            flops=int(flops), bytes_accessed=int(bytes_accessed), transcendentals=int(transcendentals)
        ),
    )


def standardise(value):
    middle = jnp.mean(value, axis=-1, keepdims=True)
    centred = value - middle
    spread = jnp.mean(centred * centred, axis=-1, keepdims=True)
    rstd = lax.rsqrt(spread + 1e-06)
    return centred * rstd, rstd


def norm_pull(grad_normed, gain, xhat, rstd):
    scaled = grad_normed * gain
    first = jnp.mean(scaled, axis=-1, keepdims=True)
    second = jnp.mean(scaled * xhat, axis=-1, keepdims=True)
    return rstd * (scaled - first - xhat * second)


def gelu_pair(x):
    size = jnp.abs(x)
    t = 1.0 / (1.0 + 0.23164189 * size)
    bell = jnp.exp2(x * x * (-0.5 * LOG2E))
    poly = t * (0.127414796 + t * (-0.142248368 + t * (0.7107068705 + t * (-0.7265760135 + t * 0.5307027145))))
    tail = poly * bell
    phi = jnp.where(x >= 0.0, 1.0 - tail, tail)
    return x * phi, phi + x * bell * 0.3989422804014327


def project_kernel(own_ref, other_ref, w_ref, pack_ref, shift_ref, normed_ref, mixed_ref):
    which = pl.program_id(0)
    value = jnp.where(which == 0, own_ref[0].astype(f32), other_ref[0].astype(f32))
    xhat, _ = standardise(value)
    normed = (xhat * pack_ref[0:1, :] + pack_ref[1:2, :]).astype(bf16)
    normed_ref[0, 0] = normed
    mixed = jnp.dot(normed, w_ref[...], preferred_element_type=f32) + shift_ref[...]
    mixed_ref[0, 0] = mixed.astype(bf16)


def attend_kernel(flag_ref, mixed_ref, qx_ref, kx_ref, out_ref, lse_ref, q_s, k_s, v_s, acc_s):
    row = pl.program_id(0)
    length = q_s.shape[1]
    heads = q_s.shape[0]
    wide = heads * HEAD_DIM
    half = length // 2
    low = lax.broadcasted_iota(jnp.int32, (length, 128), 1) < HEAD_DIM
    qx = qx_ref[0].astype(f32)
    kx = kx_ref[0].astype(f32)
    for pair in range(heads // 2):
        lanes = slice(128 * pair, 128 * pair + 128)
        q = mixed_ref[:, 0, :, lanes].reshape(length, 128).astype(f32)
        k = mixed_ref[:, 0, :, wide + 128 * pair : wide + 128 * pair + 128].reshape(length, 128).astype(f32)
        v = mixed_ref[:, 0, :, 2 * wide + 128 * pair : 2 * wide + 128 * pair + 128].reshape(length, 128).astype(f32)
        q_s[2 * pair] = jnp.where(low, q, qx).astype(bf16)
        q_s[2 * pair + 1] = jnp.where(low, qx, q).astype(bf16)
        k_s[2 * pair] = jnp.where(low, k, kx).astype(bf16)
        k_s[2 * pair + 1] = jnp.where(low, kx, k).astype(bf16)
        v_s[2 * pair] = jnp.where(low, v, 1.0).astype(bf16)
        v_s[2 * pair + 1] = jnp.where(low, 1.0, v).astype(bf16)
    acc_s[...] = jnp.zeros_like(acc_s)
    key_blocks = length // TK_F

    def step(index, carry):
        @pl.when(flag_ref[row, index] != 0)
        def _():
            q_at = pl.ds(pl.multiple_of((index // key_blocks) * TQ_F, TQ_F), TQ_F)
            k_at = pl.ds(pl.multiple_of((index % key_blocks) * TK_F, TK_F), TK_F)
            for head in range(heads):
                score = lax.dot_general(
                    q_s[head, q_at, :], k_s[head, k_at, :], NT, preferred_element_type=f32
                )
                expo = jnp.exp2(score * SCORE).astype(bf16)
                acc_s[head, q_at, :] += jnp.dot(expo, v_s[head, k_at, :], preferred_element_type=f32)

        return carry

    lax.fori_loop(0, (length // TQ_F) * key_blocks, step, 0)
    for pair in range(heads // 2):
        lanes = slice(128 * pair, 128 * pair + 128)
        first, second = acc_s[2 * pair], acc_s[2 * pair + 1]
        top = jnp.where(low, first, second)
        crossed = jnp.where(low, second, first)
        totals = pltpu.roll(crossed, HEAD_DIM, 1)
        attended = (top / totals).astype(bf16)
        lse = 8.0 * jnp.log(crossed)
        for side in range(2):
            out_ref[side, 0, :, lanes] = attended[side * half : (side + 1) * half]
            lse_ref[side, 0, :, lanes] = lse[side * half : (side + 1) * half]


def forward_kernel(
    side_ref, x_ref, mine_ref, recv_ref, wo_ref, up_ref, down_ref, grad_ref, pack_ref,
    out_ref, middle_ref, normed_ref, slope_ref, gdown_ref, bias_ref, acc_s,
):
    turn = pl.program_id(0)
    side = side_ref[0]
    chunks = acc_s.shape[0]
    size = acc_s.shape[2]
    middle = (
        x_ref[0].astype(f32)
        + jnp.dot(mine_ref[0, 0], wo_ref[side], preferred_element_type=f32)
        + jnp.dot(recv_ref[0], wo_ref[1 - side], preferred_element_type=f32)
        + pack_ref[2:3, :]
    )
    middle_ref[0] = middle
    xhat, _ = standardise(middle)
    normed = (xhat * pack_ref[3:4, :] + pack_ref[4:5, :]).astype(bf16)
    normed_ref[0] = normed
    grad = grad_ref[0]
    grad_t = grad.T
    total = middle + pack_ref[5:6, :]

    @pl.when(turn == 0)
    def _():
        acc_s[...] = jnp.zeros_like(acc_s)
        bias_ref[...] = jnp.zeros_like(bias_ref)

    bias_ref[0:1, :] += jnp.sum(grad.astype(f32), axis=0, keepdims=True)
    for f in range(chunks):
        at = slice(f * size, (f + 1) * size)
        pre = jnp.dot(normed, up_ref[:, at], preferred_element_type=f32) + pack_ref[8 + f : 9 + f, :]
        hidden, slope = gelu_pair(pre)
        slope_ref[0, :, at] = slope.astype(bf16)
        hidden = hidden.astype(bf16)
        total = total + jnp.dot(hidden, down_ref[at, :], preferred_element_type=f32)
        acc_s[f] += jnp.dot(grad_t, hidden, preferred_element_type=f32)
    out_ref[0] = total.astype(bf16)

    @pl.when(turn == pl.num_programs(0) - 1)
    def _():
        half = chunks // 2
        for f in range(chunks):
            target = jnp.where(side == f // half, 0, 1)
            gdown_ref[target, f % half] = acc_s[f].T.astype(bf16)


def backward_kernel(
    side_ref, grad_ref, slope_ref, up_ref, down_ref, normed_ref, middle_ref, pack_ref,
    gmid_ref, glow_ref, gup_ref, gbias_ref, gnorm_ref, acc_s,
):
    turn = pl.program_id(0)
    side = side_ref[0]
    chunks = acc_s.shape[0]
    size = acc_s.shape[2]
    grad = grad_ref[0]
    normed_t = normed_ref[0].T

    @pl.when(turn == 0)
    def _():
        acc_s[...] = jnp.zeros_like(acc_s)
        gbias_ref[...] = jnp.zeros_like(gbias_ref)
        gnorm_ref[...] = jnp.zeros_like(gnorm_ref)

    gnormed = None
    for f in range(chunks):
        at = slice(f * size, (f + 1) * size)
        ghidden = lax.dot_general(grad, down_ref[at, :], NT, preferred_element_type=f32)
        gpre = (ghidden * slope_ref[0, :, at].astype(f32)).astype(bf16)
        gbias_ref[f] += jnp.sum(gpre.astype(f32), axis=0, keepdims=True)
        part = lax.dot_general(gpre, up_ref[:, at], NT, preferred_element_type=f32)
        gnormed = part if gnormed is None else gnormed + part
        acc_s[f] += jnp.dot(normed_t, gpre, preferred_element_type=f32)
    xhat, rstd = standardise(middle_ref[0])
    gmid = grad.astype(f32) + norm_pull(gnormed, pack_ref[3:4, :], xhat, rstd)
    gmid_ref[0] = gmid
    low = gmid.astype(bf16)
    glow_ref[0] = low
    gnorm_ref[0:1, :] += jnp.sum(gnormed * xhat, axis=0, keepdims=True)
    gnorm_ref[1:2, :] += jnp.sum(gnormed, axis=0, keepdims=True)
    gnorm_ref[2:3, :] += jnp.sum(low.astype(f32), axis=0, keepdims=True)

    @pl.when(turn == pl.num_programs(0) - 1)
    def _():
        rows = acc_s.shape[1] // 2
        mine = pl.ds(pl.multiple_of(side * rows, rows), rows)
        other = pl.ds(pl.multiple_of((1 - side) * rows, rows), rows)
        for f in range(chunks):
            gup_ref[0, f] = acc_s[f, mine, :].astype(bf16)
            gup_ref[1, f] = acc_s[f, other, :].astype(bf16)


def attend_back_kernel(
    flag_ref, mixed_ref, lse_ref, att_ref, own_ref, other_ref, wo_ref, qx_ref, kx_ref,
    gmixed_ref, gout_ref, gbias_ref,
    q_s, k_s, v_s, d_s, qz_s, dz_s, kt_s, gq_s, gk_s, gv_s, go_s,
):
    row = pl.program_id(0)
    heads, length = q_s.shape[0], q_s.shape[1]
    wide = heads * HEAD_DIM
    half = length // 2
    lane = lax.broadcasted_iota(jnp.int32, (length, 128), 1)
    low = lane < HEAD_DIM
    place = lane % HEAD_DIM
    square_row = lax.broadcasted_iota(jnp.int32, (128, 128), 0) < HEAD_DIM
    square_col = lax.broadcasted_iota(jnp.int32, (128, 128), 1) < HEAD_DIM
    crossing = jnp.where(square_row == square_col, 0.0, 1.0).astype(bf16)
    qx = qx_ref[0].astype(f32)
    kx = kx_ref[0].astype(f32)
    vx = jnp.where(place < 2, 1.0, 0.0)

    @pl.when(row == 0)
    def _():
        go_s[...] = jnp.zeros_like(go_s)
        gbias_ref[...] = jnp.zeros_like(gbias_ref)

    att = att_ref[:, 0].reshape(length, wide)
    gates = jnp.concatenate([own_ref[0], other_ref[0]], axis=0)
    go_s[...] += jnp.dot(att.T, gates, preferred_element_type=f32)
    gatt = lax.dot_general(gates, wo_ref[...], NT, preferred_element_type=f32)
    for pair in range(heads // 2):
        lanes = slice(128 * pair, 128 * pair + 128)
        q = mixed_ref[:, 0, :, lanes].reshape(length, 128).astype(f32)
        k = mixed_ref[:, 0, :, wide + 128 * pair : wide + 128 * pair + 128].reshape(length, 128).astype(f32)
        v = mixed_ref[:, 0, :, 2 * wide + 128 * pair : 2 * wide + 128 * pair + 128].reshape(length, 128).astype(f32)
        lse = -lse_ref[:, 0, :, lanes].reshape(length, 128)
        lse_a = lse.astype(bf16).astype(f32)
        lse_b = (lse - lse_a).astype(bf16).astype(f32)
        lse_c = lse - lse_a - lse_b
        ext = jnp.where(
            place == LANE_LOG,
            lse_a,
            jnp.where(place == LANE_LOG + 1, lse_b, jnp.where(place == LANE_LOG + 2, lse_c, qx)),
        )
        q_s[2 * pair] = jnp.where(low, q, ext).astype(bf16)
        q_s[2 * pair + 1] = jnp.where(low, ext, q).astype(bf16)
        k_s[2 * pair] = jnp.where(low, k, kx).astype(bf16)
        k_s[2 * pair + 1] = jnp.where(low, kx, k).astype(bf16)
        v_s[2 * pair] = jnp.where(low, v, vx).astype(bf16)
        v_s[2 * pair + 1] = jnp.where(low, vx, v).astype(bf16)
        d = gatt[:, lanes]
        moved = d * att[:, lanes].astype(f32)
        moved_a = moved.astype(bf16)
        moved_b = (moved - moved_a.astype(f32)).astype(bf16)
        shift = -(
            jnp.dot(moved_a, crossing, preferred_element_type=f32)
            + jnp.dot(moved_b, crossing, preferred_element_type=f32)
        )
        shift_a = shift.astype(bf16).astype(f32)
        dx = jnp.where(place == 0, shift_a, jnp.where(place == 1, shift - shift_a, 0.0))
        d_s[2 * pair] = jnp.where(low, d, dx).astype(bf16)
        d_s[2 * pair + 1] = jnp.where(low, dx, d).astype(bf16)
        qa, qb = jnp.where(low, q, 0.0).astype(bf16), jnp.where(low, 0.0, q).astype(bf16)
        da, db = jnp.where(low, d, 0.0).astype(bf16), jnp.where(low, 0.0, d).astype(bf16)
        for i in range(length // TQ_B):
            at = slice(i * TQ_B, (i + 1) * TQ_B)
            qz_s[pair, i, :TQ_B] = qa[at]
            qz_s[pair, i, TQ_B:] = qb[at]
            dz_s[pair, i, :TQ_B] = da[at]
            dz_s[pair, i, TQ_B:] = db[at]
        kt = k.T.astype(bf16)
        for i in range(length // TK_B):
            kt_s[i, lanes, :] = kt[:, i * TK_B : (i + 1) * TK_B]
    gq_s[...] = jnp.zeros_like(gq_s)
    gk_s[...] = jnp.zeros_like(gk_s)
    gv_s[...] = jnp.zeros_like(gv_s)
    query_blocks = length // TQ_B

    def step(index, carry):
        @pl.when(flag_ref[row, index] != 0)
        def _():
            qi = index % query_blocks
            ki = index // query_blocks
            q_at = pl.ds(pl.multiple_of(qi * TQ_B, TQ_B), TQ_B)
            k_at = pl.ds(pl.multiple_of(ki * TK_B, TK_B), TK_B)
            for pair in range(heads // 2):
                probs, grads = [], []
                for head in (2 * pair, 2 * pair + 1):
                    score = lax.dot_general(
                        k_s[head, k_at, :], q_s[head, q_at, :], NT, preferred_element_type=f32
                    )
                    prob = jnp.exp2(score * SCORE)
                    inner = lax.dot_general(
                        v_s[head, k_at, :], d_s[head, q_at, :], NT, preferred_element_type=f32
                    )
                    gscore = (prob * inner).astype(bf16)
                    probs.append(prob.astype(bf16))
                    grads.append(gscore)
                    at = slice(head * HEAD_DIM, (head + 1) * HEAD_DIM)
                    gq_s[qi, at, :] += jnp.dot(kt_s[ki, at, :], gscore, preferred_element_type=f32)
                gv_s[pair, k_at, :] += jnp.dot(
                    jnp.concatenate(probs, axis=1), dz_s[pair, qi], preferred_element_type=f32
                )
                gk_s[pair, k_at, :] += jnp.dot(
                    jnp.concatenate(grads, axis=1), qz_s[pair, qi], preferred_element_type=f32
                )

        return carry

    lax.fori_loop(0, query_blocks * (length // TK_B), step, 0)
    for i in range(query_blocks):
        gq = (0.125 * gq_s[i].T).astype(bf16)
        at = (i * TQ_B) % half
        gmixed_ref[(i * TQ_B) // half, 0, at : at + TQ_B, 0:wide] = gq
        gbias_ref[0:1, 0:wide] += jnp.sum(gq.astype(f32), axis=0, keepdims=True)
    for pair in range(heads // 2):
        gk = (0.125 * gk_s[pair]).astype(bf16)
        gv = gv_s[pair].astype(bf16)
        k_lanes = slice(wide + 128 * pair, wide + 128 * pair + 128)
        v_lanes = slice(2 * wide + 128 * pair, 2 * wide + 128 * pair + 128)
        gbias_ref[0:1, v_lanes] += jnp.sum(gv.astype(f32), axis=0, keepdims=True)
        for side in range(2):
            gmixed_ref[side, 0, :, k_lanes] = gk[side * half : (side + 1) * half]
            gmixed_ref[side, 0, :, v_lanes] = gv[side * half : (side + 1) * half]

    @pl.when(row == pl.num_programs(0) - 1)
    def _():
        gout_ref[...] = go_s[...].astype(bf16)


def input_kernel(gmixed_ref, w_ref, recv_ref, x_ref, gmid_ref, pack_ref, ginput_ref, gnorm_ref):
    turn = pl.program_id(0)
    gnormed = lax.dot_general(gmixed_ref[0, 0], w_ref[...], NT, preferred_element_type=f32)
    gnormed = gnormed + recv_ref[0].astype(f32)
    xhat, rstd = standardise(x_ref[0].astype(f32))
    ginput_ref[0] = gmid_ref[0] + norm_pull(gnormed, pack_ref[0:1, :], xhat, rstd)

    @pl.when(turn == 0)
    def _():
        gnorm_ref[...] = jnp.zeros_like(gnorm_ref)

    gnorm_ref[0:1, :] += jnp.sum(gnormed * xhat, axis=0, keepdims=True)
    gnorm_ref[1:2, :] += jnp.sum(gnormed, axis=0, keepdims=True)


def partner(value):
    return lax.ppermute(value, "seq", [(0, 1), (1, 0)])


def exchange(value, axis):
    return lax.all_to_all(value, axis, 0, 0, tiled=True)


def spread_line(value, lines):
    return exchange(jnp.broadcast_to(value[None], (lines,) + value.shape), "line")


def flip(value, axis):
    return lax.ppermute(value, axis, [(0, 1), (1, 0)])


def in_order(index, own, received):
    return jnp.where(index == 0, jnp.stack([own, received]), jnp.stack([received, own]))


def spread_plane(value, axes):
    first, second = axes
    pairs = in_order(lax.axis_index(first), value, flip(value, first))
    return pairs, flip(pairs, second)


def after(value, *others):
    return lax.optimization_barrier((value,) + others)[0]


def place(pieces, spots, axes, rows, cols):
    moved = [jnp.swapaxes(piece[:, :, rows, cols], 0, 1) for piece in pieces]
    out = None
    for piece, (side, spot) in zip(moved, spots):
        if axes == ("x", "y"):
            piece, start = piece[None, :, None], (side, 0, spot, 0, 0, 0)
            whole = (2, piece.shape[1], 2, 2) + piece.shape[4:]
        else:
            piece, start = piece[None, :, :, None], (side, 0, 0, spot, 0, 0)
            whole = (2, piece.shape[1], 2, 2) + piece.shape[4:]
        if out is None:
            out = jnp.broadcast_to(piece, whole)
        else:
            out = lax.dynamic_update_slice(out, piece, start)
    return out


def sum_rows(value):
    across = jnp.sum(exchange(value, ("y", "x")).astype(f32), axis=0).astype(bf16)
    return jnp.sum(exchange(across, "line").astype(f32), axis=0)


def masks(seg, pos):
    pad = seg == CLIPS - 1
    lane = jnp.arange(128, dtype=jnp.int32) % HEAD_DIM
    seg, pos, pad = seg[..., None], pos[..., None], pad[..., None]
    clip_lane = lane < CLIPS - 1
    digit = jnp.where(lane < 9, pos // 256, jnp.where(lane < 25, (pos // 16) % 16, pos % 16))
    digit_base = jnp.where(lane < 9, 5, jnp.where(lane < 25, 9, 25))
    digit_lane = (lane >= 5) & (lane < LANE_LOG)
    hit_clip = lane == seg
    hit_digit = lane - digit_base == digit
    log_lane = (lane >= LANE_LOG) & (lane < LANE_PAD)
    pad_lane = lane == LANE_PAD
    bad = (clip_lane & ~hit_clip) | (digit_lane & pad & ~hit_digit) | (pad_lane & ~pad)
    qx = jnp.where(bad, -BIG, 0.0).astype(bf16)
    on = (clip_lane & hit_clip) | (digit_lane & pad & hit_digit) | log_lane | (pad_lane & pad)
    kx = jnp.where(on, 1.0, 0.0).astype(bf16)
    return qx, kx


def block_flags(ident, rows_block, cols_block):
    count, length = ident.shape
    by_row = ident.reshape(count, length // rows_block, rows_block)
    by_col = ident.reshape(count, length // cols_block, cols_block)
    low_row, high_row = jnp.min(by_row, axis=2)[:, :, None], jnp.max(by_row, axis=2)[:, :, None]
    low_col, high_col = jnp.min(by_col, axis=2)[:, None, :], jnp.max(by_col, axis=2)[:, None, :]
    meets = (low_row <= high_col) & (low_col <= high_row)
    return meets.astype(jnp.int32).reshape(count, -1)


def pair_device(
    lines, planes,
    tokens, segment_ids, cotangent, ln1_gain, ln1_bias, qkv_weight, qv_bias, out_weight, out_bias,
    ln2_gain, ln2_bias, up_weight, up_bias, down_weight, down_bias, avg_qkv, avg_out, avg_up, avg_down,
):
    count, part, width = tokens.shape
    length = 2 * part
    wide = width // 2
    heads = HEADS // 2
    hidden_width = up_weight.shape[1]
    chunks = hidden_width // width
    share = qkv_weight.shape[0]
    side = lax.axis_index("seq").astype(jnp.int32)
    first = side == 0
    side_arr = side.reshape(1)
    const = lambda *shape: pl.BlockSpec(shape, lambda *_: (0,) * len(shape), pipeline_mode=pl.Buffered(1))
    row_block = lambda *shape: pl.BlockSpec((1,) + shape, lambda j, *_: (j,) + (0,) * len(shape))
    both_block = lambda lanes: pl.BlockSpec((2, 1, part, lanes), lambda j, *_: (0, j, 0, 0))
    own_block = lambda lanes: pl.BlockSpec((1, 1, part, lanes), lambda j, *_: (0, j, 0, 0))

    split_cols = qkv_weight.reshape(share, 3, 2, wide)
    pick = lambda which: lax.dynamic_index_in_dim(split_cols, which, 2, keepdims=False).reshape(share, 3 * wide)
    small = jnp.stack([ln1_gain, ln1_bias, out_bias, ln2_gain, ln2_bias, down_bias], axis=0)
    small = jnp.concatenate([small, qv_bias.reshape(2, share), up_bias.reshape(chunks, share)], axis=0)
    small_rows = small.shape[0]
    small = jnp.pad(small.T, ((0, 0), (0, 128 - small_rows)))
    mine = jnp.concatenate([pick(side), small], axis=1)
    give = jnp.concatenate([pick(1 - side), small], axis=1)
    take = partner(give)
    tokens_other = partner(tokens)
    seg_other = partner(segment_ids)
    start = jnp.where(first, jnp.stack([mine, take]), jnp.stack([take, mine]))
    x_at, y_at = lax.axis_index("x"), lax.axis_index("y")
    first_line = spread_line(start, lines)
    one_m, one_r = spread_plane(first_line[:, 0], ("x", "y"))
    two_m, two_r = spread_plane(first_line[:, 1], ("y", "x"))
    one = in_order(y_at, one_m, one_r).transpose(2, 0, 1, 3, 4)
    two = in_order(x_at, two_m, two_r).transpose(2, 1, 0, 3, 4)
    first_all = jnp.stack([one, two])
    w_qkv = first_all[..., : 3 * wide].reshape(width, 3 * wide)
    small_all = jnp.moveaxis(first_all[..., 3 * wide : 3 * wide + small_rows].astype(f32), -1, -2)
    vector = lambda i: small_all[..., i, :].reshape(width)
    bias_qv = small_all[..., 6:8, :].reshape(2 * width)
    bias_up = small_all[..., 8 : 8 + chunks, :].reshape(chunks, width)
    pack = jnp.concatenate(
        [jnp.stack([vector(i) for i in range(6)]), jnp.zeros((2, width), f32), bias_up, jnp.zeros((4, width), f32)],
        axis=0,
    )
    bias_here = lambda base: lax.dynamic_slice_in_dim(bias_qv, base + side * wide, wide, 0)
    shift = jnp.concatenate([bias_here(0), jnp.zeros((wide,), f32), bias_here(width)])[None]

    up_start, down_start = up_weight, jnp.concatenate([down_weight, out_weight], axis=0)
    up_line = spread_line(after(up_start, first_line), lines)
    down_line = spread_line(after(down_start, up_line), lines)
    up_line, down_line = after(up_line, one_r, two_r), after(down_line, one_r, two_r)
    up_pieces = spread_plane(up_line, ("x", "y"))
    down_pieces = spread_plane(down_line, ("y", "x"))
    up_pieces += (partner(up_pieces[0]), partner(up_pieces[1]))
    down_pieces += (partner(down_pieces[0]), partner(down_pieces[1]))
    up_spots = ((side, y_at), (side, 1 - y_at), (1 - side, y_at), (1 - side, 1 - y_at))
    down_spots = ((side, x_at), (side, 1 - x_at), (1 - side, x_at), (1 - side, 1 - x_at))
    own_rows, every = chunks * share, slice(None)
    w_up = place(up_pieces, up_spots, ("x", "y"), every, every).reshape(width, hidden_width)
    w_down = place(down_pieces, down_spots, ("y", "x"), slice(0, own_rows), every).reshape(hidden_width, width)
    w_out = place(down_pieces, down_spots, ("y", "x"), slice(own_rows, None), every).reshape(2, wide, width)
    wo_mine = lax.dynamic_index_in_dim(w_out, side, 0, keepdims=False)

    seg = jnp.concatenate([segment_ids, seg_other], axis=1)
    spots = jnp.arange(part, dtype=jnp.int32)
    pos = jnp.concatenate([side * part + spots, (1 - side) * part + spots])
    qx, kx = masks(seg, jnp.broadcast_to(pos, seg.shape))
    ident = jnp.where(seg == CLIPS - 1, CLIPS + pos, seg)
    flags_f = block_flags(ident, TQ_F, TK_F)
    flags_b = block_flags(ident, TK_B, TQ_B)

    sds = jax.ShapeDtypeStruct
    normed, mixed = pl.pallas_call(
        project_kernel,
        grid=(2, count),
        in_specs=[
            pl.BlockSpec((1, part, width), lambda h, j: (jnp.where(h == 0, j, count - 1), 0, 0)),
            pl.BlockSpec((1, part, width), lambda h, j: (jnp.where(h == 0, 0, j), 0, 0)),
            const(width, 3 * wide),
            const(16, width),
            const(1, 3 * wide),
        ],
        out_specs=[
            pl.BlockSpec((1, 1, part, width), lambda h, j: (h, j, 0, 0)),
            pl.BlockSpec((1, 1, part, 3 * wide), lambda h, j: (h, j, 0, 0)),
        ],
        out_shape=[sds((2, count, part, width), bf16), sds((2, count, part, 3 * wide), bf16)],
        name="project",
        **kernel_params(
            2 * 2 * count * part * width * 3 * wide, 20e6, order=("arbitrary", "arbitrary")
        ),
    )(tokens, tokens_other, w_qkv, pack, shift)

    attended, lse = pl.pallas_call(
        attend_kernel,
        grid_spec=pltpu.PrefetchScalarGridSpec(
            num_scalar_prefetch=1,
            grid=(count,),
            in_specs=[both_block(3 * wide), row_block(length, 128), row_block(length, 128)],
            out_specs=[both_block(wide), both_block(wide)],
            scratch_shapes=[pltpu.VMEM((heads, length, 128), bf16)] * 3
            + [pltpu.VMEM((heads, length, 128), f32)],
        ),
        out_shape=[sds((2, count, part, wide), bf16), sds((2, count, part, wide), f32)],
        name="attend",
        **kernel_params(16e9, 20e6, 12e6),
    )(flags_f, mixed, qx, kx)

    attended_recv = partner(attended[1])

    out_tokens, middle, normed_two, slope, gdown, gdown_bias = pl.pallas_call(
        forward_kernel,
        grid_spec=pltpu.PrefetchScalarGridSpec(
            num_scalar_prefetch=1,
            grid=(count,),
            in_specs=[
                row_block(part, width),
                own_block(wide),
                row_block(part, wide),
                const(2, wide, width),
                const(width, hidden_width),
                const(hidden_width, width),
                row_block(part, width),
                const(16, width),
            ],
            out_specs=[
                row_block(part, width),
                row_block(part, width),
                row_block(part, width),
                row_block(part, hidden_width),
                const(2, chunks // 2, width, width),
                const(8, width),
            ],
            scratch_shapes=[pltpu.VMEM((chunks, width, width), f32)],
        ),
        out_shape=[
            sds((count, part, width), bf16),
            sds((count, part, width), f32),
            sds((count, part, width), bf16),
            sds((count, part, hidden_width), bf16),
            sds((2, chunks // 2, width, width), bf16),
            sds((8, width), f32),
        ],
        name="forward",
        **kernel_params(2 * count * part * width * (width + 3 * hidden_width), 45e6, 4.7e6),
    )(side_arr, tokens, attended, attended_recv, w_out, w_up, w_down, cotangent, pack)

    gdown = gdown.reshape(2, hidden_width // 2, width)
    gdown_recv = partner(gdown[1])
    gdown_sum = (gdown[0].astype(f32) + gdown_recv.astype(f32)).astype(bf16)
    gdown_sum = gdown_sum.reshape(lines, planes, chunks * share, width).transpose(1, 0, 2, 3)
    grad_down = sum_rows(gdown_sum)

    gmid, glow, gup, gup_bias, gnorm_two = pl.pallas_call(
        backward_kernel,
        grid_spec=pltpu.PrefetchScalarGridSpec(
            num_scalar_prefetch=1,
            grid=(count,),
            in_specs=[
                row_block(part, width),
                row_block(part, hidden_width),
                const(width, hidden_width),
                const(hidden_width, width),
                row_block(part, width),
                row_block(part, width),
                const(16, width),
            ],
            out_specs=[
                row_block(part, width),
                row_block(part, width),
                const(2, chunks, wide, width),
                const(chunks, 1, width),
                const(8, width),
            ],
            scratch_shapes=[pltpu.VMEM((chunks, width, width), f32)],
        ),
        out_shape=[
            sds((count, part, width), f32),
            sds((count, part, width), bf16),
            sds((2, chunks, wide, width), bf16),
            sds((chunks, 1, width), f32),
            sds((8, width), f32),
        ],
        name="backward",
        **kernel_params(2 * count * part * width * 3 * hidden_width, 45e6),
    )(side_arr, cotangent, slope, w_up, w_down, normed_two, middle, pack)

    glow_other = partner(glow)
    gup_recv = partner(gup[1])
    gup_sum = (gup[0].astype(f32) + gup_recv.astype(f32)).astype(bf16)
    gup_sum = gup_sum.reshape(chunks, lines, planes, share, width).transpose(2, 1, 0, 3, 4)
    grad_up = sum_rows(gup_sum)
    grad_up = grad_up.transpose(1, 0, 2).reshape(share, hidden_width)

    gmixed, gout, gmixed_bias = pl.pallas_call(
        attend_back_kernel,
        grid_spec=pltpu.PrefetchScalarGridSpec(
            num_scalar_prefetch=1,
            grid=(count,),
            in_specs=[
                both_block(3 * wide),
                both_block(wide),
                both_block(wide),
                row_block(part, width),
                row_block(part, width),
                const(wide, width),
                row_block(length, 128),
                row_block(length, 128),
            ],
            out_specs=[both_block(3 * wide), const(wide, width), const(8, 3 * wide)],
            scratch_shapes=[pltpu.VMEM((heads, length, 128), bf16)] * 4
            + [pltpu.VMEM((heads // 2, length // TQ_B, 2 * TQ_B, 128), bf16)] * 2
            + [
                pltpu.VMEM((length // TK_B, wide, TK_B), bf16),
                pltpu.VMEM((length // TQ_B, wide, TQ_B), f32),
                pltpu.VMEM((heads // 2, length, 128), f32),
                pltpu.VMEM((heads // 2, length, 128), f32),
                pltpu.VMEM((wide, width), f32),
            ],
        ),
        out_shape=[
            sds((2, count, part, 3 * wide), bf16),
            sds((wide, width), bf16),
            sds((8, 3 * wide), f32),
        ],
        name="attend_back",
        **kernel_params(50e9, 30e6, 12e6),
    )(flags_b, mixed, lse, attended, glow, glow_other, wo_mine, qx, kx)

    tall = 2 * count * part
    gqkv = lax.dot_general(
        normed.reshape(tall, width),
        gmixed.reshape(tall, 3 * wide),
        (((0,), (0,)), ((), ())),
        preferred_element_type=f32,
    ).astype(bf16)
    give_back = lax.dot_general(
        gmixed[1].reshape(count * part, 3 * wide), w_qkv, NT, preferred_element_type=f32
    ).astype(bf16)
    recv_back = partner(give_back.reshape(count, part, width))

    grad_input, gnorm_one = pl.pallas_call(
        input_kernel,
        grid=(count,),
        in_specs=[
            own_block(3 * wide),
            const(width, 3 * wide),
            row_block(part, width),
            row_block(part, width),
            row_block(part, width),
            const(16, width),
        ],
        out_specs=[row_block(part, width), const(8, width)],
        out_shape=[sds((count, part, width), f32), sds((8, width), f32)],
        name="input_grad",
        **kernel_params(2 * count * part * width * 3 * wide, 25e6),
    )(gmixed, w_qkv, recv_back, tokens, gmid, pack)

    spots_of = lambda vec: vec.reshape(2, lines, planes, 1, share)
    zeros = jnp.zeros((wide,), f32)
    place_half = lambda vec: jnp.concatenate([jnp.where(first, vec, zeros), jnp.where(first, zeros, vec)])
    gqv = jnp.concatenate([place_half(gmixed_bias[0, :wide]), place_half(gmixed_bias[0, 2 * wide :])])
    gup_vec = gup_bias.reshape(hidden_width)
    gsmall = jnp.concatenate(
        [
            spots_of(gnorm_one[0]),
            spots_of(gnorm_one[1]),
            spots_of(gnorm_two[2]),
            spots_of(gnorm_two[0]),
            spots_of(gnorm_two[1]),
            spots_of(gdown_bias[0]),
            gqv.reshape(2, lines, planes, 2, share),
            gup_vec.reshape(2, lines, planes, chunks, share),
        ],
        axis=3,
    )
    gsmall = jnp.pad(jnp.swapaxes(gsmall, 3, 4), ((0, 0),) * 4 + ((0, 128 - small_rows),)).astype(bf16)
    gout = gout.reshape(lines, planes, share, 2, wide).transpose(3, 0, 1, 2, 4)
    last = jnp.concatenate([gqkv.reshape(2, lines, planes, share, 3 * wide), gsmall, gout], axis=4)
    last = sum_rows(last.transpose(2, 1, 0, 3, 4))
    keep = lax.dynamic_index_in_dim(last, side, 0, keepdims=False)
    pass_on = lax.dynamic_index_in_dim(last, 1 - side, 0, keepdims=False)
    got = partner(pass_on[:, : 3 * wide + 128])
    mine_q = keep[:, : 3 * wide].reshape(share, 3, 1, wide)
    other_q = got[:, : 3 * wide].reshape(share, 3, 1, wide)
    grad_qkv = jnp.where(
        first, jnp.concatenate([mine_q, other_q], axis=2), jnp.concatenate([other_q, mine_q], axis=2)
    ).reshape(share, 6 * wide)
    vecs = (keep[:, 3 * wide : 3 * wide + small_rows] + got[:, 3 * wide : 3 * wide + small_rows]).T
    both = last[:, :, 3 * wide + 128 :]
    halves = lax.dynamic_index_in_dim(both, 0, 0, keepdims=False), lax.dynamic_index_in_dim(both, 1, 0, keepdims=False)
    grad_out = jnp.concatenate(halves, axis=1)

    new_qkv = 0.9 * avg_qkv + 0.1 * qkv_weight.astype(f32)
    new_out = 0.9 * avg_out + 0.1 * out_weight.astype(f32)
    new_up = 0.9 * avg_up + 0.1 * up_weight.astype(f32)
    new_down = 0.9 * avg_down + 0.1 * down_weight.astype(f32)
    return (
        out_tokens,
        grad_input,
        vecs[0],
        vecs[1],
        grad_qkv,
        vecs[6:8].reshape(2 * share),
        grad_out,
        vecs[2],
        vecs[3],
        vecs[4],
        grad_up,
        vecs[8 : 8 + chunks].reshape(chunks * share),
        grad_down,
        vecs[5],
        new_qkv,
        new_out,
        new_up,
        new_down,
    )


def specs_for(rows):
    flat = ("seq",) + (rows if isinstance(rows, tuple) else (rows,))
    grid, ids, vec, mat = P(rows, "seq", None), P(rows, "seq"), P(flat), P(flat, None)
    ins = (grid, ids, grid, vec, vec, mat, vec, mat, vec, vec, vec, mat, vec, mat, vec, mat, mat, mat, mat)
    outs = (grid, grid, vec, vec, mat, vec, mat, vec, vec, vec, mat, vec, mat, vec, mat, mat, mat, mat)
    return ins, outs


def solution(mesh):
    parts, rows = mesh.shape["seq"], mesh.shape["rows"]
    planes = 4
    if parts != 2 or rows % planes:
        ins, outs = specs_for("rows")
        return jax.shard_map(on_device, mesh=mesh, in_specs=ins, out_specs=outs, check_vma=False)
    lines = rows // planes
    finer = Mesh(mesh.devices.reshape(parts, lines, 2, 2), ("seq", "line", "y", "x"))
    ins, outs = specs_for(("line", "y", "x"))
    return jax.shard_map(
        functools.partial(pair_device, lines, planes), mesh=finer, in_specs=ins, out_specs=outs, check_vma=False
    )
```

```python
import functools

import jax
import jax.numpy as jnp
from jax import lax
from jax.experimental import pallas as pl
from jax.experimental.pallas import tpu as pltpu
from jax.sharding import Mesh
from jax.sharding import PartitionSpec as P

HEADS = 12
HEAD_DIM = 64
CLIPS = 6


def layer_norm(value, gain, bias):
    middle = jnp.mean(value, axis=-1, keepdims=True)
    centred = value - middle
    spread = jnp.mean(centred * centred, axis=-1, keepdims=True)
    return centred * lax.rsqrt(spread + 1e-06) * gain + bias


def exact_gelu(value):
    return jax.nn.gelu(value, approximate=False)


def permitted(seg_query, seg_key, pos_query, pos_key):
    same_clip = seg_query[:, :, None] == seg_key[:, None, :]
    open_key = (seg_key != CLIPS - 1)[:, None, :]
    diagonal = (pos_query[:, None] == pos_key[None, :])[None]
    return (same_clip & (open_key | diagonal))[:, :, None, :]


def scores(query_part, key_part):
    return 0.125 * jnp.einsum(
        "rqhe,rkhe->rqhk", query_part, key_part, preferred_element_type=jnp.float32
    )


def exponent(score_vals, allowed):
    return jnp.where(allowed, jnp.exp(jnp.where(allowed, score_vals, 0.0)), 0.0)


def on_device(
    tokens,
    segment_ids,
    cotangent,
    ln1_gain,
    ln1_bias,
    qkv_weight,
    qv_bias,
    out_weight,
    out_bias,
    ln2_gain,
    ln2_bias,
    up_weight,
    up_bias,
    down_weight,
    down_bias,
    avg_qkv,
    avg_out,
    avg_up,
    avg_down,
):
    f32 = jnp.float32
    bf16 = jnp.bfloat16
    rows_here, shard_len, width = tokens.shape
    count_rows = rows_here * shard_len
    own_pos = lax.axis_index("seq") * shard_len + jnp.arange(shard_len, dtype=jnp.int32)
    head_shape = (rows_here, shard_len, HEADS, HEAD_DIM)
    gain_one, bias_one, w_qkv, b_qv, w_out, b_out = (
        lax.all_gather(ln1_gain, ("seq", "rows"), axis=0, tiled=True),
        lax.all_gather(ln1_bias, ("seq", "rows"), axis=0, tiled=True),
        lax.all_gather(qkv_weight, ("seq", "rows"), axis=0, tiled=True),
        lax.all_gather(qv_bias, ("seq", "rows"), axis=0, tiled=True),
        lax.all_gather(out_weight, ("seq", "rows"), axis=0, tiled=True),
        lax.all_gather(out_bias, ("seq", "rows"), axis=0, tiled=True),
    )
    residual = tokens.astype(f32).reshape(count_rows, width)
    normed, norm_one_pull = jax.vjp(
        layer_norm, residual, gain_one.astype(f32), bias_one.astype(f32)
    )
    normed_low = normed.astype(bf16)
    mixed = jnp.dot(normed_low, w_qkv, preferred_element_type=f32)
    bias_qv = b_qv.astype(f32)
    query_heads = (mixed[:, :width] + bias_qv[:width]).astype(bf16).reshape(head_shape)
    key_heads = mixed[:, width : 2 * width].astype(bf16).reshape(head_shape)
    value_heads = (mixed[:, 2 * width :] + bias_qv[width:]).astype(bf16).reshape(head_shape)
    start_state = (jnp.zeros((rows_here, shard_len, HEADS), f32), jnp.zeros(head_shape, f32))
    piece_keys = lax.all_gather(key_heads, "seq", axis=1, tiled=True)
    piece_values = lax.all_gather(value_heads, "seq", axis=1, tiled=True)
    piece_seg = lax.all_gather(segment_ids, "seq", axis=1, tiled=True)
    piece_len = piece_keys.shape[1]
    block_len = min(piece_len, shard_len)

    def forward_advance(turn, state):
        totals, weighted = state
        offset = turn * block_len
        key_block = lax.dynamic_slice_in_dim(piece_keys, offset, block_len, 1)
        value_block = lax.dynamic_slice_in_dim(piece_values, offset, block_len, 1)
        seg_block = lax.dynamic_slice_in_dim(piece_seg, offset, block_len, 1)
        key_pos = offset + jnp.arange(block_len, dtype=jnp.int32)
        allowed = permitted(segment_ids, seg_block, own_pos, key_pos)
        expo = exponent(scores(query_heads, key_block), allowed)
        totals = totals + jnp.sum(expo, axis=-1)
        weighted = weighted + jnp.einsum(
            "rqhk,rkhe->rqhe", expo.astype(bf16), value_block, preferred_element_type=f32
        )
        return (totals, weighted)

    totals, weighted = lax.fori_loop(0, piece_len // block_len, forward_advance, start_state)
    attended = weighted / totals[..., None]
    attn_in = attended.reshape(count_rows, width).astype(bf16)
    middle = residual + jnp.dot(attn_in, w_out, preferred_element_type=f32) + b_out.astype(f32)
    gain_two, bias_two, w_up, b_up, w_down, b_down = (
        lax.all_gather(ln2_gain, ("seq", "rows"), axis=0, tiled=True),
        lax.all_gather(ln2_bias, ("seq", "rows"), axis=0, tiled=True),
        lax.all_gather(up_weight, ("seq", "rows"), axis=0, tiled=True),
        lax.all_gather(up_bias, ("seq", "rows"), axis=0, tiled=True),
        lax.all_gather(down_weight, ("seq", "rows"), axis=0, tiled=True),
        lax.all_gather(down_bias, ("seq", "rows"), axis=0, tiled=True),
    )
    normed_two, norm_two_pull = jax.vjp(
        layer_norm, middle, gain_two.astype(f32), bias_two.astype(f32)
    )
    normed_two_low = normed_two.astype(bf16)
    hidden_pre = jnp.dot(normed_two_low, w_up, preferred_element_type=f32) + b_up.astype(f32)
    hidden, gelu_pull = jax.vjp(exact_gelu, hidden_pre)
    hidden_low = hidden.astype(bf16)
    final = middle + jnp.dot(hidden_low, w_down, preferred_element_type=f32) + b_down.astype(f32)
    out_tokens = final.astype(bf16).reshape(tokens.shape)
    w_up_back, w_down_back = (
        lax.all_gather(up_weight, ("seq", "rows"), axis=0, tiled=True),
        lax.all_gather(down_weight, ("seq", "rows"), axis=0, tiled=True),
    )
    grad_out = cotangent.astype(f32).reshape(count_rows, width)
    grad_low = grad_out.astype(bf16)
    grad_down = jnp.einsum("nf,nd->fd", hidden_low, grad_low, preferred_element_type=f32)
    grad_down_b = jnp.sum(grad_low, axis=0, dtype=f32)
    grad_hidden = jnp.einsum("nd,fd->nf", grad_low, w_down_back, preferred_element_type=f32)
    (grad_pre,) = gelu_pull(grad_hidden)
    grad_pre_low = grad_pre.astype(bf16)
    grad_up = jnp.einsum("nd,nf->df", normed_two_low, grad_pre_low, preferred_element_type=f32)
    grad_up_b = jnp.sum(grad_pre_low, axis=0, dtype=f32)
    grad_normed_two = jnp.einsum("nf,df->nd", grad_pre_low, w_up_back, preferred_element_type=f32)
    grad_mid_norm, grad_gain_two, grad_bias_two = norm_two_pull(grad_normed_two)
    grad_mid = grad_out + grad_mid_norm
    mlp_sums = (
        lax.psum_scatter(grad_gain_two, ("seq", "rows"), scatter_dimension=0, tiled=True),
        lax.psum_scatter(grad_bias_two, ("seq", "rows"), scatter_dimension=0, tiled=True),
        lax.psum_scatter(grad_up, ("seq", "rows"), scatter_dimension=0, tiled=True),
        lax.psum_scatter(grad_up_b, ("seq", "rows"), scatter_dimension=0, tiled=True),
        lax.psum_scatter(grad_down, ("seq", "rows"), scatter_dimension=0, tiled=True),
        lax.psum_scatter(grad_down_b, ("seq", "rows"), scatter_dimension=0, tiled=True),
    )
    w_qkv_back, w_out_back = (
        lax.all_gather(qkv_weight, ("seq", "rows"), axis=0, tiled=True),
        lax.all_gather(out_weight, ("seq", "rows"), axis=0, tiled=True),
    )
    grad_mid_low = grad_mid.astype(bf16)
    grad_wout = jnp.einsum("nd,ne->de", attn_in, grad_mid_low, preferred_element_type=f32)
    grad_bout = jnp.sum(grad_mid_low, axis=0, dtype=f32)
    grad_att = jnp.einsum(
        "ne,de->nd", grad_mid_low, w_out_back, preferred_element_type=f32
    ).reshape(head_shape)
    grad_acc = (grad_att / totals[..., None]).astype(bf16)
    shift_low = (jnp.sum(grad_att * attended, axis=-1) / totals).astype(bf16)
    shift_wide = shift_low.astype(f32)
    query_piece_keys = lax.all_gather(key_heads, "seq", axis=1, tiled=True)
    query_piece_values = lax.all_gather(value_heads, "seq", axis=1, tiled=True)
    query_piece_seg = lax.all_gather(segment_ids, "seq", axis=1, tiled=True)
    piece_len = query_piece_keys.shape[1]
    query_block_len = min(piece_len, shard_len)

    def query_advance(turn, grad_query):
        offset = turn * query_block_len
        key_block = lax.dynamic_slice_in_dim(query_piece_keys, offset, query_block_len, 1)
        value_block = lax.dynamic_slice_in_dim(query_piece_values, offset, query_block_len, 1)
        seg_block = lax.dynamic_slice_in_dim(query_piece_seg, offset, query_block_len, 1)
        key_pos = offset + jnp.arange(query_block_len, dtype=jnp.int32)
        allowed = permitted(segment_ids, seg_block, own_pos, key_pos)
        expo = exponent(scores(query_heads, key_block), allowed)
        inner = jnp.einsum("rqhe,rkhe->rqhk", grad_acc, value_block, preferred_element_type=f32)
        grad_score = (expo * (inner - shift_wide[..., None])).astype(bf16)
        return grad_query + jnp.einsum(
            "rqhk,rkhe->rqhe", grad_score, key_block, preferred_element_type=f32
        )

    grad_query = lax.fori_loop(
        0, piece_len // query_block_len, query_advance, jnp.zeros(head_shape, f32)
    )
    key_start = (jnp.zeros(head_shape, f32), jnp.zeros(head_shape, f32))
    piece_queries = lax.all_gather(query_heads, "seq", axis=1, tiled=True)
    piece_grads = lax.all_gather(grad_acc, "seq", axis=1, tiled=True)
    key_piece_seg = lax.all_gather(segment_ids, "seq", axis=1, tiled=True)
    piece_shift = lax.all_gather(shift_low, "seq", axis=1, tiled=True)
    piece_len = piece_queries.shape[1]
    key_block_len = min(piece_len, shard_len)

    def key_advance(turn, state):
        grad_key, grad_value = state
        offset = turn * key_block_len
        query_block = lax.dynamic_slice_in_dim(piece_queries, offset, key_block_len, 1)
        grad_block = lax.dynamic_slice_in_dim(piece_grads, offset, key_block_len, 1)
        seg_block = lax.dynamic_slice_in_dim(key_piece_seg, offset, key_block_len, 1)
        shift_block = lax.dynamic_slice_in_dim(piece_shift, offset, key_block_len, 1).astype(f32)
        query_pos = offset + jnp.arange(key_block_len, dtype=jnp.int32)
        allowed = permitted(seg_block, segment_ids, query_pos, own_pos)
        expo = exponent(scores(query_block, key_heads), allowed)
        inner = jnp.einsum("rqhe,rkhe->rqhk", grad_block, value_heads, preferred_element_type=f32)
        grad_score = (expo * (inner - shift_block[..., None])).astype(bf16)
        grad_key = grad_key + jnp.einsum(
            "rqhk,rqhe->rkhe", grad_score, query_block, preferred_element_type=f32
        )
        grad_value = grad_value + jnp.einsum(
            "rqhk,rqhe->rkhe", expo.astype(bf16), grad_block, preferred_element_type=f32
        )
        return (grad_key, grad_value)

    grad_key, grad_value = lax.fori_loop(0, piece_len // key_block_len, key_advance, key_start)
    grad_q_low = (0.125 * grad_query).astype(bf16).reshape(count_rows, width)
    grad_k_low = (0.125 * grad_key).astype(bf16).reshape(count_rows, width)
    grad_v_low = grad_value.astype(bf16).reshape(count_rows, width)
    grad_mixed = jnp.concatenate([grad_q_low, grad_k_low, grad_v_low], axis=1)
    grad_wqkv = jnp.einsum("nd,ne->de", normed_low, grad_mixed, preferred_element_type=f32)
    grad_bqv = jnp.concatenate(
        [jnp.sum(grad_q_low, axis=0, dtype=f32), jnp.sum(grad_v_low, axis=0, dtype=f32)], axis=0
    )
    grad_normed = jnp.einsum("ne,de->nd", grad_mixed, w_qkv_back, preferred_element_type=f32)
    grad_res_norm, grad_gain_one, grad_bias_one = norm_one_pull(grad_normed)
    grad_input = (grad_mid + grad_res_norm).reshape(tokens.shape)
    attn_sums = (
        lax.psum_scatter(grad_gain_one, ("seq", "rows"), scatter_dimension=0, tiled=True),
        lax.psum_scatter(grad_bias_one, ("seq", "rows"), scatter_dimension=0, tiled=True),
        lax.psum_scatter(grad_wqkv, ("seq", "rows"), scatter_dimension=0, tiled=True),
        lax.psum_scatter(grad_bqv, ("seq", "rows"), scatter_dimension=0, tiled=True),
        lax.psum_scatter(grad_wout, ("seq", "rows"), scatter_dimension=0, tiled=True),
        lax.psum_scatter(grad_bout, ("seq", "rows"), scatter_dimension=0, tiled=True),
    )
    new_qkv = 0.9 * avg_qkv + 0.1 * qkv_weight.astype(f32)
    new_out = 0.9 * avg_out + 0.1 * out_weight.astype(f32)
    new_up = 0.9 * avg_up + 0.1 * up_weight.astype(f32)
    new_down = 0.9 * avg_down + 0.1 * down_weight.astype(f32)
    return (
        out_tokens,
        grad_input,
        attn_sums[0],
        attn_sums[1],
        attn_sums[2],
        attn_sums[3],
        attn_sums[4],
        attn_sums[5],
        mlp_sums[0],
        mlp_sums[1],
        mlp_sums[2],
        mlp_sums[3],
        mlp_sums[4],
        mlp_sums[5],
        new_qkv,
        new_out,
        new_up,
        new_down,
    )


f32 = jnp.float32
bf16 = jnp.bfloat16
NT = (((1,), (1,)), ((), ()))
LOG2E = 1.4426950408889634
SCORE = 0.125 * LOG2E
BIG = 16384.0
VMEM_BYTES = 63 * 1024 * 1024
TQ_F, TK_F = 512, 256
TK_B, TQ_B = 512, 512
LANE_LOG = 41
LANE_PAD = 44


def kernel_params(flops, bytes_accessed, transcendentals=0, order=("arbitrary",)):
    return dict(
        compiler_params=pltpu.CompilerParams(
            vmem_limit_bytes=VMEM_BYTES, dimension_semantics=order
        ),
        cost_estimate=pl.CostEstimate(
            flops=int(flops), bytes_accessed=int(bytes_accessed), transcendentals=int(transcendentals)
        ),
    )


def standardise(value):
    middle = jnp.mean(value, axis=-1, keepdims=True)
    centred = value - middle
    spread = jnp.mean(centred * centred, axis=-1, keepdims=True)
    rstd = lax.rsqrt(spread + 1e-06)
    return centred * rstd, rstd


def norm_pull(grad_normed, gain, xhat, rstd):
    scaled = grad_normed * gain
    first = jnp.mean(scaled, axis=-1, keepdims=True)
    second = jnp.mean(scaled * xhat, axis=-1, keepdims=True)
    return rstd * (scaled - first - xhat * second)


def gelu_pair(x):
    size = jnp.abs(x)
    t = 1.0 / (1.0 + 0.23164189 * size)
    bell = jnp.exp2(x * x * (-0.5 * LOG2E))
    poly = t * (0.127414796 + t * (-0.142248368 + t * (0.7107068705 + t * (-0.7265760135 + t * 0.5307027145))))
    tail = poly * bell
    phi = jnp.where(x >= 0.0, 1.0 - tail, tail)
    return x * phi, phi + x * bell * 0.3989422804014327


def lane_masks():
    lane = lax.broadcasted_iota(jnp.int32, (1, 128), 1)
    low = jnp.where(lane < HEAD_DIM, 1.0, 0.0)
    return low.astype(bf16), (1.0 - low).astype(bf16)


def prepare_kernel(share, side_ref, w_ref, *refs):
    vectors, (mine_ref, give_ref) = refs[:-2], refs[-2:]
    wide = w_ref.shape[1] // 6
    pairs = wide // 128
    for target, side in ((mine_ref, side_ref[0]), (give_ref, 1 - side_ref[0])):
        for pair in range(pairs):
            for kind in range(3):
                start = pl.multiple_of(kind * 2 * wide + side * wide + pair * 128, 128)
                at = 384 * pair + 128 * kind
                target[:, at : at + 128] = w_ref[:, pl.ds(start, 128)]
    lane = lax.broadcasted_iota(jnp.int32, (share, 128), 1)
    small = jnp.zeros((share, 128), f32)
    column = 0
    for ref in vectors:
        row = jnp.broadcast_to(ref[...].astype(f32), (8, ref.shape[1])).T
        for start in range(0, ref.shape[1], share):
            small = jnp.where(lane == column, row[start : start + share, 0:1], small)
            column += 1
    small = small.astype(bf16)
    mine_ref[:, 3 * wide :] = small
    give_ref[:, 3 * wide :] = small


def project_kernel(
    share, side_ref, own_ref, other_ref, w_ref, small_ref, normed_ref, mixed_ref, pack_ref, shift_s
):
    which, turn = pl.program_id(0), pl.program_id(1)
    wide = shift_s.shape[1] // 3
    pairs = wide // 128

    @pl.when((which == 0) & (turn == 0))
    def _():
        small = small_ref[...].astype(f32).T
        pack_ref[...] = small[0:16]
        shift_s[...] = jnp.zeros_like(shift_s)
        spot = lax.broadcasted_iota(jnp.int32, (wide, wide), 0)
        target = lax.broadcasted_iota(jnp.int32, (wide, wide), 1) + side_ref[0] * wide
        sums = [jnp.zeros((16, wide), f32), jnp.zeros((16, wide), f32)]
        for part in range(2):
            wanted = lax.div(spot, share) * (2 * share) + part * share + lax.rem(spot, share)
            chosen = jnp.where(wanted == target, 1.0, 0.0).astype(bf16)
            for kind in range(2):
                values = small[6 + part : 7 + part, kind * wide : (kind + 1) * wide]
                values = jnp.broadcast_to(values, (16, wide)).astype(bf16)
                sums[kind] += jnp.dot(values, chosen, preferred_element_type=f32)
        for pair in range(pairs):
            lanes = slice(128 * pair, 128 * pair + 128)
            shift_s[:, 384 * pair : 384 * pair + 128] = sums[0][0:1, lanes]
            shift_s[:, 384 * pair + 256 : 384 * pair + 384] = sums[1][0:1, lanes]

    value = jnp.where(which == 0, own_ref[0].astype(f32), other_ref[0].astype(f32))
    xhat, _ = standardise(value)
    normed = (xhat * pack_ref[0:1, :] + pack_ref[1:2, :]).astype(bf16)
    normed_ref[0, 0] = normed
    for pair in range(pairs):
        lanes = slice(384 * pair, 384 * pair + 384)
        mixed = jnp.dot(normed, w_ref[:, lanes], preferred_element_type=f32) + shift_s[:, lanes]
        mixed_ref[pair, 0, 0] = mixed.astype(bf16)


def attend_kernel(row, flag_ref, mixed_ref, qx_ref, kx_ref, *rest):
    own_ref, other_ref, ext_ref, q_s, k_s, v_s, acc_s = rest[-7:]
    length = q_s.shape[1]
    heads = q_s.shape[0]
    half = length // 2
    low, high = lane_masks()
    qx, kx = qx_ref[0], kx_ref[0]
    q_low, q_high, k_low, k_high = qx * low, qx * high, kx * low, kx * high
    for pair in range(heads // 2):
        q = mixed_ref[pair, :, 0, :, 0:128].reshape(length, 128)
        k = mixed_ref[pair, :, 0, :, 128:256].reshape(length, 128)
        v = mixed_ref[pair, :, 0, :, 256:384].reshape(length, 128)
        q_s[2 * pair] = q * low + q_high
        q_s[2 * pair + 1] = q * high + q_low
        k_s[2 * pair] = k * low + k_high
        k_s[2 * pair + 1] = k * high + k_low
        v_s[2 * pair] = v * low + high
        v_s[2 * pair + 1] = v * high + low
    acc_s[...] = jnp.zeros_like(acc_s)
    key_blocks = length // TK_F

    def step(index, carry):
        @pl.when(flag_ref[row, index] != 0)
        def _():
            q_at = pl.ds(pl.multiple_of((index // key_blocks) * TQ_F, TQ_F), TQ_F)
            k_at = pl.ds(pl.multiple_of((index % key_blocks) * TK_F, TK_F), TK_F)
            for head in range(heads):
                score = lax.dot_general(
                    q_s[head, q_at, :], k_s[head, k_at, :], NT, preferred_element_type=f32
                )
                expo = jnp.exp2(score * SCORE).astype(bf16)
                acc_s[head, q_at, :] += jnp.dot(expo, v_s[head, k_at, :], preferred_element_type=f32)

        return carry

    lax.fori_loop(0, (length // TQ_F) * key_blocks, step, 0)
    lane = lax.broadcasted_iota(jnp.int32, (half, 128), 1)
    first_half = lane < HEAD_DIM
    spot = lane % HEAD_DIM
    for pair in range(heads // 2):
        for side in range(2):
            rows = slice(side * half, (side + 1) * half)
            first, second = acc_s[2 * pair, rows], acc_s[2 * pair + 1, rows]
            top = jnp.where(first_half, first, second)
            crossed = jnp.where(first_half, second, first)
            totals = pltpu.roll(crossed, HEAD_DIM, 1)
            target = own_ref if side == 0 else other_ref
            target[pair, 0] = (top / totals).astype(bf16)
            lse = -8.0 * jnp.log(crossed)
            lse_a = lse.astype(bf16).astype(f32)
            lse_b = (lse - lse_a).astype(bf16).astype(f32)
            ext = jnp.where(
                spot == LANE_LOG,
                lse_a,
                jnp.where(
                    spot == LANE_LOG + 1,
                    lse_b,
                    jnp.where(spot == LANE_LOG + 2, lse - lse_a - lse_b, qx[rows].astype(f32)),
                ),
            )
            ext_ref[pair, side, 0] = ext.astype(bf16)


def join_lanes(ref):
    return jnp.concatenate([ref[i, 0] for i in range(ref.shape[0])], axis=1)


def mlp_kernel(
    planes, share, side_ref, x_ref, mine_ref, recv_ref, wo_ref, up_ref, down_ref, grad_ref, pack_ref, upb_ref,
    out_ref, gmid_ref, glow_ref, gdown_own, gdown_other, gup_own, gup_other, gbias_ref, gvec_ref,
    down_s, up_s,
):
    turn = pl.program_id(0)
    side = side_ref[0]
    chunks, size = down_s.shape[0], down_s.shape[2]
    middle = (
        x_ref[0].astype(f32)
        + jnp.dot(join_lanes(mine_ref), wo_ref[side], preferred_element_type=f32)
        + jnp.dot(join_lanes(recv_ref), wo_ref[1 - side], preferred_element_type=f32)
        + pack_ref[2:3, :]
    )
    xhat, rstd = standardise(middle)
    normed = (xhat * pack_ref[3:4, :] + pack_ref[4:5, :]).astype(bf16)
    normed_t = normed.T
    grad = grad_ref[0]
    grad_t = grad.T
    total = middle + pack_ref[5:6, :]

    @pl.when(turn == 0)
    def _():
        down_s[...] = jnp.zeros_like(down_s)
        up_s[...] = jnp.zeros_like(up_s)
        gbias_ref[...] = jnp.zeros_like(gbias_ref)
        gvec_ref[...] = jnp.zeros_like(gvec_ref)

    gnormed = None
    for f in range(chunks):
        at = slice(f * size, (f + 1) * size)
        ghidden = lax.dot_general(grad, down_ref[at, :], NT, preferred_element_type=f32)
        pre = jnp.dot(normed, up_ref[:, at], preferred_element_type=f32) + upb_ref[f : f + 1, :]
        hidden, slope = gelu_pair(pre)
        hidden = hidden.astype(bf16)
        gpre = (ghidden * slope).astype(bf16)
        total = total + jnp.dot(hidden, down_ref[at, :], preferred_element_type=f32)
        part = lax.dot_general(gpre, up_ref[:, at], NT, preferred_element_type=f32)
        gnormed = part if gnormed is None else gnormed + part
        down_s[f] += jnp.dot(grad_t, hidden, preferred_element_type=f32)
        up_s[f] += jnp.dot(normed_t, gpre, preferred_element_type=f32)
        gbias_ref[f] += jnp.sum(gpre.astype(f32), axis=0, keepdims=True)
    out_ref[0] = total.astype(bf16)
    gmid = grad.astype(f32) + norm_pull(gnormed, pack_ref[3:4, :], xhat, rstd)
    gmid_ref[0] = gmid
    low = gmid.astype(bf16)
    glow_ref[0] = low
    gvec_ref[0:1, :] += jnp.sum(gnormed * xhat, axis=0, keepdims=True)
    gvec_ref[1:2, :] += jnp.sum(gnormed, axis=0, keepdims=True)
    gvec_ref[2:3, :] += jnp.sum(low.astype(f32), axis=0, keepdims=True)
    gvec_ref[3:4, :] += jnp.sum(grad.astype(f32), axis=0, keepdims=True)

    @pl.when(turn == pl.num_programs(0) - 1)
    def _():
        half = chunks // 2
        rows = chunks * share
        per_chunk = size // rows
        for f in range(chunks):
            whole = down_s[f].astype(bf16).T
            for target, wanted in ((gdown_own, f // half), (gdown_other, 1 - f // half)):

                @pl.when(side == wanted)
                def _(target=target, whole=whole, f=f):
                    for i in range(per_chunk):
                        at = (f % half) * per_chunk + i
                        target[at % planes, at // planes] = whole[i * rows : (i + 1) * rows]

        wide = up_s.shape[1] // 2
        for target, base in ((gup_own, side * wide), (gup_other, (1 - side) * wide)):
            for f in range(chunks):
                for at in range(wide // share):
                    start = pl.multiple_of(base + at * share, 8)
                    target[at % planes, at // planes, f] = up_s[f, pl.ds(start, share), :].astype(bf16)


def attend_back_kernel(
    flag_ref, mixed_ref, ext_ref, att_own, att_other, own_ref, other_ref, wo_ref, kx_ref,
    gmixed_ref, gbias_ref,
    q_s, k_s, v_s, d_s, qz_s, dz_s, kt_s, gq_s, gk_s, gv_s,
):
    row = pl.program_id(0)
    length = q_s.shape[1]
    half = length // 2
    low, high = lane_masks()
    lane = lax.broadcasted_iota(jnp.int32, (1, 128), 1)
    spot = lane % HEAD_DIM
    square_row = lax.broadcasted_iota(jnp.int32, (128, 128), 0) < HEAD_DIM
    square_col = lax.broadcasted_iota(jnp.int32, (128, 128), 1) < HEAD_DIM
    crossing = jnp.where(square_row == square_col, 0.0, -1.0).astype(bf16)
    one_hot_a = jnp.where(spot == 0, 1.0, 0.0)
    one_hot_b = jnp.where(spot == 1, 1.0, 0.0)
    v_ext = (one_hot_a + one_hot_b).astype(bf16)

    @pl.when(row == 0)
    def _():
        gbias_ref[...] = jnp.zeros_like(gbias_ref)

    q = mixed_ref[0, :, 0, :, 0:128].reshape(length, 128)
    k = mixed_ref[0, :, 0, :, 128:256].reshape(length, 128)
    v = mixed_ref[0, :, 0, :, 256:384].reshape(length, 128)
    ext = ext_ref[0, :, 0].reshape(length, 128)
    kx = kx_ref[0]
    q_a, q_b = q * low, q * high
    q_s[0] = q_a + ext * high
    q_s[1] = q_b + ext * low
    k_s[0] = k * low + kx * high
    k_s[1] = k * high + kx * low
    v_s[0] = v * low + v_ext * high
    v_s[1] = v * high + v_ext * low
    for side in range(2):
        rows = slice(side * half, (side + 1) * half)
        gates = own_ref[0] if side == 0 else other_ref[0]
        d = lax.dot_general(gates, wo_ref[...], NT, preferred_element_type=f32)
        moved = d * (att_own if side == 0 else att_other)[0, 0].astype(f32)
        moved_a = moved.astype(bf16)
        moved_b = (moved - moved_a.astype(f32)).astype(bf16)
        shift = jnp.dot(moved_a, crossing, preferred_element_type=f32) + jnp.dot(
            moved_b, crossing, preferred_element_type=f32
        )
        shift_a = shift.astype(bf16).astype(f32)
        dx = (shift_a * one_hot_a + (shift - shift_a) * one_hot_b).astype(bf16)
        d = d.astype(bf16)
        d_a, d_b = d * low, d * high
        d_s[0, rows] = d_a + dx * high
        d_s[1, rows] = d_b + dx * low
        for i in range(half // TQ_B):
            at = slice(i * TQ_B, (i + 1) * TQ_B)
            dz_s[side * (half // TQ_B) + i, :TQ_B] = d_a[at]
            dz_s[side * (half // TQ_B) + i, TQ_B:] = d_b[at]
    for i in range(length // TQ_B):
        at = slice(i * TQ_B, (i + 1) * TQ_B)
        qz_s[i, :TQ_B] = q_a[at]
        qz_s[i, TQ_B:] = q_b[at]
    for i in range(length // TK_B):
        kt_s[i] = k[i * TK_B : (i + 1) * TK_B].T
    gq_s[...] = jnp.zeros_like(gq_s)
    gk_s[...] = jnp.zeros_like(gk_s)
    gv_s[...] = jnp.zeros_like(gv_s)
    query_blocks = length // TQ_B

    def step(index, carry):
        @pl.when(flag_ref[row, index] != 0)
        def _():
            qi = index % query_blocks
            ki = index // query_blocks
            q_at = pl.ds(pl.multiple_of(qi * TQ_B, TQ_B), TQ_B)
            k_at = pl.ds(pl.multiple_of(ki * TK_B, TK_B), TK_B)
            probs, grads = [], []
            for head in range(2):
                score = lax.dot_general(
                    k_s[head, k_at, :], q_s[head, q_at, :], NT, preferred_element_type=f32
                )
                inner = lax.dot_general(
                    v_s[head, k_at, :], d_s[head, q_at, :], NT, preferred_element_type=f32
                )
                prob = jnp.exp2(score * SCORE)
                probs.append(prob.astype(bf16))
                grads.append((prob * inner).astype(bf16))
            for head in range(2):
                at = slice(head * HEAD_DIM, (head + 1) * HEAD_DIM)
                gq_s[qi, at, :] += jnp.dot(kt_s[ki, at, :], grads[head], preferred_element_type=f32)
            gv_s[k_at, :] += jnp.dot(
                jnp.concatenate(probs, axis=1), dz_s[qi], preferred_element_type=f32
            )
            gk_s[k_at, :] += jnp.dot(
                jnp.concatenate(grads, axis=1), qz_s[qi], preferred_element_type=f32
            )

        return carry

    lax.fori_loop(0, query_blocks * (length // TK_B), step, 0)
    for i in range(query_blocks):
        gq = (0.125 * gq_s[i].T).astype(bf16)
        for start in range(0, TQ_B, min(TQ_B, half)):
            at = i * TQ_B + start
            size = min(TQ_B, half)
            gmixed_ref[at // half, 0, at % half : at % half + size, 0:128] = gq[start : start + size]
        gbias_ref[0:1, 0:128] += jnp.sum(gq.astype(f32), axis=0, keepdims=True)
    gk = (0.125 * gk_s[...]).astype(bf16)
    gv = gv_s[...].astype(bf16)
    gbias_ref[0:1, 128:256] += jnp.sum(gk.astype(f32), axis=0, keepdims=True)
    gbias_ref[0:1, 256:384] += jnp.sum(gv.astype(f32), axis=0, keepdims=True)
    for side in range(2):
        gmixed_ref[side, 0, :, 128:256] = gk[side * half : (side + 1) * half]
        gmixed_ref[side, 0, :, 256:384] = gv[side * half : (side + 1) * half]


def weight_dot(normed_ref, piece_ref):
    total = None
    for side in range(2):
        part = lax.dot_general(
            normed_ref[side, 0], piece_ref[side, 0], (((0,), (0,)), ((), ())), preferred_element_type=f32
        )
        total = part if total is None else total + part
    return total


def fold_lanes(value):
    total = value[:, 0:128]
    for at in range(128, value.shape[1], 128):
        total = total + value[:, at : at + 128]
    return total


def early_kernel(
    planes, share, normed_ref, g0_ref, g1_ref, b0_ref, b1_ref, mine_ref, other_ref, low_ref, low_other_ref, w_ref,
    unit_ref, first_ref, second_ref, acc_s, out_s,
):
    turn = pl.program_id(0)

    @pl.when(turn == 0)
    def _():
        acc_s[...] = jnp.zeros_like(acc_s)
        out_s[...] = jnp.zeros_like(out_s)

    acc_s[:, 0:384] += weight_dot(normed_ref, g0_ref)
    acc_s[:, 384:768] += weight_dot(normed_ref, g1_ref)
    across = (((0,), (0,)), ((), ()))
    out_s[...] += lax.dot_general(
        join_lanes(mine_ref), low_ref[0], across, preferred_element_type=f32
    ) + lax.dot_general(join_lanes(other_ref), low_other_ref[0], across, preferred_element_type=f32)

    @pl.when(turn == pl.num_programs(0) - 1)
    def _():
        weights = w_ref[...].astype(f32)
        sums = jnp.concatenate([b0_ref[0:1, :], b1_ref[0:1, :]], axis=1)
        first_ref[...] = fold_lanes(weights * acc_s[...])
        second_ref[...] = fold_lanes(weights * sums)
        count = out_s.shape[0] // share
        for at in range(count):
            spot = (at % planes, at // planes)
            for side in range(2):
                start = (side * count + at) * share
                unit_ref[spot + (side,)] = acc_s[start : start + share, :].astype(bf16)
            unit_ref[spot + (2,)] = out_s[at * share : (at + 1) * share, :].astype(bf16)


def scatter_rows(vector, step, offset, owners):
    n = vector.shape[1]
    owner = lax.broadcasted_iota(jnp.int32, (owners, n), 0) - offset
    mask = lax.div(lax.broadcasted_iota(jnp.int32, (owners, n), 1), step) == owner
    spread = jnp.where(mask, jnp.broadcast_to(vector, (owners, n)), 0.0).astype(bf16)
    lane = lax.rem(lax.broadcasted_iota(jnp.int32, (128, n), 1), step)
    chosen = jnp.where(lane == lax.broadcasted_iota(jnp.int32, (128, n), 0), 1.0, 0.0).astype(bf16)
    return lax.dot_general(spread, chosen, NT, preferred_element_type=f32)


def late_kernel(
    planes, share, side_ref, normed_ref, g_ref, w_ref, first_ref, second_ref, b0_ref, b1_ref, b2_ref, pack_ref,
    gvec_ref, gup_ref, unit_ref, acc_s,
):
    turn = pl.program_id(0)

    @pl.when(turn == 0)
    def _():
        acc_s[...] = jnp.zeros_like(acc_s)

    acc_s[...] += weight_dot(normed_ref, g_ref)

    @pl.when(turn == pl.num_programs(0) - 1)
    def _():
        side = side_ref[0]
        weights = w_ref[...].astype(f32)
        width = weights.shape[0]
        owners = width // share
        count = owners // 2
        inner = first_ref[...] + fold_lanes(weights * acc_s[...])
        plain = second_ref[...] + fold_lanes(weights * b2_ref[0:1, :])
        inner = jnp.sum(inner.T, axis=0, keepdims=True)
        plain = jnp.sum(plain.T, axis=0, keepdims=True)
        gain, bias = pack_ref[0:1, :], pack_ref[1:2, :]
        g_gain = (inner - bias * plain) / gain
        biases = (b0_ref, b1_ref, b2_ref)
        query = jnp.concatenate([b[0:1, 0:128] for b in biases], axis=1)
        value = jnp.concatenate([b[0:1, 256:384] for b in biases], axis=1)
        chunks = gup_ref.shape[0]
        rows_up = chunks * share
        up_bias = None
        for f in range(chunks):
            part = scatter_rows(gup_ref[f], rows_up, f * (width // rows_up), owners)
            up_bias = part if up_bias is None else up_bias + part
        wide = width // 2
        first_owner = side * (wide // (2 * share))
        qv_bias = scatter_rows(query, 2 * share, first_owner, owners) + scatter_rows(
            value, 2 * share, first_owner + count, owners
        )
        plain_rows = lambda vec: scatter_rows(vec, share, 0, owners)
        slots = [
            plain_rows(g_gain),
            plain_rows(plain),
            plain_rows(gvec_ref[2:3, :]),
            plain_rows(gvec_ref[0:1, :]),
            plain_rows(gvec_ref[1:2, :]),
            plain_rows(gvec_ref[3:4, :]),
            qv_bias,
            up_bias,
            jnp.zeros((owners, 128), f32),
        ]
        lines_of = [jnp.concatenate(slots[3 * i : 3 * i + 3], axis=1) for i in range(3)]
        for at in range(count):
            for half in range(2):
                owner = half * count + at
                start = owner * share
                rows = [acc_s[start : start + share, :]]
                rows += [line[owner : owner + 1, :] for line in lines_of]
                rows += [jnp.zeros((5, 384), f32)]
                unit_ref[at % planes, at // planes, half] = jnp.concatenate(rows, axis=0).astype(bf16)


def back_through(pieces, w_ref, side):
    total = None
    for i, piece in enumerate(pieces):
        part = lax.dot_general(
            piece[side, 0], w_ref[:, 384 * i : 384 * i + 384], NT, preferred_element_type=f32
        )
        total = part if total is None else total + part
    return total


def give_kernel(*refs):
    pieces, (w_ref, out_ref) = refs[:-2], refs[-2:]
    out_ref[0] = back_through(pieces, w_ref, 0).astype(bf16)


def input_kernel(*refs):
    pieces, (w_ref, recv_ref, x_ref, gmid_ref, pack_ref, ginput_ref) = refs[:-6], refs[-6:]
    gnormed = back_through(pieces, w_ref, 0) + recv_ref[0].astype(f32)
    xhat, rstd = standardise(x_ref[0].astype(f32))
    ginput_ref[0] = gmid_ref[0] + norm_pull(gnormed, pack_ref[0:1, :], xhat, rstd)


def partner(value):
    return lax.ppermute(value, "seq", [(0, 1), (1, 0)])


def exchange(value, axis):
    return lax.all_to_all(value, axis, 0, 0, tiled=True)


def spread_line(value, lines):
    return exchange(jnp.broadcast_to(value[None], (lines,) + value.shape), "line")


def flip(value, axis):
    return lax.ppermute(value, axis, [(0, 1), (1, 0)])


def in_order(index, own, received):
    return jnp.where(index == 0, jnp.stack([own, received]), jnp.stack([received, own]))


def spread_plane(one, two):
    got_one, got_two = lax.optimization_barrier((flip(one, "x"), flip(two, "y")))
    near_one = in_order(lax.axis_index("x"), one, got_one)
    near_two = in_order(lax.axis_index("y"), two, got_two)
    near_one, near_two = lax.optimization_barrier((near_one, near_two))
    return (near_one, flip(near_one, "y")), (near_two, flip(near_two, "x"))


def after(value, *others):
    return lax.optimization_barrier((value,) + others)[0]


def assemble_kernel(spot_ref, *refs):
    pieces, (up_ref, down_ref, out_ref), scratch, (in_sem, out_sem) = refs[:8], refs[8:11], refs[11:19], refs[19:]
    side, y, x = spot_ref[0], spot_ref[1], spot_ref[2]
    width = down_ref.shape[-1]
    own_rows, tail_rows = down_ref.shape[-2], out_ref.shape[-2]
    loads = [pltpu.make_async_copy(pieces[i], scratch[i], in_sem.at[i]) for i in range(8)]
    for load in loads:
        load.start()
    stores = []

    def send(source, target):
        stores.append(pltpu.make_async_copy(source, target, out_sem.at[len(stores)]))
        stores[-1].start()

    for index in range(8):
        loads[index].wait()
        kind, far_side, far_plane = index % 2, index // 4, (index // 2) % 2
        at_side = 1 - side if far_side else side
        held = scratch[index]
        for i in range(2):
            if kind == 0:
                row = 1 - y if far_plane else y
                for block in range(held.shape[2]):
                    lanes = slice(block * width, (block + 1) * width)
                    send(held.at[i, :, block], up_ref.at[at_side, :, row, i, :, lanes])
            else:
                column = 1 - x if far_plane else x
                send(held.at[i, :, 0:own_rows], down_ref.at[at_side, :, i, column])
                send(held.at[i, :, own_rows : own_rows + tail_rows], out_ref.at[at_side, :, i, column])
    for copy in stores:
        copy.wait()


def assemble(spot, pieces, shapes):
    anywhere = pl.BlockSpec(memory_space=pl.ANY)
    blocks = pieces[0].shape[2]
    return pl.pallas_call(
        assemble_kernel,
        grid_spec=pltpu.PrefetchScalarGridSpec(
            num_scalar_prefetch=1,
            grid=(1,),
            in_specs=[anywhere] * 8,
            out_specs=[anywhere] * 3,
            scratch_shapes=[pltpu.VMEM(p.shape, bf16) for p in pieces]
            + [pltpu.SemaphoreType.DMA((8,)), pltpu.SemaphoreType.DMA((8 * blocks + 16,))],
        ),
        out_shape=shapes,
        name="assemble",
        **kernel_params(1e6, 24e6),
    )(spot, *pieces)


def sum_plane(value):
    return jnp.sum(exchange(value, ("y", "x")).astype(f32), axis=0)


def sum_line(value, lines):
    here = lax.axis_index("line")
    total = lax.dynamic_index_in_dim(value, here, 0, keepdims=False)
    for shift in range(1, lines):
        piece = lax.dynamic_index_in_dim(value, (here + shift) % lines, 0, keepdims=False).astype(bf16)
        total = total + lax.ppermute(piece, "line", [(i, (i + shift) % lines) for i in range(lines)]).astype(f32)
    return total


def masks(seg, pos):
    pad = seg == CLIPS - 1
    lane = jnp.arange(128, dtype=jnp.int32) % HEAD_DIM
    seg, pos, pad = seg[..., None], pos[..., None], pad[..., None]
    clip_lane = lane < CLIPS - 1
    digit = jnp.where(lane < 9, pos // 256, jnp.where(lane < 25, (pos // 16) % 16, pos % 16))
    digit_base = jnp.where(lane < 9, 5, jnp.where(lane < 25, 9, 25))
    digit_lane = (lane >= 5) & (lane < LANE_LOG)
    hit_clip = lane == seg
    hit_digit = lane - digit_base == digit
    log_lane = (lane >= LANE_LOG) & (lane < LANE_PAD)
    pad_lane = lane == LANE_PAD
    bad = (clip_lane & ~hit_clip) | (digit_lane & pad & ~hit_digit) | (pad_lane & ~pad)
    qx = jnp.where(bad, -BIG, 0.0).astype(bf16)
    on = (clip_lane & hit_clip) | (digit_lane & pad & hit_digit) | log_lane | (pad_lane & pad)
    kx = jnp.where(on, 1.0, 0.0).astype(bf16)
    return qx, kx


def block_flags(ident, rows_block, cols_block):
    count, length = ident.shape
    by_row = ident.reshape(count, length // rows_block, rows_block)
    by_col = ident.reshape(count, length // cols_block, cols_block)
    low_row, high_row = jnp.min(by_row, axis=2)[:, :, None], jnp.max(by_row, axis=2)[:, :, None]
    low_col, high_col = jnp.min(by_col, axis=2)[:, None, :], jnp.max(by_col, axis=2)[:, None, :]
    meets = (low_row <= high_col) & (low_col <= high_row)
    return meets.astype(jnp.int32).reshape(count, -1)


def pair_device(
    lines, planes,
    tokens, segment_ids, cotangent, ln1_gain, ln1_bias, qkv_weight, qv_bias, out_weight, out_bias,
    ln2_gain, ln2_bias, up_weight, up_bias, down_weight, down_bias, avg_qkv, avg_out, avg_up, avg_down,
):
    count, part, width = tokens.shape
    length = 2 * part
    wide = width // 2
    heads = HEADS // 2
    hidden_width = up_weight.shape[1]
    chunks = hidden_width // width
    share = qkv_weight.shape[0]
    side = lax.axis_index("seq").astype(jnp.int32)
    first = side == 0
    side_arr = side.reshape(1)
    const = lambda *shape: pl.BlockSpec(shape, lambda *_: (0,) * len(shape), pipeline_mode=pl.Buffered(1))
    row_block = lambda *shape: pl.BlockSpec((1,) + shape, lambda j, *_: (j,) + (0,) * len(shape))
    both_block = lambda lanes: pl.BlockSpec((2, 1, part, lanes), lambda j, *_: (0, j, 0, 0))
    own_block = lambda lanes: pl.BlockSpec((1, 1, part, lanes), lambda j, *_: (0, j, 0, 0))

    pairs = heads // 2
    sds = jax.ShapeDtypeStruct
    small_vectors = [ln1_gain, ln1_bias, out_bias, ln2_gain, ln2_bias, down_bias, qv_bias, up_bias]
    mine, give = pl.pallas_call(
        functools.partial(prepare_kernel, share),
        grid_spec=pltpu.PrefetchScalarGridSpec(
            num_scalar_prefetch=1,
            grid=(1,),
            in_specs=[pl.BlockSpec((share, 6 * wide), lambda *_: (0, 0))]
            + [pl.BlockSpec((1, v.shape[0]), lambda *_: (0, 0)) for v in small_vectors],
            out_specs=[pl.BlockSpec((share, 3 * wide + 128), lambda *_: (0, 0))] * 2,
        ),
        out_shape=[sds((share, 3 * wide + 128), bf16)] * 2,
        name="prepare",
        **kernel_params(1e6, 4e5),
    )(side_arr, qkv_weight, *[v[None] for v in small_vectors])
    take = partner(give)
    tokens_other = partner(tokens)
    seg_other = partner(segment_ids)
    seg = jnp.concatenate([segment_ids, seg_other], axis=1)
    spots = jnp.arange(part, dtype=jnp.int32)
    pos = jnp.concatenate([side * part + spots, (1 - side) * part + spots])
    qx, kx = masks(seg, jnp.broadcast_to(pos, seg.shape))
    ident = jnp.where(seg == CLIPS - 1, CLIPS + pos, seg)
    flags_f = block_flags(ident, TQ_F, TK_F)
    flags_b = block_flags(ident, TK_B, TQ_B)

    start = jnp.where(first, jnp.stack([mine, take]), jnp.stack([take, mine]))
    x_at, y_at = lax.axis_index("x"), lax.axis_index("y")
    first_line = after(spread_line(start, lines), qx, kx, flags_f, flags_b)
    (one_m, one_r), (two_m, two_r) = spread_plane(first_line[:, 0], first_line[:, 1])
    one = in_order(y_at, one_m, one_r).transpose(2, 0, 1, 3, 4)
    two = in_order(x_at, two_m, two_r).transpose(2, 1, 0, 3, 4)
    w_first = jnp.stack([one, two]).reshape(width, 3 * wide + 128)

    own_rows, tail_rows = chunks * share, 32
    second = jnp.concatenate(
        [up_weight[:, i * width : (i + 1) * width] for i in range(chunks)]
        + [down_weight, out_weight, jnp.zeros((tail_rows - share, width), bf16)],
        axis=0,
    )
    second = after(second, first_line)
    second_line = after(spread_line(second, lines), one_r, two_r)
    up_pair, down_pair = spread_plane(
        second_line[:, :own_rows].reshape(lines, chunks, share, width), second_line[:, own_rows:]
    )
    half_way = (up_pair[0], down_pair[0])
    spot = jnp.stack([side, y_at.astype(jnp.int32), x_at.astype(jnp.int32)])
    pieces = [up_pair[0], down_pair[0], up_pair[1], down_pair[1]]
    pieces += [partner(piece) for piece in pieces]
    w_up, w_down, w_out = assemble(
        spot,
        pieces,
        [
            sds((2, lines, 2, 2, share, hidden_width), bf16),
            sds((2, lines, 2, 2, own_rows, width), bf16),
            sds((2, lines, 2, 2, tail_rows, width), bf16),
        ],
    )
    w_up = w_up.reshape(width, hidden_width)
    w_down = w_down.reshape(hidden_width, width)
    w_out = w_out[..., :share, :].reshape(2, wide, width)
    wo_mine = lax.dynamic_index_in_dim(w_out, side, 0, keepdims=False)

    small_at = 3 * wide // 128
    normed, mixed, pack = pl.pallas_call(
        functools.partial(project_kernel, share),
        grid_spec=pltpu.PrefetchScalarGridSpec(
            num_scalar_prefetch=1,
            grid=(2, count),
            in_specs=[
                pl.BlockSpec((1, part, width), lambda h, j, *_: (jnp.where(h == 0, j, count - 1), 0, 0)),
                pl.BlockSpec((1, part, width), lambda h, j, *_: (jnp.where(h == 0, 0, j), 0, 0)),
                const(width, 3 * wide),
                pl.BlockSpec((width, 128), lambda *_: (0, small_at), pipeline_mode=pl.Buffered(1)),
            ],
            out_specs=[
                pl.BlockSpec((1, 1, part, width), lambda h, j, *_: (h, j, 0, 0)),
                pl.BlockSpec((pairs, 1, 1, part, 384), lambda h, j, *_: (0, h, j, 0, 0)),
                pl.BlockSpec((16, width), lambda *_: (0, 0)),
            ],
            scratch_shapes=[pltpu.VMEM((1, 3 * wide), f32)],
        ),
        out_shape=[
            sds((2, count, part, width), bf16),
            sds((pairs, 2, count, part, 384), bf16),
            sds((16, width), f32),
        ],
        name="project",
        **kernel_params(
            2 * 2 * count * part * width * 3 * wide, 20e6, order=("arbitrary", "arbitrary")
        ),
    )(side_arr, tokens, tokens_other, w_first, w_first)
    up_bias_all = pack[8 : 8 + chunks].reshape(chunks, -1, share).transpose(1, 0, 2).reshape(chunks, width)

    same = ()
    for row in range(count):
        row_mixed = mixed if row != 1 else after(mixed, *half_way)
        row_both = lambda lanes, row=row: pl.BlockSpec((pairs, 2, 1, part, lanes), lambda *_: (0, 0, row, 0, 0))
        row_one = pl.BlockSpec((pairs, 1, part, 128), lambda *_, row=row: (0, row, 0, 0))
        row_flat = pl.BlockSpec((1, length, 128), lambda *_, row=row: (row, 0, 0))
        same = pl.pallas_call(
            functools.partial(attend_kernel, row),
            grid_spec=pltpu.PrefetchScalarGridSpec(
                num_scalar_prefetch=1,
                grid=(1,),
                in_specs=[row_both(384), row_flat, row_flat] + [pl.BlockSpec(memory_space=pl.ANY)] * len(same),
                out_specs=[row_one, row_one, row_both(128)],
                scratch_shapes=[pltpu.VMEM((heads, length, 128), bf16)] * 3
                + [pltpu.VMEM((heads, length, 128), f32)],
            ),
            out_shape=[sds((pairs, count, part, 128), bf16)] * 2 + [sds((pairs, 2, count, part, 128), bf16)],
            input_output_aliases={4 + i: i for i in range(len(same))},
            name="attend",
            **kernel_params(8e9, 7e6, 4e6),
        )(flags_f, row_mixed, qx, kx, *same)
    att_own, att_other, ext = same
    att_recv = partner(att_other)

    head_block = pl.BlockSpec((pairs, 1, part, 128), lambda j, *_: (0, j, 0, 0))
    out_tokens, gmid, glow, gdown_own, gdown_other, gup_own, gup_other, gup_bias, gvec = pl.pallas_call(
        functools.partial(mlp_kernel, planes, share),
        grid_spec=pltpu.PrefetchScalarGridSpec(
            num_scalar_prefetch=1,
            grid=(count,),
            in_specs=[
                row_block(part, width),
                head_block,
                head_block,
                const(2, wide, width),
                const(width, hidden_width),
                const(hidden_width, width),
                row_block(part, width),
                const(16, width),
                const(chunks, width),
            ],
            out_specs=[row_block(part, width)] * 3
            + [const(planes, lines, own_rows, width)] * 2
            + [const(planes, lines, chunks, share, width)] * 2
            + [const(chunks, 1, width), const(8, width)],
            scratch_shapes=[pltpu.VMEM((chunks, width, width), f32)] * 2,
        ),
        out_shape=[
            sds((count, part, width), bf16),
            sds((count, part, width), f32),
            sds((count, part, width), bf16),
        ]
        + [sds((planes, lines, own_rows, width), bf16)] * 2
        + [sds((planes, lines, chunks, share, width), bf16)] * 2
        + [sds((chunks, 1, width), f32), sds((8, width), f32)],
        name="mlp",
        **kernel_params(2 * count * part * width * (width + 6 * hidden_width), 36e6, 4.7e6),
    )(side_arr, tokens, att_own, att_recv, w_out, w_up, w_down, cotangent, pack, up_bias_all)

    glow_other = partner(glow)
    add = lambda one, two: (one.astype(f32) + two.astype(f32)).astype(bf16)
    gdown_plane = sum_plane(add(gdown_own, partner(gdown_other)))
    gup_sum = add(gup_own, partner(gup_other))

    gmixed, gmixed_bias = [], []
    ties = ()
    for pair in range(pairs):
        lane_block = lambda lanes, pair=pair: pl.BlockSpec((1, 2, 1, part, lanes), lambda j, *_: (pair, 0, j, 0, 0))
        att_block = pl.BlockSpec((1, 1, part, 128), lambda j, *_, pair=pair: (pair, j, 0, 0))
        piece, piece_bias = pl.pallas_call(
            attend_back_kernel,
            grid_spec=pltpu.PrefetchScalarGridSpec(
                num_scalar_prefetch=1,
                grid=(count,),
                in_specs=[
                    lane_block(384),
                    lane_block(128),
                    att_block,
                    att_block,
                    row_block(part, width),
                    row_block(part, width),
                    pl.BlockSpec((128, width), lambda j, *_, pair=pair: (pair, 0)),
                    row_block(length, 128),
                ],
                out_specs=[both_block(384), const(8, 384)],
                scratch_shapes=[pltpu.VMEM((2, length, 128), bf16)] * 4
                + [pltpu.VMEM((length // TQ_B, 2 * TQ_B, 128), bf16)] * 2
                + [
                    pltpu.VMEM((length // TK_B, 128, TK_B), bf16),
                    pltpu.VMEM((length // TQ_B, 128, TQ_B), f32),
                    pltpu.VMEM((length, 128), f32),
                    pltpu.VMEM((length, 128), f32),
                ],
            ),
            out_shape=[sds((2, count, part, 384), bf16), sds((8, 384), f32)],
            name="attend_back",
            **kernel_params(25e9, 20e6, 4e6),
        )(flags_b, after(mixed, *ties), ext, att_own, att_other, glow, glow_other, wo_mine, kx)
        gmixed.append(piece)
        gmixed_bias.append(piece_bias)
        if pair == 0:
            gup_plane = sum_plane(after(gup_sum, gdown_plane))
            grad_down = sum_line(gdown_plane, lines)
            ties = (gdown_plane,)
        if pair == 1:
            early, inner_sum, plain_sum = pl.pallas_call(
                functools.partial(early_kernel, planes, share),
                grid=(count,),
                in_specs=[both_block(width), both_block(384), both_block(384), const(8, 384), const(8, 384)]
                + [head_block, head_block, row_block(part, width), row_block(part, width), const(width, 768)],
                out_specs=[const(planes, lines, 3, share, width), const(width, 128), const(width, 128)],
                out_shape=[
                    sds((planes, lines, 3, share, width), bf16),
                    sds((width, 128), f32),
                    sds((width, 128), f32),
                ],
                scratch_shapes=[pltpu.VMEM((width, 768), f32), pltpu.VMEM((wide, width), f32)],
                name="early",
                **kernel_params(9e9, 25e6),
            )(normed, *gmixed, *gmixed_bias, att_own, att_other, glow, glow_other, w_first)
            early_plane = sum_plane(after(early, gup_plane))
            gup_line = sum_line(gup_plane, lines)
            ties = (gup_plane, grad_down, early)
    grad_up = gup_line.transpose(1, 0, 2).reshape(share, hidden_width)

    late = pl.pallas_call(
        functools.partial(late_kernel, planes, share),
        grid_spec=pltpu.PrefetchScalarGridSpec(
            num_scalar_prefetch=1,
            grid=(count,),
            in_specs=[
                both_block(width),
                both_block(384),
                pl.BlockSpec((width, 384), lambda *_: (0, 2), pipeline_mode=pl.Buffered(1)),
                const(width, 128),
                const(width, 128),
                const(8, 384),
                const(8, 384),
                const(8, 384),
                const(16, width),
                const(8, width),
                const(chunks, 1, width),
            ],
            out_specs=const(planes, lines, 2, share + 8, 384),
            scratch_shapes=[pltpu.VMEM((width, 384), f32)],
        ),
        out_shape=sds((planes, lines, 2, share + 8, 384), bf16),
        name="late",
        **kernel_params(4e9, 10e6),
    )(side_arr, normed, after(gmixed[2], early_plane), w_first, inner_sum, plain_sum, *gmixed_bias, pack, gvec, gup_bias)

    early_line = sum_line(early_plane, lines)
    late_plane = sum_plane(late)
    piece_spec = lambda side: pl.BlockSpec((1, 1, part, 384), lambda j, *_: (side, j, 0, 0))
    give_back = pl.pallas_call(
        give_kernel,
        grid=(count,),
        in_specs=[piece_spec(1)] * pairs + [const(width, 3 * wide)],
        out_specs=row_block(part, width),
        out_shape=sds((count, part, width), bf16),
        name="give_back",
        **kernel_params(2 * count * part * width * 3 * wide, 12e6),
    )(*gmixed[:2], after(gmixed[2], late, early_line), w_first)
    recv_back = partner(give_back)

    grad_input = pl.pallas_call(
        input_kernel,
        grid=(count,),
        in_specs=[piece_spec(0)] * pairs
        + [
            const(width, 3 * wide),
            row_block(part, width),
            row_block(part, width),
            row_block(part, width),
            const(16, width),
        ],
        out_specs=row_block(part, width),
        out_shape=sds((count, part, width), f32),
        name="input_grad",
        **kernel_params(2 * count * part * width * 3 * wide, 25e6),
    )(*gmixed, w_first, after(recv_back, late_plane), tokens, gmid, pack)

    late_line = sum_line(late_plane, lines)
    grad_out = early_line[2]
    whole = jnp.concatenate([early_line[:2], late_line[:, :share]], axis=2)
    keep = lax.dynamic_index_in_dim(whole, side, 0, keepdims=False)
    keep_small = lax.dynamic_index_in_dim(late_line[:, share:], side, 0, keepdims=False)
    give_big = lax.dynamic_index_in_dim(whole, 1 - side, 0, keepdims=False)
    give_small = lax.dynamic_index_in_dim(late_line[:, share:], 1 - side, 0, keepdims=False)
    got = partner(jnp.concatenate([give_big, jnp.pad(give_small, ((0, 0), (0, 768)))], axis=0))
    pick = lambda value: [
        jnp.concatenate([value[:share, 384 * p + 128 * k : 384 * p + 128 * k + 128] for p in range(pairs)], axis=1)
        for k in range(3)
    ]
    mine_q, other_q = pick(keep), pick(got)
    grad_qkv = jnp.concatenate(
        [
            jnp.where(first, jnp.concatenate([m, o], axis=1), jnp.concatenate([o, m], axis=1))
            for m, o in zip(mine_q, other_q)
        ],
        axis=1,
    )
    vec_rows = keep_small + got[share:, :384]
    vec = lambda slot, size: vec_rows[slot // 3, 128 * (slot % 3) : 128 * (slot % 3) + size]

    new_qkv = 0.9 * avg_qkv + 0.1 * qkv_weight.astype(f32)
    new_out = 0.9 * avg_out + 0.1 * out_weight.astype(f32)
    new_up = 0.9 * avg_up + 0.1 * up_weight.astype(f32)
    new_down = 0.9 * avg_down + 0.1 * down_weight.astype(f32)
    return (
        out_tokens,
        grad_input,
        vec(0, share),
        vec(1, share),
        grad_qkv,
        vec(6, 2 * share),
        grad_out,
        vec(2, share),
        vec(3, share),
        vec(4, share),
        grad_up,
        vec(7, chunks * share),
        grad_down,
        vec(5, share),
        new_qkv,
        new_out,
        new_up,
        new_down,
    )


def specs_for(rows):
    flat = ("seq",) + (rows if isinstance(rows, tuple) else (rows,))
    grid, ids, vec, mat = P(rows, "seq", None), P(rows, "seq"), P(flat), P(flat, None)
    ins = (grid, ids, grid, vec, vec, mat, vec, mat, vec, vec, vec, mat, vec, mat, vec, mat, mat, mat, mat)
    outs = (grid, grid, vec, vec, mat, vec, mat, vec, vec, vec, mat, vec, mat, vec, mat, mat, mat, mat)
    return ins, outs


def solution(mesh):
    parts, rows = mesh.shape["seq"], mesh.shape["rows"]
    planes = 4
    if parts != 2 or rows % planes:
        ins, outs = specs_for("rows")
        return jax.shard_map(on_device, mesh=mesh, in_specs=ins, out_specs=outs, check_vma=False)
    lines = rows // planes
    finer = Mesh(mesh.devices.reshape(parts, lines, 2, 2), ("seq", "line", "y", "x"))
    ins, outs = specs_for(("line", "y", "x"))
    return jax.shard_map(
        functools.partial(pair_device, lines, planes), mesh=finer, in_specs=ins, out_specs=outs, check_vma=False
    )
```

```python
import functools

import jax
import jax.numpy as jnp
from jax import lax
from jax.experimental import pallas as pl
from jax.experimental.pallas import tpu as pltpu
from jax.sharding import Mesh
from jax.sharding import PartitionSpec as P

HEADS = 12
HEAD_DIM = 64
CLIPS = 6


def layer_norm(value, gain, bias):
    middle = jnp.mean(value, axis=-1, keepdims=True)
    centred = value - middle
    spread = jnp.mean(centred * centred, axis=-1, keepdims=True)
    return centred * lax.rsqrt(spread + 1e-06) * gain + bias


def exact_gelu(value):
    return jax.nn.gelu(value, approximate=False)


def permitted(seg_query, seg_key, pos_query, pos_key):
    same_clip = seg_query[:, :, None] == seg_key[:, None, :]
    open_key = (seg_key != CLIPS - 1)[:, None, :]
    diagonal = (pos_query[:, None] == pos_key[None, :])[None]
    return (same_clip & (open_key | diagonal))[:, :, None, :]


def scores(query_part, key_part):
    return 0.125 * jnp.einsum(
        "rqhe,rkhe->rqhk", query_part, key_part, preferred_element_type=jnp.float32
    )


def exponent(score_vals, allowed):
    return jnp.where(allowed, jnp.exp(jnp.where(allowed, score_vals, 0.0)), 0.0)


def on_device(
    tokens,
    segment_ids,
    cotangent,
    ln1_gain,
    ln1_bias,
    qkv_weight,
    qv_bias,
    out_weight,
    out_bias,
    ln2_gain,
    ln2_bias,
    up_weight,
    up_bias,
    down_weight,
    down_bias,
    avg_qkv,
    avg_out,
    avg_up,
    avg_down,
):
    f32 = jnp.float32
    bf16 = jnp.bfloat16
    rows_here, shard_len, width = tokens.shape
    count_rows = rows_here * shard_len
    own_pos = lax.axis_index("seq") * shard_len + jnp.arange(shard_len, dtype=jnp.int32)
    head_shape = (rows_here, shard_len, HEADS, HEAD_DIM)
    gain_one, bias_one, w_qkv, b_qv, w_out, b_out = (
        lax.all_gather(ln1_gain, ("seq", "rows"), axis=0, tiled=True),
        lax.all_gather(ln1_bias, ("seq", "rows"), axis=0, tiled=True),
        lax.all_gather(qkv_weight, ("seq", "rows"), axis=0, tiled=True),
        lax.all_gather(qv_bias, ("seq", "rows"), axis=0, tiled=True),
        lax.all_gather(out_weight, ("seq", "rows"), axis=0, tiled=True),
        lax.all_gather(out_bias, ("seq", "rows"), axis=0, tiled=True),
    )
    residual = tokens.astype(f32).reshape(count_rows, width)
    normed, norm_one_pull = jax.vjp(
        layer_norm, residual, gain_one.astype(f32), bias_one.astype(f32)
    )
    normed_low = normed.astype(bf16)
    mixed = jnp.dot(normed_low, w_qkv, preferred_element_type=f32)
    bias_qv = b_qv.astype(f32)
    query_heads = (mixed[:, :width] + bias_qv[:width]).astype(bf16).reshape(head_shape)
    key_heads = mixed[:, width : 2 * width].astype(bf16).reshape(head_shape)
    value_heads = (mixed[:, 2 * width :] + bias_qv[width:]).astype(bf16).reshape(head_shape)
    start_state = (jnp.zeros((rows_here, shard_len, HEADS), f32), jnp.zeros(head_shape, f32))
    piece_keys = lax.all_gather(key_heads, "seq", axis=1, tiled=True)
    piece_values = lax.all_gather(value_heads, "seq", axis=1, tiled=True)
    piece_seg = lax.all_gather(segment_ids, "seq", axis=1, tiled=True)
    piece_len = piece_keys.shape[1]
    block_len = min(piece_len, shard_len)

    def forward_advance(turn, state):
        totals, weighted = state
        offset = turn * block_len
        key_block = lax.dynamic_slice_in_dim(piece_keys, offset, block_len, 1)
        value_block = lax.dynamic_slice_in_dim(piece_values, offset, block_len, 1)
        seg_block = lax.dynamic_slice_in_dim(piece_seg, offset, block_len, 1)
        key_pos = offset + jnp.arange(block_len, dtype=jnp.int32)
        allowed = permitted(segment_ids, seg_block, own_pos, key_pos)
        expo = exponent(scores(query_heads, key_block), allowed)
        totals = totals + jnp.sum(expo, axis=-1)
        weighted = weighted + jnp.einsum(
            "rqhk,rkhe->rqhe", expo.astype(bf16), value_block, preferred_element_type=f32
        )
        return (totals, weighted)

    totals, weighted = lax.fori_loop(0, piece_len // block_len, forward_advance, start_state)
    attended = weighted / totals[..., None]
    attn_in = attended.reshape(count_rows, width).astype(bf16)
    middle = residual + jnp.dot(attn_in, w_out, preferred_element_type=f32) + b_out.astype(f32)
    gain_two, bias_two, w_up, b_up, w_down, b_down = (
        lax.all_gather(ln2_gain, ("seq", "rows"), axis=0, tiled=True),
        lax.all_gather(ln2_bias, ("seq", "rows"), axis=0, tiled=True),
        lax.all_gather(up_weight, ("seq", "rows"), axis=0, tiled=True),
        lax.all_gather(up_bias, ("seq", "rows"), axis=0, tiled=True),
        lax.all_gather(down_weight, ("seq", "rows"), axis=0, tiled=True),
        lax.all_gather(down_bias, ("seq", "rows"), axis=0, tiled=True),
    )
    normed_two, norm_two_pull = jax.vjp(
        layer_norm, middle, gain_two.astype(f32), bias_two.astype(f32)
    )
    normed_two_low = normed_two.astype(bf16)
    hidden_pre = jnp.dot(normed_two_low, w_up, preferred_element_type=f32) + b_up.astype(f32)
    hidden, gelu_pull = jax.vjp(exact_gelu, hidden_pre)
    hidden_low = hidden.astype(bf16)
    final = middle + jnp.dot(hidden_low, w_down, preferred_element_type=f32) + b_down.astype(f32)
    out_tokens = final.astype(bf16).reshape(tokens.shape)
    w_up_back, w_down_back = (
        lax.all_gather(up_weight, ("seq", "rows"), axis=0, tiled=True),
        lax.all_gather(down_weight, ("seq", "rows"), axis=0, tiled=True),
    )
    grad_out = cotangent.astype(f32).reshape(count_rows, width)
    grad_low = grad_out.astype(bf16)
    grad_down = jnp.einsum("nf,nd->fd", hidden_low, grad_low, preferred_element_type=f32)
    grad_down_b = jnp.sum(grad_low, axis=0, dtype=f32)
    grad_hidden = jnp.einsum("nd,fd->nf", grad_low, w_down_back, preferred_element_type=f32)
    (grad_pre,) = gelu_pull(grad_hidden)
    grad_pre_low = grad_pre.astype(bf16)
    grad_up = jnp.einsum("nd,nf->df", normed_two_low, grad_pre_low, preferred_element_type=f32)
    grad_up_b = jnp.sum(grad_pre_low, axis=0, dtype=f32)
    grad_normed_two = jnp.einsum("nf,df->nd", grad_pre_low, w_up_back, preferred_element_type=f32)
    grad_mid_norm, grad_gain_two, grad_bias_two = norm_two_pull(grad_normed_two)
    grad_mid = grad_out + grad_mid_norm
    mlp_sums = (
        lax.psum_scatter(grad_gain_two, ("seq", "rows"), scatter_dimension=0, tiled=True),
        lax.psum_scatter(grad_bias_two, ("seq", "rows"), scatter_dimension=0, tiled=True),
        lax.psum_scatter(grad_up, ("seq", "rows"), scatter_dimension=0, tiled=True),
        lax.psum_scatter(grad_up_b, ("seq", "rows"), scatter_dimension=0, tiled=True),
        lax.psum_scatter(grad_down, ("seq", "rows"), scatter_dimension=0, tiled=True),
        lax.psum_scatter(grad_down_b, ("seq", "rows"), scatter_dimension=0, tiled=True),
    )
    w_qkv_back, w_out_back = (
        lax.all_gather(qkv_weight, ("seq", "rows"), axis=0, tiled=True),
        lax.all_gather(out_weight, ("seq", "rows"), axis=0, tiled=True),
    )
    grad_mid_low = grad_mid.astype(bf16)
    grad_wout = jnp.einsum("nd,ne->de", attn_in, grad_mid_low, preferred_element_type=f32)
    grad_bout = jnp.sum(grad_mid_low, axis=0, dtype=f32)
    grad_att = jnp.einsum(
        "ne,de->nd", grad_mid_low, w_out_back, preferred_element_type=f32
    ).reshape(head_shape)
    grad_acc = (grad_att / totals[..., None]).astype(bf16)
    shift_low = (jnp.sum(grad_att * attended, axis=-1) / totals).astype(bf16)
    shift_wide = shift_low.astype(f32)
    query_piece_keys = lax.all_gather(key_heads, "seq", axis=1, tiled=True)
    query_piece_values = lax.all_gather(value_heads, "seq", axis=1, tiled=True)
    query_piece_seg = lax.all_gather(segment_ids, "seq", axis=1, tiled=True)
    piece_len = query_piece_keys.shape[1]
    query_block_len = min(piece_len, shard_len)

    def query_advance(turn, grad_query):
        offset = turn * query_block_len
        key_block = lax.dynamic_slice_in_dim(query_piece_keys, offset, query_block_len, 1)
        value_block = lax.dynamic_slice_in_dim(query_piece_values, offset, query_block_len, 1)
        seg_block = lax.dynamic_slice_in_dim(query_piece_seg, offset, query_block_len, 1)
        key_pos = offset + jnp.arange(query_block_len, dtype=jnp.int32)
        allowed = permitted(segment_ids, seg_block, own_pos, key_pos)
        expo = exponent(scores(query_heads, key_block), allowed)
        inner = jnp.einsum("rqhe,rkhe->rqhk", grad_acc, value_block, preferred_element_type=f32)
        grad_score = (expo * (inner - shift_wide[..., None])).astype(bf16)
        return grad_query + jnp.einsum(
            "rqhk,rkhe->rqhe", grad_score, key_block, preferred_element_type=f32
        )

    grad_query = lax.fori_loop(
        0, piece_len // query_block_len, query_advance, jnp.zeros(head_shape, f32)
    )
    key_start = (jnp.zeros(head_shape, f32), jnp.zeros(head_shape, f32))
    piece_queries = lax.all_gather(query_heads, "seq", axis=1, tiled=True)
    piece_grads = lax.all_gather(grad_acc, "seq", axis=1, tiled=True)
    key_piece_seg = lax.all_gather(segment_ids, "seq", axis=1, tiled=True)
    piece_shift = lax.all_gather(shift_low, "seq", axis=1, tiled=True)
    piece_len = piece_queries.shape[1]
    key_block_len = min(piece_len, shard_len)

    def key_advance(turn, state):
        grad_key, grad_value = state
        offset = turn * key_block_len
        query_block = lax.dynamic_slice_in_dim(piece_queries, offset, key_block_len, 1)
        grad_block = lax.dynamic_slice_in_dim(piece_grads, offset, key_block_len, 1)
        seg_block = lax.dynamic_slice_in_dim(key_piece_seg, offset, key_block_len, 1)
        shift_block = lax.dynamic_slice_in_dim(piece_shift, offset, key_block_len, 1).astype(f32)
        query_pos = offset + jnp.arange(key_block_len, dtype=jnp.int32)
        allowed = permitted(seg_block, segment_ids, query_pos, own_pos)
        expo = exponent(scores(query_block, key_heads), allowed)
        inner = jnp.einsum("rqhe,rkhe->rqhk", grad_block, value_heads, preferred_element_type=f32)
        grad_score = (expo * (inner - shift_block[..., None])).astype(bf16)
        grad_key = grad_key + jnp.einsum(
            "rqhk,rqhe->rkhe", grad_score, query_block, preferred_element_type=f32
        )
        grad_value = grad_value + jnp.einsum(
            "rqhk,rqhe->rkhe", expo.astype(bf16), grad_block, preferred_element_type=f32
        )
        return (grad_key, grad_value)

    grad_key, grad_value = lax.fori_loop(0, piece_len // key_block_len, key_advance, key_start)
    grad_q_low = (0.125 * grad_query).astype(bf16).reshape(count_rows, width)
    grad_k_low = (0.125 * grad_key).astype(bf16).reshape(count_rows, width)
    grad_v_low = grad_value.astype(bf16).reshape(count_rows, width)
    grad_mixed = jnp.concatenate([grad_q_low, grad_k_low, grad_v_low], axis=1)
    grad_wqkv = jnp.einsum("nd,ne->de", normed_low, grad_mixed, preferred_element_type=f32)
    grad_bqv = jnp.concatenate(
        [jnp.sum(grad_q_low, axis=0, dtype=f32), jnp.sum(grad_v_low, axis=0, dtype=f32)], axis=0
    )
    grad_normed = jnp.einsum("ne,de->nd", grad_mixed, w_qkv_back, preferred_element_type=f32)
    grad_res_norm, grad_gain_one, grad_bias_one = norm_one_pull(grad_normed)
    grad_input = (grad_mid + grad_res_norm).reshape(tokens.shape)
    attn_sums = (
        lax.psum_scatter(grad_gain_one, ("seq", "rows"), scatter_dimension=0, tiled=True),
        lax.psum_scatter(grad_bias_one, ("seq", "rows"), scatter_dimension=0, tiled=True),
        lax.psum_scatter(grad_wqkv, ("seq", "rows"), scatter_dimension=0, tiled=True),
        lax.psum_scatter(grad_bqv, ("seq", "rows"), scatter_dimension=0, tiled=True),
        lax.psum_scatter(grad_wout, ("seq", "rows"), scatter_dimension=0, tiled=True),
        lax.psum_scatter(grad_bout, ("seq", "rows"), scatter_dimension=0, tiled=True),
    )
    new_qkv = 0.9 * avg_qkv + 0.1 * qkv_weight.astype(f32)
    new_out = 0.9 * avg_out + 0.1 * out_weight.astype(f32)
    new_up = 0.9 * avg_up + 0.1 * up_weight.astype(f32)
    new_down = 0.9 * avg_down + 0.1 * down_weight.astype(f32)
    return (
        out_tokens,
        grad_input,
        attn_sums[0],
        attn_sums[1],
        attn_sums[2],
        attn_sums[3],
        attn_sums[4],
        attn_sums[5],
        mlp_sums[0],
        mlp_sums[1],
        mlp_sums[2],
        mlp_sums[3],
        mlp_sums[4],
        mlp_sums[5],
        new_qkv,
        new_out,
        new_up,
        new_down,
    )


f32 = jnp.float32
bf16 = jnp.bfloat16
NT = (((1,), (1,)), ((), ()))
LOG2E = 1.4426950408889634
SCORE = 0.125 * LOG2E
BIG = 16384.0
VMEM_BYTES = 63 * 1024 * 1024
TQ_F, TK_F = 512, 256
TK_B, TQ_B = 512, 512
LANE_LOG = 41
LANE_PAD = 44


def kernel_params(flops, bytes_accessed, transcendentals=0, order=("arbitrary",)):
    return dict(
        compiler_params=pltpu.CompilerParams(
            vmem_limit_bytes=VMEM_BYTES, dimension_semantics=order
        ),
        cost_estimate=pl.CostEstimate(
            flops=int(flops), bytes_accessed=int(bytes_accessed), transcendentals=int(transcendentals)
        ),
    )


def standardise(value):
    middle = jnp.mean(value, axis=-1, keepdims=True)
    centred = value - middle
    spread = jnp.mean(centred * centred, axis=-1, keepdims=True)
    rstd = lax.rsqrt(spread + 1e-06)
    return centred * rstd, rstd


def norm_pull(grad_normed, gain, xhat, rstd):
    scaled = grad_normed * gain
    first = jnp.mean(scaled, axis=-1, keepdims=True)
    second = jnp.mean(scaled * xhat, axis=-1, keepdims=True)
    return rstd * (scaled - first - xhat * second)


def gelu_pair(x):
    size = jnp.abs(x)
    base = 1.0 + 0.23164189 * size
    t = 1.0 / base
    bell = jnp.exp2(x * x * (-0.5 * LOG2E))
    poly = t * (0.127414796 + t * (-0.142248368 + t * (0.7107068705 + t * (-0.7265760135 + t * 0.5307027145))))
    tail = poly * bell
    phi = jnp.where(x >= 0.0, 1.0 - tail, tail)
    return x * phi, phi + x * bell * 0.3989422804014327


def lane_masks():
    lane = lax.broadcasted_iota(jnp.int32, (1, 128), 1)
    low = jnp.where(lane < HEAD_DIM, 1.0, 0.0)
    return low.astype(bf16), (1.0 - low).astype(bf16)


def prepare_kernel(share, side_ref, w_ref, *refs):
    vectors, (mine_ref, give_ref) = refs[:-2], refs[-2:]
    wide = w_ref.shape[1] // 6
    pairs = wide // 128
    for target, side in ((mine_ref, side_ref[0]), (give_ref, 1 - side_ref[0])):
        for pair in range(pairs):
            for kind in range(3):
                start = pl.multiple_of(kind * 2 * wide + side * wide + pair * 128, 128)
                at = 384 * pair + 128 * kind
                target[:, at : at + 128] = w_ref[:, pl.ds(start, 128)]
    lane = lax.broadcasted_iota(jnp.int32, (share, 128), 1)
    small = jnp.zeros((share, 128), f32)
    column = 0
    for ref in vectors:
        row = jnp.broadcast_to(ref[...].astype(f32), (8, ref.shape[1])).T
        for start in range(0, ref.shape[1], share):
            small = jnp.where(lane == column, row[start : start + share, 0:1], small)
            column += 1
    small = small.astype(bf16)
    mine_ref[:, 3 * wide :] = small
    give_ref[:, 3 * wide :] = small


def project_kernel(
    share, side_ref, own_ref, other_ref, w_ref, small_ref, normed_ref, mixed_ref, pack_ref, shift_s
):
    which, turn = pl.program_id(0), pl.program_id(1)
    wide = shift_s.shape[1] // 3
    pairs = wide // 128

    @pl.when((which == 0) & (turn == 0))
    def _():
        small = small_ref[...].astype(f32).T
        pack_ref[...] = small[0:16]
        shift_s[...] = jnp.zeros_like(shift_s)
        spot = lax.broadcasted_iota(jnp.int32, (wide, wide), 0)
        target = lax.broadcasted_iota(jnp.int32, (wide, wide), 1) + side_ref[0] * wide
        sums = [jnp.zeros((16, wide), f32), jnp.zeros((16, wide), f32)]
        for part in range(2):
            wanted = lax.div(spot, share) * (2 * share) + part * share + lax.rem(spot, share)
            chosen = jnp.where(wanted == target, 1.0, 0.0).astype(bf16)
            for kind in range(2):
                values = small[6 + part : 7 + part, kind * wide : (kind + 1) * wide]
                values = jnp.broadcast_to(values, (16, wide)).astype(bf16)
                sums[kind] += jnp.dot(values, chosen, preferred_element_type=f32)
        for pair in range(pairs):
            lanes = slice(128 * pair, 128 * pair + 128)
            shift_s[:, 384 * pair : 384 * pair + 128] = sums[0][0:1, lanes]
            shift_s[:, 384 * pair + 256 : 384 * pair + 384] = sums[1][0:1, lanes]

    tiles = 2
    size = normed_ref.shape[2] // tiles

    def normed_tile(i):
        rows = slice(i * size, (i + 1) * size)
        value = jnp.where(which == 0, own_ref[0, rows], other_ref[0, rows]).astype(f32)
        xhat, _ = standardise(value)
        normed = (xhat * pack_ref[0:1, :] + pack_ref[1:2, :]).astype(bf16)
        normed_ref[0, 0, rows] = normed
        return normed

    normed = normed_tile(0)
    for i in range(tiles):
        mixed = jnp.dot(normed, w_ref[...], preferred_element_type=f32) + shift_s[...]
        mixed = mixed.astype(bf16)
        if i + 1 < tiles:
            normed = normed_tile(i + 1)
        for pair in range(pairs):
            lanes = slice(384 * pair, 384 * pair + 384)
            mixed_ref[pair, 0, 0, i * size : (i + 1) * size] = mixed[:, lanes]


def attend_kernel(row, flag_ref, mixed_ref, qx_ref, kx_ref, *rest):
    own_ref, other_ref, ext_ref, q_s, k_s, v_s, acc_s = rest[-7:]
    length = q_s.shape[1]
    heads = q_s.shape[0]
    half = length // 2
    low, high = lane_masks()
    qx, kx = qx_ref[0], kx_ref[0]
    q_low, q_high, k_low, k_high = qx * low, qx * high, kx * low, kx * high
    for pair in range(heads // 2):
        q = mixed_ref[pair, :, 0, :, 0:128].reshape(length, 128)
        k = mixed_ref[pair, :, 0, :, 128:256].reshape(length, 128)
        v = mixed_ref[pair, :, 0, :, 256:384].reshape(length, 128)
        q_s[2 * pair] = q * low + q_high
        q_s[2 * pair + 1] = q * high + q_low
        k_s[2 * pair] = k * low + k_high
        k_s[2 * pair + 1] = k * high + k_low
        v_s[2 * pair] = v * low + high
        v_s[2 * pair + 1] = v * high + low
    acc_s[...] = jnp.zeros_like(acc_s)
    key_blocks = length // TK_F

    def step(index, carry):
        @pl.when(flag_ref[row, index] != 0)
        def _():
            q_at = pl.ds(pl.multiple_of((index // key_blocks) * TQ_F, TQ_F), TQ_F)
            k_at = pl.ds(pl.multiple_of((index % key_blocks) * TK_F, TK_F), TK_F)
            for head in range(heads):
                score = lax.dot_general(
                    q_s[head, q_at, :], k_s[head, k_at, :], NT, preferred_element_type=f32
                )
                expo = jnp.exp2(score * SCORE).astype(bf16)
                acc_s[head, q_at, :] += jnp.dot(expo, v_s[head, k_at, :], preferred_element_type=f32)

        return carry

    lax.fori_loop(0, (length // TQ_F) * key_blocks, step, 0)
    lane = lax.broadcasted_iota(jnp.int32, (half, 128), 1)
    first_half = lane < HEAD_DIM
    spot = lane % HEAD_DIM
    for pair in range(heads // 2):
        for side in range(2):
            rows = slice(side * half, (side + 1) * half)
            first, second = acc_s[2 * pair, rows], acc_s[2 * pair + 1, rows]
            top = jnp.where(first_half, first, second)
            crossed = jnp.where(first_half, second, first)
            totals = pltpu.roll(crossed, HEAD_DIM, 1)
            target = own_ref if side == 0 else other_ref
            target[pair, 0] = (top / totals).astype(bf16)
            lse = -8.0 * jnp.log(crossed)
            lse_a = lse.astype(bf16).astype(f32)
            lse_b = (lse - lse_a).astype(bf16).astype(f32)
            ext = jnp.where(
                spot == LANE_LOG,
                lse_a,
                jnp.where(
                    spot == LANE_LOG + 1,
                    lse_b,
                    jnp.where(spot == LANE_LOG + 2, lse - lse_a - lse_b, qx[rows].astype(f32)),
                ),
            )
            ext_ref[pair, side, 0] = ext.astype(bf16)


def join_lanes(ref):
    return jnp.concatenate([ref[i, 0] for i in range(ref.shape[0])], axis=1)


def mlp_kernel(
    planes, share, side_ref, x_ref, mine_ref, recv_ref, wo_ref, up_ref, down_ref, grad_ref, pack_ref, upb_ref,
    out_ref, glow_ref, gdown_own, gdown_other, gup_own, gup_other, gbias_ref, gvec_ref,
    down_s, up_s,
):
    turn = pl.program_id(0)
    side = side_ref[0]
    chunks, size = down_s.shape[0], down_s.shape[2]
    middle = (
        x_ref[0].astype(f32)
        + jnp.dot(join_lanes(mine_ref), wo_ref[side], preferred_element_type=f32)
        + jnp.dot(join_lanes(recv_ref), wo_ref[1 - side], preferred_element_type=f32)
        + pack_ref[2:3, :]
    )
    xhat, rstd = standardise(middle)
    normed = (xhat * pack_ref[3:4, :] + pack_ref[4:5, :]).astype(bf16)
    normed_t = normed.T
    grad = grad_ref[0]
    grad_t = grad.T
    total = middle + pack_ref[5:6, :]

    @pl.when(turn == 0)
    def _():
        down_s[...] = jnp.zeros_like(down_s)
        up_s[...] = jnp.zeros_like(up_s)
        gbias_ref[...] = jnp.zeros_like(gbias_ref)
        gvec_ref[...] = jnp.zeros_like(gvec_ref)

    def first_layer(f):
        at = slice(f * size, (f + 1) * size)
        return jnp.dot(normed, up_ref[:, at], preferred_element_type=f32) + upb_ref[f : f + 1, :]

    gnormed = None
    pre = first_layer(0)
    for f in range(chunks):
        at = slice(f * size, (f + 1) * size)
        hidden, slope = gelu_pair(pre)
        ghidden = lax.dot_general(grad, down_ref[at, :], NT, preferred_element_type=f32)
        if f + 1 < chunks:
            pre = first_layer(f + 1)
        hidden = hidden.astype(bf16)
        gpre = (ghidden * slope).astype(bf16)
        total = total + jnp.dot(hidden, down_ref[at, :], preferred_element_type=f32)
        part = lax.dot_general(gpre, up_ref[:, at], NT, preferred_element_type=f32)
        gnormed = part if gnormed is None else gnormed + part
        down_s[f] += jnp.dot(grad_t, hidden, preferred_element_type=f32)
        up_s[f] += jnp.dot(normed_t, gpre, preferred_element_type=f32)
        gbias_ref[f] += jnp.sum(gpre.astype(f32), axis=0, keepdims=True)
    out_ref[0] = total.astype(bf16)
    gmid = grad.astype(f32) + norm_pull(gnormed, pack_ref[3:4, :], xhat, rstd)
    low = gmid.astype(bf16)
    glow_ref[0] = low
    gvec_ref[0:1, :] += jnp.sum(gnormed * xhat, axis=0, keepdims=True)
    gvec_ref[1:2, :] += jnp.sum(gnormed, axis=0, keepdims=True)
    gvec_ref[2:3, :] += jnp.sum(low.astype(f32), axis=0, keepdims=True)
    gvec_ref[3:4, :] += jnp.sum(grad.astype(f32), axis=0, keepdims=True)

    @pl.when(turn == pl.num_programs(0) - 1)
    def _():
        half = chunks // 2
        rows = chunks * share
        per_chunk = size // rows
        for f in range(chunks):
            whole = down_s[f].astype(bf16).T
            for target, wanted in ((gdown_own, f // half), (gdown_other, 1 - f // half)):

                @pl.when(side == wanted)
                def _(target=target, whole=whole, f=f):
                    for i in range(per_chunk):
                        at = (f % half) * per_chunk + i
                        target[at % planes, at // planes] = whole[i * rows : (i + 1) * rows]

        wide = up_s.shape[1] // 2
        for target, base in ((gup_own, side * wide), (gup_other, (1 - side) * wide)):
            for f in range(chunks):
                for at in range(wide // share):
                    start = pl.multiple_of(base + at * share, 8)
                    target[at % planes, at // planes, f] = up_s[f, pl.ds(start, share), :].astype(bf16)


def attend_back_kernel(
    flag_ref, mixed_ref, ext_ref, att_own, att_other, own_ref, other_ref, wo_ref, kx_ref,
    gmixed_ref, gbias_ref,
    q_s, d_s, k_s, v_s, kt_s, gq_s, gk_s, gv_s,
):
    row = pl.program_id(0)
    length = k_s.shape[0]
    half = length // 2
    low, high = lane_masks()
    lane = lax.broadcasted_iota(jnp.int32, (1, 128), 1)
    spot = lane % HEAD_DIM
    square_row = lax.broadcasted_iota(jnp.int32, (128, 128), 0) < HEAD_DIM
    square_col = lax.broadcasted_iota(jnp.int32, (128, 128), 1) < HEAD_DIM
    crossing = jnp.where(square_row == square_col, 0.0, -1.0).astype(bf16)
    one_hot_a = jnp.where(spot == 0, 1.0, 0.0)
    one_hot_b = jnp.where(spot == 1, 1.0, 0.0)
    v_ext = (one_hot_a + one_hot_b).astype(bf16)

    @pl.when(row == 0)
    def _():
        gbias_ref[...] = jnp.zeros_like(gbias_ref)

    mixed_at = lambda lanes: mixed_ref[0, :, 0, :, lanes].reshape(length, 128)
    q, k = mixed_at(slice(0, 128)), mixed_at(slice(128, 256))
    ext = ext_ref[0, :, 0].reshape(length, 128)
    k_s[:, 0:128] = k
    k_s[:, 128:256] = kx_ref[0]
    v_s[:, 0:128] = mixed_at(slice(256, 384))
    v_s[:, 128:256] = jnp.broadcast_to(v_ext, (length, 128))
    for head, (mine, other) in enumerate(((low, high), (high, low))):
        q_part, ext_part = q * mine, ext * other
        for i in range(length // TQ_B):
            at = slice(i * TQ_B, (i + 1) * TQ_B)
            rows = slice(head * TQ_B, (head + 1) * TQ_B)
            q_s[i, rows, 0:128] = q_part[at]
            q_s[i, rows, 128:256] = ext_part[at]
    for side in range(2):
        gates = own_ref[0] if side == 0 else other_ref[0]
        d = lax.dot_general(gates, wo_ref[...], NT, preferred_element_type=f32)
        moved = d * (att_own if side == 0 else att_other)[0, 0].astype(f32)
        moved_a = moved.astype(bf16)
        moved_b = (moved - moved_a.astype(f32)).astype(bf16)
        shift = jnp.dot(moved_a, crossing, preferred_element_type=f32) + jnp.dot(
            moved_b, crossing, preferred_element_type=f32
        )
        shift_a = shift.astype(bf16).astype(f32)
        dx = (shift_a * one_hot_a + (shift - shift_a) * one_hot_b).astype(bf16)
        d = d.astype(bf16)
        tile = min(TQ_B, half)
        for head, (mine, other) in enumerate(((low, high), (high, low))):
            d_part, dx_part = d * mine, dx * other
            for i in range(half // tile):
                at = slice(i * tile, (i + 1) * tile)
                start = side * half + i * tile
                rows = slice(head * TQ_B + start % TQ_B, head * TQ_B + start % TQ_B + tile)
                d_s[start // TQ_B, rows, 0:128] = d_part[at]
                d_s[start // TQ_B, rows, 128:256] = dx_part[at]
    for i in range(length // TK_B):
        kt_s[i] = k[i * TK_B : (i + 1) * TK_B].T
    gq_s[...] = jnp.zeros_like(gq_s)
    gk_s[...] = jnp.zeros_like(gk_s)
    gv_s[...] = jnp.zeros_like(gv_s)
    query_blocks = length // TQ_B

    def step(index, carry):
        @pl.when(flag_ref[row, index] != 0)
        def _():
            qi = index % query_blocks
            ki = index // query_blocks
            k_at = pl.ds(pl.multiple_of(ki * TK_B, TK_B), TK_B)
            probs, grads = [], []
            for head in range(2):
                rows = slice(head * TQ_B, (head + 1) * TQ_B)
                score = lax.dot_general(
                    k_s[k_at, :], q_s[qi, rows, :], NT, preferred_element_type=f32
                )
                inner = lax.dot_general(
                    v_s[k_at, :], d_s[qi, rows, :], NT, preferred_element_type=f32
                )
                prob = jnp.exp2(score * SCORE)
                probs.append(prob.astype(bf16))
                grads.append((prob * inner).astype(bf16))
            for head in range(2):
                at = slice(head * HEAD_DIM, (head + 1) * HEAD_DIM)
                gq_s[qi, at, :] += jnp.dot(kt_s[ki, at, :], grads[head], preferred_element_type=f32)
            gv_s[k_at, :] += jnp.dot(
                jnp.concatenate(probs, axis=1), d_s[qi, :, 0:128], preferred_element_type=f32
            )
            gk_s[k_at, :] += jnp.dot(
                jnp.concatenate(grads, axis=1), q_s[qi, :, 0:128], preferred_element_type=f32
            )

        return carry

    lax.fori_loop(0, query_blocks * (length // TK_B), step, 0)
    for i in range(query_blocks):
        gq = (0.125 * gq_s[i].T).astype(bf16)
        for start in range(0, TQ_B, min(TQ_B, half)):
            at = i * TQ_B + start
            size = min(TQ_B, half)
            gmixed_ref[at // half, 0, at % half : at % half + size, 0:128] = gq[start : start + size]
        gbias_ref[0:1, 0:128] += jnp.sum(gq.astype(f32), axis=0, keepdims=True)
    gk = (0.125 * gk_s[...]).astype(bf16)
    gv = gv_s[...].astype(bf16)
    gbias_ref[0:1, 128:256] += jnp.sum(gk.astype(f32), axis=0, keepdims=True)
    gbias_ref[0:1, 256:384] += jnp.sum(gv.astype(f32), axis=0, keepdims=True)
    for side in range(2):
        gmixed_ref[side, 0, :, 128:256] = gk[side * half : (side + 1) * half]
        gmixed_ref[side, 0, :, 256:384] = gv[side * half : (side + 1) * half]


def weight_dot(normed_ref, *piece_refs):
    normed_t = jnp.concatenate([normed_ref[0, 0], normed_ref[1, 0]], axis=0).T
    sides = []
    for side in range(2):
        sides.append(jnp.concatenate([ref[side, 0] for ref in piece_refs], axis=1))
    return jnp.dot(normed_t, jnp.concatenate(sides, axis=0), preferred_element_type=f32)


def fold_lanes(value):
    total = value[:, 0:128]
    for at in range(128, value.shape[1], 128):
        total = total + value[:, at : at + 128]
    return total


def early_kernel(
    planes, share, normed_ref, g0_ref, g1_ref, b0_ref, b1_ref, mine_ref, other_ref, low_ref, low_other_ref, w_ref,
    unit_ref, first_ref, second_ref, acc_s, out_s,
):
    turn = pl.program_id(0)

    @pl.when(turn == 0)
    def _():
        acc_s[...] = jnp.zeros_like(acc_s)
        out_s[...] = jnp.zeros_like(out_s)

    acc_s[...] += weight_dot(normed_ref, g0_ref, g1_ref)
    across = (((0,), (0,)), ((), ()))
    out_s[...] += lax.dot_general(
        join_lanes(mine_ref), low_ref[0], across, preferred_element_type=f32
    ) + lax.dot_general(join_lanes(other_ref), low_other_ref[0], across, preferred_element_type=f32)

    @pl.when(turn == pl.num_programs(0) - 1)
    def _():
        weights = w_ref[...].astype(f32)
        sums = jnp.concatenate([b0_ref[0:1, :], b1_ref[0:1, :]], axis=1)
        first_ref[...] = fold_lanes(weights * acc_s[...])
        second_ref[...] = fold_lanes(weights * sums)
        count = out_s.shape[0] // share
        for at in range(count):
            spot = (at % planes, at // planes)
            for side in range(2):
                start = (side * count + at) * share
                unit_ref[spot + (side,)] = acc_s[start : start + share, :].astype(bf16)
            unit_ref[spot + (2,)] = out_s[at * share : (at + 1) * share, :].astype(bf16)


def scatter_rows(vector, step, offset, owners):
    n = vector.shape[1]
    owner = lax.broadcasted_iota(jnp.int32, (owners, n), 0) - offset
    mask = lax.div(lax.broadcasted_iota(jnp.int32, (owners, n), 1), step) == owner
    spread = jnp.where(mask, jnp.broadcast_to(vector, (owners, n)), 0.0).astype(bf16)
    lane = lax.rem(lax.broadcasted_iota(jnp.int32, (128, n), 1), step)
    chosen = jnp.where(lane == lax.broadcasted_iota(jnp.int32, (128, n), 0), 1.0, 0.0).astype(bf16)
    return lax.dot_general(spread, chosen, NT, preferred_element_type=f32)


def late_kernel(
    planes, share, side_ref, normed_ref, g_ref, w_ref, first_ref, second_ref, b0_ref, b1_ref, b2_ref, pack_ref,
    gvec_ref, gup_ref, unit_ref, acc_s,
):
    turn = pl.program_id(0)

    @pl.when(turn == 0)
    def _():
        acc_s[...] = jnp.zeros_like(acc_s)

    acc_s[...] += weight_dot(normed_ref, g_ref)

    @pl.when(turn == pl.num_programs(0) - 1)
    def _():
        side = side_ref[0]
        weights = w_ref[...].astype(f32)
        width = weights.shape[0]
        owners = width // share
        count = owners // 2
        inner = first_ref[...] + fold_lanes(weights * acc_s[...])
        plain = second_ref[...] + fold_lanes(weights * b2_ref[0:1, :])
        inner = jnp.sum(inner.T, axis=0, keepdims=True)
        plain = jnp.sum(plain.T, axis=0, keepdims=True)
        gain, bias = pack_ref[0:1, :], pack_ref[1:2, :]
        g_gain = (inner - bias * plain) / gain
        biases = (b0_ref, b1_ref, b2_ref)
        query = jnp.concatenate([b[0:1, 0:128] for b in biases], axis=1)
        value = jnp.concatenate([b[0:1, 256:384] for b in biases], axis=1)
        chunks = gup_ref.shape[0]
        rows_up = chunks * share
        up_bias = None
        for f in range(chunks):
            part = scatter_rows(gup_ref[f], rows_up, f * (width // rows_up), owners)
            up_bias = part if up_bias is None else up_bias + part
        wide = width // 2
        first_owner = side * (wide // (2 * share))
        qv_bias = scatter_rows(query, 2 * share, first_owner, owners) + scatter_rows(
            value, 2 * share, first_owner + count, owners
        )
        plain_rows = lambda vec: scatter_rows(vec, share, 0, owners)
        slots = [
            plain_rows(g_gain),
            plain_rows(plain),
            plain_rows(gvec_ref[2:3, :]),
            plain_rows(gvec_ref[0:1, :]),
            plain_rows(gvec_ref[1:2, :]),
            plain_rows(gvec_ref[3:4, :]),
            qv_bias,
            up_bias,
            jnp.zeros((owners, 128), f32),
        ]
        lines_of = [jnp.concatenate(slots[3 * i : 3 * i + 3], axis=1) for i in range(3)]
        for at in range(count):
            for half in range(2):
                owner = half * count + at
                start = owner * share
                rows = [acc_s[start : start + share, :]]
                rows += [line[owner : owner + 1, :] for line in lines_of]
                rows += [jnp.zeros((5, 384), f32)]
                unit_ref[at % planes, at // planes, half] = jnp.concatenate(rows, axis=0).astype(bf16)


def back_through(pieces, w_ref, side):
    total = None
    for i, piece in enumerate(pieces):
        part = lax.dot_general(
            piece[side, 0], w_ref[:, 384 * i : 384 * i + 384], NT, preferred_element_type=f32
        )
        total = part if total is None else total + part
    return total


def give_kernel(*refs):
    pieces, (w_ref, out_ref) = refs[:-2], refs[-2:]
    out_ref[0] = back_through(pieces, w_ref, 0).astype(bf16)


def input_kernel(*refs):
    pieces, (w_ref, recv_ref, x_ref, gmid_ref, pack_ref, ginput_ref) = refs[:-6], refs[-6:]
    gnormed = back_through(pieces, w_ref, 0) + recv_ref[0].astype(f32)
    xhat, rstd = standardise(x_ref[0].astype(f32))
    ginput_ref[0] = gmid_ref[0].astype(f32) + norm_pull(gnormed, pack_ref[0:1, :], xhat, rstd)


def partner(value):
    return lax.ppermute(value, "seq", [(0, 1), (1, 0)])


def exchange(value, axis):
    return lax.all_to_all(value, axis, 0, 0, tiled=True)


def spread_line(value, lines):
    return exchange(jnp.broadcast_to(value[None], (lines,) + value.shape), "line")


def flip(value, axis):
    return lax.ppermute(value, axis, [(0, 1), (1, 0)])


def in_order(index, own, received):
    return jnp.where(index == 0, jnp.stack([own, received]), jnp.stack([received, own]))


def spread_first(one, two):
    return lax.optimization_barrier((flip(one, "x"), flip(two, "y")))


def spread_second(one, two, got_one, got_two):
    near_one = in_order(lax.axis_index("x"), one, got_one)
    near_two = in_order(lax.axis_index("y"), two, got_two)
    near_one, near_two = lax.optimization_barrier((near_one, near_two))
    return (near_one, flip(near_one, "y")), (near_two, flip(near_two, "x"))


def spread_plane(one, two):
    return spread_second(one, two, *spread_first(one, two))


def after(value, *others):
    return lax.optimization_barrier((value,) + others)[0]


def assemble_kernel(far_plane, spot_ref, *refs):
    pieces, targets, scratch, (in_sem, out_sem) = refs[:4], refs[-9:-6], refs[-6:-2], refs[-2:]
    up_ref, down_ref, out_ref = targets
    side, y, x = spot_ref[0], spot_ref[1], spot_ref[2]
    width = down_ref.shape[-1]
    blocks = up_ref.shape[-1] // width
    loads = [pltpu.make_async_copy(pieces[i], scratch[i], in_sem.at[i]) for i in range(4)]
    for load in loads:
        load.start()
    stores = []

    def send(source, target):
        stores.append(pltpu.make_async_copy(source, target, out_sem.at[len(stores)]))
        stores[-1].start()

    for index in range(4):
        loads[index].wait()
        at_side = 1 - side if index // 2 else side
        held = scratch[index]
        for i in range(2):
            if index % 2 == 0:
                row = 1 - y if far_plane else y
                for block in range(blocks):
                    lanes = slice(block * width, (block + 1) * width)
                    send(held.at[i, :, block], up_ref.at[at_side, :, row, i, :, lanes])
                send(held.at[i, :, blocks], out_ref.at[at_side, :, row, i])
            else:
                column = 1 - x if far_plane else x
                send(held.at[i], down_ref.at[at_side, :, i, column])
    for copy in stores:
        copy.wait()


def assemble(spot, far_plane, pieces, targets, shapes):
    anywhere = pl.BlockSpec(memory_space=pl.ANY)
    blocks = pieces[0].shape[2]
    return pl.pallas_call(
        functools.partial(assemble_kernel, far_plane),
        grid_spec=pltpu.PrefetchScalarGridSpec(
            num_scalar_prefetch=1,
            grid=(1,),
            in_specs=[anywhere] * (4 + len(targets)),
            out_specs=[anywhere] * 3,
            scratch_shapes=[pltpu.VMEM(p.shape, bf16) for p in pieces]
            + [pltpu.SemaphoreType.DMA((4,)), pltpu.SemaphoreType.DMA((4 * blocks + 4,))],
        ),
        out_shape=shapes,
        input_output_aliases={5 + i: i for i in range(len(targets))},
        name="assemble",
        **kernel_params(1e6, 12e6),
    )(spot, *pieces, *targets)


def sum_plane(value):
    return jnp.sum(exchange(value, ("y", "x")).astype(f32), axis=0)


def sum_line(value, lines):
    here = lax.axis_index("line")
    total = lax.dynamic_index_in_dim(value, here, 0, keepdims=False)
    for shift in range(1, lines):
        piece = lax.dynamic_index_in_dim(value, (here + shift) % lines, 0, keepdims=False).astype(bf16)
        total = total + lax.ppermute(piece, "line", [(i, (i + shift) % lines) for i in range(lines)]).astype(f32)
    return total


def masks(seg, pos):
    pad = seg == CLIPS - 1
    lane = jnp.arange(128, dtype=jnp.int32) % HEAD_DIM
    seg, pos, pad = seg[..., None], pos[..., None], pad[..., None]
    clip_lane = lane < CLIPS - 1
    digit = jnp.where(lane < 9, pos // 256, jnp.where(lane < 25, (pos // 16) % 16, pos % 16))
    digit_base = jnp.where(lane < 9, 5, jnp.where(lane < 25, 9, 25))
    digit_lane = (lane >= 5) & (lane < LANE_LOG)
    hit_clip = lane == seg
    hit_digit = lane - digit_base == digit
    log_lane = (lane >= LANE_LOG) & (lane < LANE_PAD)
    pad_lane = lane == LANE_PAD
    bad = (clip_lane & ~hit_clip) | (digit_lane & pad & ~hit_digit) | (pad_lane & ~pad)
    qx = jnp.where(bad, -BIG, 0.0).astype(bf16)
    on = (clip_lane & hit_clip) | (digit_lane & pad & hit_digit) | log_lane | (pad_lane & pad)
    kx = jnp.where(on, 1.0, 0.0).astype(bf16)
    return qx, kx


def block_flags(ident, rows_block, cols_block):
    count, length = ident.shape
    by_row = ident.reshape(count, length // rows_block, rows_block)
    by_col = ident.reshape(count, length // cols_block, cols_block)
    low_row, high_row = jnp.min(by_row, axis=2)[:, :, None], jnp.max(by_row, axis=2)[:, :, None]
    low_col, high_col = jnp.min(by_col, axis=2)[:, None, :], jnp.max(by_col, axis=2)[:, None, :]
    meets = (low_row <= high_col) & (low_col <= high_row)
    return meets.astype(jnp.int32).reshape(count, -1)


def pair_device(
    lines, planes,
    tokens, segment_ids, cotangent, ln1_gain, ln1_bias, qkv_weight, qv_bias, out_weight, out_bias,
    ln2_gain, ln2_bias, up_weight, up_bias, down_weight, down_bias, avg_qkv, avg_out, avg_up, avg_down,
):
    count, part, width = tokens.shape
    length = 2 * part
    wide = width // 2
    heads = HEADS // 2
    hidden_width = up_weight.shape[1]
    chunks = hidden_width // width
    share = qkv_weight.shape[0]
    side = lax.axis_index("seq").astype(jnp.int32)
    first = side == 0
    side_arr = side.reshape(1)
    const = lambda *shape: pl.BlockSpec(shape, lambda *_: (0,) * len(shape), pipeline_mode=pl.Buffered(1))
    row_block = lambda *shape: pl.BlockSpec((1,) + shape, lambda j, *_: (j,) + (0,) * len(shape))
    both_block = lambda lanes: pl.BlockSpec((2, 1, part, lanes), lambda j, *_: (0, j, 0, 0))
    own_block = lambda lanes: pl.BlockSpec((1, 1, part, lanes), lambda j, *_: (0, j, 0, 0))

    pairs = heads // 2
    sds = jax.ShapeDtypeStruct
    small_vectors = [ln1_gain, ln1_bias, out_bias, ln2_gain, ln2_bias, down_bias, qv_bias, up_bias]
    mine, give = pl.pallas_call(
        functools.partial(prepare_kernel, share),
        grid_spec=pltpu.PrefetchScalarGridSpec(
            num_scalar_prefetch=1,
            grid=(1,),
            in_specs=[pl.BlockSpec((share, 6 * wide), lambda *_: (0, 0))]
            + [pl.BlockSpec((1, v.shape[0]), lambda *_: (0, 0)) for v in small_vectors],
            out_specs=[pl.BlockSpec((share, 3 * wide + 128), lambda *_: (0, 0))] * 2,
        ),
        out_shape=[sds((share, 3 * wide + 128), bf16)] * 2,
        name="prepare",
        **kernel_params(1e6, 4e5),
    )(side_arr, qkv_weight, *[v[None] for v in small_vectors])
    take = partner(give)
    tokens_other = partner(tokens)
    seg_other = partner(segment_ids)
    seg = jnp.concatenate([segment_ids, seg_other], axis=1)
    spots = jnp.arange(part, dtype=jnp.int32)
    pos = jnp.concatenate([side * part + spots, (1 - side) * part + spots])
    qx, kx = masks(seg, jnp.broadcast_to(pos, seg.shape))
    ident = jnp.where(seg == CLIPS - 1, CLIPS + pos, seg)
    flags_f = block_flags(ident, TQ_F, TK_F)
    flags_b = block_flags(ident, TK_B, TQ_B)

    start = jnp.where(first, jnp.stack([mine, take]), jnp.stack([take, mine]))
    x_at, y_at = lax.axis_index("x"), lax.axis_index("y")
    first_line = after(spread_line(start, lines), qx, kx, flags_f, flags_b)
    (one_m, one_r), (two_m, two_r) = spread_plane(first_line[:, 0], first_line[:, 1])
    one = in_order(y_at, one_m, one_r).transpose(2, 0, 1, 3, 4)
    two = in_order(x_at, two_m, two_r).transpose(2, 1, 0, 3, 4)
    w_first = jnp.stack([one, two]).reshape(width, 3 * wide + 128)

    own_rows = chunks * share
    up_sent, out_sent, down_sent, _ = lax.optimization_barrier((up_weight, out_weight, down_weight, qx))
    second = jnp.concatenate(
        [up_sent[:, i * width : (i + 1) * width] for i in range(chunks)]
        + [out_sent, down_sent],
        axis=0,
    )
    second = after(second, first_line)
    up_rows = own_rows + share
    second_line = spread_line(second, lines)

    small_at = 3 * wide // 128
    normed, mixed, pack = pl.pallas_call(
        functools.partial(project_kernel, share),
        grid_spec=pltpu.PrefetchScalarGridSpec(
            num_scalar_prefetch=1,
            grid=(2, count),
            in_specs=[
                pl.BlockSpec((1, part, width), lambda h, j, *_: (jnp.where(h == 0, j, count - 1), 0, 0)),
                pl.BlockSpec((1, part, width), lambda h, j, *_: (jnp.where(h == 0, 0, j), 0, 0)),
                const(width, 3 * wide),
                pl.BlockSpec((width, 128), lambda *_: (0, small_at), pipeline_mode=pl.Buffered(1)),
            ],
            out_specs=[
                pl.BlockSpec((1, 1, part, width), lambda h, j, *_: (h, j, 0, 0)),
                pl.BlockSpec((pairs, 1, 1, part, 384), lambda h, j, *_: (0, h, j, 0, 0)),
                pl.BlockSpec((16, width), lambda *_: (0, 0)),
            ],
            scratch_shapes=[pltpu.VMEM((1, 3 * wide), f32)],
        ),
        out_shape=[
            sds((2, count, part, width), bf16),
            sds((pairs, 2, count, part, 384), bf16),
            sds((16, width), f32),
        ],
        name="project",
        **kernel_params(
            2 * 2 * count * part * width * 3 * wide, 20e6, order=("arbitrary", "arbitrary")
        ),
    )(side_arr, tokens, tokens_other, w_first, w_first)
    up_bias_all = pack[8 : 8 + chunks].reshape(chunks, -1, share).transpose(1, 0, 2).reshape(chunks, width)

    second_line = after(second_line, one_r, two_r, pack)
    halves = (second_line[:, :up_rows].reshape(lines, chunks + 1, share, width), second_line[:, up_rows:])
    halves_got = spread_first(*halves)
    same, row_mixed = (), mixed
    for row in range(count):
        if row == 1:
            halves_got = lax.optimization_barrier(halves_got + (same[0],))[:2]
            up_pair, down_pair = spread_second(*halves, *halves_got)
            row_mixed = after(mixed, up_pair[0], down_pair[0])
        row_both = lambda lanes, row=row: pl.BlockSpec((pairs, 2, 1, part, lanes), lambda *_: (0, 0, row, 0, 0))
        row_one = pl.BlockSpec((pairs, 1, part, 128), lambda *_, row=row: (0, row, 0, 0))
        row_flat = pl.BlockSpec((1, length, 128), lambda *_, row=row: (row, 0, 0))
        same = pl.pallas_call(
            functools.partial(attend_kernel, row),
            grid_spec=pltpu.PrefetchScalarGridSpec(
                num_scalar_prefetch=1,
                grid=(1,),
                in_specs=[row_both(384), row_flat, row_flat] + [pl.BlockSpec(memory_space=pl.ANY)] * len(same),
                out_specs=[row_one, row_one, row_both(128)],
                scratch_shapes=[pltpu.VMEM((heads, length, 128), bf16)] * 3
                + [pltpu.VMEM((heads, length, 128), f32)],
            ),
            out_shape=[sds((pairs, count, part, 128), bf16)] * 2 + [sds((pairs, 2, count, part, 128), bf16)],
            input_output_aliases={4 + i: i for i in range(len(same))},
            name="attend",
            **kernel_params(8e9, 7e6, 4e6),
        )(flags_f, row_mixed, qx, kx, *same)
    att_own, att_other, ext = same
    spot = jnp.stack([side, y_at.astype(jnp.int32), x_at.astype(jnp.int32)])
    near = [up_pair[0], down_pair[0]]
    near += [partner(piece) for piece in near]
    far = list(lax.optimization_barrier((up_pair[1], down_pair[1], att_own))[:2])
    near = list(lax.optimization_barrier(tuple(near) + tuple(far))[:4])
    far += [partner(piece) for piece in far]
    shapes = [
        sds((2, lines, 2, 2, share, hidden_width), bf16),
        sds((2, lines, 2, 2, own_rows, width), bf16),
        sds((2, lines, 2, 2, share, width), bf16),
    ]
    targets = assemble(spot, False, near, (), shapes)
    w_up, w_down, w_out = assemble(spot, True, far, targets, shapes)
    w_up = w_up.reshape(width, hidden_width)
    w_down = w_down.reshape(hidden_width, width)
    w_out = w_out.reshape(2, wide, width)
    wo_mine = lax.dynamic_index_in_dim(w_out, side, 0, keepdims=False)

    att_recv = partner(att_other)

    head_block = pl.BlockSpec((pairs, 1, part, 128), lambda j, *_: (0, j, 0, 0))
    out_tokens, glow, gdown_own, gdown_other, gup_own, gup_other, gup_bias, gvec = pl.pallas_call(
        functools.partial(mlp_kernel, planes, share),
        grid_spec=pltpu.PrefetchScalarGridSpec(
            num_scalar_prefetch=1,
            grid=(count,),
            in_specs=[
                row_block(part, width),
                head_block,
                head_block,
                const(2, wide, width),
                const(width, hidden_width),
                const(hidden_width, width),
                row_block(part, width),
                const(16, width),
                const(chunks, width),
            ],
            out_specs=[row_block(part, width)] * 2
            + [const(planes, lines, own_rows, width)] * 2
            + [const(planes, lines, chunks, share, width)] * 2
            + [const(chunks, 1, width), const(8, width)],
            scratch_shapes=[pltpu.VMEM((chunks, width, width), f32)] * 2,
        ),
        out_shape=[
            sds((count, part, width), bf16),
            sds((count, part, width), bf16),
        ]
        + [sds((planes, lines, own_rows, width), bf16)] * 2
        + [sds((planes, lines, chunks, share, width), bf16)] * 2
        + [sds((chunks, 1, width), f32), sds((8, width), f32)],
        name="mlp",
        **kernel_params(2 * count * part * width * (width + 6 * hidden_width), 36e6, 4.7e6),
    )(side_arr, tokens, att_own, att_recv, w_out, w_up, w_down, cotangent, pack, up_bias_all)

    glow_other = partner(glow)
    add = lambda one, two: (one.astype(f32) + two.astype(f32)).astype(bf16)
    gdown_plane = sum_plane(add(gdown_own, partner(gdown_other)))
    gup_sum = add(gup_own, partner(gup_other))

    gmixed, gmixed_bias = [], []
    ties = ()
    for pair in range(pairs):
        lane_block = lambda lanes, pair=pair: pl.BlockSpec((1, 2, 1, part, lanes), lambda j, *_: (pair, 0, j, 0, 0))
        att_block = pl.BlockSpec((1, 1, part, 128), lambda j, *_, pair=pair: (pair, j, 0, 0))
        piece, piece_bias = pl.pallas_call(
            attend_back_kernel,
            grid_spec=pltpu.PrefetchScalarGridSpec(
                num_scalar_prefetch=1,
                grid=(count,),
                in_specs=[
                    lane_block(384),
                    lane_block(128),
                    att_block,
                    att_block,
                    row_block(part, width),
                    row_block(part, width),
                    pl.BlockSpec((128, width), lambda j, *_, pair=pair: (pair, 0)),
                    row_block(length, 128),
                ],
                out_specs=[both_block(384), const(8, 384)],
                scratch_shapes=[pltpu.VMEM((length // TQ_B, 2 * TQ_B, 256), bf16)] * 2
                + [pltpu.VMEM((length, 256), bf16)] * 2
                + [
                    pltpu.VMEM((length // TK_B, 128, TK_B), bf16),
                    pltpu.VMEM((length // TQ_B, 128, TQ_B), f32),
                    pltpu.VMEM((length, 128), f32),
                    pltpu.VMEM((length, 128), f32),
                ],
            ),
            out_shape=[sds((2, count, part, 384), bf16), sds((8, 384), f32)],
            name="attend_back",
            **kernel_params(25e9, 20e6, 4e6),
        )(flags_b, after(mixed, *ties), ext, att_own, att_other, glow, glow_other, wo_mine, kx)
        gmixed.append(piece)
        gmixed_bias.append(piece_bias)
        if pair == 0:
            gup_plane = sum_plane(after(gup_sum, gdown_plane))
            grad_down = sum_line(gdown_plane, lines)
            ties = (gdown_plane,)
        if pair == 1:
            early, inner_sum, plain_sum = pl.pallas_call(
                functools.partial(early_kernel, planes, share),
                grid=(count,),
                in_specs=[both_block(width), both_block(384), both_block(384), const(8, 384), const(8, 384)]
                + [head_block, head_block, row_block(part, width), row_block(part, width), const(width, 768)],
                out_specs=[const(planes, lines, 3, share, width), const(width, 128), const(width, 128)],
                out_shape=[
                    sds((planes, lines, 3, share, width), bf16),
                    sds((width, 128), f32),
                    sds((width, 128), f32),
                ],
                scratch_shapes=[pltpu.VMEM((width, 768), f32), pltpu.VMEM((wide, width), f32)],
                name="early",
                **kernel_params(9e9, 25e6),
            )(normed, *gmixed, *gmixed_bias, att_own, att_other, glow, glow_other, w_first)
            early_plane = sum_plane(after(early, gup_plane))
            gup_line = sum_line(gup_plane, lines)
            ties = (gup_plane, grad_down, early)
    grad_up = gup_line.transpose(1, 0, 2).reshape(share, hidden_width)

    late = pl.pallas_call(
        functools.partial(late_kernel, planes, share),
        grid_spec=pltpu.PrefetchScalarGridSpec(
            num_scalar_prefetch=1,
            grid=(count,),
            in_specs=[
                both_block(width),
                both_block(384),
                pl.BlockSpec((width, 384), lambda *_: (0, 2), pipeline_mode=pl.Buffered(1)),
                const(width, 128),
                const(width, 128),
                const(8, 384),
                const(8, 384),
                const(8, 384),
                const(16, width),
                const(8, width),
                const(chunks, 1, width),
            ],
            out_specs=const(planes, lines, 2, share + 8, 384),
            scratch_shapes=[pltpu.VMEM((width, 384), f32)],
        ),
        out_shape=sds((planes, lines, 2, share + 8, 384), bf16),
        name="late",
        **kernel_params(4e9, 10e6),
    )(side_arr, normed, after(gmixed[2], early_plane), w_first, inner_sum, plain_sum, *gmixed_bias, pack, gvec, gup_bias)

    early_line = sum_line(early_plane, lines)
    late_plane = sum_plane(late)
    piece_spec = lambda side: pl.BlockSpec((1, 1, part, 384), lambda j, *_: (side, j, 0, 0))
    give_back = pl.pallas_call(
        give_kernel,
        grid=(count,),
        in_specs=[piece_spec(1)] * pairs + [const(width, 3 * wide)],
        out_specs=row_block(part, width),
        out_shape=sds((count, part, width), bf16),
        name="give_back",
        **kernel_params(2 * count * part * width * 3 * wide, 12e6),
    )(*gmixed[:2], after(gmixed[2], late, early_line), w_first)
    recv_back = partner(give_back)

    grad_input = pl.pallas_call(
        input_kernel,
        grid=(count,),
        in_specs=[piece_spec(0)] * pairs
        + [
            const(width, 3 * wide),
            row_block(part, width),
            row_block(part, width),
            row_block(part, width),
            const(16, width),
        ],
        out_specs=row_block(part, width),
        out_shape=sds((count, part, width), f32),
        name="input_grad",
        **kernel_params(2 * count * part * width * 3 * wide, 25e6),
    )(*gmixed, w_first, after(recv_back, late_plane), tokens, glow, pack)

    late_line = sum_line(late_plane, lines)
    grad_out = early_line[2]
    whole = jnp.concatenate([early_line[:2], late_line[:, :share]], axis=2)
    keep = lax.dynamic_index_in_dim(whole, side, 0, keepdims=False)
    keep_small = lax.dynamic_index_in_dim(late_line[:, share:], side, 0, keepdims=False)
    give_big = lax.dynamic_index_in_dim(whole, 1 - side, 0, keepdims=False)
    give_small = lax.dynamic_index_in_dim(late_line[:, share:], 1 - side, 0, keepdims=False)
    got = partner(jnp.concatenate([give_big, jnp.pad(give_small, ((0, 0), (0, 768)))], axis=0))
    pick = lambda value: [
        jnp.concatenate([value[:share, 384 * p + 128 * k : 384 * p + 128 * k + 128] for p in range(pairs)], axis=1)
        for k in range(3)
    ]
    mine_q, other_q = pick(keep), pick(got)
    grad_qkv = jnp.concatenate(
        [
            jnp.where(first, jnp.concatenate([m, o], axis=1), jnp.concatenate([o, m], axis=1))
            for m, o in zip(mine_q, other_q)
        ],
        axis=1,
    )
    vec_rows = keep_small + got[share:, :384]
    vec = lambda slot, size: vec_rows[slot // 3, 128 * (slot % 3) : 128 * (slot % 3) + size]

    new_qkv = 0.9 * avg_qkv + 0.1 * qkv_weight.astype(f32)
    new_out = 0.9 * avg_out + 0.1 * out_weight.astype(f32)
    new_up = 0.9 * avg_up + 0.1 * up_weight.astype(f32)
    new_down = 0.9 * avg_down + 0.1 * down_weight.astype(f32)
    return (
        out_tokens,
        grad_input,
        vec(0, share),
        vec(1, share),
        grad_qkv,
        vec(6, 2 * share),
        grad_out,
        vec(2, share),
        vec(3, share),
        vec(4, share),
        grad_up,
        vec(7, chunks * share),
        grad_down,
        vec(5, share),
        new_qkv,
        new_out,
        new_up,
        new_down,
    )


def specs_for(rows):
    flat = ("seq",) + (rows if isinstance(rows, tuple) else (rows,))
    grid, ids, vec, mat = P(rows, "seq", None), P(rows, "seq"), P(flat), P(flat, None)
    ins = (grid, ids, grid, vec, vec, mat, vec, mat, vec, vec, vec, mat, vec, mat, vec, mat, mat, mat, mat)
    outs = (grid, grid, vec, vec, mat, vec, mat, vec, vec, vec, mat, vec, mat, vec, mat, mat, mat, mat)
    return ins, outs


def solution(mesh):
    parts, rows = mesh.shape["seq"], mesh.shape["rows"]
    planes = 4
    if parts != 2 or rows % planes:
        ins, outs = specs_for("rows")
        return jax.shard_map(on_device, mesh=mesh, in_specs=ins, out_specs=outs, check_vma=False)
    lines = rows // planes
    finer = Mesh(mesh.devices.reshape(parts, lines, 2, 2), ("seq", "line", "y", "x"))
    ins, outs = specs_for(("line", "y", "x"))
    return jax.shard_map(
        functools.partial(pair_device, lines, planes), mesh=finer, in_specs=ins, out_specs=outs, check_vma=False
    )
```

```python
import functools

import jax
import jax.numpy as jnp
from jax import lax
from jax.experimental import pallas as pl
from jax.experimental.pallas import tpu as pltpu
from jax.sharding import Mesh
from jax.sharding import PartitionSpec as P

HEADS = 12
HEAD_DIM = 64
CLIPS = 6


def layer_norm(value, gain, bias):
    middle = jnp.mean(value, axis=-1, keepdims=True)
    centred = value - middle
    spread = jnp.mean(centred * centred, axis=-1, keepdims=True)
    return centred * lax.rsqrt(spread + 1e-06) * gain + bias


def exact_gelu(value):
    return jax.nn.gelu(value, approximate=False)


def permitted(seg_query, seg_key, pos_query, pos_key):
    same_clip = seg_query[:, :, None] == seg_key[:, None, :]
    open_key = (seg_key != CLIPS - 1)[:, None, :]
    diagonal = (pos_query[:, None] == pos_key[None, :])[None]
    return (same_clip & (open_key | diagonal))[:, :, None, :]


def scores(query_part, key_part):
    return 0.125 * jnp.einsum(
        "rqhe,rkhe->rqhk", query_part, key_part, preferred_element_type=jnp.float32
    )


def exponent(score_vals, allowed):
    return jnp.where(allowed, jnp.exp(jnp.where(allowed, score_vals, 0.0)), 0.0)


def on_device(
    tokens,
    segment_ids,
    cotangent,
    ln1_gain,
    ln1_bias,
    qkv_weight,
    qv_bias,
    out_weight,
    out_bias,
    ln2_gain,
    ln2_bias,
    up_weight,
    up_bias,
    down_weight,
    down_bias,
    avg_qkv,
    avg_out,
    avg_up,
    avg_down,
):
    f32 = jnp.float32
    bf16 = jnp.bfloat16
    rows_here, shard_len, width = tokens.shape
    count_rows = rows_here * shard_len
    own_pos = lax.axis_index("seq") * shard_len + jnp.arange(shard_len, dtype=jnp.int32)
    head_shape = (rows_here, shard_len, HEADS, HEAD_DIM)
    gain_one, bias_one, w_qkv, b_qv, w_out, b_out = (
        lax.all_gather(ln1_gain, ("seq", "rows"), axis=0, tiled=True),
        lax.all_gather(ln1_bias, ("seq", "rows"), axis=0, tiled=True),
        lax.all_gather(qkv_weight, ("seq", "rows"), axis=0, tiled=True),
        lax.all_gather(qv_bias, ("seq", "rows"), axis=0, tiled=True),
        lax.all_gather(out_weight, ("seq", "rows"), axis=0, tiled=True),
        lax.all_gather(out_bias, ("seq", "rows"), axis=0, tiled=True),
    )
    residual = tokens.astype(f32).reshape(count_rows, width)
    normed, norm_one_pull = jax.vjp(
        layer_norm, residual, gain_one.astype(f32), bias_one.astype(f32)
    )
    normed_low = normed.astype(bf16)
    mixed = jnp.dot(normed_low, w_qkv, preferred_element_type=f32)
    bias_qv = b_qv.astype(f32)
    query_heads = (mixed[:, :width] + bias_qv[:width]).astype(bf16).reshape(head_shape)
    key_heads = mixed[:, width : 2 * width].astype(bf16).reshape(head_shape)
    value_heads = (mixed[:, 2 * width :] + bias_qv[width:]).astype(bf16).reshape(head_shape)
    start_state = (jnp.zeros((rows_here, shard_len, HEADS), f32), jnp.zeros(head_shape, f32))
    piece_keys = lax.all_gather(key_heads, "seq", axis=1, tiled=True)
    piece_values = lax.all_gather(value_heads, "seq", axis=1, tiled=True)
    piece_seg = lax.all_gather(segment_ids, "seq", axis=1, tiled=True)
    piece_len = piece_keys.shape[1]
    block_len = min(piece_len, shard_len)

    def forward_advance(turn, state):
        totals, weighted = state
        offset = turn * block_len
        key_block = lax.dynamic_slice_in_dim(piece_keys, offset, block_len, 1)
        value_block = lax.dynamic_slice_in_dim(piece_values, offset, block_len, 1)
        seg_block = lax.dynamic_slice_in_dim(piece_seg, offset, block_len, 1)
        key_pos = offset + jnp.arange(block_len, dtype=jnp.int32)
        allowed = permitted(segment_ids, seg_block, own_pos, key_pos)
        expo = exponent(scores(query_heads, key_block), allowed)
        totals = totals + jnp.sum(expo, axis=-1)
        weighted = weighted + jnp.einsum(
            "rqhk,rkhe->rqhe", expo.astype(bf16), value_block, preferred_element_type=f32
        )
        return (totals, weighted)

    totals, weighted = lax.fori_loop(0, piece_len // block_len, forward_advance, start_state)
    attended = weighted / totals[..., None]
    attn_in = attended.reshape(count_rows, width).astype(bf16)
    middle = residual + jnp.dot(attn_in, w_out, preferred_element_type=f32) + b_out.astype(f32)
    gain_two, bias_two, w_up, b_up, w_down, b_down = (
        lax.all_gather(ln2_gain, ("seq", "rows"), axis=0, tiled=True),
        lax.all_gather(ln2_bias, ("seq", "rows"), axis=0, tiled=True),
        lax.all_gather(up_weight, ("seq", "rows"), axis=0, tiled=True),
        lax.all_gather(up_bias, ("seq", "rows"), axis=0, tiled=True),
        lax.all_gather(down_weight, ("seq", "rows"), axis=0, tiled=True),
        lax.all_gather(down_bias, ("seq", "rows"), axis=0, tiled=True),
    )
    normed_two, norm_two_pull = jax.vjp(
        layer_norm, middle, gain_two.astype(f32), bias_two.astype(f32)
    )
    normed_two_low = normed_two.astype(bf16)
    hidden_pre = jnp.dot(normed_two_low, w_up, preferred_element_type=f32) + b_up.astype(f32)
    hidden, gelu_pull = jax.vjp(exact_gelu, hidden_pre)
    hidden_low = hidden.astype(bf16)
    final = middle + jnp.dot(hidden_low, w_down, preferred_element_type=f32) + b_down.astype(f32)
    out_tokens = final.astype(bf16).reshape(tokens.shape)
    w_up_back, w_down_back = (
        lax.all_gather(up_weight, ("seq", "rows"), axis=0, tiled=True),
        lax.all_gather(down_weight, ("seq", "rows"), axis=0, tiled=True),
    )
    grad_out = cotangent.astype(f32).reshape(count_rows, width)
    grad_low = grad_out.astype(bf16)
    grad_down = jnp.einsum("nf,nd->fd", hidden_low, grad_low, preferred_element_type=f32)
    grad_down_b = jnp.sum(grad_low, axis=0, dtype=f32)
    grad_hidden = jnp.einsum("nd,fd->nf", grad_low, w_down_back, preferred_element_type=f32)
    (grad_pre,) = gelu_pull(grad_hidden)
    grad_pre_low = grad_pre.astype(bf16)
    grad_up = jnp.einsum("nd,nf->df", normed_two_low, grad_pre_low, preferred_element_type=f32)
    grad_up_b = jnp.sum(grad_pre_low, axis=0, dtype=f32)
    grad_normed_two = jnp.einsum("nf,df->nd", grad_pre_low, w_up_back, preferred_element_type=f32)
    grad_mid_norm, grad_gain_two, grad_bias_two = norm_two_pull(grad_normed_two)
    grad_mid = grad_out + grad_mid_norm
    mlp_sums = (
        lax.psum_scatter(grad_gain_two, ("seq", "rows"), scatter_dimension=0, tiled=True),
        lax.psum_scatter(grad_bias_two, ("seq", "rows"), scatter_dimension=0, tiled=True),
        lax.psum_scatter(grad_up, ("seq", "rows"), scatter_dimension=0, tiled=True),
        lax.psum_scatter(grad_up_b, ("seq", "rows"), scatter_dimension=0, tiled=True),
        lax.psum_scatter(grad_down, ("seq", "rows"), scatter_dimension=0, tiled=True),
        lax.psum_scatter(grad_down_b, ("seq", "rows"), scatter_dimension=0, tiled=True),
    )
    w_qkv_back, w_out_back = (
        lax.all_gather(qkv_weight, ("seq", "rows"), axis=0, tiled=True),
        lax.all_gather(out_weight, ("seq", "rows"), axis=0, tiled=True),
    )
    grad_mid_low = grad_mid.astype(bf16)
    grad_wout = jnp.einsum("nd,ne->de", attn_in, grad_mid_low, preferred_element_type=f32)
    grad_bout = jnp.sum(grad_mid_low, axis=0, dtype=f32)
    grad_att = jnp.einsum(
        "ne,de->nd", grad_mid_low, w_out_back, preferred_element_type=f32
    ).reshape(head_shape)
    grad_acc = (grad_att / totals[..., None]).astype(bf16)
    shift_low = (jnp.sum(grad_att * attended, axis=-1) / totals).astype(bf16)
    shift_wide = shift_low.astype(f32)
    query_piece_keys = lax.all_gather(key_heads, "seq", axis=1, tiled=True)
    query_piece_values = lax.all_gather(value_heads, "seq", axis=1, tiled=True)
    query_piece_seg = lax.all_gather(segment_ids, "seq", axis=1, tiled=True)
    piece_len = query_piece_keys.shape[1]
    query_block_len = min(piece_len, shard_len)

    def query_advance(turn, grad_query):
        offset = turn * query_block_len
        key_block = lax.dynamic_slice_in_dim(query_piece_keys, offset, query_block_len, 1)
        value_block = lax.dynamic_slice_in_dim(query_piece_values, offset, query_block_len, 1)
        seg_block = lax.dynamic_slice_in_dim(query_piece_seg, offset, query_block_len, 1)
        key_pos = offset + jnp.arange(query_block_len, dtype=jnp.int32)
        allowed = permitted(segment_ids, seg_block, own_pos, key_pos)
        expo = exponent(scores(query_heads, key_block), allowed)
        inner = jnp.einsum("rqhe,rkhe->rqhk", grad_acc, value_block, preferred_element_type=f32)
        grad_score = (expo * (inner - shift_wide[..., None])).astype(bf16)
        return grad_query + jnp.einsum(
            "rqhk,rkhe->rqhe", grad_score, key_block, preferred_element_type=f32
        )

    grad_query = lax.fori_loop(
        0, piece_len // query_block_len, query_advance, jnp.zeros(head_shape, f32)
    )
    key_start = (jnp.zeros(head_shape, f32), jnp.zeros(head_shape, f32))
    piece_queries = lax.all_gather(query_heads, "seq", axis=1, tiled=True)
    piece_grads = lax.all_gather(grad_acc, "seq", axis=1, tiled=True)
    key_piece_seg = lax.all_gather(segment_ids, "seq", axis=1, tiled=True)
    piece_shift = lax.all_gather(shift_low, "seq", axis=1, tiled=True)
    piece_len = piece_queries.shape[1]
    key_block_len = min(piece_len, shard_len)

    def key_advance(turn, state):
        grad_key, grad_value = state
        offset = turn * key_block_len
        query_block = lax.dynamic_slice_in_dim(piece_queries, offset, key_block_len, 1)
        grad_block = lax.dynamic_slice_in_dim(piece_grads, offset, key_block_len, 1)
        seg_block = lax.dynamic_slice_in_dim(key_piece_seg, offset, key_block_len, 1)
        shift_block = lax.dynamic_slice_in_dim(piece_shift, offset, key_block_len, 1).astype(f32)
        query_pos = offset + jnp.arange(key_block_len, dtype=jnp.int32)
        allowed = permitted(seg_block, segment_ids, query_pos, own_pos)
        expo = exponent(scores(query_block, key_heads), allowed)
        inner = jnp.einsum("rqhe,rkhe->rqhk", grad_block, value_heads, preferred_element_type=f32)
        grad_score = (expo * (inner - shift_block[..., None])).astype(bf16)
        grad_key = grad_key + jnp.einsum(
            "rqhk,rqhe->rkhe", grad_score, query_block, preferred_element_type=f32
        )
        grad_value = grad_value + jnp.einsum(
            "rqhk,rqhe->rkhe", expo.astype(bf16), grad_block, preferred_element_type=f32
        )
        return (grad_key, grad_value)

    grad_key, grad_value = lax.fori_loop(0, piece_len // key_block_len, key_advance, key_start)
    grad_q_low = (0.125 * grad_query).astype(bf16).reshape(count_rows, width)
    grad_k_low = (0.125 * grad_key).astype(bf16).reshape(count_rows, width)
    grad_v_low = grad_value.astype(bf16).reshape(count_rows, width)
    grad_mixed = jnp.concatenate([grad_q_low, grad_k_low, grad_v_low], axis=1)
    grad_wqkv = jnp.einsum("nd,ne->de", normed_low, grad_mixed, preferred_element_type=f32)
    grad_bqv = jnp.concatenate(
        [jnp.sum(grad_q_low, axis=0, dtype=f32), jnp.sum(grad_v_low, axis=0, dtype=f32)], axis=0
    )
    grad_normed = jnp.einsum("ne,de->nd", grad_mixed, w_qkv_back, preferred_element_type=f32)
    grad_res_norm, grad_gain_one, grad_bias_one = norm_one_pull(grad_normed)
    grad_input = (grad_mid + grad_res_norm).reshape(tokens.shape)
    attn_sums = (
        lax.psum_scatter(grad_gain_one, ("seq", "rows"), scatter_dimension=0, tiled=True),
        lax.psum_scatter(grad_bias_one, ("seq", "rows"), scatter_dimension=0, tiled=True),
        lax.psum_scatter(grad_wqkv, ("seq", "rows"), scatter_dimension=0, tiled=True),
        lax.psum_scatter(grad_bqv, ("seq", "rows"), scatter_dimension=0, tiled=True),
        lax.psum_scatter(grad_wout, ("seq", "rows"), scatter_dimension=0, tiled=True),
        lax.psum_scatter(grad_bout, ("seq", "rows"), scatter_dimension=0, tiled=True),
    )
    new_qkv = 0.9 * avg_qkv + 0.1 * qkv_weight.astype(f32)
    new_out = 0.9 * avg_out + 0.1 * out_weight.astype(f32)
    new_up = 0.9 * avg_up + 0.1 * up_weight.astype(f32)
    new_down = 0.9 * avg_down + 0.1 * down_weight.astype(f32)
    return (
        out_tokens,
        grad_input,
        attn_sums[0],
        attn_sums[1],
        attn_sums[2],
        attn_sums[3],
        attn_sums[4],
        attn_sums[5],
        mlp_sums[0],
        mlp_sums[1],
        mlp_sums[2],
        mlp_sums[3],
        mlp_sums[4],
        mlp_sums[5],
        new_qkv,
        new_out,
        new_up,
        new_down,
    )


f32 = jnp.float32
bf16 = jnp.bfloat16
NT = (((1,), (1,)), ((), ()))
LOG2E = 1.4426950408889634
SCORE = 0.125 * LOG2E
BIG = 16384.0
VMEM_BYTES = 63 * 1024 * 1024
TQ_F, TK_F = 512, 256
TK_B, TQ_B = 512, 512
LANE_LOG = 41
LANE_PAD = 44


def kernel_params(flops, bytes_accessed, transcendentals=0, order=("arbitrary",)):
    return dict(
        compiler_params=pltpu.CompilerParams(
            vmem_limit_bytes=VMEM_BYTES, dimension_semantics=order
        ),
        cost_estimate=pl.CostEstimate(
            flops=int(flops), bytes_accessed=int(bytes_accessed), transcendentals=int(transcendentals)
        ),
    )


def standardise(value):
    middle = jnp.mean(value, axis=-1, keepdims=True)
    centred = value - middle
    spread = jnp.mean(centred * centred, axis=-1, keepdims=True)
    rstd = lax.rsqrt(spread + 1e-06)
    return centred * rstd, rstd


def norm_pull(grad_normed, gain, xhat, rstd):
    scaled = grad_normed * gain
    first = jnp.mean(scaled, axis=-1, keepdims=True)
    second = jnp.mean(scaled * xhat, axis=-1, keepdims=True)
    return rstd * (scaled - first - xhat * second)


def gelu_pair(x):
    size = jnp.abs(x)
    base = 1.0 + 0.23164189 * size
    t = 1.0 / base
    bell = jnp.exp2(x * x * (-0.5 * LOG2E))
    poly = t * (0.127414796 + t * (-0.142248368 + t * (0.7107068705 + t * (-0.7265760135 + t * 0.5307027145))))
    tail = poly * bell
    phi = jnp.where(x >= 0.0, 1.0 - tail, tail)
    return x * phi, phi + x * bell * 0.3989422804014327


def lane_masks():
    lane = lax.broadcasted_iota(jnp.int32, (1, 128), 1)
    low = jnp.where(lane < HEAD_DIM, 1.0, 0.0)
    return low.astype(bf16), (1.0 - low).astype(bf16)


def prepare_kernel(share, side_ref, w_ref, up_ref, out_ref, down_ref, *refs):
    vectors, (mine_ref, give_ref, second_ref) = refs[:-3], refs[-3:]
    width = down_ref.shape[1]
    blocks = up_ref.shape[1] // width
    for block in range(blocks):
        second_ref[block * share : (block + 1) * share] = up_ref[:, block * width : (block + 1) * width]
    second_ref[blocks * share : (blocks + 1) * share] = out_ref[...]
    second_ref[(blocks + 1) * share :] = down_ref[...]
    wide = w_ref.shape[1] // 6
    pairs = wide // 128
    for target, side in ((mine_ref, side_ref[0]), (give_ref, 1 - side_ref[0])):
        for pair in range(pairs):
            for kind in range(3):
                start = pl.multiple_of(kind * 2 * wide + side * wide + pair * 128, 128)
                at = 384 * pair + 128 * kind
                target[:, at : at + 128] = w_ref[:, pl.ds(start, 128)]
    lane = lax.broadcasted_iota(jnp.int32, (share, 128), 1)
    small = jnp.zeros((share, 128), f32)
    column = 0
    for ref in vectors:
        row = jnp.broadcast_to(ref[...].astype(f32), (8, ref.shape[1])).T
        for start in range(0, ref.shape[1], share):
            small = jnp.where(lane == column, row[start : start + share, 0:1], small)
            column += 1
    small = small.astype(bf16)
    mine_ref[:, 3 * wide :] = small
    give_ref[:, 3 * wide :] = small


def project_kernel(
    share, side_ref, own_ref, other_ref, w_ref, small_ref, normed_ref, mixed_ref, pack_ref, shift_s
):
    which, turn = pl.program_id(0), pl.program_id(1)
    wide = shift_s.shape[1] // 3
    pairs = wide // 128

    @pl.when((which == 0) & (turn == 0))
    def _():
        small = small_ref[...].astype(f32).T
        pack_ref[...] = small[0:16]
        shift_s[...] = jnp.zeros_like(shift_s)
        spot = lax.broadcasted_iota(jnp.int32, (wide, wide), 0)
        target = lax.broadcasted_iota(jnp.int32, (wide, wide), 1) + side_ref[0] * wide
        sums = [jnp.zeros((16, wide), f32), jnp.zeros((16, wide), f32)]
        for part in range(2):
            wanted = lax.div(spot, share) * (2 * share) + part * share + lax.rem(spot, share)
            chosen = jnp.where(wanted == target, 1.0, 0.0).astype(bf16)
            for kind in range(2):
                values = small[6 + part : 7 + part, kind * wide : (kind + 1) * wide]
                values = jnp.broadcast_to(values, (16, wide)).astype(bf16)
                sums[kind] += jnp.dot(values, chosen, preferred_element_type=f32)
        for pair in range(pairs):
            lanes = slice(128 * pair, 128 * pair + 128)
            shift_s[:, 384 * pair : 384 * pair + 128] = sums[0][0:1, lanes]
            shift_s[:, 384 * pair + 256 : 384 * pair + 384] = sums[1][0:1, lanes]

    tiles = 2
    size = normed_ref.shape[2] // tiles

    def normed_tile(i):
        rows = slice(i * size, (i + 1) * size)
        value = jnp.where(which == 0, own_ref[0, rows], other_ref[0, rows]).astype(f32)
        xhat, _ = standardise(value)
        normed = (xhat * pack_ref[0:1, :] + pack_ref[1:2, :]).astype(bf16)
        normed_ref[0, 0, rows] = normed
        return normed

    normed = normed_tile(0)
    for i in range(tiles):
        mixed = jnp.dot(normed, w_ref[...], preferred_element_type=f32) + shift_s[...]
        mixed = mixed.astype(bf16)
        if i + 1 < tiles:
            normed = normed_tile(i + 1)
        for pair in range(pairs):
            lanes = slice(384 * pair, 384 * pair + 384)
            mixed_ref[pair, 0, 0, i * size : (i + 1) * size] = mixed[:, lanes]


def attend_kernel(row, flag_ref, mixed_ref, qx_ref, kx_ref, *rest):
    own_ref, other_ref, ext_ref, q_s, k_s, v_s, acc_s = rest[-7:]
    length = q_s.shape[1]
    heads = q_s.shape[0]
    half = length // 2
    low, high = lane_masks()
    qx, kx = qx_ref[0], kx_ref[0]
    q_low, q_high, k_low, k_high = qx * low, qx * high, kx * low, kx * high
    for pair in range(heads // 2):
        q = mixed_ref[pair, :, 0, :, 0:128].reshape(length, 128)
        k = mixed_ref[pair, :, 0, :, 128:256].reshape(length, 128)
        v = mixed_ref[pair, :, 0, :, 256:384].reshape(length, 128)
        q_s[2 * pair] = q * low + q_high
        q_s[2 * pair + 1] = q * high + q_low
        k_s[2 * pair] = k * low + k_high
        k_s[2 * pair + 1] = k * high + k_low
        v_s[2 * pair] = v * low + high
        v_s[2 * pair + 1] = v * high + low
    acc_s[...] = jnp.zeros_like(acc_s)
    key_blocks = length // TK_F

    def step(index, carry):
        @pl.when(flag_ref[row, index] != 0)
        def _():
            q_at = pl.ds(pl.multiple_of((index // key_blocks) * TQ_F, TQ_F), TQ_F)
            k_at = pl.ds(pl.multiple_of((index % key_blocks) * TK_F, TK_F), TK_F)
            for head in range(heads):
                score = lax.dot_general(
                    q_s[head, q_at, :], k_s[head, k_at, :], NT, preferred_element_type=f32
                )
                expo = jnp.exp2(score * SCORE).astype(bf16)
                acc_s[head, q_at, :] += jnp.dot(expo, v_s[head, k_at, :], preferred_element_type=f32)

        return carry

    lax.fori_loop(0, (length // TQ_F) * key_blocks, step, 0)
    lane = lax.broadcasted_iota(jnp.int32, (half, 128), 1)
    first_half = lane < HEAD_DIM
    spot = lane % HEAD_DIM
    for pair in range(heads // 2):
        for side in range(2):
            rows = slice(side * half, (side + 1) * half)
            first, second = acc_s[2 * pair, rows], acc_s[2 * pair + 1, rows]
            top = jnp.where(first_half, first, second)
            crossed = jnp.where(first_half, second, first)
            totals = pltpu.roll(crossed, HEAD_DIM, 1)
            target = own_ref if side == 0 else other_ref
            target[pair, 0] = (top / totals).astype(bf16)
            lse = -8.0 * jnp.log(crossed)
            lse_a = lse.astype(bf16).astype(f32)
            lse_b = (lse - lse_a).astype(bf16).astype(f32)
            ext = jnp.where(
                spot == LANE_LOG,
                lse_a,
                jnp.where(
                    spot == LANE_LOG + 1,
                    lse_b,
                    jnp.where(spot == LANE_LOG + 2, lse - lse_a - lse_b, qx[rows].astype(f32)),
                ),
            )
            ext_ref[pair, side, 0] = ext.astype(bf16)


def join_lanes(ref):
    return jnp.concatenate([ref[i, 0] for i in range(ref.shape[0])], axis=1)


def mlp_kernel(
    planes, share, side_ref, x_ref, mine_ref, recv_ref, wo_ref, up_ref, down_ref, grad_ref, pack_ref, upb_ref,
    out_ref, glow_ref, gdown_own, gdown_other, gup_own, gup_other, gbias_ref, gvec_ref,
    down_s, up_s, wo_v, up_v, down_v, gd_own, gd_other, gu_own, gu_other, load_sem, store_sem,
):
    turn = pl.program_id(0)
    side = side_ref[0]
    chunks, size = down_s.shape[0], down_s.shape[2]
    load_out = pltpu.make_async_copy(wo_ref, wo_v, load_sem.at[0])
    load_up = pltpu.make_async_copy(up_ref, up_v, load_sem.at[1])
    load_down = pltpu.make_async_copy(down_ref, down_v, load_sem.at[2])

    @pl.when(turn == 0)
    def _():
        load_out.start()
        load_up.start()
        load_down.start()
        down_s[...] = jnp.zeros_like(down_s)
        up_s[...] = jnp.zeros_like(up_s)
        gbias_ref[...] = jnp.zeros_like(gbias_ref)
        gvec_ref[...] = jnp.zeros_like(gvec_ref)
        load_out.wait()

    middle = (
        x_ref[0].astype(f32)
        + jnp.dot(join_lanes(mine_ref), wo_v[side], preferred_element_type=f32)
        + jnp.dot(join_lanes(recv_ref), wo_v[1 - side], preferred_element_type=f32)
        + pack_ref[2:3, :]
    )
    xhat, rstd = standardise(middle)
    normed = (xhat * pack_ref[3:4, :] + pack_ref[4:5, :]).astype(bf16)
    normed_t = normed.T
    grad = grad_ref[0]
    grad_t = grad.T
    total = middle + pack_ref[5:6, :]

    @pl.when(turn == 0)
    def _():
        load_up.wait()
        load_down.wait()

    def first_layer(f):
        at = slice(f * size, (f + 1) * size)
        return jnp.dot(normed, up_v[:, at], preferred_element_type=f32) + upb_ref[f : f + 1, :]

    gnormed = None
    pre = first_layer(0)
    for f in range(chunks):
        at = slice(f * size, (f + 1) * size)
        hidden, slope = gelu_pair(pre)
        ghidden = lax.dot_general(grad, down_v[at, :], NT, preferred_element_type=f32)
        if f + 1 < chunks:
            pre = first_layer(f + 1)
        hidden = hidden.astype(bf16)
        gpre = (ghidden * slope).astype(bf16)
        total = total + jnp.dot(hidden, down_v[at, :], preferred_element_type=f32)
        part = lax.dot_general(gpre, up_v[:, at], NT, preferred_element_type=f32)
        gnormed = part if gnormed is None else gnormed + part
        down_s[f] += jnp.dot(grad_t, hidden, preferred_element_type=f32)
        up_s[f] += jnp.dot(normed_t, gpre, preferred_element_type=f32)
        gbias_ref[f] += jnp.sum(gpre.astype(f32), axis=0, keepdims=True)
    out_ref[0] = total.astype(bf16)
    gmid = grad.astype(f32) + norm_pull(gnormed, pack_ref[3:4, :], xhat, rstd)
    low = gmid.astype(bf16)
    glow_ref[0] = low
    gvec_ref[0:1, :] += jnp.sum(gnormed * xhat, axis=0, keepdims=True)
    gvec_ref[1:2, :] += jnp.sum(gnormed, axis=0, keepdims=True)
    gvec_ref[2:3, :] += jnp.sum(low.astype(f32), axis=0, keepdims=True)
    gvec_ref[3:4, :] += jnp.sum(grad.astype(f32), axis=0, keepdims=True)

    @pl.when(turn == pl.num_programs(0) - 1)
    def _():
        half = chunks // 2
        rows = chunks * share
        per_chunk = size // rows
        lines_chunk = per_chunk // planes
        for f in range(chunks):
            whole = down_s[f].astype(bf16).T
            at_line = (f % half) * lines_chunk
            span = slice(at_line, at_line + lines_chunk)
            for target, result, wanted in ((gd_own, gdown_own, f // half), (gd_other, gdown_other, 1 - f // half)):

                @pl.when(side == wanted)
                def _(target=target, result=result, whole=whole, f=f, at_line=at_line, span=span):
                    for i in range(per_chunk):
                        target[i % planes, at_line + i // planes] = whole[i * rows : (i + 1) * rows]
                    pltpu.make_async_copy(target.at[:, span], result.at[:, span], store_sem.at[f]).start()

        wide = up_s.shape[1] // 2
        ups = ((gu_own, gup_own, side * wide), (gu_other, gup_other, (1 - side) * wide))
        for which, (target, result, base) in enumerate(ups):
            for f in range(chunks):
                for at in range(wide // share):
                    start = pl.multiple_of(base + at * share, 8)
                    target[at % planes, at // planes, f] = up_s[f, pl.ds(start, share), :].astype(bf16)
                pltpu.make_async_copy(
                    target.at[:, :, f], result.at[:, :, f], store_sem.at[chunks * (1 + which) + f]
                ).start()
        for f in range(chunks):
            span = slice(0, lines_chunk)
            pltpu.make_async_copy(gd_own.at[:, span], gdown_own.at[:, span], store_sem.at[f]).wait()
        for which, (target, result, base) in enumerate(ups):
            for f in range(chunks):
                pltpu.make_async_copy(
                    target.at[:, :, f], result.at[:, :, f], store_sem.at[chunks * (1 + which) + f]
                ).wait()


def attend_back_kernel(
    flag_ref, mixed_ref, ext_ref, att_own, att_other, own_ref, other_ref, wo_ref, kx_ref,
    gmixed_ref, gbias_ref,
    q_s, d_s, k_s, v_s, kt_s, gq_s, gk_s, gv_s,
):
    row = pl.program_id(0)
    length = k_s.shape[0]
    half = length // 2
    low, high = lane_masks()
    lane = lax.broadcasted_iota(jnp.int32, (1, 128), 1)
    spot = lane % HEAD_DIM
    square_row = lax.broadcasted_iota(jnp.int32, (128, 128), 0) < HEAD_DIM
    square_col = lax.broadcasted_iota(jnp.int32, (128, 128), 1) < HEAD_DIM
    crossing = jnp.where(square_row == square_col, 0.0, -1.0).astype(bf16)
    one_hot_a = jnp.where(spot == 0, 1.0, 0.0)
    one_hot_b = jnp.where(spot == 1, 1.0, 0.0)
    v_ext = (one_hot_a + one_hot_b).astype(bf16)

    @pl.when(row == 0)
    def _():
        gbias_ref[...] = jnp.zeros_like(gbias_ref)

    mixed_at = lambda lanes: mixed_ref[0, :, 0, :, lanes].reshape(length, 128)
    q, k = mixed_at(slice(0, 128)), mixed_at(slice(128, 256))
    ext = ext_ref[0, :, 0].reshape(length, 128)
    k_s[:, 0:128] = k
    k_s[:, 128:256] = kx_ref[0]
    v_s[:, 0:128] = mixed_at(slice(256, 384))
    v_s[:, 128:256] = jnp.broadcast_to(v_ext, (length, 128))
    for head, (mine, other) in enumerate(((low, high), (high, low))):
        q_part, ext_part = q * mine, ext * other
        for i in range(length // TQ_B):
            at = slice(i * TQ_B, (i + 1) * TQ_B)
            rows = slice(head * TQ_B, (head + 1) * TQ_B)
            q_s[i, rows, 0:128] = q_part[at]
            q_s[i, rows, 128:256] = ext_part[at]
    for side in range(2):
        gates = own_ref[0] if side == 0 else other_ref[0]
        d = lax.dot_general(gates, wo_ref[...], NT, preferred_element_type=f32)
        moved = d * (att_own if side == 0 else att_other)[0, 0].astype(f32)
        moved_a = moved.astype(bf16)
        moved_b = (moved - moved_a.astype(f32)).astype(bf16)
        shift = jnp.dot(moved_a, crossing, preferred_element_type=f32) + jnp.dot(
            moved_b, crossing, preferred_element_type=f32
        )
        shift_a = shift.astype(bf16).astype(f32)
        dx = (shift_a * one_hot_a + (shift - shift_a) * one_hot_b).astype(bf16)
        d = d.astype(bf16)
        tile = min(TQ_B, half)
        for head, (mine, other) in enumerate(((low, high), (high, low))):
            d_part, dx_part = d * mine, dx * other
            for i in range(half // tile):
                at = slice(i * tile, (i + 1) * tile)
                start = side * half + i * tile
                rows = slice(head * TQ_B + start % TQ_B, head * TQ_B + start % TQ_B + tile)
                d_s[start // TQ_B, rows, 0:128] = d_part[at]
                d_s[start // TQ_B, rows, 128:256] = dx_part[at]
    for i in range(length // TK_B):
        kt_s[i] = k[i * TK_B : (i + 1) * TK_B].T
    gq_s[...] = jnp.zeros_like(gq_s)
    gk_s[...] = jnp.zeros_like(gk_s)
    gv_s[...] = jnp.zeros_like(gv_s)
    query_blocks = length // TQ_B

    def step(index, carry):
        @pl.when(flag_ref[row, index] != 0)
        def _():
            qi = index % query_blocks
            ki = index // query_blocks
            k_at = pl.ds(pl.multiple_of(ki * TK_B, TK_B), TK_B)
            probs, grads = [], []
            for head in range(2):
                rows = slice(head * TQ_B, (head + 1) * TQ_B)
                score = lax.dot_general(
                    k_s[k_at, :], q_s[qi, rows, :], NT, preferred_element_type=f32
                )
                inner = lax.dot_general(
                    v_s[k_at, :], d_s[qi, rows, :], NT, preferred_element_type=f32
                )
                prob = jnp.exp2(score * SCORE)
                probs.append(prob.astype(bf16))
                grads.append((prob * inner).astype(bf16))
            for head in range(2):
                at = slice(head * HEAD_DIM, (head + 1) * HEAD_DIM)
                gq_s[qi, at, :] += jnp.dot(kt_s[ki, at, :], grads[head], preferred_element_type=f32)
            gv_s[k_at, :] += jnp.dot(
                jnp.concatenate(probs, axis=1), d_s[qi, :, 0:128], preferred_element_type=f32
            )
            gk_s[k_at, :] += jnp.dot(
                jnp.concatenate(grads, axis=1), q_s[qi, :, 0:128], preferred_element_type=f32
            )

        return carry

    lax.fori_loop(0, query_blocks * (length // TK_B), step, 0)
    for i in range(query_blocks):
        gq = (0.125 * gq_s[i].T).astype(bf16)
        for start in range(0, TQ_B, min(TQ_B, half)):
            at = i * TQ_B + start
            size = min(TQ_B, half)
            gmixed_ref[at // half, 0, at % half : at % half + size, 0:128] = gq[start : start + size]
        gbias_ref[0:1, 0:128] += jnp.sum(gq.astype(f32), axis=0, keepdims=True)
    gk = (0.125 * gk_s[...]).astype(bf16)
    gv = gv_s[...].astype(bf16)
    gbias_ref[0:1, 128:256] += jnp.sum(gk.astype(f32), axis=0, keepdims=True)
    gbias_ref[0:1, 256:384] += jnp.sum(gv.astype(f32), axis=0, keepdims=True)
    for side in range(2):
        gmixed_ref[side, 0, :, 128:256] = gk[side * half : (side + 1) * half]
        gmixed_ref[side, 0, :, 256:384] = gv[side * half : (side + 1) * half]


def weight_dot(normed_ref, *piece_refs):
    normed_t = jnp.concatenate([normed_ref[0, 0], normed_ref[1, 0]], axis=0).T
    sides = []
    for side in range(2):
        sides.append(jnp.concatenate([ref[side, 0] for ref in piece_refs], axis=1))
    return jnp.dot(normed_t, jnp.concatenate(sides, axis=0), preferred_element_type=f32)


def fold_lanes(value):
    total = value[:, 0:128]
    for at in range(128, value.shape[1], 128):
        total = total + value[:, at : at + 128]
    return total


def early_kernel(
    planes, share, normed_ref, g0_ref, g1_ref, b0_ref, b1_ref, mine_ref, other_ref, low_ref, low_other_ref, w_ref,
    unit_ref, first_ref, second_ref, acc_s, out_s,
):
    turn = pl.program_id(0)

    @pl.when(turn == 0)
    def _():
        acc_s[...] = jnp.zeros_like(acc_s)
        out_s[...] = jnp.zeros_like(out_s)

    acc_s[...] += weight_dot(normed_ref, g0_ref, g1_ref)
    across = (((0,), (0,)), ((), ()))
    out_s[...] += lax.dot_general(
        join_lanes(mine_ref), low_ref[0], across, preferred_element_type=f32
    ) + lax.dot_general(join_lanes(other_ref), low_other_ref[0], across, preferred_element_type=f32)

    @pl.when(turn == pl.num_programs(0) - 1)
    def _():
        weights = w_ref[...].astype(f32)
        sums = jnp.concatenate([b0_ref[0:1, :], b1_ref[0:1, :]], axis=1)
        first_ref[...] = fold_lanes(weights * acc_s[...])
        second_ref[...] = fold_lanes(weights * sums)
        count = out_s.shape[0] // share
        for at in range(count):
            spot = (at % planes, at // planes)
            for half in range(2):
                lanes = slice(384 * half, 384 * half + 384)
                for side in range(2):
                    start = (side * count + at) * share
                    unit_ref[spot + (2 * side + half,)] = acc_s[start : start + share, lanes].astype(bf16)
                unit_ref[spot + (4 + half,)] = out_s[at * share : (at + 1) * share, lanes].astype(bf16)


def scatter_rows(vector, step, offset, owners):
    n = vector.shape[1]
    owner = lax.broadcasted_iota(jnp.int32, (owners, n), 0) - offset
    mask = lax.div(lax.broadcasted_iota(jnp.int32, (owners, n), 1), step) == owner
    spread = jnp.where(mask, jnp.broadcast_to(vector, (owners, n)), 0.0).astype(bf16)
    lane = lax.rem(lax.broadcasted_iota(jnp.int32, (128, n), 1), step)
    chosen = jnp.where(lane == lax.broadcasted_iota(jnp.int32, (128, n), 0), 1.0, 0.0).astype(bf16)
    return lax.dot_general(spread, chosen, NT, preferred_element_type=f32)


def late_kernel(
    planes, share, side_ref, normed_ref, g_ref, w_ref, first_ref, second_ref, b0_ref, b1_ref, b2_ref, pack_ref,
    gvec_ref, gup_ref, unit_ref, acc_s,
):
    turn = pl.program_id(0)

    @pl.when(turn == 0)
    def _():
        acc_s[...] = jnp.zeros_like(acc_s)

    acc_s[...] += weight_dot(normed_ref, g_ref)

    @pl.when(turn == pl.num_programs(0) - 1)
    def _():
        side = side_ref[0]
        weights = w_ref[...].astype(f32)
        width = weights.shape[0]
        owners = width // share
        count = owners // 2
        inner = first_ref[...] + fold_lanes(weights * acc_s[...])
        plain = second_ref[...] + fold_lanes(weights * b2_ref[0:1, :])
        inner = jnp.sum(inner.T, axis=0, keepdims=True)
        plain = jnp.sum(plain.T, axis=0, keepdims=True)
        gain, bias = pack_ref[0:1, :], pack_ref[1:2, :]
        g_gain = (inner - bias * plain) / gain
        biases = (b0_ref, b1_ref, b2_ref)
        query = jnp.concatenate([b[0:1, 0:128] for b in biases], axis=1)
        value = jnp.concatenate([b[0:1, 256:384] for b in biases], axis=1)
        chunks = gup_ref.shape[0]
        rows_up = chunks * share
        up_bias = None
        for f in range(chunks):
            part = scatter_rows(gup_ref[f], rows_up, f * (width // rows_up), owners)
            up_bias = part if up_bias is None else up_bias + part
        wide = width // 2
        first_owner = side * (wide // (2 * share))
        qv_bias = scatter_rows(query, 2 * share, first_owner, owners) + scatter_rows(
            value, 2 * share, first_owner + count, owners
        )
        plain_rows = lambda vec: scatter_rows(vec, share, 0, owners)
        slots = [
            plain_rows(g_gain),
            plain_rows(plain),
            plain_rows(gvec_ref[2:3, :]),
            plain_rows(gvec_ref[0:1, :]),
            plain_rows(gvec_ref[1:2, :]),
            plain_rows(gvec_ref[3:4, :]),
            qv_bias,
            up_bias,
            jnp.zeros((owners, 128), f32),
        ]
        lines_of = [jnp.concatenate(slots[3 * i : 3 * i + 3], axis=1) for i in range(3)]
        blank = jnp.zeros((5, 384), f32)
        for at in range(count):
            spot = (at % planes, at // planes)
            small = []
            for half in range(2):
                owner = half * count + at
                start = owner * share
                unit_ref[spot + (half,)] = acc_s[start : start + share, :].astype(bf16)
                small += [line[owner : owner + 1, :] for line in lines_of] + [blank]
            small.append(jnp.zeros((share - 16, 384), f32))
            unit_ref[spot + (2,)] = jnp.concatenate(small, axis=0).astype(bf16)


def finish_kernel(side_ref, line_ref, got_ref, qkv_ref, out_ref, small_ref):
    side = side_ref[0]
    wide = qkv_ref.shape[1] // 6
    for pair in range(wide // 128):
        own = line_ref[2 * side + pair] if pair < 2 else line_ref[6 + side]
        other = got_ref[pair]
        for kind in range(3):
            lanes = slice(128 * kind, 128 * kind + 128)
            for half in range(2):
                at = kind * 2 * wide + half * wide + 128 * pair
                qkv_ref[:, at : at + 128] = jnp.where(side == half, own[:, lanes], other[:, lanes])
    out_ref[:, 0:384] = line_ref[4]
    out_ref[:, 384:768] = line_ref[5]
    start = pl.multiple_of(8 * side, 8)
    small_ref[...] = line_ref[8, pl.ds(start, 8), :] + got_ref[3, pl.ds(start, 8), :]


def back_through(pieces, w_ref, side):
    total = None
    for i, piece in enumerate(pieces):
        part = lax.dot_general(
            piece[side, 0], w_ref[:, 384 * i : 384 * i + 384], NT, preferred_element_type=f32
        )
        total = part if total is None else total + part
    return total


def give_kernel(*refs):
    pieces, (w_ref, out_ref) = refs[:-2], refs[-2:]
    out_ref[0] = back_through(pieces, w_ref, 0).astype(bf16)


def input_kernel(*refs):
    pieces, (w_ref, recv_ref, x_ref, gmid_ref, pack_ref, ginput_ref) = refs[:-6], refs[-6:]
    gnormed = back_through(pieces, w_ref, 0) + recv_ref[0].astype(f32)
    xhat, rstd = standardise(x_ref[0].astype(f32))
    ginput_ref[0] = gmid_ref[0].astype(f32) + norm_pull(gnormed, pack_ref[0:1, :], xhat, rstd)


def partner(value):
    return lax.ppermute(value, "seq", [(0, 1), (1, 0)])


def exchange(value, axis):
    return lax.all_to_all(value, axis, 0, 0, tiled=True)


def spread_line(value, lines):
    return exchange(jnp.broadcast_to(value[None], (lines,) + value.shape), "line")


def flip(value, axis):
    return lax.ppermute(value, axis, [(0, 1), (1, 0)])


def in_order(index, own, received):
    return jnp.where(index == 0, jnp.stack([own, received]), jnp.stack([received, own]))


def spread_first(one, two):
    return lax.optimization_barrier((flip(one, "x"), flip(two, "y")))


def spread_second(one, two, got_one, got_two):
    near_one = in_order(lax.axis_index("x"), one, got_one)
    near_two = in_order(lax.axis_index("y"), two, got_two)
    near_one, near_two = lax.optimization_barrier((near_one, near_two))
    return (near_one, flip(near_one, "y")), (near_two, flip(near_two, "x"))


def spread_plane(one, two):
    return spread_second(one, two, *spread_first(one, two))


def after(value, *others):
    return lax.optimization_barrier((value,) + others)[0]


def assemble_kernel(far_plane, spot_ref, *refs):
    pieces, targets, scratch, (in_sem, out_sem) = refs[:4], refs[-9:-6], refs[-6:-2], refs[-2:]
    up_ref, down_ref, out_ref = targets
    side, y, x = spot_ref[0], spot_ref[1], spot_ref[2]
    width = down_ref.shape[-1]
    blocks = up_ref.shape[-1] // width
    loads = [pltpu.make_async_copy(pieces[i], scratch[i], in_sem.at[i]) for i in range(4)]
    for load in loads:
        load.start()
    stores = []

    def send(source, target):
        stores.append(pltpu.make_async_copy(source, target, out_sem.at[len(stores)]))
        stores[-1].start()

    for index in range(4):
        loads[index].wait()
        at_side = 1 - side if index // 2 else side
        held = scratch[index]
        for i in range(2):
            if index % 2 == 0:
                row = 1 - y if far_plane else y
                for block in range(blocks):
                    lanes = slice(block * width, (block + 1) * width)
                    send(held.at[i, :, block], up_ref.at[at_side, :, row, i, :, lanes])
                send(held.at[i, :, blocks], out_ref.at[at_side, :, row, i])
            else:
                column = 1 - x if far_plane else x
                send(held.at[i], down_ref.at[at_side, :, i, column])
    for copy in stores:
        copy.wait()


def assemble(spot, far_plane, pieces, targets, shapes):
    anywhere = pl.BlockSpec(memory_space=pl.ANY)
    blocks = pieces[0].shape[2]
    return pl.pallas_call(
        functools.partial(assemble_kernel, far_plane),
        grid_spec=pltpu.PrefetchScalarGridSpec(
            num_scalar_prefetch=1,
            grid=(1,),
            in_specs=[anywhere] * (4 + len(targets)),
            out_specs=[anywhere] * 3,
            scratch_shapes=[pltpu.VMEM(p.shape, bf16) for p in pieces]
            + [pltpu.SemaphoreType.DMA((4,)), pltpu.SemaphoreType.DMA((4 * blocks + 4,))],
        ),
        out_shape=shapes,
        input_output_aliases={5 + i: i for i in range(len(targets))},
        name="assemble",
        **kernel_params(1e6, 12e6),
    )(spot, *pieces, *targets)


def sum_plane(value, *waits):
    received = exchange(value, ("y", "x"))
    if waits:
        received = after(received, *waits)
    return jnp.sum(received.astype(f32), axis=0)


def send_line(value, lines):
    here = lax.axis_index("line")
    pieces = []
    for shift in range(1, lines):
        piece = lax.dynamic_index_in_dim(value, (here + shift) % lines, 0, keepdims=False).astype(bf16)
        pieces.append(lax.ppermute(piece, "line", [(i, (i + shift) % lines) for i in range(lines)]))
    return pieces


def sum_line(value, lines, *waits):
    total = lax.dynamic_index_in_dim(value, lax.axis_index("line"), 0, keepdims=False)
    pieces = send_line(value, lines)
    if waits:
        pieces = lax.optimization_barrier(tuple(pieces) + waits)[: len(pieces)]
    for piece in pieces:
        total = total + piece.astype(f32)
    return total


def masks(seg, pos):
    pad = seg == CLIPS - 1
    lane = jnp.arange(128, dtype=jnp.int32) % HEAD_DIM
    seg, pos, pad = seg[..., None], pos[..., None], pad[..., None]
    clip_lane = lane < CLIPS - 1
    digit = jnp.where(lane < 9, pos // 256, jnp.where(lane < 25, (pos // 16) % 16, pos % 16))
    digit_base = jnp.where(lane < 9, 5, jnp.where(lane < 25, 9, 25))
    digit_lane = (lane >= 5) & (lane < LANE_LOG)
    hit_clip = lane == seg
    hit_digit = lane - digit_base == digit
    log_lane = (lane >= LANE_LOG) & (lane < LANE_PAD)
    pad_lane = lane == LANE_PAD
    bad = (clip_lane & ~hit_clip) | (digit_lane & pad & ~hit_digit) | (pad_lane & ~pad)
    qx = jnp.where(bad, -BIG, 0.0).astype(bf16)
    on = (clip_lane & hit_clip) | (digit_lane & pad & hit_digit) | log_lane | (pad_lane & pad)
    kx = jnp.where(on, 1.0, 0.0).astype(bf16)
    return qx, kx


def block_flags(ident, rows_block, cols_block):
    count, length = ident.shape
    by_row = ident.reshape(count, length // rows_block, rows_block)
    by_col = ident.reshape(count, length // cols_block, cols_block)
    low_row, high_row = jnp.min(by_row, axis=2)[:, :, None], jnp.max(by_row, axis=2)[:, :, None]
    low_col, high_col = jnp.min(by_col, axis=2)[:, None, :], jnp.max(by_col, axis=2)[:, None, :]
    meets = (low_row <= high_col) & (low_col <= high_row)
    return meets.astype(jnp.int32).reshape(count, -1)


def pair_device(
    lines, planes,
    tokens, segment_ids, cotangent, ln1_gain, ln1_bias, qkv_weight, qv_bias, out_weight, out_bias,
    ln2_gain, ln2_bias, up_weight, up_bias, down_weight, down_bias, avg_qkv, avg_out, avg_up, avg_down,
):
    count, part, width = tokens.shape
    length = 2 * part
    wide = width // 2
    heads = HEADS // 2
    hidden_width = up_weight.shape[1]
    chunks = hidden_width // width
    share = qkv_weight.shape[0]
    side = lax.axis_index("seq").astype(jnp.int32)
    first = side == 0
    side_arr = side.reshape(1)
    const = lambda *shape: pl.BlockSpec(shape, lambda *_: (0,) * len(shape), pipeline_mode=pl.Buffered(1))
    row_block = lambda *shape: pl.BlockSpec((1,) + shape, lambda j, *_: (j,) + (0,) * len(shape))
    both_block = lambda lanes: pl.BlockSpec((2, 1, part, lanes), lambda j, *_: (0, j, 0, 0))
    own_block = lambda lanes: pl.BlockSpec((1, 1, part, lanes), lambda j, *_: (0, j, 0, 0))

    pairs = heads // 2
    sds = jax.ShapeDtypeStruct
    small_vectors = [ln1_gain, ln1_bias, out_bias, ln2_gain, ln2_bias, down_bias, qv_bias, up_bias]
    mine, give, second = pl.pallas_call(
        functools.partial(prepare_kernel, share),
        grid_spec=pltpu.PrefetchScalarGridSpec(
            num_scalar_prefetch=1,
            grid=(1,),
            in_specs=[
                pl.BlockSpec((share, 6 * wide), lambda *_: (0, 0)),
                pl.BlockSpec((share, hidden_width), lambda *_: (0, 0)),
                pl.BlockSpec((share, width), lambda *_: (0, 0)),
                pl.BlockSpec((chunks * share, width), lambda *_: (0, 0)),
            ]
            + [pl.BlockSpec((1, v.shape[0]), lambda *_: (0, 0)) for v in small_vectors],
            out_specs=[pl.BlockSpec((share, 3 * wide + 128), lambda *_: (0, 0))] * 2
            + [pl.BlockSpec(((2 * chunks + 1) * share, width), lambda *_: (0, 0))],
        ),
        out_shape=[sds((share, 3 * wide + 128), bf16)] * 2 + [sds(((2 * chunks + 1) * share, width), bf16)],
        name="prepare",
        **kernel_params(1e6, 1e6),
    )(side_arr, qkv_weight, up_weight, out_weight, down_weight, *[v[None] for v in small_vectors])
    take = partner(give)
    tokens_other = partner(tokens)
    seg_other = partner(segment_ids)
    seg = jnp.concatenate([segment_ids, seg_other], axis=1)
    spots = jnp.arange(part, dtype=jnp.int32)
    pos = jnp.concatenate([side * part + spots, (1 - side) * part + spots])
    qx, kx = masks(seg, jnp.broadcast_to(pos, seg.shape))
    ident = jnp.where(seg == CLIPS - 1, CLIPS + pos, seg)
    flags_f = block_flags(ident, TQ_F, TK_F)
    flags_b = block_flags(ident, TK_B, TQ_B)

    start = jnp.where(first, jnp.stack([mine, take]), jnp.stack([take, mine]))
    x_at, y_at = lax.axis_index("x"), lax.axis_index("y")
    first_line = after(spread_line(start, lines), qx, kx, flags_f, flags_b)
    (one_m, one_r), (two_m, two_r) = spread_plane(first_line[:, 0], first_line[:, 1])
    one = in_order(y_at, one_m, one_r).transpose(2, 0, 1, 3, 4)
    two = in_order(x_at, two_m, two_r).transpose(2, 1, 0, 3, 4)
    w_first = jnp.stack([one, two]).reshape(width, 3 * wide + 128)

    own_rows = chunks * share
    second = after(second, first_line)
    up_rows = own_rows + share
    second_line = spread_line(second, lines)

    small_at = 3 * wide // 128
    normed, mixed, pack = pl.pallas_call(
        functools.partial(project_kernel, share),
        grid_spec=pltpu.PrefetchScalarGridSpec(
            num_scalar_prefetch=1,
            grid=(2, count),
            in_specs=[
                pl.BlockSpec((1, part, width), lambda h, j, *_: (jnp.where(h == 0, j, count - 1), 0, 0)),
                pl.BlockSpec((1, part, width), lambda h, j, *_: (jnp.where(h == 0, 0, j), 0, 0)),
                const(width, 3 * wide),
                pl.BlockSpec((width, 128), lambda *_: (0, small_at), pipeline_mode=pl.Buffered(1)),
            ],
            out_specs=[
                pl.BlockSpec((1, 1, part, width), lambda h, j, *_: (h, j, 0, 0)),
                pl.BlockSpec((pairs, 1, 1, part, 384), lambda h, j, *_: (0, h, j, 0, 0)),
                pl.BlockSpec((16, width), lambda *_: (0, 0)),
            ],
            scratch_shapes=[pltpu.VMEM((1, 3 * wide), f32)],
        ),
        out_shape=[
            sds((2, count, part, width), bf16),
            sds((pairs, 2, count, part, 384), bf16),
            sds((16, width), f32),
        ],
        name="project",
        **kernel_params(
            2 * 2 * count * part * width * 3 * wide, 20e6, order=("arbitrary", "arbitrary")
        ),
    )(side_arr, tokens, tokens_other, w_first, w_first)
    up_bias_all = pack[8 : 8 + chunks].reshape(chunks, -1, share).transpose(1, 0, 2).reshape(chunks, width)

    second_line = after(second_line, one_r, two_r, pack)
    halves = (second_line[:, :up_rows].reshape(lines, chunks + 1, share, width), second_line[:, up_rows:])
    halves_got = spread_first(*halves)
    same, row_mixed = (), mixed
    for row in range(count):
        if row == 1:
            halves_got = lax.optimization_barrier(halves_got + (same[0],))[:2]
            up_pair, down_pair = spread_second(*halves, *halves_got)
            row_mixed = after(mixed, up_pair[0], down_pair[0])
        row_both = lambda lanes, row=row: pl.BlockSpec((pairs, 2, 1, part, lanes), lambda *_: (0, 0, row, 0, 0))
        row_one = pl.BlockSpec((pairs, 1, part, 128), lambda *_, row=row: (0, row, 0, 0))
        row_flat = pl.BlockSpec((1, length, 128), lambda *_, row=row: (row, 0, 0))
        same = pl.pallas_call(
            functools.partial(attend_kernel, row),
            grid_spec=pltpu.PrefetchScalarGridSpec(
                num_scalar_prefetch=1,
                grid=(1,),
                in_specs=[row_both(384), row_flat, row_flat] + [pl.BlockSpec(memory_space=pl.ANY)] * len(same),
                out_specs=[row_one, row_one, row_both(128)],
                scratch_shapes=[pltpu.VMEM((heads, length, 128), bf16)] * 3
                + [pltpu.VMEM((heads, length, 128), f32)],
            ),
            out_shape=[sds((pairs, count, part, 128), bf16)] * 2 + [sds((pairs, 2, count, part, 128), bf16)],
            input_output_aliases={4 + i: i for i in range(len(same))},
            name="attend",
            **kernel_params(8e9, 7e6, 4e6),
        )(flags_f, row_mixed, qx, kx, *same)
    att_own, att_other, ext = same
    spot = jnp.stack([side, y_at.astype(jnp.int32), x_at.astype(jnp.int32)])
    near = [up_pair[0], down_pair[0]]
    near += [partner(piece) for piece in near]
    far = list(lax.optimization_barrier((up_pair[1], down_pair[1], att_own))[:2])
    near = list(lax.optimization_barrier(tuple(near) + tuple(far))[:4])
    far += [partner(piece) for piece in far]
    shapes = [
        sds((2, lines, 2, 2, share, hidden_width), bf16),
        sds((2, lines, 2, 2, own_rows, width), bf16),
        sds((2, lines, 2, 2, share, width), bf16),
    ]
    targets = assemble(spot, False, near, (), shapes)
    w_up, w_down, w_out = assemble(spot, True, far, targets, shapes)
    w_up = w_up.reshape(width, hidden_width)
    w_down = w_down.reshape(hidden_width, width)
    w_out = w_out.reshape(2, wide, width)
    wo_mine = lax.dynamic_index_in_dim(w_out, side, 0, keepdims=False)

    att_recv = partner(att_other)

    head_block = pl.BlockSpec((pairs, 1, part, 128), lambda j, *_: (0, j, 0, 0))
    out_tokens, glow, gdown_own, gdown_other, gup_own, gup_other, gup_bias, gvec = pl.pallas_call(
        functools.partial(mlp_kernel, planes, share),
        grid_spec=pltpu.PrefetchScalarGridSpec(
            num_scalar_prefetch=1,
            grid=(count,),
            in_specs=[
                row_block(part, width),
                head_block,
                head_block,
            ]
            + [pl.BlockSpec(memory_space=pl.ANY)] * 3
            + [
                row_block(part, width),
                const(16, width),
                const(chunks, width),
            ],
            out_specs=[row_block(part, width)] * 2
            + [pl.BlockSpec(memory_space=pl.ANY)] * 4
            + [const(chunks, 1, width), const(8, width)],
            scratch_shapes=[pltpu.VMEM((chunks, width, width), f32)] * 2
            + [
                pltpu.VMEM((2, wide, width), bf16),
                pltpu.VMEM((width, hidden_width), bf16),
                pltpu.VMEM((hidden_width, width), bf16),
            ]
            + [pltpu.VMEM((planes, lines, own_rows, width), bf16)] * 2
            + [pltpu.VMEM((planes, lines, chunks, share, width), bf16)] * 2
            + [pltpu.SemaphoreType.DMA((3,)), pltpu.SemaphoreType.DMA((3 * chunks,))],
        ),
        out_shape=[
            sds((count, part, width), bf16),
            sds((count, part, width), bf16),
        ]
        + [sds((planes, lines, own_rows, width), bf16)] * 2
        + [sds((planes, lines, chunks, share, width), bf16)] * 2
        + [sds((chunks, 1, width), f32), sds((8, width), f32)],
        name="mlp",
        **kernel_params(2 * count * part * width * (width + 6 * hidden_width), 36e6, 4.7e6),
    )(side_arr, tokens, att_own, att_recv, w_out, w_up, w_down, cotangent, pack, up_bias_all)

    glow_other = partner(glow)
    avg_qkv, avg_out, avg_up, avg_down, _ = lax.optimization_barrier((avg_qkv, avg_out, avg_up, avg_down, glow))
    new_qkv = 0.9 * avg_qkv + 0.1 * qkv_weight.astype(f32)
    new_out = 0.9 * avg_out + 0.1 * out_weight.astype(f32)
    new_up = 0.9 * avg_up + 0.1 * up_weight.astype(f32)
    new_down = 0.9 * avg_down + 0.1 * down_weight.astype(f32)
    add = lambda one, two: (one.astype(f32) + two.astype(f32)).astype(bf16)
    gdown_plane = sum_plane(add(gdown_own, partner(gdown_other)))
    gup_sum = add(gup_own, partner(gup_other))

    gmixed, gmixed_bias = [], []
    ties = ()
    for pair in range(pairs):
        lane_block = lambda lanes, pair=pair: pl.BlockSpec((1, 2, 1, part, lanes), lambda j, *_: (pair, 0, j, 0, 0))
        att_block = pl.BlockSpec((1, 1, part, 128), lambda j, *_, pair=pair: (pair, j, 0, 0))
        piece, piece_bias = pl.pallas_call(
            attend_back_kernel,
            grid_spec=pltpu.PrefetchScalarGridSpec(
                num_scalar_prefetch=1,
                grid=(count,),
                in_specs=[
                    lane_block(384),
                    lane_block(128),
                    att_block,
                    att_block,
                    row_block(part, width),
                    row_block(part, width),
                    pl.BlockSpec((128, width), lambda j, *_, pair=pair: (pair, 0)),
                    row_block(length, 128),
                ],
                out_specs=[both_block(384), const(8, 384)],
                scratch_shapes=[pltpu.VMEM((length // TQ_B, 2 * TQ_B, 256), bf16)] * 2
                + [pltpu.VMEM((length, 256), bf16)] * 2
                + [
                    pltpu.VMEM((length // TK_B, 128, TK_B), bf16),
                    pltpu.VMEM((length // TQ_B, 128, TQ_B), f32),
                    pltpu.VMEM((length, 128), f32),
                    pltpu.VMEM((length, 128), f32),
                ],
            ),
            out_shape=[sds((2, count, part, 384), bf16), sds((8, 384), f32)],
            name="attend_back",
            **kernel_params(25e9, 20e6, 4e6),
        )(flags_b, after(mixed, *ties), ext, att_own, att_other, glow, glow_other, wo_mine, kx)
        gmixed.append(piece)
        gmixed_bias.append(piece_bias)
        if pair == 0:
            gup_plane = sum_plane(after(gup_sum, gdown_plane))
            grad_down = sum_line(gdown_plane, lines)
            ties = (gdown_plane,)
        if pair == 1:
            early, inner_sum, plain_sum = pl.pallas_call(
                functools.partial(early_kernel, planes, share),
                grid=(count,),
                in_specs=[both_block(width), both_block(384), both_block(384), const(8, 384), const(8, 384)]
                + [head_block, head_block, row_block(part, width), row_block(part, width), const(width, 768)],
                out_specs=[const(planes, lines, 6, share, 384), const(width, 128), const(width, 128)],
                out_shape=[
                    sds((planes, lines, 6, share, 384), bf16),
                    sds((width, 128), f32),
                    sds((width, 128), f32),
                ],
                scratch_shapes=[pltpu.VMEM((width, 768), f32), pltpu.VMEM((wide, width), f32)],
                name="early",
                **kernel_params(9e9, 25e6),
            )(normed, *gmixed, *gmixed_bias, att_own, att_other, glow, glow_other, w_first)
            early_plane = sum_plane(after(early, gup_plane))
            gup_line = sum_line(gup_plane, lines)
            ties = (gup_plane, grad_down, early)
    grad_up = gup_line.transpose(1, 0, 2).reshape(share, hidden_width)

    late = pl.pallas_call(
        functools.partial(late_kernel, planes, share),
        grid_spec=pltpu.PrefetchScalarGridSpec(
            num_scalar_prefetch=1,
            grid=(count,),
            in_specs=[
                both_block(width),
                both_block(384),
                pl.BlockSpec((width, 384), lambda *_: (0, 2), pipeline_mode=pl.Buffered(1)),
                const(width, 128),
                const(width, 128),
                const(8, 384),
                const(8, 384),
                const(8, 384),
                const(16, width),
                const(8, width),
                const(chunks, 1, width),
            ],
            out_specs=const(planes, lines, 3, share, 384),
            scratch_shapes=[pltpu.VMEM((width, 384), f32)],
        ),
        out_shape=sds((planes, lines, 3, share, 384), bf16),
        name="late",
        **kernel_params(4e9, 10e6),
    )(side_arr, normed, after(gmixed[2], early_plane, gup_line), w_first, inner_sum, plain_sum, *gmixed_bias, pack, gvec, gup_bias)

    piece_spec = lambda side: pl.BlockSpec((1, 1, part, 384), lambda j, *_: (side, j, 0, 0))
    give_back = pl.pallas_call(
        give_kernel,
        grid=(count,),
        in_specs=[piece_spec(1)] * pairs + [const(width, 3 * wide)],
        out_specs=row_block(part, width),
        out_shape=sds((count, part, width), bf16),
        name="give_back",
        **kernel_params(2 * count * part * width * 3 * wide, 12e6),
    )(*gmixed[:2], after(gmixed[2], late), w_first)
    recv_back = partner(give_back)

    grad_input = pl.pallas_call(
        input_kernel,
        grid=(count,),
        in_specs=[piece_spec(0)] * pairs
        + [
            const(width, 3 * wide),
            row_block(part, width),
            row_block(part, width),
            row_block(part, width),
            const(16, width),
        ],
        out_specs=row_block(part, width),
        out_shape=sds((count, part, width), f32),
        name="input_grad",
        **kernel_params(2 * count * part * width * 3 * wide, 25e6),
    )(*gmixed, w_first, recv_back, tokens, glow, pack)

    late_plane = sum_plane(late, grad_input)
    unit_line = sum_line(jnp.concatenate([early_plane, late_plane], axis=1), lines)
    theirs = lax.dynamic_slice_in_dim(unit_line, 2 * (1 - side), 2, 0)
    theirs_late = lax.dynamic_slice_in_dim(unit_line, 7 - side, 1, 0)
    got = partner(jnp.concatenate([theirs, theirs_late, unit_line[8:]], axis=0))
    grad_qkv, grad_out, vec_rows = pl.pallas_call(
        finish_kernel,
        grid_spec=pltpu.PrefetchScalarGridSpec(
            num_scalar_prefetch=1,
            grid=(1,),
            in_specs=[
                pl.BlockSpec((9, share, 384), lambda *_: (0, 0, 0)),
                pl.BlockSpec((4, share, 384), lambda *_: (0, 0, 0)),
            ],
            out_specs=[
                pl.BlockSpec((share, 6 * wide), lambda *_: (0, 0)),
                pl.BlockSpec((share, width), lambda *_: (0, 0)),
                pl.BlockSpec((8, 384), lambda *_: (0, 0)),
            ],
        ),
        out_shape=[sds((share, 6 * wide), f32), sds((share, width), f32), sds((8, 384), f32)],
        name="finish",
        **kernel_params(1e6, 1e6),
    )(side_arr, unit_line, got)
    vec = lambda slot, size: vec_rows[slot // 3, 128 * (slot % 3) : 128 * (slot % 3) + size]

    return (
        out_tokens,
        grad_input,
        vec(0, share),
        vec(1, share),
        grad_qkv,
        vec(6, 2 * share),
        grad_out,
        vec(2, share),
        vec(3, share),
        vec(4, share),
        grad_up,
        vec(7, chunks * share),
        grad_down,
        vec(5, share),
        new_qkv,
        new_out,
        new_up,
        new_down,
    )


def specs_for(rows):
    flat = ("seq",) + (rows if isinstance(rows, tuple) else (rows,))
    grid, ids, vec, mat = P(rows, "seq", None), P(rows, "seq"), P(flat), P(flat, None)
    ins = (grid, ids, grid, vec, vec, mat, vec, mat, vec, vec, vec, mat, vec, mat, vec, mat, mat, mat, mat)
    outs = (grid, grid, vec, vec, mat, vec, mat, vec, vec, vec, mat, vec, mat, vec, mat, mat, mat, mat)
    return ins, outs


def solution(mesh):
    parts, rows = mesh.shape["seq"], mesh.shape["rows"]
    planes = 4
    if parts != 2 or rows % planes:
        ins, outs = specs_for("rows")
        return jax.shard_map(on_device, mesh=mesh, in_specs=ins, out_specs=outs, check_vma=False)
    lines = rows // planes
    finer = Mesh(mesh.devices.reshape(parts, lines, 2, 2), ("seq", "line", "y", "x"))
    ins, outs = specs_for(("line", "y", "x"))
    return jax.shard_map(
        functools.partial(pair_device, lines, planes), mesh=finer, in_specs=ins, out_specs=outs, check_vma=False
    )
```

```python
import functools

import jax
import jax.numpy as jnp
from jax import lax
from jax.experimental import pallas as pl
from jax.experimental.pallas import tpu as pltpu
from jax.sharding import Mesh
from jax.sharding import PartitionSpec as P

HEADS = 12
HEAD_DIM = 64
CLIPS = 6


def layer_norm(value, gain, bias):
    middle = jnp.mean(value, axis=-1, keepdims=True)
    centred = value - middle
    spread = jnp.mean(centred * centred, axis=-1, keepdims=True)
    return centred * lax.rsqrt(spread + 1e-06) * gain + bias


def exact_gelu(value):
    return jax.nn.gelu(value, approximate=False)


def permitted(seg_query, seg_key, pos_query, pos_key):
    same_clip = seg_query[:, :, None] == seg_key[:, None, :]
    open_key = (seg_key != CLIPS - 1)[:, None, :]
    diagonal = (pos_query[:, None] == pos_key[None, :])[None]
    return (same_clip & (open_key | diagonal))[:, :, None, :]


def scores(query_part, key_part):
    return 0.125 * jnp.einsum(
        "rqhe,rkhe->rqhk", query_part, key_part, preferred_element_type=jnp.float32
    )


def exponent(score_vals, allowed):
    return jnp.where(allowed, jnp.exp(jnp.where(allowed, score_vals, 0.0)), 0.0)


def on_device(
    tokens,
    segment_ids,
    cotangent,
    ln1_gain,
    ln1_bias,
    qkv_weight,
    qv_bias,
    out_weight,
    out_bias,
    ln2_gain,
    ln2_bias,
    up_weight,
    up_bias,
    down_weight,
    down_bias,
    avg_qkv,
    avg_out,
    avg_up,
    avg_down,
):
    f32 = jnp.float32
    bf16 = jnp.bfloat16
    rows_here, shard_len, width = tokens.shape
    count_rows = rows_here * shard_len
    own_pos = lax.axis_index("seq") * shard_len + jnp.arange(shard_len, dtype=jnp.int32)
    head_shape = (rows_here, shard_len, HEADS, HEAD_DIM)
    gain_one, bias_one, w_qkv, b_qv, w_out, b_out = (
        lax.all_gather(ln1_gain, ("seq", "rows"), axis=0, tiled=True),
        lax.all_gather(ln1_bias, ("seq", "rows"), axis=0, tiled=True),
        lax.all_gather(qkv_weight, ("seq", "rows"), axis=0, tiled=True),
        lax.all_gather(qv_bias, ("seq", "rows"), axis=0, tiled=True),
        lax.all_gather(out_weight, ("seq", "rows"), axis=0, tiled=True),
        lax.all_gather(out_bias, ("seq", "rows"), axis=0, tiled=True),
    )
    residual = tokens.astype(f32).reshape(count_rows, width)
    normed, norm_one_pull = jax.vjp(
        layer_norm, residual, gain_one.astype(f32), bias_one.astype(f32)
    )
    normed_low = normed.astype(bf16)
    mixed = jnp.dot(normed_low, w_qkv, preferred_element_type=f32)
    bias_qv = b_qv.astype(f32)
    query_heads = (mixed[:, :width] + bias_qv[:width]).astype(bf16).reshape(head_shape)
    key_heads = mixed[:, width : 2 * width].astype(bf16).reshape(head_shape)
    value_heads = (mixed[:, 2 * width :] + bias_qv[width:]).astype(bf16).reshape(head_shape)
    start_state = (jnp.zeros((rows_here, shard_len, HEADS), f32), jnp.zeros(head_shape, f32))
    piece_keys = lax.all_gather(key_heads, "seq", axis=1, tiled=True)
    piece_values = lax.all_gather(value_heads, "seq", axis=1, tiled=True)
    piece_seg = lax.all_gather(segment_ids, "seq", axis=1, tiled=True)
    piece_len = piece_keys.shape[1]
    block_len = min(piece_len, shard_len)

    def forward_advance(turn, state):
        totals, weighted = state
        offset = turn * block_len
        key_block = lax.dynamic_slice_in_dim(piece_keys, offset, block_len, 1)
        value_block = lax.dynamic_slice_in_dim(piece_values, offset, block_len, 1)
        seg_block = lax.dynamic_slice_in_dim(piece_seg, offset, block_len, 1)
        key_pos = offset + jnp.arange(block_len, dtype=jnp.int32)
        allowed = permitted(segment_ids, seg_block, own_pos, key_pos)
        expo = exponent(scores(query_heads, key_block), allowed)
        totals = totals + jnp.sum(expo, axis=-1)
        weighted = weighted + jnp.einsum(
            "rqhk,rkhe->rqhe", expo.astype(bf16), value_block, preferred_element_type=f32
        )
        return (totals, weighted)

    totals, weighted = lax.fori_loop(0, piece_len // block_len, forward_advance, start_state)
    attended = weighted / totals[..., None]
    attn_in = attended.reshape(count_rows, width).astype(bf16)
    middle = residual + jnp.dot(attn_in, w_out, preferred_element_type=f32) + b_out.astype(f32)
    gain_two, bias_two, w_up, b_up, w_down, b_down = (
        lax.all_gather(ln2_gain, ("seq", "rows"), axis=0, tiled=True),
        lax.all_gather(ln2_bias, ("seq", "rows"), axis=0, tiled=True),
        lax.all_gather(up_weight, ("seq", "rows"), axis=0, tiled=True),
        lax.all_gather(up_bias, ("seq", "rows"), axis=0, tiled=True),
        lax.all_gather(down_weight, ("seq", "rows"), axis=0, tiled=True),
        lax.all_gather(down_bias, ("seq", "rows"), axis=0, tiled=True),
    )
    normed_two, norm_two_pull = jax.vjp(
        layer_norm, middle, gain_two.astype(f32), bias_two.astype(f32)
    )
    normed_two_low = normed_two.astype(bf16)
    hidden_pre = jnp.dot(normed_two_low, w_up, preferred_element_type=f32) + b_up.astype(f32)
    hidden, gelu_pull = jax.vjp(exact_gelu, hidden_pre)
    hidden_low = hidden.astype(bf16)
    final = middle + jnp.dot(hidden_low, w_down, preferred_element_type=f32) + b_down.astype(f32)
    out_tokens = final.astype(bf16).reshape(tokens.shape)
    w_up_back, w_down_back = (
        lax.all_gather(up_weight, ("seq", "rows"), axis=0, tiled=True),
        lax.all_gather(down_weight, ("seq", "rows"), axis=0, tiled=True),
    )
    grad_out = cotangent.astype(f32).reshape(count_rows, width)
    grad_low = grad_out.astype(bf16)
    grad_down = jnp.einsum("nf,nd->fd", hidden_low, grad_low, preferred_element_type=f32)
    grad_down_b = jnp.sum(grad_low, axis=0, dtype=f32)
    grad_hidden = jnp.einsum("nd,fd->nf", grad_low, w_down_back, preferred_element_type=f32)
    (grad_pre,) = gelu_pull(grad_hidden)
    grad_pre_low = grad_pre.astype(bf16)
    grad_up = jnp.einsum("nd,nf->df", normed_two_low, grad_pre_low, preferred_element_type=f32)
    grad_up_b = jnp.sum(grad_pre_low, axis=0, dtype=f32)
    grad_normed_two = jnp.einsum("nf,df->nd", grad_pre_low, w_up_back, preferred_element_type=f32)
    grad_mid_norm, grad_gain_two, grad_bias_two = norm_two_pull(grad_normed_two)
    grad_mid = grad_out + grad_mid_norm
    mlp_sums = (
        lax.psum_scatter(grad_gain_two, ("seq", "rows"), scatter_dimension=0, tiled=True),
        lax.psum_scatter(grad_bias_two, ("seq", "rows"), scatter_dimension=0, tiled=True),
        lax.psum_scatter(grad_up, ("seq", "rows"), scatter_dimension=0, tiled=True),
        lax.psum_scatter(grad_up_b, ("seq", "rows"), scatter_dimension=0, tiled=True),
        lax.psum_scatter(grad_down, ("seq", "rows"), scatter_dimension=0, tiled=True),
        lax.psum_scatter(grad_down_b, ("seq", "rows"), scatter_dimension=0, tiled=True),
    )
    w_qkv_back, w_out_back = (
        lax.all_gather(qkv_weight, ("seq", "rows"), axis=0, tiled=True),
        lax.all_gather(out_weight, ("seq", "rows"), axis=0, tiled=True),
    )
    grad_mid_low = grad_mid.astype(bf16)
    grad_wout = jnp.einsum("nd,ne->de", attn_in, grad_mid_low, preferred_element_type=f32)
    grad_bout = jnp.sum(grad_mid_low, axis=0, dtype=f32)
    grad_att = jnp.einsum(
        "ne,de->nd", grad_mid_low, w_out_back, preferred_element_type=f32
    ).reshape(head_shape)
    grad_acc = (grad_att / totals[..., None]).astype(bf16)
    shift_low = (jnp.sum(grad_att * attended, axis=-1) / totals).astype(bf16)
    shift_wide = shift_low.astype(f32)
    query_piece_keys = lax.all_gather(key_heads, "seq", axis=1, tiled=True)
    query_piece_values = lax.all_gather(value_heads, "seq", axis=1, tiled=True)
    query_piece_seg = lax.all_gather(segment_ids, "seq", axis=1, tiled=True)
    piece_len = query_piece_keys.shape[1]
    query_block_len = min(piece_len, shard_len)

    def query_advance(turn, grad_query):
        offset = turn * query_block_len
        key_block = lax.dynamic_slice_in_dim(query_piece_keys, offset, query_block_len, 1)
        value_block = lax.dynamic_slice_in_dim(query_piece_values, offset, query_block_len, 1)
        seg_block = lax.dynamic_slice_in_dim(query_piece_seg, offset, query_block_len, 1)
        key_pos = offset + jnp.arange(query_block_len, dtype=jnp.int32)
        allowed = permitted(segment_ids, seg_block, own_pos, key_pos)
        expo = exponent(scores(query_heads, key_block), allowed)
        inner = jnp.einsum("rqhe,rkhe->rqhk", grad_acc, value_block, preferred_element_type=f32)
        grad_score = (expo * (inner - shift_wide[..., None])).astype(bf16)
        return grad_query + jnp.einsum(
            "rqhk,rkhe->rqhe", grad_score, key_block, preferred_element_type=f32
        )

    grad_query = lax.fori_loop(
        0, piece_len // query_block_len, query_advance, jnp.zeros(head_shape, f32)
    )
    key_start = (jnp.zeros(head_shape, f32), jnp.zeros(head_shape, f32))
    piece_queries = lax.all_gather(query_heads, "seq", axis=1, tiled=True)
    piece_grads = lax.all_gather(grad_acc, "seq", axis=1, tiled=True)
    key_piece_seg = lax.all_gather(segment_ids, "seq", axis=1, tiled=True)
    piece_shift = lax.all_gather(shift_low, "seq", axis=1, tiled=True)
    piece_len = piece_queries.shape[1]
    key_block_len = min(piece_len, shard_len)

    def key_advance(turn, state):
        grad_key, grad_value = state
        offset = turn * key_block_len
        query_block = lax.dynamic_slice_in_dim(piece_queries, offset, key_block_len, 1)
        grad_block = lax.dynamic_slice_in_dim(piece_grads, offset, key_block_len, 1)
        seg_block = lax.dynamic_slice_in_dim(key_piece_seg, offset, key_block_len, 1)
        shift_block = lax.dynamic_slice_in_dim(piece_shift, offset, key_block_len, 1).astype(f32)
        query_pos = offset + jnp.arange(key_block_len, dtype=jnp.int32)
        allowed = permitted(seg_block, segment_ids, query_pos, own_pos)
        expo = exponent(scores(query_block, key_heads), allowed)
        inner = jnp.einsum("rqhe,rkhe->rqhk", grad_block, value_heads, preferred_element_type=f32)
        grad_score = (expo * (inner - shift_block[..., None])).astype(bf16)
        grad_key = grad_key + jnp.einsum(
            "rqhk,rqhe->rkhe", grad_score, query_block, preferred_element_type=f32
        )
        grad_value = grad_value + jnp.einsum(
            "rqhk,rqhe->rkhe", expo.astype(bf16), grad_block, preferred_element_type=f32
        )
        return (grad_key, grad_value)

    grad_key, grad_value = lax.fori_loop(0, piece_len // key_block_len, key_advance, key_start)
    grad_q_low = (0.125 * grad_query).astype(bf16).reshape(count_rows, width)
    grad_k_low = (0.125 * grad_key).astype(bf16).reshape(count_rows, width)
    grad_v_low = grad_value.astype(bf16).reshape(count_rows, width)
    grad_mixed = jnp.concatenate([grad_q_low, grad_k_low, grad_v_low], axis=1)
    grad_wqkv = jnp.einsum("nd,ne->de", normed_low, grad_mixed, preferred_element_type=f32)
    grad_bqv = jnp.concatenate(
        [jnp.sum(grad_q_low, axis=0, dtype=f32), jnp.sum(grad_v_low, axis=0, dtype=f32)], axis=0
    )
    grad_normed = jnp.einsum("ne,de->nd", grad_mixed, w_qkv_back, preferred_element_type=f32)
    grad_res_norm, grad_gain_one, grad_bias_one = norm_one_pull(grad_normed)
    grad_input = (grad_mid + grad_res_norm).reshape(tokens.shape)
    attn_sums = (
        lax.psum_scatter(grad_gain_one, ("seq", "rows"), scatter_dimension=0, tiled=True),
        lax.psum_scatter(grad_bias_one, ("seq", "rows"), scatter_dimension=0, tiled=True),
        lax.psum_scatter(grad_wqkv, ("seq", "rows"), scatter_dimension=0, tiled=True),
        lax.psum_scatter(grad_bqv, ("seq", "rows"), scatter_dimension=0, tiled=True),
        lax.psum_scatter(grad_wout, ("seq", "rows"), scatter_dimension=0, tiled=True),
        lax.psum_scatter(grad_bout, ("seq", "rows"), scatter_dimension=0, tiled=True),
    )
    new_qkv = 0.9 * avg_qkv + 0.1 * qkv_weight.astype(f32)
    new_out = 0.9 * avg_out + 0.1 * out_weight.astype(f32)
    new_up = 0.9 * avg_up + 0.1 * up_weight.astype(f32)
    new_down = 0.9 * avg_down + 0.1 * down_weight.astype(f32)
    return (
        out_tokens,
        grad_input,
        attn_sums[0],
        attn_sums[1],
        attn_sums[2],
        attn_sums[3],
        attn_sums[4],
        attn_sums[5],
        mlp_sums[0],
        mlp_sums[1],
        mlp_sums[2],
        mlp_sums[3],
        mlp_sums[4],
        mlp_sums[5],
        new_qkv,
        new_out,
        new_up,
        new_down,
    )


f32 = jnp.float32
bf16 = jnp.bfloat16
NT = (((1,), (1,)), ((), ()))
LOG2E = 1.4426950408889634
SCORE = 0.125 * LOG2E
BIG = 16384.0
VMEM_BYTES = 63 * 1024 * 1024
TQ_F, TK_F = 512, 256
TK_B, TQ_B = 512, 512
LANE_LOG = 41
LANE_PAD = 44


def kernel_params(flops, bytes_accessed, transcendentals=0, order=("arbitrary",)):
    return dict(
        compiler_params=pltpu.CompilerParams(
            vmem_limit_bytes=VMEM_BYTES, dimension_semantics=order
        ),
        cost_estimate=pl.CostEstimate(
            flops=int(flops), bytes_accessed=int(bytes_accessed), transcendentals=int(transcendentals)
        ),
    )


def standardise(value):
    middle = jnp.mean(value, axis=-1, keepdims=True)
    centred = value - middle
    spread = jnp.mean(centred * centred, axis=-1, keepdims=True)
    rstd = lax.rsqrt(spread + 1e-06)
    return centred * rstd, rstd


def norm_pull(grad_normed, gain, xhat, rstd):
    scaled = grad_normed * gain
    first = jnp.mean(scaled, axis=-1, keepdims=True)
    second = jnp.mean(scaled * xhat, axis=-1, keepdims=True)
    return rstd * (scaled - first - xhat * second)


def gelu_pair(x):
    size = jnp.abs(x)
    base = 1.0 + 0.23164189 * size
    t = 1.0 / base
    bell = jnp.exp2(x * x * (-0.5 * LOG2E))
    poly = t * (0.127414796 + t * (-0.142248368 + t * (0.7107068705 + t * (-0.7265760135 + t * 0.5307027145))))
    tail = poly * bell
    phi = jnp.where(x >= 0.0, 1.0 - tail, tail)
    return x * phi, phi + x * bell * 0.3989422804014327


def lane_masks():
    lane = lax.broadcasted_iota(jnp.int32, (1, 128), 1)
    low = jnp.where(lane < HEAD_DIM, 1.0, 0.0)
    return low.astype(bf16), (1.0 - low).astype(bf16)


def prepare_kernel(share, side_ref, w_ref, up_ref, out_ref, down_ref, *refs):
    vectors, (mine_ref, give_ref, second_ref) = refs[:-3], refs[-3:]
    width = down_ref.shape[1]
    blocks = up_ref.shape[1] // width
    for block in range(blocks):
        second_ref[block * share : (block + 1) * share] = up_ref[:, block * width : (block + 1) * width]
    second_ref[blocks * share : (blocks + 1) * share] = out_ref[...]
    second_ref[(blocks + 1) * share :] = down_ref[...]
    wide = w_ref.shape[1] // 6
    pairs = wide // 128
    for target, side in ((mine_ref, side_ref[0]), (give_ref, 1 - side_ref[0])):
        for pair in range(pairs):
            for kind in range(3):
                start = pl.multiple_of(kind * 2 * wide + side * wide + pair * 128, 128)
                at = 384 * pair + 128 * kind
                target[:, at : at + 128] = w_ref[:, pl.ds(start, 128)]
    lane = lax.broadcasted_iota(jnp.int32, (share, 128), 1)
    small = jnp.zeros((share, 128), f32)
    column = 0
    for ref in vectors:
        row = jnp.broadcast_to(ref[...].astype(f32), (8, ref.shape[1])).T
        for start in range(0, ref.shape[1], share):
            small = jnp.where(lane == column, row[start : start + share, 0:1], small)
            column += 1
    small = small.astype(bf16)
    mine_ref[:, 3 * wide :] = small
    give_ref[:, 3 * wide :] = small


def project_kernel(
    share, side_ref, own_ref, other_ref, w_ref, small_ref, normed_ref, mixed_ref, pack_ref, shift_s
):
    which, turn = pl.program_id(0), pl.program_id(1)
    wide = shift_s.shape[1] // 3
    pairs = wide // 128

    @pl.when((which == 0) & (turn == 0))
    def _():
        small = small_ref[...].astype(f32).T
        pack_ref[...] = small[0:16]
        shift_s[...] = jnp.zeros_like(shift_s)
        spot = lax.broadcasted_iota(jnp.int32, (wide, wide), 0)
        target = lax.broadcasted_iota(jnp.int32, (wide, wide), 1) + side_ref[0] * wide
        sums = [jnp.zeros((16, wide), f32), jnp.zeros((16, wide), f32)]
        for part in range(2):
            wanted = lax.div(spot, share) * (2 * share) + part * share + lax.rem(spot, share)
            chosen = jnp.where(wanted == target, 1.0, 0.0).astype(bf16)
            for kind in range(2):
                values = small[6 + part : 7 + part, kind * wide : (kind + 1) * wide]
                values = jnp.broadcast_to(values, (16, wide)).astype(bf16)
                sums[kind] += jnp.dot(values, chosen, preferred_element_type=f32)
        for pair in range(pairs):
            lanes = slice(128 * pair, 128 * pair + 128)
            shift_s[:, 384 * pair : 384 * pair + 128] = sums[0][0:1, lanes]
            shift_s[:, 384 * pair + 256 : 384 * pair + 384] = sums[1][0:1, lanes]

    tiles = 2
    size = normed_ref.shape[2] // tiles

    def normed_tile(i):
        rows = slice(i * size, (i + 1) * size)
        value = jnp.where(which == 0, own_ref[0, rows], other_ref[0, rows]).astype(f32)
        xhat, _ = standardise(value)
        normed = (xhat * pack_ref[0:1, :] + pack_ref[1:2, :]).astype(bf16)
        normed_ref[0, 0, rows] = normed
        return normed

    normed = normed_tile(0)
    for i in range(tiles):
        mixed = jnp.dot(normed, w_ref[...], preferred_element_type=f32) + shift_s[...]
        mixed = mixed.astype(bf16)
        if i + 1 < tiles:
            normed = normed_tile(i + 1)
        for pair in range(pairs):
            lanes = slice(384 * pair, 384 * pair + 384)
            mixed_ref[pair, 0, 0, i * size : (i + 1) * size] = mixed[:, lanes]


def attend_kernel(base, flag_ref, mixed_ref, qx_ref, kx_ref, *rest):
    own_ref, other_ref, ext_ref, q_s, k_s, v_s, acc_s = rest[-7:]
    row = base + pl.program_id(0)
    length = q_s.shape[1]
    heads = q_s.shape[0]
    half = length // 2
    low, high = lane_masks()
    qx, kx = qx_ref[0], kx_ref[0]
    q_low, q_high, k_low, k_high = qx * low, qx * high, kx * low, kx * high
    for pair in range(heads // 2):
        q = mixed_ref[pair, :, 0, :, 0:128].reshape(length, 128)
        k = mixed_ref[pair, :, 0, :, 128:256].reshape(length, 128)
        v = mixed_ref[pair, :, 0, :, 256:384].reshape(length, 128)
        q_s[2 * pair] = q * low + q_high
        q_s[2 * pair + 1] = q * high + q_low
        k_s[2 * pair] = k * low + k_high
        k_s[2 * pair + 1] = k * high + k_low
        v_s[2 * pair] = v * low + high
        v_s[2 * pair + 1] = v * high + low
    acc_s[...] = jnp.zeros_like(acc_s)
    key_blocks = length // TK_F

    def step(index, carry):
        @pl.when(flag_ref[row, index] != 0)
        def _():
            q_at = pl.ds(pl.multiple_of((index // key_blocks) * TQ_F, TQ_F), TQ_F)
            k_at = pl.ds(pl.multiple_of((index % key_blocks) * TK_F, TK_F), TK_F)
            for head in range(heads):
                score = lax.dot_general(
                    q_s[head, q_at, :], k_s[head, k_at, :], NT, preferred_element_type=f32
                )
                expo = jnp.exp2(score * SCORE).astype(bf16)
                acc_s[head, q_at, :] += jnp.dot(expo, v_s[head, k_at, :], preferred_element_type=f32)

        return carry

    lax.fori_loop(0, (length // TQ_F) * key_blocks, step, 0)
    lane = lax.broadcasted_iota(jnp.int32, (half, 128), 1)
    first_half = lane < HEAD_DIM
    spot = lane % HEAD_DIM
    for pair in range(heads // 2):
        for side in range(2):
            rows = slice(side * half, (side + 1) * half)
            first, second = acc_s[2 * pair, rows], acc_s[2 * pair + 1, rows]
            top = jnp.where(first_half, first, second)
            crossed = jnp.where(first_half, second, first)
            totals = pltpu.roll(crossed, HEAD_DIM, 1)
            target = own_ref if side == 0 else other_ref
            target[pair, 0] = (top / totals).astype(bf16)
            lse = -8.0 * jnp.log(crossed)
            lse_a = lse.astype(bf16).astype(f32)
            lse_b = (lse - lse_a).astype(bf16).astype(f32)
            ext = jnp.where(
                spot == LANE_LOG,
                lse_a,
                jnp.where(
                    spot == LANE_LOG + 1,
                    lse_b,
                    jnp.where(spot == LANE_LOG + 2, lse - lse_a - lse_b, qx[rows].astype(f32)),
                ),
            )
            ext_ref[pair, side, 0] = ext.astype(bf16)


def join_lanes(ref):
    return jnp.concatenate([ref[i, 0] for i in range(ref.shape[0])], axis=1)


def mlp_kernel(
    planes, share, spot_ref, x_ref, mine_ref, recv_ref, wo_ref, up_ref, near_own, far_own, near_other, far_other,
    grad_ref, pack_ref, upb_ref,
    out_ref, glow_ref, gdown_own, gdown_other, gup_own, gup_other, gbias_ref, gvec_ref,
    down_s, up_s, wo_v, up_v, down_v, gd_own, gd_other, gu_own, gu_other, load_sem, store_sem,
):
    turn = pl.program_id(0)
    side, x_at = spot_ref[0], spot_ref[2]
    chunks, size = down_s.shape[0], down_s.shape[2]
    load_out = pltpu.make_async_copy(wo_ref, wo_v, load_sem.at[0])
    load_up = pltpu.make_async_copy(up_ref, up_v, load_sem.at[1])
    load_down = []
    for index, piece in enumerate((near_own, far_own, near_other, far_other)):
        at_side = 1 - side if index // 2 else side
        column = 1 - x_at if index % 2 else x_at
        for i in range(2):
            target = down_v.at[at_side, :, i, column]
            load_down.append(pltpu.make_async_copy(piece.at[i], target, load_sem.at[2 + 2 * index + i]))

    @pl.when(turn == 0)
    def _():
        load_out.start()
        load_up.start()
        for load in load_down:
            load.start()
        down_s[...] = jnp.zeros_like(down_s)
        up_s[...] = jnp.zeros_like(up_s)
        gbias_ref[...] = jnp.zeros_like(gbias_ref)
        gvec_ref[...] = jnp.zeros_like(gvec_ref)
        load_out.wait()

    middle = (
        x_ref[0].astype(f32)
        + jnp.dot(join_lanes(mine_ref), wo_v[side], preferred_element_type=f32)
        + jnp.dot(join_lanes(recv_ref), wo_v[1 - side], preferred_element_type=f32)
        + pack_ref[2:3, :]
    )
    xhat, rstd = standardise(middle)
    normed = (xhat * pack_ref[3:4, :] + pack_ref[4:5, :]).astype(bf16)
    normed_t = normed.T
    grad = grad_ref[0]
    grad_t = grad.T
    total = middle + pack_ref[5:6, :]

    @pl.when(turn == 0)
    def _():
        load_up.wait()
        for load in load_down:
            load.wait()

    half_lines = down_v.shape[1] // (chunks // 2)

    def down_chunk(f):
        line = (f % (chunks // 2)) * half_lines
        return down_v[f // (chunks // 2), line : line + half_lines].reshape(size, down_v.shape[-1])

    def first_layer(f):
        at = slice(f * size, (f + 1) * size)
        return jnp.dot(normed, up_v[:, at], preferred_element_type=f32) + upb_ref[f : f + 1, :]

    gnormed = None
    pre = first_layer(0)
    for f in range(chunks):
        at = slice(f * size, (f + 1) * size)
        hidden, slope = gelu_pair(pre)
        ghidden = lax.dot_general(grad, down_chunk(f), NT, preferred_element_type=f32)
        if f + 1 < chunks:
            pre = first_layer(f + 1)
        hidden = hidden.astype(bf16)
        gpre = (ghidden * slope).astype(bf16)
        total = total + jnp.dot(hidden, down_chunk(f), preferred_element_type=f32)
        part = lax.dot_general(gpre, up_v[:, at], NT, preferred_element_type=f32)
        gnormed = part if gnormed is None else gnormed + part
        down_s[f] += jnp.dot(grad_t, hidden, preferred_element_type=f32)
        up_s[f] += jnp.dot(normed_t, gpre, preferred_element_type=f32)
        gbias_ref[f] += jnp.sum(gpre.astype(f32), axis=0, keepdims=True)
    out_ref[0] = total.astype(bf16)
    gmid = grad.astype(f32) + norm_pull(gnormed, pack_ref[3:4, :], xhat, rstd)
    low = gmid.astype(bf16)
    glow_ref[0] = low
    gvec_ref[0:1, :] += jnp.sum(gnormed * xhat, axis=0, keepdims=True)
    gvec_ref[1:2, :] += jnp.sum(gnormed, axis=0, keepdims=True)
    gvec_ref[2:3, :] += jnp.sum(low.astype(f32), axis=0, keepdims=True)
    gvec_ref[3:4, :] += jnp.sum(grad.astype(f32), axis=0, keepdims=True)

    @pl.when(turn == pl.num_programs(0) - 1)
    def _():
        half = chunks // 2
        rows = chunks * share
        per_chunk = size // rows
        lines_chunk = per_chunk // planes
        for f in range(chunks):
            whole = down_s[f].astype(bf16).T
            at_line = (f % half) * lines_chunk
            span = slice(at_line, at_line + lines_chunk)
            for target, result, wanted in ((gd_own, gdown_own, f // half), (gd_other, gdown_other, 1 - f // half)):

                @pl.when(side == wanted)
                def _(target=target, result=result, whole=whole, f=f, at_line=at_line, span=span):
                    for i in range(per_chunk):
                        target[i % planes, at_line + i // planes] = whole[i * rows : (i + 1) * rows]
                    pltpu.make_async_copy(target.at[:, span], result.at[:, span], store_sem.at[f]).start()

        wide = up_s.shape[1] // 2
        ups = ((gu_own, gup_own, side * wide), (gu_other, gup_other, (1 - side) * wide))
        for which, (target, result, base) in enumerate(ups):
            for f in range(chunks):
                for at in range(wide // share):
                    start = pl.multiple_of(base + at * share, 8)
                    target[at % planes, at // planes, f] = up_s[f, pl.ds(start, share), :].astype(bf16)
                pltpu.make_async_copy(
                    target.at[:, :, f], result.at[:, :, f], store_sem.at[chunks * (1 + which) + f]
                ).start()
        for f in range(chunks):
            span = slice(0, lines_chunk)
            pltpu.make_async_copy(gd_own.at[:, span], gdown_own.at[:, span], store_sem.at[f]).wait()
        for which, (target, result, base) in enumerate(ups):
            for f in range(chunks):
                pltpu.make_async_copy(
                    target.at[:, :, f], result.at[:, :, f], store_sem.at[chunks * (1 + which) + f]
                ).wait()


def attend_back_kernel(
    flag_ref, side_ref, mixed_ref, ext_ref, att_own, att_other, own_ref, other_ref, wo_ref, kx_ref,
    gmixed_ref, gbias_ref,
    q_s, d_s, k_s, v_s, kt_s, gq_s, gk_s, gv_s,
):
    row = pl.program_id(0)
    length = k_s.shape[0]
    half = length // 2
    low, high = lane_masks()
    lane = lax.broadcasted_iota(jnp.int32, (1, 128), 1)
    spot = lane % HEAD_DIM
    square_row = lax.broadcasted_iota(jnp.int32, (128, 128), 0) < HEAD_DIM
    square_col = lax.broadcasted_iota(jnp.int32, (128, 128), 1) < HEAD_DIM
    crossing = jnp.where(square_row == square_col, 0.0, -1.0).astype(bf16)
    one_hot_a = jnp.where(spot == 0, 1.0, 0.0)
    one_hot_b = jnp.where(spot == 1, 1.0, 0.0)
    v_ext = (one_hot_a + one_hot_b).astype(bf16)

    @pl.when(row == 0)
    def _():
        gbias_ref[...] = jnp.zeros_like(gbias_ref)

    mixed_at = lambda lanes: mixed_ref[0, :, 0, :, lanes].reshape(length, 128)
    q, k = mixed_at(slice(0, 128)), mixed_at(slice(128, 256))
    ext = ext_ref[0, :, 0].reshape(length, 128)
    k_s[:, 0:128] = k
    k_s[:, 128:256] = kx_ref[0]
    v_s[:, 0:128] = mixed_at(slice(256, 384))
    v_s[:, 128:256] = jnp.broadcast_to(v_ext, (length, 128))
    for head, (mine, other) in enumerate(((low, high), (high, low))):
        q_part, ext_part = q * mine, ext * other
        for i in range(length // TQ_B):
            at = slice(i * TQ_B, (i + 1) * TQ_B)
            rows = slice(head * TQ_B, (head + 1) * TQ_B)
            q_s[i, rows, 0:128] = q_part[at]
            q_s[i, rows, 128:256] = ext_part[at]
    for side in range(2):
        gates = own_ref[0] if side == 0 else other_ref[0]
        d = lax.dot_general(gates, wo_ref[...], NT, preferred_element_type=f32)
        moved = d * (att_own if side == 0 else att_other)[0, 0].astype(f32)
        moved_a = moved.astype(bf16)
        moved_b = (moved - moved_a.astype(f32)).astype(bf16)
        shift = jnp.dot(moved_a, crossing, preferred_element_type=f32) + jnp.dot(
            moved_b, crossing, preferred_element_type=f32
        )
        shift_a = shift.astype(bf16).astype(f32)
        dx = (shift_a * one_hot_a + (shift - shift_a) * one_hot_b).astype(bf16)
        d = d.astype(bf16)
        tile = min(TQ_B, half)
        for head, (mine, other) in enumerate(((low, high), (high, low))):
            d_part, dx_part = d * mine, dx * other
            for i in range(half // tile):
                at = slice(i * tile, (i + 1) * tile)
                start = side * half + i * tile
                rows = slice(head * TQ_B + start % TQ_B, head * TQ_B + start % TQ_B + tile)
                d_s[start // TQ_B, rows, 0:128] = d_part[at]
                d_s[start // TQ_B, rows, 128:256] = dx_part[at]
    for i in range(length // TK_B):
        kt_s[i] = k[i * TK_B : (i + 1) * TK_B].T
    gq_s[...] = jnp.zeros_like(gq_s)
    gk_s[...] = jnp.zeros_like(gk_s)
    gv_s[...] = jnp.zeros_like(gv_s)
    query_blocks = length // TQ_B

    def step(index, carry):
        @pl.when(flag_ref[row, index] != 0)
        def _():
            qi = index % query_blocks
            ki = index // query_blocks
            k_at = pl.ds(pl.multiple_of(ki * TK_B, TK_B), TK_B)
            probs, grads = [], []
            for head in range(2):
                rows = slice(head * TQ_B, (head + 1) * TQ_B)
                score = lax.dot_general(
                    k_s[k_at, :], q_s[qi, rows, :], NT, preferred_element_type=f32
                )
                inner = lax.dot_general(
                    v_s[k_at, :], d_s[qi, rows, :], NT, preferred_element_type=f32
                )
                prob = jnp.exp2(score * SCORE)
                probs.append(prob.astype(bf16))
                grads.append((prob * inner).astype(bf16))
            for head in range(2):
                at = slice(head * HEAD_DIM, (head + 1) * HEAD_DIM)
                gq_s[qi, at, :] += jnp.dot(kt_s[ki, at, :], grads[head], preferred_element_type=f32)
            gv_s[k_at, :] += jnp.dot(
                jnp.concatenate(probs, axis=1), d_s[qi, :, 0:128], preferred_element_type=f32
            )
            gk_s[k_at, :] += jnp.dot(
                jnp.concatenate(grads, axis=1), q_s[qi, :, 0:128], preferred_element_type=f32
            )

        return carry

    lax.fori_loop(0, query_blocks * (length // TK_B), step, 0)
    for i in range(query_blocks):
        gq = (0.125 * gq_s[i].T).astype(bf16)
        for start in range(0, TQ_B, min(TQ_B, half)):
            at = i * TQ_B + start
            size = min(TQ_B, half)
            gmixed_ref[at // half, 0, at % half : at % half + size, 0:128] = gq[start : start + size]
        gbias_ref[0:1, 0:128] += jnp.sum(gq.astype(f32), axis=0, keepdims=True)
    gk = (0.125 * gk_s[...]).astype(bf16)
    gv = gv_s[...].astype(bf16)
    gbias_ref[0:1, 128:256] += jnp.sum(gk.astype(f32), axis=0, keepdims=True)
    gbias_ref[0:1, 256:384] += jnp.sum(gv.astype(f32), axis=0, keepdims=True)
    for side in range(2):
        gmixed_ref[side, 0, :, 128:256] = gk[side * half : (side + 1) * half]
        gmixed_ref[side, 0, :, 256:384] = gv[side * half : (side + 1) * half]


def weight_dot(normed_ref, *piece_refs):
    normed_t = jnp.concatenate([normed_ref[0, 0], normed_ref[1, 0]], axis=0).T
    sides = []
    for side in range(2):
        sides.append(jnp.concatenate([ref[side, 0] for ref in piece_refs], axis=1))
    return jnp.dot(normed_t, jnp.concatenate(sides, axis=0), preferred_element_type=f32)


def fold_lanes(value):
    total = value[:, 0:128]
    for at in range(128, value.shape[1], 128):
        total = total + value[:, at : at + 128]
    return total


def early_kernel(
    planes, share, normed_ref, g0_ref, g1_ref, b0_ref, b1_ref, mine_ref, other_ref, low_ref, low_other_ref, w_ref,
    unit_ref, first_ref, second_ref, acc_s, out_s,
):
    turn = pl.program_id(0)

    @pl.when(turn == 0)
    def _():
        acc_s[...] = jnp.zeros_like(acc_s)
        out_s[...] = jnp.zeros_like(out_s)

    acc_s[...] += weight_dot(normed_ref, g0_ref, g1_ref)
    across = (((0,), (0,)), ((), ()))
    out_s[...] += lax.dot_general(
        join_lanes(mine_ref), low_ref[0], across, preferred_element_type=f32
    ) + lax.dot_general(join_lanes(other_ref), low_other_ref[0], across, preferred_element_type=f32)

    @pl.when(turn == pl.num_programs(0) - 1)
    def _():
        weights = w_ref[...].astype(f32)
        sums = jnp.concatenate([b0_ref[0:1, :], b1_ref[0:1, :]], axis=1)
        first_ref[...] = fold_lanes(weights * acc_s[...])
        second_ref[...] = fold_lanes(weights * sums)
        count = out_s.shape[0] // share
        for at in range(count):
            spot = (at % planes, at // planes)
            for half in range(2):
                lanes = slice(384 * half, 384 * half + 384)
                for side in range(2):
                    start = (side * count + at) * share
                    unit_ref[spot + (2 * side + half,)] = acc_s[start : start + share, lanes].astype(bf16)
                unit_ref[spot + (4 + half,)] = out_s[at * share : (at + 1) * share, lanes].astype(bf16)


def scatter_rows(vector, step, offset, owners):
    n = vector.shape[1]
    owner = lax.broadcasted_iota(jnp.int32, (owners, n), 0) - offset
    mask = lax.div(lax.broadcasted_iota(jnp.int32, (owners, n), 1), step) == owner
    spread = jnp.where(mask, jnp.broadcast_to(vector, (owners, n)), 0.0).astype(bf16)
    lane = lax.rem(lax.broadcasted_iota(jnp.int32, (128, n), 1), step)
    chosen = jnp.where(lane == lax.broadcasted_iota(jnp.int32, (128, n), 0), 1.0, 0.0).astype(bf16)
    return lax.dot_general(spread, chosen, NT, preferred_element_type=f32)


def late_kernel(
    planes, share, side_ref, normed_ref, g_ref, w_ref, first_ref, second_ref, b0_ref, b1_ref, b2_ref, pack_ref,
    gvec_ref, gup_ref, unit_ref, acc_s,
):
    turn = pl.program_id(0)

    @pl.when(turn == 0)
    def _():
        acc_s[...] = jnp.zeros_like(acc_s)

    acc_s[...] += weight_dot(normed_ref, g_ref)

    @pl.when(turn == pl.num_programs(0) - 1)
    def _():
        side = side_ref[0]
        weights = w_ref[...].astype(f32)
        width = weights.shape[0]
        owners = width // share
        count = owners // 2
        inner = first_ref[...] + fold_lanes(weights * acc_s[...])
        plain = second_ref[...] + fold_lanes(weights * b2_ref[0:1, :])
        inner = jnp.sum(inner.T, axis=0, keepdims=True)
        plain = jnp.sum(plain.T, axis=0, keepdims=True)
        gain, bias = pack_ref[0:1, :], pack_ref[1:2, :]
        g_gain = (inner - bias * plain) / gain
        biases = (b0_ref, b1_ref, b2_ref)
        query = jnp.concatenate([b[0:1, 0:128] for b in biases], axis=1)
        value = jnp.concatenate([b[0:1, 256:384] for b in biases], axis=1)
        chunks = gup_ref.shape[0]
        rows_up = chunks * share
        up_bias = None
        for f in range(chunks):
            part = scatter_rows(gup_ref[f], rows_up, f * (width // rows_up), owners)
            up_bias = part if up_bias is None else up_bias + part
        wide = width // 2
        first_owner = side * (wide // (2 * share))
        qv_bias = scatter_rows(query, 2 * share, first_owner, owners) + scatter_rows(
            value, 2 * share, first_owner + count, owners
        )
        plain_rows = lambda vec: scatter_rows(vec, share, 0, owners)
        slots = [
            plain_rows(g_gain),
            plain_rows(plain),
            plain_rows(gvec_ref[2:3, :]),
            plain_rows(gvec_ref[0:1, :]),
            plain_rows(gvec_ref[1:2, :]),
            plain_rows(gvec_ref[3:4, :]),
            qv_bias,
            up_bias,
            jnp.zeros((owners, 128), f32),
        ]
        lines_of = [jnp.concatenate(slots[3 * i : 3 * i + 3], axis=1) for i in range(3)]
        blank = jnp.zeros((5, 384), f32)
        for at in range(count):
            spot = (at % planes, at // planes)
            small = []
            for half in range(2):
                owner = half * count + at
                start = owner * share
                unit_ref[spot + (half,)] = acc_s[start : start + share, :].astype(bf16)
                small += [line[owner : owner + 1, :] for line in lines_of] + [blank]
            small.append(jnp.zeros((share - 16, 384), f32))
            unit_ref[spot + (2,)] = jnp.concatenate(small, axis=0).astype(bf16)


def finish_kernel(side_ref, line_ref, got_ref, qkv_ref, out_ref, *vec_refs):
    side = side_ref[0]
    wide = qkv_ref.shape[1] // 6
    for pair in range(wide // 128):
        own = line_ref[2 * side + pair] if pair < 2 else line_ref[6 + side]
        other = got_ref[pair]
        for kind in range(3):
            lanes = slice(128 * kind, 128 * kind + 128)
            for half in range(2):
                at = kind * 2 * wide + half * wide + 128 * pair
                qkv_ref[:, at : at + 128] = jnp.where(side == half, own[:, lanes], other[:, lanes])
    out_ref[:, 0:384] = line_ref[4]
    out_ref[:, 384:768] = line_ref[5]
    start = pl.multiple_of(8 * side, 8)
    small = line_ref[8, pl.ds(start, 8), :] + got_ref[3, pl.ds(start, 8), :]
    for slot, ref in enumerate(vec_refs):
        at = 128 * (slot % 3)
        ref[...] = small[slot // 3 : slot // 3 + 1, at : at + ref.shape[1]]


def back_through(pieces, w_ref, side):
    total = None
    for i, piece in enumerate(pieces):
        part = lax.dot_general(
            piece[side, 0], w_ref[:, 384 * i : 384 * i + 384], NT, preferred_element_type=f32
        )
        total = part if total is None else total + part
    return total


def give_kernel(*refs):
    pieces, (w_ref, out_ref) = refs[:-2], refs[-2:]
    out_ref[0] = back_through(pieces, w_ref, 0).astype(bf16)


def input_kernel(*refs):
    pieces, (w_ref, recv_ref, x_ref, gmid_ref, pack_ref, ginput_ref) = refs[:-6], refs[-6:]
    gnormed = back_through(pieces, w_ref, 0) + recv_ref[0].astype(f32)
    xhat, rstd = standardise(x_ref[0].astype(f32))
    ginput_ref[0] = gmid_ref[0].astype(f32) + norm_pull(gnormed, pack_ref[0:1, :], xhat, rstd)


def partner(value):
    return lax.ppermute(value, "seq", [(0, 1), (1, 0)])


def exchange(value, axis):
    return lax.all_to_all(value, axis, 0, 0, tiled=True)


def spread_line(value, lines):
    return exchange(jnp.broadcast_to(value[None], (lines,) + value.shape), "line")


def flip(value, axis):
    return lax.ppermute(value, axis, [(0, 1), (1, 0)])


def in_order(index, own, received):
    return jnp.where(index == 0, jnp.stack([own, received]), jnp.stack([received, own]))


def spread_first(one, two):
    return lax.optimization_barrier((flip(one, "x"), flip(two, "y")))


def spread_second(one, two, got_one, got_two):
    near_one = in_order(lax.axis_index("x"), one, got_one)
    near_two = in_order(lax.axis_index("y"), two, got_two)
    near_one, near_two = lax.optimization_barrier((near_one, near_two))
    return (near_one, flip(near_one, "y")), (near_two, flip(near_two, "x"))


def spread_plane(one, two):
    return spread_second(one, two, *spread_first(one, two))


def after(value, *others):
    return lax.optimization_barrier((value,) + others)[0]


def assemble_kernel(far_plane, spot_ref, *refs):
    pieces, targets, scratch, (in_sem, out_sem) = refs[:2], refs[-6:-4], refs[-4:-2], refs[-2:]
    up_ref, out_ref = targets
    side, y = spot_ref[0], spot_ref[1]
    width = out_ref.shape[-1]
    blocks = up_ref.shape[-1] // width
    loads = [pltpu.make_async_copy(pieces[i], scratch[i], in_sem.at[i]) for i in range(2)]
    for load in loads:
        load.start()
    stores = []

    def send(source, target):
        stores.append(pltpu.make_async_copy(source, target, out_sem.at[len(stores)]))
        stores[-1].start()

    row = 1 - y if far_plane else y
    for index in range(2):
        loads[index].wait()
        at_side = 1 - side if index else side
        held = scratch[index]
        for i in range(2):
            for block in range(blocks):
                lanes = slice(block * width, (block + 1) * width)
                send(held.at[i, :, block], up_ref.at[at_side, :, row, i, :, lanes])
            send(held.at[i, :, blocks], out_ref.at[at_side, :, row, i])
    for copy in stores:
        copy.wait()


def assemble(spot, far_plane, pieces, targets, shapes):
    anywhere = pl.BlockSpec(memory_space=pl.ANY)
    blocks = pieces[0].shape[2]
    return pl.pallas_call(
        functools.partial(assemble_kernel, far_plane),
        grid_spec=pltpu.PrefetchScalarGridSpec(
            num_scalar_prefetch=1,
            grid=(1,),
            in_specs=[anywhere] * (2 + len(targets)),
            out_specs=[anywhere] * 2,
            scratch_shapes=[pltpu.VMEM(p.shape, bf16) for p in pieces]
            + [pltpu.SemaphoreType.DMA((2,)), pltpu.SemaphoreType.DMA((4 * blocks,))],
        ),
        out_shape=shapes,
        input_output_aliases={3 + i: i for i in range(len(targets))},
        name="assemble",
        **kernel_params(1e6, 12e6),
    )(spot, *pieces, *targets)


def sum_plane(value, *waits):
    received = exchange(value, ("y", "x"))
    if waits:
        received = after(received, *waits)
    return jnp.sum(received.astype(f32), axis=0)


def send_line(value, lines):
    here = lax.axis_index("line")
    pieces = []
    for shift in range(1, lines):
        piece = lax.dynamic_index_in_dim(value, (here + shift) % lines, 0, keepdims=False).astype(bf16)
        pieces.append(lax.ppermute(piece, "line", [(i, (i + shift) % lines) for i in range(lines)]))
    return pieces


def sum_line(value, lines, *waits):
    total = lax.dynamic_index_in_dim(value, lax.axis_index("line"), 0, keepdims=False)
    pieces = send_line(value, lines)
    if waits:
        pieces = lax.optimization_barrier(tuple(pieces) + waits)[: len(pieces)]
    for piece in pieces:
        total = total + piece.astype(f32)
    return total


def masks(seg, pos):
    pad = seg == CLIPS - 1
    lane = jnp.arange(128, dtype=jnp.int32) % HEAD_DIM
    seg, pos, pad = seg[..., None], pos[..., None], pad[..., None]
    clip_lane = lane < CLIPS - 1
    digit = jnp.where(lane < 9, pos // 256, jnp.where(lane < 25, (pos // 16) % 16, pos % 16))
    digit_base = jnp.where(lane < 9, 5, jnp.where(lane < 25, 9, 25))
    digit_lane = (lane >= 5) & (lane < LANE_LOG)
    hit_clip = lane == seg
    hit_digit = lane - digit_base == digit
    log_lane = (lane >= LANE_LOG) & (lane < LANE_PAD)
    pad_lane = lane == LANE_PAD
    bad = (clip_lane & ~hit_clip) | (digit_lane & pad & ~hit_digit) | (pad_lane & ~pad)
    qx = jnp.where(bad, -BIG, 0.0).astype(bf16)
    on = (clip_lane & hit_clip) | (digit_lane & pad & hit_digit) | log_lane | (pad_lane & pad)
    kx = jnp.where(on, 1.0, 0.0).astype(bf16)
    return qx, kx


def block_flags(ident, rows_block, cols_block):
    count, length = ident.shape
    by_row = ident.reshape(count, length // rows_block, rows_block)
    by_col = ident.reshape(count, length // cols_block, cols_block)
    low_row, high_row = jnp.min(by_row, axis=2)[:, :, None], jnp.max(by_row, axis=2)[:, :, None]
    low_col, high_col = jnp.min(by_col, axis=2)[:, None, :], jnp.max(by_col, axis=2)[:, None, :]
    meets = (low_row <= high_col) & (low_col <= high_row)
    return meets.astype(jnp.int32).reshape(count, -1)


def pair_device(
    lines, planes,
    tokens, segment_ids, cotangent, ln1_gain, ln1_bias, qkv_weight, qv_bias, out_weight, out_bias,
    ln2_gain, ln2_bias, up_weight, up_bias, down_weight, down_bias, avg_qkv, avg_out, avg_up, avg_down,
):
    count, part, width = tokens.shape
    length = 2 * part
    wide = width // 2
    heads = HEADS // 2
    hidden_width = up_weight.shape[1]
    chunks = hidden_width // width
    share = qkv_weight.shape[0]
    side = lax.axis_index("seq").astype(jnp.int32)
    first = side == 0
    side_arr = side.reshape(1)
    const = lambda *shape: pl.BlockSpec(shape, lambda *_: (0,) * len(shape), pipeline_mode=pl.Buffered(1))
    row_block = lambda *shape: pl.BlockSpec((1,) + shape, lambda j, *_: (j,) + (0,) * len(shape))
    both_block = lambda lanes: pl.BlockSpec((2, 1, part, lanes), lambda j, *_: (0, j, 0, 0))
    own_block = lambda lanes: pl.BlockSpec((1, 1, part, lanes), lambda j, *_: (0, j, 0, 0))

    pairs = heads // 2
    sds = jax.ShapeDtypeStruct
    small_vectors = [ln1_gain, ln1_bias, out_bias, ln2_gain, ln2_bias, down_bias, qv_bias, up_bias]
    mine, give, second = pl.pallas_call(
        functools.partial(prepare_kernel, share),
        grid_spec=pltpu.PrefetchScalarGridSpec(
            num_scalar_prefetch=1,
            grid=(1,),
            in_specs=[
                pl.BlockSpec((share, 6 * wide), lambda *_: (0, 0)),
                pl.BlockSpec((share, hidden_width), lambda *_: (0, 0)),
                pl.BlockSpec((share, width), lambda *_: (0, 0)),
                pl.BlockSpec((chunks * share, width), lambda *_: (0, 0)),
            ]
            + [pl.BlockSpec((1, v.shape[0]), lambda *_: (0, 0)) for v in small_vectors],
            out_specs=[pl.BlockSpec((share, 3 * wide + 128), lambda *_: (0, 0))] * 2
            + [pl.BlockSpec(((2 * chunks + 1) * share, width), lambda *_: (0, 0))],
        ),
        out_shape=[sds((share, 3 * wide + 128), bf16)] * 2 + [sds(((2 * chunks + 1) * share, width), bf16)],
        name="prepare",
        **kernel_params(1e6, 1e6),
    )(side_arr, qkv_weight, up_weight, out_weight, down_weight, *[v[None] for v in small_vectors])
    take = partner(give)
    tokens_other = partner(tokens)
    seg_other = partner(segment_ids)
    seg = jnp.concatenate([segment_ids, seg_other], axis=1)
    spots = jnp.arange(part, dtype=jnp.int32)
    pos = jnp.concatenate([side * part + spots, (1 - side) * part + spots])
    qx, kx = masks(seg, jnp.broadcast_to(pos, seg.shape))
    ident = jnp.where(seg == CLIPS - 1, CLIPS + pos, seg)
    flags_f = block_flags(ident, TQ_F, TK_F)
    flags_b = block_flags(ident, TK_B, TQ_B)

    start = jnp.where(first, jnp.stack([mine, take]), jnp.stack([take, mine]))
    x_at, y_at = lax.axis_index("x"), lax.axis_index("y")
    first_line = after(spread_line(start, lines), qx, kx, flags_f, flags_b)
    (one_m, one_r), (two_m, two_r) = spread_plane(first_line[:, 0], first_line[:, 1])
    one = in_order(y_at, one_m, one_r).transpose(2, 0, 1, 3, 4)
    two = in_order(x_at, two_m, two_r).transpose(2, 1, 0, 3, 4)
    w_first = jnp.stack([one, two]).reshape(width, 3 * wide + 128)

    own_rows = chunks * share
    second = after(second, first_line)
    up_rows = own_rows + share
    second_line = spread_line(second, lines)

    small_at = 3 * wide // 128
    normed, mixed, pack = pl.pallas_call(
        functools.partial(project_kernel, share),
        grid_spec=pltpu.PrefetchScalarGridSpec(
            num_scalar_prefetch=1,
            grid=(2, count),
            in_specs=[
                pl.BlockSpec((1, part, width), lambda h, j, *_: (jnp.where(h == 0, j, count - 1), 0, 0)),
                pl.BlockSpec((1, part, width), lambda h, j, *_: (jnp.where(h == 0, 0, j), 0, 0)),
                const(width, 3 * wide),
                pl.BlockSpec((width, 128), lambda *_: (0, small_at), pipeline_mode=pl.Buffered(1)),
            ],
            out_specs=[
                pl.BlockSpec((1, 1, part, width), lambda h, j, *_: (h, j, 0, 0)),
                pl.BlockSpec((pairs, 1, 1, part, 384), lambda h, j, *_: (0, h, j, 0, 0)),
                pl.BlockSpec((16, width), lambda *_: (0, 0)),
            ],
            scratch_shapes=[pltpu.VMEM((1, 3 * wide), f32)],
        ),
        out_shape=[
            sds((2, count, part, width), bf16),
            sds((pairs, 2, count, part, 384), bf16),
            sds((16, width), f32),
        ],
        name="project",
        **kernel_params(
            2 * 2 * count * part * width * 3 * wide, 20e6, order=("arbitrary", "arbitrary")
        ),
    )(side_arr, tokens, tokens_other, w_first, w_first)
    up_bias_all = pack[8 : 8 + chunks].reshape(chunks, -1, share).transpose(1, 0, 2).reshape(chunks, width)

    second_line = after(second_line, one_r, two_r, pack)
    halves = (second_line[:, :up_rows].reshape(lines, chunks + 1, share, width), second_line[:, up_rows:])
    halves_got = spread_first(*halves)
    same, row_mixed = (), mixed
    for base, rows_now in ((0, 1), (1, count - 1)):
        if base == 1:
            halves_got = lax.optimization_barrier(halves_got + (same[0],))[:2]
            up_pair, down_pair = spread_second(*halves, *halves_got)
            row_mixed = after(mixed, up_pair[0], down_pair[0])
        row_both = lambda lanes, base=base: pl.BlockSpec(
            (pairs, 2, 1, part, lanes), lambda j, *_: (0, 0, base + j, 0, 0)
        )
        row_one = pl.BlockSpec((pairs, 1, part, 128), lambda j, *_, base=base: (0, base + j, 0, 0))
        row_flat = pl.BlockSpec((1, length, 128), lambda j, *_, base=base: (base + j, 0, 0))
        same = pl.pallas_call(
            functools.partial(attend_kernel, base),
            grid_spec=pltpu.PrefetchScalarGridSpec(
                num_scalar_prefetch=1,
                grid=(rows_now,),
                in_specs=[row_both(384), row_flat, row_flat] + [pl.BlockSpec(memory_space=pl.ANY)] * len(same),
                out_specs=[row_one, row_one, row_both(128)],
                scratch_shapes=[pltpu.VMEM((heads, length, 128), bf16)] * 3
                + [pltpu.VMEM((heads, length, 128), f32)],
            ),
            out_shape=[sds((pairs, count, part, 128), bf16)] * 2 + [sds((pairs, 2, count, part, 128), bf16)],
            input_output_aliases={4 + i: i for i in range(len(same))},
            name="attend",
            **kernel_params(8e9, 7e6, 4e6),
        )(flags_f, row_mixed, qx, kx, *same)
    att_own, att_other, ext = same
    spot = jnp.stack([side, y_at.astype(jnp.int32), x_at.astype(jnp.int32)])
    near = [up_pair[0], down_pair[0]]
    near += [partner(piece) for piece in near]
    far = list(lax.optimization_barrier((up_pair[1], down_pair[1], att_own))[:2])
    near = list(lax.optimization_barrier(tuple(near) + tuple(far))[:4])
    far += [partner(piece) for piece in far]
    shapes = [
        sds((2, lines, 2, 2, share, hidden_width), bf16),
        sds((2, lines, 2, 2, share, width), bf16),
    ]
    targets = assemble(spot, False, near[::2], (), shapes)
    w_up, w_out = assemble(spot, True, far[::2], targets, shapes)
    w_up = w_up.reshape(width, hidden_width)
    down_pieces = [near[1], far[1], near[3], far[3]]
    w_out = w_out.reshape(2, wide, width)
    w_out_flat = w_out.reshape(2 * wide, width)

    att_recv = partner(att_other)

    head_block = pl.BlockSpec((pairs, 1, part, 128), lambda j, *_: (0, j, 0, 0))
    out_tokens, glow, gdown_own, gdown_other, gup_own, gup_other, gup_bias, gvec = pl.pallas_call(
        functools.partial(mlp_kernel, planes, share),
        grid_spec=pltpu.PrefetchScalarGridSpec(
            num_scalar_prefetch=1,
            grid=(count,),
            in_specs=[
                row_block(part, width),
                head_block,
                head_block,
            ]
            + [pl.BlockSpec(memory_space=pl.ANY)] * 6
            + [
                row_block(part, width),
                const(16, width),
                const(chunks, width),
            ],
            out_specs=[row_block(part, width)] * 2
            + [pl.BlockSpec(memory_space=pl.ANY)] * 4
            + [const(chunks, 1, width), const(8, width)],
            scratch_shapes=[pltpu.VMEM((chunks, width, width), f32)] * 2
            + [
                pltpu.VMEM((2, wide, width), bf16),
                pltpu.VMEM((width, hidden_width), bf16),
                pltpu.VMEM((2, lines, 2, 2, own_rows, width), bf16),
            ]
            + [pltpu.VMEM((planes, lines, own_rows, width), bf16)] * 2
            + [pltpu.VMEM((planes, lines, chunks, share, width), bf16)] * 2
            + [pltpu.SemaphoreType.DMA((10,)), pltpu.SemaphoreType.DMA((3 * chunks,))],
        ),
        out_shape=[
            sds((count, part, width), bf16),
            sds((count, part, width), bf16),
        ]
        + [sds((planes, lines, own_rows, width), bf16)] * 2
        + [sds((planes, lines, chunks, share, width), bf16)] * 2
        + [sds((chunks, 1, width), f32), sds((8, width), f32)],
        name="mlp",
        **kernel_params(2 * count * part * width * (width + 6 * hidden_width), 36e6, 4.7e6),
    )(spot, tokens, att_own, att_recv, w_out, w_up, *down_pieces, cotangent, pack, up_bias_all)

    glow_other = partner(glow)
    avg_qkv, avg_out, avg_up, avg_down, _ = lax.optimization_barrier((avg_qkv, avg_out, avg_up, avg_down, glow))
    new_qkv = 0.9 * avg_qkv + 0.1 * qkv_weight.astype(f32)
    new_out = 0.9 * avg_out + 0.1 * out_weight.astype(f32)
    new_up = 0.9 * avg_up + 0.1 * up_weight.astype(f32)
    new_down = 0.9 * avg_down + 0.1 * down_weight.astype(f32)
    add = lambda one, two: (one.astype(f32) + two.astype(f32)).astype(bf16)
    gdown_plane = sum_plane(add(gdown_own, partner(gdown_other)))
    gup_sum = add(gup_own, partner(gup_other))

    gmixed, gmixed_bias = [], []
    ties = ()
    for pair in range(pairs):
        lane_block = lambda lanes, pair=pair: pl.BlockSpec((1, 2, 1, part, lanes), lambda j, *_: (pair, 0, j, 0, 0))
        att_block = pl.BlockSpec((1, 1, part, 128), lambda j, *_, pair=pair: (pair, j, 0, 0))
        piece, piece_bias = pl.pallas_call(
            attend_back_kernel,
            grid_spec=pltpu.PrefetchScalarGridSpec(
                num_scalar_prefetch=2,
                grid=(count,),
                in_specs=[
                    lane_block(384),
                    lane_block(128),
                    att_block,
                    att_block,
                    row_block(part, width),
                    row_block(part, width),
                    pl.BlockSpec((128, width), lambda j, flags, where, pair=pair: (where[0] * pairs + pair, 0)),
                    row_block(length, 128),
                ],
                out_specs=[both_block(384), const(8, 384)],
                scratch_shapes=[pltpu.VMEM((length // TQ_B, 2 * TQ_B, 256), bf16)] * 2
                + [pltpu.VMEM((length, 256), bf16)] * 2
                + [
                    pltpu.VMEM((length // TK_B, 128, TK_B), bf16),
                    pltpu.VMEM((length // TQ_B, 128, TQ_B), f32),
                    pltpu.VMEM((length, 128), f32),
                    pltpu.VMEM((length, 128), f32),
                ],
            ),
            out_shape=[sds((2, count, part, 384), bf16), sds((8, 384), f32)],
            name="attend_back",
            **kernel_params(25e9, 20e6, 4e6),
        )(flags_b, side_arr, after(mixed, *ties), ext, att_own, att_other, glow, glow_other, w_out_flat, kx)
        gmixed.append(piece)
        gmixed_bias.append(piece_bias)
        if pair == 0:
            gup_plane = sum_plane(after(gup_sum, gdown_plane))
            grad_down = sum_line(gdown_plane, lines)
            ties = (gdown_plane,)
        if pair == 1:
            early, inner_sum, plain_sum = pl.pallas_call(
                functools.partial(early_kernel, planes, share),
                grid=(count,),
                in_specs=[both_block(width), both_block(384), both_block(384), const(8, 384), const(8, 384)]
                + [head_block, head_block, row_block(part, width), row_block(part, width), const(width, 768)],
                out_specs=[const(planes, lines, 6, share, 384), const(width, 128), const(width, 128)],
                out_shape=[
                    sds((planes, lines, 6, share, 384), bf16),
                    sds((width, 128), f32),
                    sds((width, 128), f32),
                ],
                scratch_shapes=[pltpu.VMEM((width, 768), f32), pltpu.VMEM((wide, width), f32)],
                name="early",
                **kernel_params(9e9, 25e6),
            )(normed, *gmixed, *gmixed_bias, att_own, att_other, glow, glow_other, w_first)
            early_plane = sum_plane(after(early, gup_plane))
            gup_line = sum_line(gup_plane, lines)
            ties = (gup_plane, grad_down, early)
    grad_up = gup_line.transpose(1, 0, 2).reshape(share, hidden_width)

    late = pl.pallas_call(
        functools.partial(late_kernel, planes, share),
        grid_spec=pltpu.PrefetchScalarGridSpec(
            num_scalar_prefetch=1,
            grid=(count,),
            in_specs=[
                both_block(width),
                both_block(384),
                pl.BlockSpec((width, 384), lambda *_: (0, 2), pipeline_mode=pl.Buffered(1)),
                const(width, 128),
                const(width, 128),
                const(8, 384),
                const(8, 384),
                const(8, 384),
                const(16, width),
                const(8, width),
                const(chunks, 1, width),
            ],
            out_specs=const(planes, lines, 3, share, 384),
            scratch_shapes=[pltpu.VMEM((width, 384), f32)],
        ),
        out_shape=sds((planes, lines, 3, share, 384), bf16),
        name="late",
        **kernel_params(4e9, 10e6),
    )(side_arr, normed, after(gmixed[2], early_plane, gup_line), w_first, inner_sum, plain_sum, *gmixed_bias, pack, gvec, gup_bias)

    piece_spec = lambda side: pl.BlockSpec((1, 1, part, 384), lambda j, *_: (side, j, 0, 0))
    give_back = pl.pallas_call(
        give_kernel,
        grid=(count,),
        in_specs=[piece_spec(1)] * pairs + [const(width, 3 * wide)],
        out_specs=row_block(part, width),
        out_shape=sds((count, part, width), bf16),
        name="give_back",
        **kernel_params(2 * count * part * width * 3 * wide, 12e6),
    )(*gmixed[:2], after(gmixed[2], late), w_first)
    recv_back = partner(give_back)

    grad_input = pl.pallas_call(
        input_kernel,
        grid=(count,),
        in_specs=[piece_spec(0)] * pairs
        + [
            const(width, 3 * wide),
            row_block(part, width),
            row_block(part, width),
            row_block(part, width),
            const(16, width),
        ],
        out_specs=row_block(part, width),
        out_shape=sds((count, part, width), f32),
        name="input_grad",
        **kernel_params(2 * count * part * width * 3 * wide, 25e6),
    )(*gmixed, w_first, recv_back, tokens, glow, pack)

    late_plane = sum_plane(late, grad_input)
    unit_line = sum_line(jnp.concatenate([early_plane, late_plane], axis=1), lines)
    theirs = lax.dynamic_slice_in_dim(unit_line, 2 * (1 - side), 2, 0)
    theirs_late = lax.dynamic_slice_in_dim(unit_line, 7 - side, 1, 0)
    got = partner(jnp.concatenate([theirs, theirs_late, unit_line[8:]], axis=0))
    sizes = [share] * 6 + [2 * share, chunks * share]
    grad_qkv, grad_out, *vecs = pl.pallas_call(
        finish_kernel,
        grid_spec=pltpu.PrefetchScalarGridSpec(
            num_scalar_prefetch=1,
            grid=(1,),
            in_specs=[
                pl.BlockSpec((9, share, 384), lambda *_: (0, 0, 0)),
                pl.BlockSpec((4, share, 384), lambda *_: (0, 0, 0)),
            ],
            out_specs=[
                pl.BlockSpec((share, 6 * wide), lambda *_: (0, 0)),
                pl.BlockSpec((share, width), lambda *_: (0, 0)),
            ]
            + [pl.BlockSpec((1, size), lambda *_: (0, 0)) for size in sizes],
        ),
        out_shape=[sds((share, 6 * wide), f32), sds((share, width), f32)] + [sds((1, size), f32) for size in sizes],
        name="finish",
        **kernel_params(1e6, 1e6),
    )(side_arr, unit_line, got)
    vec = lambda slot, size: vecs[slot].reshape(size)

    return (
        out_tokens,
        grad_input,
        vec(0, share),
        vec(1, share),
        grad_qkv,
        vec(6, 2 * share),
        grad_out,
        vec(2, share),
        vec(3, share),
        vec(4, share),
        grad_up,
        vec(7, chunks * share),
        grad_down,
        vec(5, share),
        new_qkv,
        new_out,
        new_up,
        new_down,
    )


def specs_for(rows):
    flat = ("seq",) + (rows if isinstance(rows, tuple) else (rows,))
    grid, ids, vec, mat = P(rows, "seq", None), P(rows, "seq"), P(flat), P(flat, None)
    ins = (grid, ids, grid, vec, vec, mat, vec, mat, vec, vec, vec, mat, vec, mat, vec, mat, mat, mat, mat)
    outs = (grid, grid, vec, vec, mat, vec, mat, vec, vec, vec, mat, vec, mat, vec, mat, mat, mat, mat)
    return ins, outs


def solution(mesh):
    parts, rows = mesh.shape["seq"], mesh.shape["rows"]
    planes = 4
    if parts != 2 or rows % planes:
        ins, outs = specs_for("rows")
        return jax.shard_map(on_device, mesh=mesh, in_specs=ins, out_specs=outs, check_vma=False)
    lines = rows // planes
    finer = Mesh(mesh.devices.reshape(parts, lines, 2, 2), ("seq", "line", "y", "x"))
    ins, outs = specs_for(("line", "y", "x"))
    return jax.shard_map(
        functools.partial(pair_device, lines, planes), mesh=finer, in_specs=ins, out_specs=outs, check_vma=False
    )
```

```python
import functools

import jax
import jax.numpy as jnp
from jax import lax
from jax.experimental import pallas as pl
from jax.experimental.pallas import tpu as pltpu
from jax.sharding import Mesh
from jax.sharding import PartitionSpec as P

HEADS = 12
HEAD_DIM = 64
CLIPS = 6


def layer_norm(value, gain, bias):
    middle = jnp.mean(value, axis=-1, keepdims=True)
    centred = value - middle
    spread = jnp.mean(centred * centred, axis=-1, keepdims=True)
    return centred * lax.rsqrt(spread + 1e-06) * gain + bias


def exact_gelu(value):
    return jax.nn.gelu(value, approximate=False)


def permitted(seg_query, seg_key, pos_query, pos_key):
    same_clip = seg_query[:, :, None] == seg_key[:, None, :]
    open_key = (seg_key != CLIPS - 1)[:, None, :]
    diagonal = (pos_query[:, None] == pos_key[None, :])[None]
    return (same_clip & (open_key | diagonal))[:, :, None, :]


def scores(query_part, key_part):
    return 0.125 * jnp.einsum(
        "rqhe,rkhe->rqhk", query_part, key_part, preferred_element_type=jnp.float32
    )


def exponent(score_vals, allowed):
    return jnp.where(allowed, jnp.exp(jnp.where(allowed, score_vals, 0.0)), 0.0)


def on_device(
    tokens,
    segment_ids,
    cotangent,
    ln1_gain,
    ln1_bias,
    qkv_weight,
    qv_bias,
    out_weight,
    out_bias,
    ln2_gain,
    ln2_bias,
    up_weight,
    up_bias,
    down_weight,
    down_bias,
    avg_qkv,
    avg_out,
    avg_up,
    avg_down,
):
    f32 = jnp.float32
    bf16 = jnp.bfloat16
    rows_here, shard_len, width = tokens.shape
    count_rows = rows_here * shard_len
    own_pos = lax.axis_index("seq") * shard_len + jnp.arange(shard_len, dtype=jnp.int32)
    head_shape = (rows_here, shard_len, HEADS, HEAD_DIM)
    gain_one, bias_one, w_qkv, b_qv, w_out, b_out = (
        lax.all_gather(ln1_gain, ("seq", "rows"), axis=0, tiled=True),
        lax.all_gather(ln1_bias, ("seq", "rows"), axis=0, tiled=True),
        lax.all_gather(qkv_weight, ("seq", "rows"), axis=0, tiled=True),
        lax.all_gather(qv_bias, ("seq", "rows"), axis=0, tiled=True),
        lax.all_gather(out_weight, ("seq", "rows"), axis=0, tiled=True),
        lax.all_gather(out_bias, ("seq", "rows"), axis=0, tiled=True),
    )
    residual = tokens.astype(f32).reshape(count_rows, width)
    normed, norm_one_pull = jax.vjp(
        layer_norm, residual, gain_one.astype(f32), bias_one.astype(f32)
    )
    normed_low = normed.astype(bf16)
    mixed = jnp.dot(normed_low, w_qkv, preferred_element_type=f32)
    bias_qv = b_qv.astype(f32)
    query_heads = (mixed[:, :width] + bias_qv[:width]).astype(bf16).reshape(head_shape)
    key_heads = mixed[:, width : 2 * width].astype(bf16).reshape(head_shape)
    value_heads = (mixed[:, 2 * width :] + bias_qv[width:]).astype(bf16).reshape(head_shape)
    start_state = (jnp.zeros((rows_here, shard_len, HEADS), f32), jnp.zeros(head_shape, f32))
    piece_keys = lax.all_gather(key_heads, "seq", axis=1, tiled=True)
    piece_values = lax.all_gather(value_heads, "seq", axis=1, tiled=True)
    piece_seg = lax.all_gather(segment_ids, "seq", axis=1, tiled=True)
    piece_len = piece_keys.shape[1]
    block_len = min(piece_len, shard_len)

    def forward_advance(turn, state):
        totals, weighted = state
        offset = turn * block_len
        key_block = lax.dynamic_slice_in_dim(piece_keys, offset, block_len, 1)
        value_block = lax.dynamic_slice_in_dim(piece_values, offset, block_len, 1)
        seg_block = lax.dynamic_slice_in_dim(piece_seg, offset, block_len, 1)
        key_pos = offset + jnp.arange(block_len, dtype=jnp.int32)
        allowed = permitted(segment_ids, seg_block, own_pos, key_pos)
        expo = exponent(scores(query_heads, key_block), allowed)
        totals = totals + jnp.sum(expo, axis=-1)
        weighted = weighted + jnp.einsum(
            "rqhk,rkhe->rqhe", expo.astype(bf16), value_block, preferred_element_type=f32
        )
        return (totals, weighted)

    totals, weighted = lax.fori_loop(0, piece_len // block_len, forward_advance, start_state)
    attended = weighted / totals[..., None]
    attn_in = attended.reshape(count_rows, width).astype(bf16)
    middle = residual + jnp.dot(attn_in, w_out, preferred_element_type=f32) + b_out.astype(f32)
    gain_two, bias_two, w_up, b_up, w_down, b_down = (
        lax.all_gather(ln2_gain, ("seq", "rows"), axis=0, tiled=True),
        lax.all_gather(ln2_bias, ("seq", "rows"), axis=0, tiled=True),
        lax.all_gather(up_weight, ("seq", "rows"), axis=0, tiled=True),
        lax.all_gather(up_bias, ("seq", "rows"), axis=0, tiled=True),
        lax.all_gather(down_weight, ("seq", "rows"), axis=0, tiled=True),
        lax.all_gather(down_bias, ("seq", "rows"), axis=0, tiled=True),
    )
    normed_two, norm_two_pull = jax.vjp(
        layer_norm, middle, gain_two.astype(f32), bias_two.astype(f32)
    )
    normed_two_low = normed_two.astype(bf16)
    hidden_pre = jnp.dot(normed_two_low, w_up, preferred_element_type=f32) + b_up.astype(f32)
    hidden, gelu_pull = jax.vjp(exact_gelu, hidden_pre)
    hidden_low = hidden.astype(bf16)
    final = middle + jnp.dot(hidden_low, w_down, preferred_element_type=f32) + b_down.astype(f32)
    out_tokens = final.astype(bf16).reshape(tokens.shape)
    w_up_back, w_down_back = (
        lax.all_gather(up_weight, ("seq", "rows"), axis=0, tiled=True),
        lax.all_gather(down_weight, ("seq", "rows"), axis=0, tiled=True),
    )
    grad_out = cotangent.astype(f32).reshape(count_rows, width)
    grad_low = grad_out.astype(bf16)
    grad_down = jnp.einsum("nf,nd->fd", hidden_low, grad_low, preferred_element_type=f32)
    grad_down_b = jnp.sum(grad_low, axis=0, dtype=f32)
    grad_hidden = jnp.einsum("nd,fd->nf", grad_low, w_down_back, preferred_element_type=f32)
    (grad_pre,) = gelu_pull(grad_hidden)
    grad_pre_low = grad_pre.astype(bf16)
    grad_up = jnp.einsum("nd,nf->df", normed_two_low, grad_pre_low, preferred_element_type=f32)
    grad_up_b = jnp.sum(grad_pre_low, axis=0, dtype=f32)
    grad_normed_two = jnp.einsum("nf,df->nd", grad_pre_low, w_up_back, preferred_element_type=f32)
    grad_mid_norm, grad_gain_two, grad_bias_two = norm_two_pull(grad_normed_two)
    grad_mid = grad_out + grad_mid_norm
    mlp_sums = (
        lax.psum_scatter(grad_gain_two, ("seq", "rows"), scatter_dimension=0, tiled=True),
        lax.psum_scatter(grad_bias_two, ("seq", "rows"), scatter_dimension=0, tiled=True),
        lax.psum_scatter(grad_up, ("seq", "rows"), scatter_dimension=0, tiled=True),
        lax.psum_scatter(grad_up_b, ("seq", "rows"), scatter_dimension=0, tiled=True),
        lax.psum_scatter(grad_down, ("seq", "rows"), scatter_dimension=0, tiled=True),
        lax.psum_scatter(grad_down_b, ("seq", "rows"), scatter_dimension=0, tiled=True),
    )
    w_qkv_back, w_out_back = (
        lax.all_gather(qkv_weight, ("seq", "rows"), axis=0, tiled=True),
        lax.all_gather(out_weight, ("seq", "rows"), axis=0, tiled=True),
    )
    grad_mid_low = grad_mid.astype(bf16)
    grad_wout = jnp.einsum("nd,ne->de", attn_in, grad_mid_low, preferred_element_type=f32)
    grad_bout = jnp.sum(grad_mid_low, axis=0, dtype=f32)
    grad_att = jnp.einsum(
        "ne,de->nd", grad_mid_low, w_out_back, preferred_element_type=f32
    ).reshape(head_shape)
    grad_acc = (grad_att / totals[..., None]).astype(bf16)
    shift_low = (jnp.sum(grad_att * attended, axis=-1) / totals).astype(bf16)
    shift_wide = shift_low.astype(f32)
    query_piece_keys = lax.all_gather(key_heads, "seq", axis=1, tiled=True)
    query_piece_values = lax.all_gather(value_heads, "seq", axis=1, tiled=True)
    query_piece_seg = lax.all_gather(segment_ids, "seq", axis=1, tiled=True)
    piece_len = query_piece_keys.shape[1]
    query_block_len = min(piece_len, shard_len)

    def query_advance(turn, grad_query):
        offset = turn * query_block_len
        key_block = lax.dynamic_slice_in_dim(query_piece_keys, offset, query_block_len, 1)
        value_block = lax.dynamic_slice_in_dim(query_piece_values, offset, query_block_len, 1)
        seg_block = lax.dynamic_slice_in_dim(query_piece_seg, offset, query_block_len, 1)
        key_pos = offset + jnp.arange(query_block_len, dtype=jnp.int32)
        allowed = permitted(segment_ids, seg_block, own_pos, key_pos)
        expo = exponent(scores(query_heads, key_block), allowed)
        inner = jnp.einsum("rqhe,rkhe->rqhk", grad_acc, value_block, preferred_element_type=f32)
        grad_score = (expo * (inner - shift_wide[..., None])).astype(bf16)
        return grad_query + jnp.einsum(
            "rqhk,rkhe->rqhe", grad_score, key_block, preferred_element_type=f32
        )

    grad_query = lax.fori_loop(
        0, piece_len // query_block_len, query_advance, jnp.zeros(head_shape, f32)
    )
    key_start = (jnp.zeros(head_shape, f32), jnp.zeros(head_shape, f32))
    piece_queries = lax.all_gather(query_heads, "seq", axis=1, tiled=True)
    piece_grads = lax.all_gather(grad_acc, "seq", axis=1, tiled=True)
    key_piece_seg = lax.all_gather(segment_ids, "seq", axis=1, tiled=True)
    piece_shift = lax.all_gather(shift_low, "seq", axis=1, tiled=True)
    piece_len = piece_queries.shape[1]
    key_block_len = min(piece_len, shard_len)

    def key_advance(turn, state):
        grad_key, grad_value = state
        offset = turn * key_block_len
        query_block = lax.dynamic_slice_in_dim(piece_queries, offset, key_block_len, 1)
        grad_block = lax.dynamic_slice_in_dim(piece_grads, offset, key_block_len, 1)
        seg_block = lax.dynamic_slice_in_dim(key_piece_seg, offset, key_block_len, 1)
        shift_block = lax.dynamic_slice_in_dim(piece_shift, offset, key_block_len, 1).astype(f32)
        query_pos = offset + jnp.arange(key_block_len, dtype=jnp.int32)
        allowed = permitted(seg_block, segment_ids, query_pos, own_pos)
        expo = exponent(scores(query_block, key_heads), allowed)
        inner = jnp.einsum("rqhe,rkhe->rqhk", grad_block, value_heads, preferred_element_type=f32)
        grad_score = (expo * (inner - shift_block[..., None])).astype(bf16)
        grad_key = grad_key + jnp.einsum(
            "rqhk,rqhe->rkhe", grad_score, query_block, preferred_element_type=f32
        )
        grad_value = grad_value + jnp.einsum(
            "rqhk,rqhe->rkhe", expo.astype(bf16), grad_block, preferred_element_type=f32
        )
        return (grad_key, grad_value)

    grad_key, grad_value = lax.fori_loop(0, piece_len // key_block_len, key_advance, key_start)
    grad_q_low = (0.125 * grad_query).astype(bf16).reshape(count_rows, width)
    grad_k_low = (0.125 * grad_key).astype(bf16).reshape(count_rows, width)
    grad_v_low = grad_value.astype(bf16).reshape(count_rows, width)
    grad_mixed = jnp.concatenate([grad_q_low, grad_k_low, grad_v_low], axis=1)
    grad_wqkv = jnp.einsum("nd,ne->de", normed_low, grad_mixed, preferred_element_type=f32)
    grad_bqv = jnp.concatenate(
        [jnp.sum(grad_q_low, axis=0, dtype=f32), jnp.sum(grad_v_low, axis=0, dtype=f32)], axis=0
    )
    grad_normed = jnp.einsum("ne,de->nd", grad_mixed, w_qkv_back, preferred_element_type=f32)
    grad_res_norm, grad_gain_one, grad_bias_one = norm_one_pull(grad_normed)
    grad_input = (grad_mid + grad_res_norm).reshape(tokens.shape)
    attn_sums = (
        lax.psum_scatter(grad_gain_one, ("seq", "rows"), scatter_dimension=0, tiled=True),
        lax.psum_scatter(grad_bias_one, ("seq", "rows"), scatter_dimension=0, tiled=True),
        lax.psum_scatter(grad_wqkv, ("seq", "rows"), scatter_dimension=0, tiled=True),
        lax.psum_scatter(grad_bqv, ("seq", "rows"), scatter_dimension=0, tiled=True),
        lax.psum_scatter(grad_wout, ("seq", "rows"), scatter_dimension=0, tiled=True),
        lax.psum_scatter(grad_bout, ("seq", "rows"), scatter_dimension=0, tiled=True),
    )
    new_qkv = 0.9 * avg_qkv + 0.1 * qkv_weight.astype(f32)
    new_out = 0.9 * avg_out + 0.1 * out_weight.astype(f32)
    new_up = 0.9 * avg_up + 0.1 * up_weight.astype(f32)
    new_down = 0.9 * avg_down + 0.1 * down_weight.astype(f32)
    return (
        out_tokens,
        grad_input,
        attn_sums[0],
        attn_sums[1],
        attn_sums[2],
        attn_sums[3],
        attn_sums[4],
        attn_sums[5],
        mlp_sums[0],
        mlp_sums[1],
        mlp_sums[2],
        mlp_sums[3],
        mlp_sums[4],
        mlp_sums[5],
        new_qkv,
        new_out,
        new_up,
        new_down,
    )


f32 = jnp.float32
bf16 = jnp.bfloat16
NT = (((1,), (1,)), ((), ()))
LOG2E = 1.4426950408889634
SCORE = 0.125 * LOG2E
BIG = 16384.0
VMEM_BYTES = 63 * 1024 * 1024
TQ_F, TK_F = 512, 256
TK_B, TQ_B, T_SIDE = 512, 512, 256
LANE_LOG = 41
LANE_PAD = 44


def kernel_params(flops, bytes_accessed, transcendentals=0, order=("arbitrary",)):
    return dict(
        compiler_params=pltpu.CompilerParams(
            vmem_limit_bytes=VMEM_BYTES, dimension_semantics=order
        ),
        cost_estimate=pl.CostEstimate(
            flops=int(flops), bytes_accessed=int(bytes_accessed), transcendentals=int(transcendentals)
        ),
    )


def standardise(value):
    middle = jnp.mean(value, axis=-1, keepdims=True)
    centred = value - middle
    spread = jnp.mean(centred * centred, axis=-1, keepdims=True)
    rstd = lax.rsqrt(spread + 1e-06)
    return centred * rstd, rstd


def norm_pull(grad_normed, gain, xhat, rstd):
    scaled = grad_normed * gain
    first = jnp.mean(scaled, axis=-1, keepdims=True)
    second = jnp.mean(scaled * xhat, axis=-1, keepdims=True)
    return rstd * (scaled - first - xhat * second)


def gelu_pair(x):
    size = jnp.abs(x)
    base = 1.0 + 0.23164189 * size
    t = 1.0 / base
    bell = jnp.exp2(x * x * (-0.5 * LOG2E))
    poly = t * (0.127414796 + t * (-0.142248368 + t * (0.7107068705 + t * (-0.7265760135 + t * 0.5307027145))))
    tail = poly * bell
    phi = jnp.where(x >= 0.0, 1.0 - tail, tail)
    return x * phi, phi + x * bell * 0.3989422804014327


def lane_masks():
    lane = lax.broadcasted_iota(jnp.int32, (1, 128), 1)
    low = jnp.where(lane < HEAD_DIM, 1.0, 0.0)
    return low.astype(bf16), (1.0 - low).astype(bf16)


def prepare_kernel(share, side_ref, w_ref, up_ref, out_ref, down_ref, *refs):
    vectors, (mine_ref, give_ref, second_ref) = refs[:-3], refs[-3:]
    width = down_ref.shape[1]
    blocks = up_ref.shape[1] // width
    for block in range(blocks):
        second_ref[block * share : (block + 1) * share] = up_ref[:, block * width : (block + 1) * width]
    second_ref[blocks * share : (blocks + 1) * share] = out_ref[...]
    second_ref[(blocks + 1) * share :] = down_ref[...]
    wide = w_ref.shape[1] // 6
    pairs = wide // 128
    for target, side in ((mine_ref, side_ref[0]), (give_ref, 1 - side_ref[0])):
        for pair in range(pairs):
            for kind in range(3):
                start = pl.multiple_of(kind * 2 * wide + side * wide + pair * 128, 128)
                at = 384 * pair + 128 * kind
                target[:, at : at + 128] = w_ref[:, pl.ds(start, 128)]
    lane = lax.broadcasted_iota(jnp.int32, (share, 128), 1)
    small = jnp.zeros((share, 128), f32)
    column = 0
    for ref in vectors:
        row = jnp.broadcast_to(ref[...].astype(f32), (8, ref.shape[1])).T
        for start in range(0, ref.shape[1], share):
            small = jnp.where(lane == column, row[start : start + share, 0:1], small)
            column += 1
    small = small.astype(bf16)
    mine_ref[:, 3 * wide :] = small
    give_ref[:, 3 * wide :] = small


def project_kernel(
    share, side_ref, own_ref, other_ref, w_ref, small_ref, normed_ref, mixed_ref, pack_ref, shift_s
):
    which, turn = pl.program_id(0), pl.program_id(1)
    wide = shift_s.shape[1] // 3
    pairs = wide // 128

    @pl.when((which == 0) & (turn == 0))
    def _():
        small = small_ref[...].astype(f32).T
        pack_ref[...] = small[0:16]
        shift_s[...] = jnp.zeros_like(shift_s)
        spot = lax.broadcasted_iota(jnp.int32, (wide, wide), 0)
        target = lax.broadcasted_iota(jnp.int32, (wide, wide), 1) + side_ref[0] * wide
        sums = [jnp.zeros((16, wide), f32), jnp.zeros((16, wide), f32)]
        for part in range(2):
            wanted = lax.div(spot, share) * (2 * share) + part * share + lax.rem(spot, share)
            chosen = jnp.where(wanted == target, 1.0, 0.0).astype(bf16)
            for kind in range(2):
                values = small[6 + part : 7 + part, kind * wide : (kind + 1) * wide]
                values = jnp.broadcast_to(values, (16, wide)).astype(bf16)
                sums[kind] += jnp.dot(values, chosen, preferred_element_type=f32)
        for pair in range(pairs):
            lanes = slice(128 * pair, 128 * pair + 128)
            shift_s[:, 384 * pair : 384 * pair + 128] = sums[0][0:1, lanes]
            shift_s[:, 384 * pair + 256 : 384 * pair + 384] = sums[1][0:1, lanes]

    tiles = 2
    size = normed_ref.shape[2] // tiles

    def normed_tile(i):
        rows = slice(i * size, (i + 1) * size)
        value = jnp.where(which == 0, own_ref[0, rows], other_ref[0, rows]).astype(f32)
        xhat, _ = standardise(value)
        normed = (xhat * pack_ref[0:1, :] + pack_ref[1:2, :]).astype(bf16)
        normed_ref[0, 0, rows] = normed
        return normed

    normed = normed_tile(0)
    for i in range(tiles):
        mixed = jnp.dot(normed, w_ref[...], preferred_element_type=f32) + shift_s[...]
        mixed = mixed.astype(bf16)
        if i + 1 < tiles:
            normed = normed_tile(i + 1)
        for pair in range(pairs):
            lanes = slice(384 * pair, 384 * pair + 384)
            mixed_ref[pair, 0, 0, i * size : (i + 1) * size] = mixed[:, lanes]


def attend_kernel(base, flag_ref, mixed_ref, qx_ref, kx_ref, *rest):
    own_ref, other_ref, ext_ref, q_s, k_s, v_s, acc_s = rest[-7:]
    row = base + pl.program_id(0)
    length = q_s.shape[1]
    heads = q_s.shape[0]
    half = length // 2
    low, high = lane_masks()
    qx, kx = qx_ref[0], kx_ref[0]
    q_low, q_high, k_low, k_high = qx * low, qx * high, kx * low, kx * high
    for pair in range(heads // 2):
        q = mixed_ref[pair, :, 0, :, 0:128].reshape(length, 128)
        k = mixed_ref[pair, :, 0, :, 128:256].reshape(length, 128)
        v = mixed_ref[pair, :, 0, :, 256:384].reshape(length, 128)
        q_s[2 * pair] = q * low + q_high
        q_s[2 * pair + 1] = q * high + q_low
        k_s[2 * pair] = k * low + k_high
        k_s[2 * pair + 1] = k * high + k_low
        v_s[2 * pair] = v * low + high
        v_s[2 * pair + 1] = v * high + low
    acc_s[...] = jnp.zeros_like(acc_s)
    key_blocks = length // TK_F

    def step(index, carry):
        @pl.when(flag_ref[row, index] != 0)
        def _():
            q_at = pl.ds(pl.multiple_of((index // key_blocks) * TQ_F, TQ_F), TQ_F)
            k_at = pl.ds(pl.multiple_of((index % key_blocks) * TK_F, TK_F), TK_F)
            for head in range(heads):
                score = lax.dot_general(
                    q_s[head, q_at, :], k_s[head, k_at, :], NT, preferred_element_type=f32
                )
                expo = jnp.exp2(score * SCORE).astype(bf16)
                acc_s[head, q_at, :] += jnp.dot(expo, v_s[head, k_at, :], preferred_element_type=f32)

        return carry

    lax.fori_loop(0, (length // TQ_F) * key_blocks, step, 0)
    lane = lax.broadcasted_iota(jnp.int32, (half, 128), 1)
    first_half = lane < HEAD_DIM
    spot = lane % HEAD_DIM
    for pair in range(heads // 2):
        for side in range(2):
            rows = slice(side * half, (side + 1) * half)
            first, second = acc_s[2 * pair, rows], acc_s[2 * pair + 1, rows]
            top = jnp.where(first_half, first, second)
            crossed = jnp.where(first_half, second, first)
            totals = pltpu.roll(crossed, HEAD_DIM, 1)
            target = own_ref if side == 0 else other_ref
            target[pair, 0] = (top / totals).astype(bf16)
            lse = -8.0 * jnp.log(crossed)
            lse_a = lse.astype(bf16).astype(f32)
            lse_b = (lse - lse_a).astype(bf16).astype(f32)
            ext = jnp.where(
                spot == LANE_LOG,
                lse_a,
                jnp.where(
                    spot == LANE_LOG + 1,
                    lse_b,
                    jnp.where(spot == LANE_LOG + 2, lse - lse_a - lse_b, qx[rows].astype(f32)),
                ),
            )
            ext_ref[pair, side, 0] = ext.astype(bf16)


def join_lanes(ref):
    return jnp.concatenate([ref[i, 0] for i in range(ref.shape[0])], axis=1)


def mlp_kernel(
    planes, share, spot_ref, x_ref, mine_ref, recv_ref, wo_ref, up_ref, near_own, far_own, near_other, far_other,
    grad_ref, pack_ref, upb_ref,
    out_ref, glow_ref, gdown_own, gdown_other, gup_own, gup_other, gbias_ref, gvec_ref,
    down_s, up_s, wo_v, up_v, down_v, gd_own, gd_other, gu_own, gu_other, load_sem, store_sem,
):
    turn = pl.program_id(0)
    side, x_at = spot_ref[0], spot_ref[2]
    chunks, size = down_s.shape[0], down_s.shape[2]
    load_out = pltpu.make_async_copy(wo_ref, wo_v, load_sem.at[0])
    load_up = pltpu.make_async_copy(up_ref, up_v, load_sem.at[1])
    load_down = []
    for index, piece in enumerate((near_own, far_own, near_other, far_other)):
        at_side = 1 - side if index // 2 else side
        column = 1 - x_at if index % 2 else x_at
        for i in range(2):
            target = down_v.at[at_side, :, i, column]
            load_down.append(pltpu.make_async_copy(piece.at[i], target, load_sem.at[2 + 2 * index + i]))

    @pl.when(turn == 0)
    def _():
        load_out.start()
        load_up.start()
        for load in load_down:
            load.start()
        down_s[...] = jnp.zeros_like(down_s)
        up_s[...] = jnp.zeros_like(up_s)
        gbias_ref[...] = jnp.zeros_like(gbias_ref)
        gvec_ref[...] = jnp.zeros_like(gvec_ref)
        load_out.wait()

    middle = (
        x_ref[0].astype(f32)
        + jnp.dot(join_lanes(mine_ref), wo_v[side], preferred_element_type=f32)
        + jnp.dot(join_lanes(recv_ref), wo_v[1 - side], preferred_element_type=f32)
        + pack_ref[2:3, :]
    )
    xhat, rstd = standardise(middle)
    normed = (xhat * pack_ref[3:4, :] + pack_ref[4:5, :]).astype(bf16)
    normed_t = normed.T
    grad = grad_ref[0]
    grad_t = grad.T
    total = middle + pack_ref[5:6, :]

    @pl.when(turn == 0)
    def _():
        load_up.wait()
        for load in load_down:
            load.wait()

    half_lines = down_v.shape[1] // (chunks // 2)

    def down_chunk(f):
        line = (f % (chunks // 2)) * half_lines
        return down_v[f // (chunks // 2), line : line + half_lines].reshape(size, down_v.shape[-1])

    def first_layer(f):
        at = slice(f * size, (f + 1) * size)
        return jnp.dot(normed, up_v[:, at], preferred_element_type=f32) + upb_ref[f : f + 1, :]

    gnormed = None
    pre = first_layer(0)
    for f in range(chunks):
        at = slice(f * size, (f + 1) * size)
        hidden, slope = gelu_pair(pre)
        ghidden = lax.dot_general(grad, down_chunk(f), NT, preferred_element_type=f32)
        if f + 1 < chunks:
            pre = first_layer(f + 1)
        hidden = hidden.astype(bf16)
        gpre = (ghidden * slope).astype(bf16)
        total = total + jnp.dot(hidden, down_chunk(f), preferred_element_type=f32)
        part = lax.dot_general(gpre, up_v[:, at], NT, preferred_element_type=f32)
        gnormed = part if gnormed is None else gnormed + part
        down_s[f] += jnp.dot(grad_t, hidden, preferred_element_type=f32)
        up_s[f] += jnp.dot(normed_t, gpre, preferred_element_type=f32)
        gbias_ref[f] += jnp.sum(gpre.astype(f32), axis=0, keepdims=True)
    out_ref[0] = total.astype(bf16)
    gmid = grad.astype(f32) + norm_pull(gnormed, pack_ref[3:4, :], xhat, rstd)
    low = gmid.astype(bf16)
    glow_ref[0] = low
    gvec_ref[0:1, :] += jnp.sum(gnormed * xhat, axis=0, keepdims=True)
    gvec_ref[1:2, :] += jnp.sum(gnormed, axis=0, keepdims=True)
    gvec_ref[2:3, :] += jnp.sum(low.astype(f32), axis=0, keepdims=True)
    gvec_ref[3:4, :] += jnp.sum(grad.astype(f32), axis=0, keepdims=True)

    @pl.when(turn == pl.num_programs(0) - 1)
    def _():
        half = chunks // 2
        rows = chunks * share
        per_chunk = size // rows
        lines_chunk = per_chunk // planes
        for f in range(chunks):
            whole = down_s[f].astype(bf16).T
            at_line = (f % half) * lines_chunk
            span = slice(at_line, at_line + lines_chunk)
            for target, result, wanted in ((gd_own, gdown_own, f // half), (gd_other, gdown_other, 1 - f // half)):

                @pl.when(side == wanted)
                def _(target=target, result=result, whole=whole, f=f, at_line=at_line, span=span):
                    for i in range(per_chunk):
                        target[i % planes, at_line + i // planes] = whole[i * rows : (i + 1) * rows]
                    pltpu.make_async_copy(target.at[:, span], result.at[:, span], store_sem.at[f]).start()

        wide = up_s.shape[1] // 2
        ups = ((gu_own, gup_own, side * wide), (gu_other, gup_other, (1 - side) * wide))
        for which, (target, result, base) in enumerate(ups):
            for f in range(chunks):
                for at in range(wide // share):
                    start = pl.multiple_of(base + at * share, 8)
                    target[at % planes, at // planes, f] = up_s[f, pl.ds(start, share), :].astype(bf16)
                pltpu.make_async_copy(
                    target.at[:, :, f], result.at[:, :, f], store_sem.at[chunks * (1 + which) + f]
                ).start()
        for f in range(chunks):
            span = slice(0, lines_chunk)
            pltpu.make_async_copy(gd_own.at[:, span], gdown_own.at[:, span], store_sem.at[f]).wait()
        for which, (target, result, base) in enumerate(ups):
            for f in range(chunks):
                pltpu.make_async_copy(
                    target.at[:, :, f], result.at[:, :, f], store_sem.at[chunks * (1 + which) + f]
                ).wait()


def attend_back_kernel(
    flag_ref, side_ref, mixed_ref, ext_ref, att_own, att_other, own_ref, other_ref, wo_ref, kx_ref,
    gmixed_ref, gbias_ref,
    q_s, d_s, k_s, v_s, kt_s, gq_s, gk_s, gv_s,
):
    row = pl.program_id(0)
    length = k_s.shape[0]
    half = length // 2
    low, high = lane_masks()
    lane = lax.broadcasted_iota(jnp.int32, (1, 128), 1)
    spot = lane % HEAD_DIM
    square_row = lax.broadcasted_iota(jnp.int32, (128, 128), 0) < HEAD_DIM
    square_col = lax.broadcasted_iota(jnp.int32, (128, 128), 1) < HEAD_DIM
    crossing = jnp.where(square_row == square_col, 0.0, -1.0).astype(bf16)
    one_hot_a = jnp.where(spot == 0, 1.0, 0.0)
    one_hot_b = jnp.where(spot == 1, 1.0, 0.0)
    v_ext = (one_hot_a + one_hot_b).astype(bf16)

    @pl.when(row == 0)
    def _():
        gbias_ref[...] = jnp.zeros_like(gbias_ref)

    mixed_at = lambda lanes: mixed_ref[0, :, 0, :, lanes].reshape(length, 128)
    q, k = mixed_at(slice(0, 128)), mixed_at(slice(128, 256))
    ext = ext_ref[0, :, 0].reshape(length, 128)
    k_s[:, 0:128] = k
    k_s[:, 128:256] = kx_ref[0]
    v_s[:, 0:128] = mixed_at(slice(256, 384))
    v_s[:, 128:256] = jnp.broadcast_to(v_ext, (length, 128))
    for head, (mine, other) in enumerate(((low, high), (high, low))):
        q_part, ext_part = q * mine, ext * other
        for i in range(length // TQ_B):
            at = slice(i * TQ_B, (i + 1) * TQ_B)
            rows = slice(head * TQ_B, (head + 1) * TQ_B)
            q_s[i, rows, 0:128] = q_part[at]
            q_s[i, rows, 128:256] = ext_part[at]
    for side in range(2):
        gates = own_ref[0] if side == 0 else other_ref[0]
        d = lax.dot_general(gates, wo_ref[...], NT, preferred_element_type=f32)
        moved = d * (att_own if side == 0 else att_other)[0, 0].astype(f32)
        moved_a = moved.astype(bf16)
        moved_b = (moved - moved_a.astype(f32)).astype(bf16)
        shift = jnp.dot(moved_a, crossing, preferred_element_type=f32) + jnp.dot(
            moved_b, crossing, preferred_element_type=f32
        )
        shift_a = shift.astype(bf16).astype(f32)
        dx = (shift_a * one_hot_a + (shift - shift_a) * one_hot_b).astype(bf16)
        d = d.astype(bf16)
        tile = min(TQ_B, half)
        for head, (mine, other) in enumerate(((low, high), (high, low))):
            d_part, dx_part = d * mine, dx * other
            for i in range(half // tile):
                at = slice(i * tile, (i + 1) * tile)
                start = side * half + i * tile
                rows = slice(head * TQ_B + start % TQ_B, head * TQ_B + start % TQ_B + tile)
                d_s[start // TQ_B, rows, 0:128] = d_part[at]
                d_s[start // TQ_B, rows, 128:256] = dx_part[at]
    for i in range(length // TK_B):
        kt_s[i] = k[i * TK_B : (i + 1) * TK_B].T
    query_blocks = length // TQ_B

    def block(k_start, q_start, size, fresh):
        k_at = slice(k_start, k_start + size)
        tile, inside = q_start // TQ_B, q_start % TQ_B
        key_tile, key_inside = k_start // TK_B, k_start % TK_B
        q_rows = [slice(head * TQ_B + inside, head * TQ_B + inside + size) for head in range(2)]
        probs, grads = [], []
        for rows in q_rows:
            score = lax.dot_general(k_s[k_at, :], q_s[tile, rows, :], NT, preferred_element_type=f32)
            inner = lax.dot_general(v_s[k_at, :], d_s[tile, rows, :], NT, preferred_element_type=f32)
            prob = jnp.exp2(score * SCORE)
            probs.append(prob.astype(bf16))
            grads.append((prob * inner).astype(bf16))
        for head in range(2):
            at = slice(head * HEAD_DIM, (head + 1) * HEAD_DIM)
            keys = kt_s[key_tile, at, key_inside : key_inside + size]
            part = jnp.dot(keys, grads[head], preferred_element_type=f32)
            if fresh:
                gq_s[tile, at, inside : inside + size] = part
            else:
                gq_s[tile, at, inside : inside + size] += part
        for target, left, right in ((gv_s, probs, d_s), (gk_s, grads, q_s)):
            if size == TQ_B:
                part = jnp.dot(jnp.concatenate(left, axis=1), right[tile, :, 0:128], preferred_element_type=f32)
            else:
                part = jnp.dot(left[0], right[tile, q_rows[0], 0:128], preferred_element_type=f32)
                part = part + jnp.dot(left[1], right[tile, q_rows[1], 0:128], preferred_element_type=f32)
            if fresh:
                target[k_at, :] = part
            else:
                target[k_at, :] += part

    for i in range(query_blocks):
        block(i * TQ_B, i * TQ_B, TQ_B, True)
    pieces = length // T_SIDE
    for ki in range(pieces):
        for qi in range(pieces):
            if ki * T_SIDE // TK_B != qi * T_SIDE // TQ_B:

                @pl.when(flag_ref[row, ki * pieces + qi] != 0)
                def _(ki=ki, qi=qi):
                    block(ki * T_SIDE, qi * T_SIDE, T_SIDE, False)

    for i in range(query_blocks):
        gq = (0.125 * gq_s[i].T).astype(bf16)
        for start in range(0, TQ_B, min(TQ_B, half)):
            at = i * TQ_B + start
            size = min(TQ_B, half)
            gmixed_ref[at // half, 0, at % half : at % half + size, 0:128] = gq[start : start + size]
        gbias_ref[0:1, 0:128] += jnp.sum(gq.astype(f32), axis=0, keepdims=True)
    gk = (0.125 * gk_s[...]).astype(bf16)
    gv = gv_s[...].astype(bf16)
    gbias_ref[0:1, 128:256] += jnp.sum(gk.astype(f32), axis=0, keepdims=True)
    gbias_ref[0:1, 256:384] += jnp.sum(gv.astype(f32), axis=0, keepdims=True)
    for side in range(2):
        gmixed_ref[side, 0, :, 128:256] = gk[side * half : (side + 1) * half]
        gmixed_ref[side, 0, :, 256:384] = gv[side * half : (side + 1) * half]


def weight_dot(normed_ref, *piece_refs):
    normed_t = jnp.concatenate([normed_ref[0, 0], normed_ref[1, 0]], axis=0).T
    sides = []
    for side in range(2):
        sides.append(jnp.concatenate([ref[side, 0] for ref in piece_refs], axis=1))
    return jnp.dot(normed_t, jnp.concatenate(sides, axis=0), preferred_element_type=f32)


def fold_lanes(value):
    total = value[:, 0:128]
    for at in range(128, value.shape[1], 128):
        total = total + value[:, at : at + 128]
    return total


def early_kernel(
    planes, share, normed_ref, g0_ref, g1_ref, b0_ref, b1_ref, mine_ref, other_ref, low_ref, low_other_ref, w_ref,
    unit_ref, first_ref, second_ref, acc_s, out_s,
):
    turn = pl.program_id(0)

    @pl.when(turn == 0)
    def _():
        acc_s[...] = jnp.zeros_like(acc_s)
        out_s[...] = jnp.zeros_like(out_s)

    acc_s[...] += weight_dot(normed_ref, g0_ref, g1_ref)
    across = (((0,), (0,)), ((), ()))
    out_s[...] += lax.dot_general(
        join_lanes(mine_ref), low_ref[0], across, preferred_element_type=f32
    ) + lax.dot_general(join_lanes(other_ref), low_other_ref[0], across, preferred_element_type=f32)

    @pl.when(turn == pl.num_programs(0) - 1)
    def _():
        weights = w_ref[...].astype(f32)
        sums = jnp.concatenate([b0_ref[0:1, :], b1_ref[0:1, :]], axis=1)
        first_ref[...] = fold_lanes(weights * acc_s[...])
        second_ref[...] = fold_lanes(weights * sums)
        count = out_s.shape[0] // share
        for at in range(count):
            spot = (at % planes, at // planes)
            for half in range(2):
                lanes = slice(384 * half, 384 * half + 384)
                for side in range(2):
                    start = (side * count + at) * share
                    unit_ref[spot + (2 * side + half,)] = acc_s[start : start + share, lanes].astype(bf16)
                unit_ref[spot + (4 + half,)] = out_s[at * share : (at + 1) * share, lanes].astype(bf16)


def scatter_rows(vector, step, offset, owners):
    n = vector.shape[1]
    owner = lax.broadcasted_iota(jnp.int32, (owners, n), 0) - offset
    mask = lax.div(lax.broadcasted_iota(jnp.int32, (owners, n), 1), step) == owner
    spread = jnp.where(mask, jnp.broadcast_to(vector, (owners, n)), 0.0).astype(bf16)
    lane = lax.rem(lax.broadcasted_iota(jnp.int32, (128, n), 1), step)
    chosen = jnp.where(lane == lax.broadcasted_iota(jnp.int32, (128, n), 0), 1.0, 0.0).astype(bf16)
    return lax.dot_general(spread, chosen, NT, preferred_element_type=f32)


def late_kernel(
    planes, share, side_ref, normed_ref, g_ref, w_ref, first_ref, second_ref, b0_ref, b1_ref, b2_ref, pack_ref,
    gvec_ref, gup_ref, unit_ref, acc_s,
):
    turn = pl.program_id(0)

    @pl.when(turn == 0)
    def _():
        acc_s[...] = jnp.zeros_like(acc_s)

    acc_s[...] += weight_dot(normed_ref, g_ref)

    @pl.when(turn == pl.num_programs(0) - 1)
    def _():
        side = side_ref[0]
        weights = w_ref[...].astype(f32)
        width = weights.shape[0]
        owners = width // share
        count = owners // 2
        inner = first_ref[...] + fold_lanes(weights * acc_s[...])
        plain = second_ref[...] + fold_lanes(weights * b2_ref[0:1, :])
        inner = jnp.sum(inner.T, axis=0, keepdims=True)
        plain = jnp.sum(plain.T, axis=0, keepdims=True)
        gain, bias = pack_ref[0:1, :], pack_ref[1:2, :]
        g_gain = (inner - bias * plain) / gain
        biases = (b0_ref, b1_ref, b2_ref)
        query = jnp.concatenate([b[0:1, 0:128] for b in biases], axis=1)
        value = jnp.concatenate([b[0:1, 256:384] for b in biases], axis=1)
        chunks = gup_ref.shape[0]
        rows_up = chunks * share
        up_bias = None
        for f in range(chunks):
            part = scatter_rows(gup_ref[f], rows_up, f * (width // rows_up), owners)
            up_bias = part if up_bias is None else up_bias + part
        wide = width // 2
        first_owner = side * (wide // (2 * share))
        qv_bias = scatter_rows(query, 2 * share, first_owner, owners) + scatter_rows(
            value, 2 * share, first_owner + count, owners
        )
        plain_rows = lambda vec: scatter_rows(vec, share, 0, owners)
        slots = [
            plain_rows(g_gain),
            plain_rows(plain),
            plain_rows(gvec_ref[2:3, :]),
            plain_rows(gvec_ref[0:1, :]),
            plain_rows(gvec_ref[1:2, :]),
            plain_rows(gvec_ref[3:4, :]),
            qv_bias,
            up_bias,
            jnp.zeros((owners, 128), f32),
        ]
        lines_of = [jnp.concatenate(slots[3 * i : 3 * i + 3], axis=1) for i in range(3)]
        blank = jnp.zeros((5, 384), f32)
        for at in range(count):
            spot = (at % planes, at // planes)
            small = []
            for half in range(2):
                owner = half * count + at
                start = owner * share
                unit_ref[spot + (half,)] = acc_s[start : start + share, :].astype(bf16)
                small += [line[owner : owner + 1, :] for line in lines_of] + [blank]
            small.append(jnp.zeros((share - 16, 384), f32))
            unit_ref[spot + (2,)] = jnp.concatenate(small, axis=0).astype(bf16)


def finish_kernel(side_ref, line_ref, got_ref, qkv_ref, out_ref, *vec_refs):
    side = side_ref[0]
    wide = qkv_ref.shape[1] // 6
    for pair in range(wide // 128):
        own = line_ref[2 * side + pair] if pair < 2 else line_ref[6 + side]
        other = got_ref[pair]
        for kind in range(3):
            lanes = slice(128 * kind, 128 * kind + 128)
            for half in range(2):
                at = kind * 2 * wide + half * wide + 128 * pair
                qkv_ref[:, at : at + 128] = jnp.where(side == half, own[:, lanes], other[:, lanes])
    out_ref[:, 0:384] = line_ref[4]
    out_ref[:, 384:768] = line_ref[5]
    start = pl.multiple_of(8 * side, 8)
    small = line_ref[8, pl.ds(start, 8), :] + got_ref[3, pl.ds(start, 8), :]
    for slot, ref in enumerate(vec_refs):
        at = 128 * (slot % 3)
        ref[...] = small[slot // 3 : slot // 3 + 1, at : at + ref.shape[1]]


def back_through(pieces, w_ref, side):
    total = None
    for i, piece in enumerate(pieces):
        part = lax.dot_general(
            piece[side, 0], w_ref[:, 384 * i : 384 * i + 384], NT, preferred_element_type=f32
        )
        total = part if total is None else total + part
    return total


def give_kernel(*refs):
    pieces, (w_ref, out_ref) = refs[:-2], refs[-2:]
    out_ref[0] = back_through(pieces, w_ref, 0).astype(bf16)


def input_kernel(*refs):
    pieces, (w_ref, recv_ref, x_ref, gmid_ref, pack_ref, ginput_ref) = refs[:-6], refs[-6:]
    gnormed = back_through(pieces, w_ref, 0) + recv_ref[0].astype(f32)
    xhat, rstd = standardise(x_ref[0].astype(f32))
    ginput_ref[0] = gmid_ref[0].astype(f32) + norm_pull(gnormed, pack_ref[0:1, :], xhat, rstd)


def partner(value):
    return lax.ppermute(value, "seq", [(0, 1), (1, 0)])


def exchange(value, axis):
    return lax.all_to_all(value, axis, 0, 0, tiled=True)


def spread_line(value, lines):
    return exchange(jnp.broadcast_to(value[None], (lines,) + value.shape), "line")


def flip(value, axis):
    return lax.ppermute(value, axis, [(0, 1), (1, 0)])


def in_order(index, own, received):
    return jnp.where(index == 0, jnp.stack([own, received]), jnp.stack([received, own]))


def spread_first(one, two):
    return lax.optimization_barrier((flip(one, "x"), flip(two, "y")))


def spread_second(one, two, got_one, got_two):
    near_one = in_order(lax.axis_index("x"), one, got_one)
    near_two = in_order(lax.axis_index("y"), two, got_two)
    near_one, near_two = lax.optimization_barrier((near_one, near_two))
    return (near_one, flip(near_one, "y")), (near_two, flip(near_two, "x"))


def spread_plane(one, two):
    return spread_second(one, two, *spread_first(one, two))


def after(value, *others):
    return lax.optimization_barrier((value,) + others)[0]


def assemble_kernel(far_plane, spot_ref, *refs):
    pieces, targets, scratch, (in_sem, out_sem) = refs[:2], refs[-6:-4], refs[-4:-2], refs[-2:]
    up_ref, out_ref = targets
    side, y = spot_ref[0], spot_ref[1]
    width = out_ref.shape[-1]
    blocks = up_ref.shape[-1] // width
    loads = [pltpu.make_async_copy(pieces[i], scratch[i], in_sem.at[i]) for i in range(2)]
    for load in loads:
        load.start()
    stores = []

    def send(source, target):
        stores.append(pltpu.make_async_copy(source, target, out_sem.at[len(stores)]))
        stores[-1].start()

    row = 1 - y if far_plane else y
    for index in range(2):
        loads[index].wait()
        at_side = 1 - side if index else side
        held = scratch[index]
        for i in range(2):
            for block in range(blocks):
                lanes = slice(block * width, (block + 1) * width)
                send(held.at[i, :, block], up_ref.at[at_side, :, row, i, :, lanes])
            send(held.at[i, :, blocks], out_ref.at[at_side, :, row, i])
    for copy in stores:
        copy.wait()


def assemble(spot, far_plane, pieces, targets, shapes):
    anywhere = pl.BlockSpec(memory_space=pl.ANY)
    blocks = pieces[0].shape[2]
    return pl.pallas_call(
        functools.partial(assemble_kernel, far_plane),
        grid_spec=pltpu.PrefetchScalarGridSpec(
            num_scalar_prefetch=1,
            grid=(1,),
            in_specs=[anywhere] * (2 + len(targets)),
            out_specs=[anywhere] * 2,
            scratch_shapes=[pltpu.VMEM(p.shape, bf16) for p in pieces]
            + [pltpu.SemaphoreType.DMA((2,)), pltpu.SemaphoreType.DMA((4 * blocks,))],
        ),
        out_shape=shapes,
        input_output_aliases={3 + i: i for i in range(len(targets))},
        name="assemble",
        **kernel_params(1e6, 12e6),
    )(spot, *pieces, *targets)


def sum_plane(value, *waits):
    received = exchange(value, ("y", "x"))
    if waits:
        received = after(received, *waits)
    return jnp.sum(received.astype(f32), axis=0)


def send_line(value, lines):
    here = lax.axis_index("line")
    pieces = []
    for shift in range(1, lines):
        piece = lax.dynamic_index_in_dim(value, (here + shift) % lines, 0, keepdims=False).astype(bf16)
        pieces.append(lax.ppermute(piece, "line", [(i, (i + shift) % lines) for i in range(lines)]))
    return pieces


def sum_line(value, lines, *waits):
    total = lax.dynamic_index_in_dim(value, lax.axis_index("line"), 0, keepdims=False)
    pieces = send_line(value, lines)
    if waits:
        pieces = lax.optimization_barrier(tuple(pieces) + waits)[: len(pieces)]
    for piece in pieces:
        total = total + piece.astype(f32)
    return total


def masks(seg, pos):
    pad = seg == CLIPS - 1
    lane = jnp.arange(128, dtype=jnp.int32) % HEAD_DIM
    seg, pos, pad = seg[..., None], pos[..., None], pad[..., None]
    clip_lane = lane < CLIPS - 1
    digit = jnp.where(lane < 9, pos // 256, jnp.where(lane < 25, (pos // 16) % 16, pos % 16))
    digit_base = jnp.where(lane < 9, 5, jnp.where(lane < 25, 9, 25))
    digit_lane = (lane >= 5) & (lane < LANE_LOG)
    hit_clip = lane == seg
    hit_digit = lane - digit_base == digit
    log_lane = (lane >= LANE_LOG) & (lane < LANE_PAD)
    pad_lane = lane == LANE_PAD
    bad = (clip_lane & ~hit_clip) | (digit_lane & pad & ~hit_digit) | (pad_lane & ~pad)
    qx = jnp.where(bad, -BIG, 0.0).astype(bf16)
    on = (clip_lane & hit_clip) | (digit_lane & pad & hit_digit) | log_lane | (pad_lane & pad)
    kx = jnp.where(on, 1.0, 0.0).astype(bf16)
    return qx, kx


def block_flags(ident, rows_block, cols_block):
    count, length = ident.shape
    by_row = ident.reshape(count, length // rows_block, rows_block)
    by_col = ident.reshape(count, length // cols_block, cols_block)
    low_row, high_row = jnp.min(by_row, axis=2)[:, :, None], jnp.max(by_row, axis=2)[:, :, None]
    low_col, high_col = jnp.min(by_col, axis=2)[:, None, :], jnp.max(by_col, axis=2)[:, None, :]
    meets = (low_row <= high_col) & (low_col <= high_row)
    return meets.astype(jnp.int32).reshape(count, -1)


def pair_device(
    lines, planes,
    tokens, segment_ids, cotangent, ln1_gain, ln1_bias, qkv_weight, qv_bias, out_weight, out_bias,
    ln2_gain, ln2_bias, up_weight, up_bias, down_weight, down_bias, avg_qkv, avg_out, avg_up, avg_down,
):
    count, part, width = tokens.shape
    length = 2 * part
    wide = width // 2
    heads = HEADS // 2
    hidden_width = up_weight.shape[1]
    chunks = hidden_width // width
    share = qkv_weight.shape[0]
    side = lax.axis_index("seq").astype(jnp.int32)
    first = side == 0
    side_arr = side.reshape(1)
    const = lambda *shape: pl.BlockSpec(shape, lambda *_: (0,) * len(shape), pipeline_mode=pl.Buffered(1))
    row_block = lambda *shape: pl.BlockSpec((1,) + shape, lambda j, *_: (j,) + (0,) * len(shape))
    both_block = lambda lanes: pl.BlockSpec((2, 1, part, lanes), lambda j, *_: (0, j, 0, 0))
    own_block = lambda lanes: pl.BlockSpec((1, 1, part, lanes), lambda j, *_: (0, j, 0, 0))

    pairs = heads // 2
    sds = jax.ShapeDtypeStruct
    small_vectors = [ln1_gain, ln1_bias, out_bias, ln2_gain, ln2_bias, down_bias, qv_bias, up_bias]
    mine, give, second = pl.pallas_call(
        functools.partial(prepare_kernel, share),
        grid_spec=pltpu.PrefetchScalarGridSpec(
            num_scalar_prefetch=1,
            grid=(1,),
            in_specs=[
                pl.BlockSpec((share, 6 * wide), lambda *_: (0, 0)),
                pl.BlockSpec((share, hidden_width), lambda *_: (0, 0)),
                pl.BlockSpec((share, width), lambda *_: (0, 0)),
                pl.BlockSpec((chunks * share, width), lambda *_: (0, 0)),
            ]
            + [pl.BlockSpec((1, v.shape[0]), lambda *_: (0, 0)) for v in small_vectors],
            out_specs=[pl.BlockSpec((share, 3 * wide + 128), lambda *_: (0, 0))] * 2
            + [pl.BlockSpec(((2 * chunks + 1) * share, width), lambda *_: (0, 0))],
        ),
        out_shape=[sds((share, 3 * wide + 128), bf16)] * 2 + [sds(((2 * chunks + 1) * share, width), bf16)],
        name="prepare",
        **kernel_params(1e6, 1e6),
    )(side_arr, qkv_weight, up_weight, out_weight, down_weight, *[v[None] for v in small_vectors])
    take = partner(give)
    tokens_other = partner(tokens)
    seg_other = partner(segment_ids)
    seg = jnp.concatenate([segment_ids, seg_other], axis=1)
    spots = jnp.arange(part, dtype=jnp.int32)
    pos = jnp.concatenate([side * part + spots, (1 - side) * part + spots])
    qx, kx = masks(seg, jnp.broadcast_to(pos, seg.shape))
    ident = jnp.where(seg == CLIPS - 1, CLIPS + pos, seg)
    flags_f = block_flags(ident, TQ_F, TK_F)
    flags_b = block_flags(ident, T_SIDE, T_SIDE)

    start = jnp.where(first, jnp.stack([mine, take]), jnp.stack([take, mine]))
    x_at, y_at = lax.axis_index("x"), lax.axis_index("y")
    first_line = after(spread_line(start, lines), qx, kx, flags_f, flags_b)
    (one_m, one_r), (two_m, two_r) = spread_plane(first_line[:, 0], first_line[:, 1])
    one = in_order(y_at, one_m, one_r).transpose(2, 0, 1, 3, 4)
    two = in_order(x_at, two_m, two_r).transpose(2, 1, 0, 3, 4)
    w_first = jnp.stack([one, two]).reshape(width, 3 * wide + 128)

    own_rows = chunks * share
    second = after(second, first_line)
    up_rows = own_rows + share
    second_line = spread_line(second, lines)

    small_at = 3 * wide // 128
    normed, mixed, pack = pl.pallas_call(
        functools.partial(project_kernel, share),
        grid_spec=pltpu.PrefetchScalarGridSpec(
            num_scalar_prefetch=1,
            grid=(2, count),
            in_specs=[
                pl.BlockSpec((1, part, width), lambda h, j, *_: (jnp.where(h == 0, j, count - 1), 0, 0)),
                pl.BlockSpec((1, part, width), lambda h, j, *_: (jnp.where(h == 0, 0, j), 0, 0)),
                const(width, 3 * wide),
                pl.BlockSpec((width, 128), lambda *_: (0, small_at), pipeline_mode=pl.Buffered(1)),
            ],
            out_specs=[
                pl.BlockSpec((1, 1, part, width), lambda h, j, *_: (h, j, 0, 0)),
                pl.BlockSpec((pairs, 1, 1, part, 384), lambda h, j, *_: (0, h, j, 0, 0)),
                pl.BlockSpec((16, width), lambda *_: (0, 0)),
            ],
            scratch_shapes=[pltpu.VMEM((1, 3 * wide), f32)],
        ),
        out_shape=[
            sds((2, count, part, width), bf16),
            sds((pairs, 2, count, part, 384), bf16),
            sds((16, width), f32),
        ],
        name="project",
        **kernel_params(
            2 * 2 * count * part * width * 3 * wide, 20e6, order=("arbitrary", "arbitrary")
        ),
    )(side_arr, tokens, tokens_other, w_first, w_first)
    up_bias_all = pack[8 : 8 + chunks].reshape(chunks, -1, share).transpose(1, 0, 2).reshape(chunks, width)

    second_line = after(second_line, one_r, two_r, pack)
    halves = (second_line[:, :up_rows].reshape(lines, chunks + 1, share, width), second_line[:, up_rows:])
    halves_got = spread_first(*halves)
    same, row_mixed = (), mixed
    for base, rows_now in ((0, 1), (1, count - 1)):
        if base == 1:
            halves_got = lax.optimization_barrier(halves_got + (same[0],))[:2]
            up_pair, down_pair = spread_second(*halves, *halves_got)
            row_mixed = after(mixed, up_pair[0], down_pair[0])
        row_both = lambda lanes, base=base: pl.BlockSpec(
            (pairs, 2, 1, part, lanes), lambda j, *_: (0, 0, base + j, 0, 0)
        )
        row_one = pl.BlockSpec((pairs, 1, part, 128), lambda j, *_, base=base: (0, base + j, 0, 0))
        row_flat = pl.BlockSpec((1, length, 128), lambda j, *_, base=base: (base + j, 0, 0))
        same = pl.pallas_call(
            functools.partial(attend_kernel, base),
            grid_spec=pltpu.PrefetchScalarGridSpec(
                num_scalar_prefetch=1,
                grid=(rows_now,),
                in_specs=[row_both(384), row_flat, row_flat] + [pl.BlockSpec(memory_space=pl.ANY)] * len(same),
                out_specs=[row_one, row_one, row_both(128)],
                scratch_shapes=[pltpu.VMEM((heads, length, 128), bf16)] * 3
                + [pltpu.VMEM((heads, length, 128), f32)],
            ),
            out_shape=[sds((pairs, count, part, 128), bf16)] * 2 + [sds((pairs, 2, count, part, 128), bf16)],
            input_output_aliases={4 + i: i for i in range(len(same))},
            name="attend",
            **kernel_params(8e9, 7e6, 4e6),
        )(flags_f, row_mixed, qx, kx, *same)
    att_own, att_other, ext = same
    spot = jnp.stack([side, y_at.astype(jnp.int32), x_at.astype(jnp.int32)])
    near = [up_pair[0], down_pair[0]]
    near += [partner(piece) for piece in near]
    far = list(lax.optimization_barrier((up_pair[1], down_pair[1], att_own))[:2])
    near = list(lax.optimization_barrier(tuple(near) + tuple(far))[:4])
    far += [partner(piece) for piece in far]
    shapes = [
        sds((2, lines, 2, 2, share, hidden_width), bf16),
        sds((2, lines, 2, 2, share, width), bf16),
    ]
    targets = assemble(spot, False, near[::2], (), shapes)
    w_up, w_out = assemble(spot, True, far[::2], targets, shapes)
    w_up = w_up.reshape(width, hidden_width)
    down_pieces = [near[1], far[1], near[3], far[3]]
    w_out = w_out.reshape(2, wide, width)
    w_out_flat = w_out.reshape(2 * wide, width)

    att_recv = partner(att_other)

    head_block = pl.BlockSpec((pairs, 1, part, 128), lambda j, *_: (0, j, 0, 0))
    out_tokens, glow, gdown_own, gdown_other, gup_own, gup_other, gup_bias, gvec = pl.pallas_call(
        functools.partial(mlp_kernel, planes, share),
        grid_spec=pltpu.PrefetchScalarGridSpec(
            num_scalar_prefetch=1,
            grid=(count,),
            in_specs=[
                row_block(part, width),
                head_block,
                head_block,
            ]
            + [pl.BlockSpec(memory_space=pl.ANY)] * 6
            + [
                row_block(part, width),
                const(16, width),
                const(chunks, width),
            ],
            out_specs=[row_block(part, width)] * 2
            + [pl.BlockSpec(memory_space=pl.ANY)] * 4
            + [const(chunks, 1, width), const(8, width)],
            scratch_shapes=[pltpu.VMEM((chunks, width, width), f32)] * 2
            + [
                pltpu.VMEM((2, wide, width), bf16),
                pltpu.VMEM((width, hidden_width), bf16),
                pltpu.VMEM((2, lines, 2, 2, own_rows, width), bf16),
            ]
            + [pltpu.VMEM((planes, lines, own_rows, width), bf16)] * 2
            + [pltpu.VMEM((planes, lines, chunks, share, width), bf16)] * 2
            + [pltpu.SemaphoreType.DMA((10,)), pltpu.SemaphoreType.DMA((3 * chunks,))],
        ),
        out_shape=[
            sds((count, part, width), bf16),
            sds((count, part, width), bf16),
        ]
        + [sds((planes, lines, own_rows, width), bf16)] * 2
        + [sds((planes, lines, chunks, share, width), bf16)] * 2
        + [sds((chunks, 1, width), f32), sds((8, width), f32)],
        name="mlp",
        **kernel_params(2 * count * part * width * (width + 6 * hidden_width), 36e6, 4.7e6),
    )(spot, tokens, att_own, att_recv, w_out, w_up, *down_pieces, cotangent, pack, up_bias_all)

    glow_other = partner(glow)
    avg_qkv, avg_out, avg_up, avg_down, _ = lax.optimization_barrier((avg_qkv, avg_out, avg_up, avg_down, glow))
    new_qkv = 0.9 * avg_qkv + 0.1 * qkv_weight.astype(f32)
    new_out = 0.9 * avg_out + 0.1 * out_weight.astype(f32)
    new_up = 0.9 * avg_up + 0.1 * up_weight.astype(f32)
    new_down = 0.9 * avg_down + 0.1 * down_weight.astype(f32)
    add = lambda one, two: (one.astype(f32) + two.astype(f32)).astype(bf16)
    gdown_plane = sum_plane(add(gdown_own, partner(gdown_other)))
    gup_sum = add(gup_own, partner(gup_other))

    gmixed, gmixed_bias = [], []
    ties = ()
    for pair in range(pairs):
        lane_block = lambda lanes, pair=pair: pl.BlockSpec((1, 2, 1, part, lanes), lambda j, *_: (pair, 0, j, 0, 0))
        att_block = pl.BlockSpec((1, 1, part, 128), lambda j, *_, pair=pair: (pair, j, 0, 0))
        piece, piece_bias = pl.pallas_call(
            attend_back_kernel,
            grid_spec=pltpu.PrefetchScalarGridSpec(
                num_scalar_prefetch=2,
                grid=(count,),
                in_specs=[
                    lane_block(384),
                    lane_block(128),
                    att_block,
                    att_block,
                    row_block(part, width),
                    row_block(part, width),
                    pl.BlockSpec((128, width), lambda j, flags, where, pair=pair: (where[0] * pairs + pair, 0)),
                    row_block(length, 128),
                ],
                out_specs=[both_block(384), const(8, 384)],
                scratch_shapes=[pltpu.VMEM((length // TQ_B, 2 * TQ_B, 256), bf16)] * 2
                + [pltpu.VMEM((length, 256), bf16)] * 2
                + [
                    pltpu.VMEM((length // TK_B, 128, TK_B), bf16),
                    pltpu.VMEM((length // TQ_B, 128, TQ_B), f32),
                    pltpu.VMEM((length, 128), f32),
                    pltpu.VMEM((length, 128), f32),
                ],
            ),
            out_shape=[sds((2, count, part, 384), bf16), sds((8, 384), f32)],
            name="attend_back",
            **kernel_params(25e9, 20e6, 4e6),
        )(flags_b, side_arr, after(mixed, *ties), ext, att_own, att_other, glow, glow_other, w_out_flat, kx)
        gmixed.append(piece)
        gmixed_bias.append(piece_bias)
        if pair == 0:
            gup_plane = sum_plane(after(gup_sum, gdown_plane))
            grad_down = sum_line(gdown_plane, lines)
            ties = (gdown_plane,)
        if pair == 1:
            early, inner_sum, plain_sum = pl.pallas_call(
                functools.partial(early_kernel, planes, share),
                grid=(count,),
                in_specs=[both_block(width), both_block(384), both_block(384), const(8, 384), const(8, 384)]
                + [head_block, head_block, row_block(part, width), row_block(part, width), const(width, 768)],
                out_specs=[const(planes, lines, 6, share, 384), const(width, 128), const(width, 128)],
                out_shape=[
                    sds((planes, lines, 6, share, 384), bf16),
                    sds((width, 128), f32),
                    sds((width, 128), f32),
                ],
                scratch_shapes=[pltpu.VMEM((width, 768), f32), pltpu.VMEM((wide, width), f32)],
                name="early",
                **kernel_params(9e9, 25e6),
            )(normed, *gmixed, *gmixed_bias, att_own, att_other, glow, glow_other, w_first)
            early_plane = sum_plane(after(early, gup_plane))
            gup_line = sum_line(gup_plane, lines)
            ties = (gup_plane, grad_down, early)
    grad_up = gup_line.transpose(1, 0, 2).reshape(share, hidden_width)

    late = pl.pallas_call(
        functools.partial(late_kernel, planes, share),
        grid_spec=pltpu.PrefetchScalarGridSpec(
            num_scalar_prefetch=1,
            grid=(count,),
            in_specs=[
                both_block(width),
                both_block(384),
                pl.BlockSpec((width, 384), lambda *_: (0, 2), pipeline_mode=pl.Buffered(1)),
                const(width, 128),
                const(width, 128),
                const(8, 384),
                const(8, 384),
                const(8, 384),
                const(16, width),
                const(8, width),
                const(chunks, 1, width),
            ],
            out_specs=const(planes, lines, 3, share, 384),
            scratch_shapes=[pltpu.VMEM((width, 384), f32)],
        ),
        out_shape=sds((planes, lines, 3, share, 384), bf16),
        name="late",
        **kernel_params(4e9, 10e6),
    )(side_arr, normed, after(gmixed[2], early_plane, gup_line), w_first, inner_sum, plain_sum, *gmixed_bias, pack, gvec, gup_bias)

    piece_spec = lambda side: pl.BlockSpec((1, 1, part, 384), lambda j, *_: (side, j, 0, 0))
    give_back = pl.pallas_call(
        give_kernel,
        grid=(count,),
        in_specs=[piece_spec(1)] * pairs + [const(width, 3 * wide)],
        out_specs=row_block(part, width),
        out_shape=sds((count, part, width), bf16),
        name="give_back",
        **kernel_params(2 * count * part * width * 3 * wide, 12e6),
    )(*gmixed[:2], after(gmixed[2], late), w_first)
    recv_back = partner(give_back)

    grad_input = pl.pallas_call(
        input_kernel,
        grid=(count,),
        in_specs=[piece_spec(0)] * pairs
        + [
            const(width, 3 * wide),
            row_block(part, width),
            row_block(part, width),
            row_block(part, width),
            const(16, width),
        ],
        out_specs=row_block(part, width),
        out_shape=sds((count, part, width), f32),
        name="input_grad",
        **kernel_params(2 * count * part * width * 3 * wide, 25e6),
    )(*gmixed, w_first, recv_back, tokens, glow, pack)

    late_plane = sum_plane(late, grad_input)
    unit_line = sum_line(jnp.concatenate([early_plane, late_plane], axis=1), lines)
    theirs = lax.dynamic_slice_in_dim(unit_line, 2 * (1 - side), 2, 0)
    theirs_late = lax.dynamic_slice_in_dim(unit_line, 7 - side, 1, 0)
    got = partner(jnp.concatenate([theirs, theirs_late, unit_line[8:]], axis=0))
    sizes = [share] * 6 + [2 * share, chunks * share]
    grad_qkv, grad_out, *vecs = pl.pallas_call(
        finish_kernel,
        grid_spec=pltpu.PrefetchScalarGridSpec(
            num_scalar_prefetch=1,
            grid=(1,),
            in_specs=[
                pl.BlockSpec((9, share, 384), lambda *_: (0, 0, 0)),
                pl.BlockSpec((4, share, 384), lambda *_: (0, 0, 0)),
            ],
            out_specs=[
                pl.BlockSpec((share, 6 * wide), lambda *_: (0, 0)),
                pl.BlockSpec((share, width), lambda *_: (0, 0)),
            ]
            + [pl.BlockSpec((1, size), lambda *_: (0, 0)) for size in sizes],
        ),
        out_shape=[sds((share, 6 * wide), f32), sds((share, width), f32)] + [sds((1, size), f32) for size in sizes],
        name="finish",
        **kernel_params(1e6, 1e6),
    )(side_arr, unit_line, got)
    vec = lambda slot, size: vecs[slot].reshape(size)

    return (
        out_tokens,
        grad_input,
        vec(0, share),
        vec(1, share),
        grad_qkv,
        vec(6, 2 * share),
        grad_out,
        vec(2, share),
        vec(3, share),
        vec(4, share),
        grad_up,
        vec(7, chunks * share),
        grad_down,
        vec(5, share),
        new_qkv,
        new_out,
        new_up,
        new_down,
    )


def specs_for(rows):
    flat = ("seq",) + (rows if isinstance(rows, tuple) else (rows,))
    grid, ids, vec, mat = P(rows, "seq", None), P(rows, "seq"), P(flat), P(flat, None)
    ins = (grid, ids, grid, vec, vec, mat, vec, mat, vec, vec, vec, mat, vec, mat, vec, mat, mat, mat, mat)
    outs = (grid, grid, vec, vec, mat, vec, mat, vec, vec, vec, mat, vec, mat, vec, mat, mat, mat, mat)
    return ins, outs


def solution(mesh):
    parts, rows = mesh.shape["seq"], mesh.shape["rows"]
    planes = 4
    if parts != 2 or rows % planes:
        ins, outs = specs_for("rows")
        return jax.shard_map(on_device, mesh=mesh, in_specs=ins, out_specs=outs, check_vma=False)
    lines = rows // planes
    finer = Mesh(mesh.devices.reshape(parts, lines, 2, 2), ("seq", "line", "y", "x"))
    ins, outs = specs_for(("line", "y", "x"))
    return jax.shard_map(
        functools.partial(pair_device, lines, planes), mesh=finer, in_specs=ins, out_specs=outs, check_vma=False
    )
```

```python
import functools

import jax
import jax.numpy as jnp
from jax import lax
from jax.experimental import pallas as pl
from jax.experimental.pallas import tpu as pltpu
from jax.sharding import Mesh
from jax.sharding import PartitionSpec as P

HEADS = 12
HEAD_DIM = 64
CLIPS = 6


def layer_norm(value, gain, bias):
    middle = jnp.mean(value, axis=-1, keepdims=True)
    centred = value - middle
    spread = jnp.mean(centred * centred, axis=-1, keepdims=True)
    return centred * lax.rsqrt(spread + 1e-06) * gain + bias


def exact_gelu(value):
    return jax.nn.gelu(value, approximate=False)


def permitted(seg_query, seg_key, pos_query, pos_key):
    same_clip = seg_query[:, :, None] == seg_key[:, None, :]
    open_key = (seg_key != CLIPS - 1)[:, None, :]
    diagonal = (pos_query[:, None] == pos_key[None, :])[None]
    return (same_clip & (open_key | diagonal))[:, :, None, :]


def scores(query_part, key_part):
    return 0.125 * jnp.einsum(
        "rqhe,rkhe->rqhk", query_part, key_part, preferred_element_type=jnp.float32
    )


def exponent(score_vals, allowed):
    return jnp.where(allowed, jnp.exp(jnp.where(allowed, score_vals, 0.0)), 0.0)


def on_device(
    tokens,
    segment_ids,
    cotangent,
    ln1_gain,
    ln1_bias,
    qkv_weight,
    qv_bias,
    out_weight,
    out_bias,
    ln2_gain,
    ln2_bias,
    up_weight,
    up_bias,
    down_weight,
    down_bias,
    avg_qkv,
    avg_out,
    avg_up,
    avg_down,
):
    f32 = jnp.float32
    bf16 = jnp.bfloat16
    rows_here, shard_len, width = tokens.shape
    count_rows = rows_here * shard_len
    own_pos = lax.axis_index("seq") * shard_len + jnp.arange(shard_len, dtype=jnp.int32)
    head_shape = (rows_here, shard_len, HEADS, HEAD_DIM)
    gain_one, bias_one, w_qkv, b_qv, w_out, b_out = (
        lax.all_gather(ln1_gain, ("seq", "rows"), axis=0, tiled=True),
        lax.all_gather(ln1_bias, ("seq", "rows"), axis=0, tiled=True),
        lax.all_gather(qkv_weight, ("seq", "rows"), axis=0, tiled=True),
        lax.all_gather(qv_bias, ("seq", "rows"), axis=0, tiled=True),
        lax.all_gather(out_weight, ("seq", "rows"), axis=0, tiled=True),
        lax.all_gather(out_bias, ("seq", "rows"), axis=0, tiled=True),
    )
    residual = tokens.astype(f32).reshape(count_rows, width)
    normed, norm_one_pull = jax.vjp(
        layer_norm, residual, gain_one.astype(f32), bias_one.astype(f32)
    )
    normed_low = normed.astype(bf16)
    mixed = jnp.dot(normed_low, w_qkv, preferred_element_type=f32)
    bias_qv = b_qv.astype(f32)
    query_heads = (mixed[:, :width] + bias_qv[:width]).astype(bf16).reshape(head_shape)
    key_heads = mixed[:, width : 2 * width].astype(bf16).reshape(head_shape)
    value_heads = (mixed[:, 2 * width :] + bias_qv[width:]).astype(bf16).reshape(head_shape)
    start_state = (jnp.zeros((rows_here, shard_len, HEADS), f32), jnp.zeros(head_shape, f32))
    piece_keys = lax.all_gather(key_heads, "seq", axis=1, tiled=True)
    piece_values = lax.all_gather(value_heads, "seq", axis=1, tiled=True)
    piece_seg = lax.all_gather(segment_ids, "seq", axis=1, tiled=True)
    piece_len = piece_keys.shape[1]
    block_len = min(piece_len, shard_len)

    def forward_advance(turn, state):
        totals, weighted = state
        offset = turn * block_len
        key_block = lax.dynamic_slice_in_dim(piece_keys, offset, block_len, 1)
        value_block = lax.dynamic_slice_in_dim(piece_values, offset, block_len, 1)
        seg_block = lax.dynamic_slice_in_dim(piece_seg, offset, block_len, 1)
        key_pos = offset + jnp.arange(block_len, dtype=jnp.int32)
        allowed = permitted(segment_ids, seg_block, own_pos, key_pos)
        expo = exponent(scores(query_heads, key_block), allowed)
        totals = totals + jnp.sum(expo, axis=-1)
        weighted = weighted + jnp.einsum(
            "rqhk,rkhe->rqhe", expo.astype(bf16), value_block, preferred_element_type=f32
        )
        return (totals, weighted)

    totals, weighted = lax.fori_loop(0, piece_len // block_len, forward_advance, start_state)
    attended = weighted / totals[..., None]
    attn_in = attended.reshape(count_rows, width).astype(bf16)
    middle = residual + jnp.dot(attn_in, w_out, preferred_element_type=f32) + b_out.astype(f32)
    gain_two, bias_two, w_up, b_up, w_down, b_down = (
        lax.all_gather(ln2_gain, ("seq", "rows"), axis=0, tiled=True),
        lax.all_gather(ln2_bias, ("seq", "rows"), axis=0, tiled=True),
        lax.all_gather(up_weight, ("seq", "rows"), axis=0, tiled=True),
        lax.all_gather(up_bias, ("seq", "rows"), axis=0, tiled=True),
        lax.all_gather(down_weight, ("seq", "rows"), axis=0, tiled=True),
        lax.all_gather(down_bias, ("seq", "rows"), axis=0, tiled=True),
    )
    normed_two, norm_two_pull = jax.vjp(
        layer_norm, middle, gain_two.astype(f32), bias_two.astype(f32)
    )
    normed_two_low = normed_two.astype(bf16)
    hidden_pre = jnp.dot(normed_two_low, w_up, preferred_element_type=f32) + b_up.astype(f32)
    hidden, gelu_pull = jax.vjp(exact_gelu, hidden_pre)
    hidden_low = hidden.astype(bf16)
    final = middle + jnp.dot(hidden_low, w_down, preferred_element_type=f32) + b_down.astype(f32)
    out_tokens = final.astype(bf16).reshape(tokens.shape)
    w_up_back, w_down_back = (
        lax.all_gather(up_weight, ("seq", "rows"), axis=0, tiled=True),
        lax.all_gather(down_weight, ("seq", "rows"), axis=0, tiled=True),
    )
    grad_out = cotangent.astype(f32).reshape(count_rows, width)
    grad_low = grad_out.astype(bf16)
    grad_down = jnp.einsum("nf,nd->fd", hidden_low, grad_low, preferred_element_type=f32)
    grad_down_b = jnp.sum(grad_low, axis=0, dtype=f32)
    grad_hidden = jnp.einsum("nd,fd->nf", grad_low, w_down_back, preferred_element_type=f32)
    (grad_pre,) = gelu_pull(grad_hidden)
    grad_pre_low = grad_pre.astype(bf16)
    grad_up = jnp.einsum("nd,nf->df", normed_two_low, grad_pre_low, preferred_element_type=f32)
    grad_up_b = jnp.sum(grad_pre_low, axis=0, dtype=f32)
    grad_normed_two = jnp.einsum("nf,df->nd", grad_pre_low, w_up_back, preferred_element_type=f32)
    grad_mid_norm, grad_gain_two, grad_bias_two = norm_two_pull(grad_normed_two)
    grad_mid = grad_out + grad_mid_norm
    mlp_sums = (
        lax.psum_scatter(grad_gain_two, ("seq", "rows"), scatter_dimension=0, tiled=True),
        lax.psum_scatter(grad_bias_two, ("seq", "rows"), scatter_dimension=0, tiled=True),
        lax.psum_scatter(grad_up, ("seq", "rows"), scatter_dimension=0, tiled=True),
        lax.psum_scatter(grad_up_b, ("seq", "rows"), scatter_dimension=0, tiled=True),
        lax.psum_scatter(grad_down, ("seq", "rows"), scatter_dimension=0, tiled=True),
        lax.psum_scatter(grad_down_b, ("seq", "rows"), scatter_dimension=0, tiled=True),
    )
    w_qkv_back, w_out_back = (
        lax.all_gather(qkv_weight, ("seq", "rows"), axis=0, tiled=True),
        lax.all_gather(out_weight, ("seq", "rows"), axis=0, tiled=True),
    )
    grad_mid_low = grad_mid.astype(bf16)
    grad_wout = jnp.einsum("nd,ne->de", attn_in, grad_mid_low, preferred_element_type=f32)
    grad_bout = jnp.sum(grad_mid_low, axis=0, dtype=f32)
    grad_att = jnp.einsum(
        "ne,de->nd", grad_mid_low, w_out_back, preferred_element_type=f32
    ).reshape(head_shape)
    grad_acc = (grad_att / totals[..., None]).astype(bf16)
    shift_low = (jnp.sum(grad_att * attended, axis=-1) / totals).astype(bf16)
    shift_wide = shift_low.astype(f32)
    query_piece_keys = lax.all_gather(key_heads, "seq", axis=1, tiled=True)
    query_piece_values = lax.all_gather(value_heads, "seq", axis=1, tiled=True)
    query_piece_seg = lax.all_gather(segment_ids, "seq", axis=1, tiled=True)
    piece_len = query_piece_keys.shape[1]
    query_block_len = min(piece_len, shard_len)

    def query_advance(turn, grad_query):
        offset = turn * query_block_len
        key_block = lax.dynamic_slice_in_dim(query_piece_keys, offset, query_block_len, 1)
        value_block = lax.dynamic_slice_in_dim(query_piece_values, offset, query_block_len, 1)
        seg_block = lax.dynamic_slice_in_dim(query_piece_seg, offset, query_block_len, 1)
        key_pos = offset + jnp.arange(query_block_len, dtype=jnp.int32)
        allowed = permitted(segment_ids, seg_block, own_pos, key_pos)
        expo = exponent(scores(query_heads, key_block), allowed)
        inner = jnp.einsum("rqhe,rkhe->rqhk", grad_acc, value_block, preferred_element_type=f32)
        grad_score = (expo * (inner - shift_wide[..., None])).astype(bf16)
        return grad_query + jnp.einsum(
            "rqhk,rkhe->rqhe", grad_score, key_block, preferred_element_type=f32
        )

    grad_query = lax.fori_loop(
        0, piece_len // query_block_len, query_advance, jnp.zeros(head_shape, f32)
    )
    key_start = (jnp.zeros(head_shape, f32), jnp.zeros(head_shape, f32))
    piece_queries = lax.all_gather(query_heads, "seq", axis=1, tiled=True)
    piece_grads = lax.all_gather(grad_acc, "seq", axis=1, tiled=True)
    key_piece_seg = lax.all_gather(segment_ids, "seq", axis=1, tiled=True)
    piece_shift = lax.all_gather(shift_low, "seq", axis=1, tiled=True)
    piece_len = piece_queries.shape[1]
    key_block_len = min(piece_len, shard_len)

    def key_advance(turn, state):
        grad_key, grad_value = state
        offset = turn * key_block_len
        query_block = lax.dynamic_slice_in_dim(piece_queries, offset, key_block_len, 1)
        grad_block = lax.dynamic_slice_in_dim(piece_grads, offset, key_block_len, 1)
        seg_block = lax.dynamic_slice_in_dim(key_piece_seg, offset, key_block_len, 1)
        shift_block = lax.dynamic_slice_in_dim(piece_shift, offset, key_block_len, 1).astype(f32)
        query_pos = offset + jnp.arange(key_block_len, dtype=jnp.int32)
        allowed = permitted(seg_block, segment_ids, query_pos, own_pos)
        expo = exponent(scores(query_block, key_heads), allowed)
        inner = jnp.einsum("rqhe,rkhe->rqhk", grad_block, value_heads, preferred_element_type=f32)
        grad_score = (expo * (inner - shift_block[..., None])).astype(bf16)
        grad_key = grad_key + jnp.einsum(
            "rqhk,rqhe->rkhe", grad_score, query_block, preferred_element_type=f32
        )
        grad_value = grad_value + jnp.einsum(
            "rqhk,rqhe->rkhe", expo.astype(bf16), grad_block, preferred_element_type=f32
        )
        return (grad_key, grad_value)

    grad_key, grad_value = lax.fori_loop(0, piece_len // key_block_len, key_advance, key_start)
    grad_q_low = (0.125 * grad_query).astype(bf16).reshape(count_rows, width)
    grad_k_low = (0.125 * grad_key).astype(bf16).reshape(count_rows, width)
    grad_v_low = grad_value.astype(bf16).reshape(count_rows, width)
    grad_mixed = jnp.concatenate([grad_q_low, grad_k_low, grad_v_low], axis=1)
    grad_wqkv = jnp.einsum("nd,ne->de", normed_low, grad_mixed, preferred_element_type=f32)
    grad_bqv = jnp.concatenate(
        [jnp.sum(grad_q_low, axis=0, dtype=f32), jnp.sum(grad_v_low, axis=0, dtype=f32)], axis=0
    )
    grad_normed = jnp.einsum("ne,de->nd", grad_mixed, w_qkv_back, preferred_element_type=f32)
    grad_res_norm, grad_gain_one, grad_bias_one = norm_one_pull(grad_normed)
    grad_input = (grad_mid + grad_res_norm).reshape(tokens.shape)
    attn_sums = (
        lax.psum_scatter(grad_gain_one, ("seq", "rows"), scatter_dimension=0, tiled=True),
        lax.psum_scatter(grad_bias_one, ("seq", "rows"), scatter_dimension=0, tiled=True),
        lax.psum_scatter(grad_wqkv, ("seq", "rows"), scatter_dimension=0, tiled=True),
        lax.psum_scatter(grad_bqv, ("seq", "rows"), scatter_dimension=0, tiled=True),
        lax.psum_scatter(grad_wout, ("seq", "rows"), scatter_dimension=0, tiled=True),
        lax.psum_scatter(grad_bout, ("seq", "rows"), scatter_dimension=0, tiled=True),
    )
    new_qkv = 0.9 * avg_qkv + 0.1 * qkv_weight.astype(f32)
    new_out = 0.9 * avg_out + 0.1 * out_weight.astype(f32)
    new_up = 0.9 * avg_up + 0.1 * up_weight.astype(f32)
    new_down = 0.9 * avg_down + 0.1 * down_weight.astype(f32)
    return (
        out_tokens,
        grad_input,
        attn_sums[0],
        attn_sums[1],
        attn_sums[2],
        attn_sums[3],
        attn_sums[4],
        attn_sums[5],
        mlp_sums[0],
        mlp_sums[1],
        mlp_sums[2],
        mlp_sums[3],
        mlp_sums[4],
        mlp_sums[5],
        new_qkv,
        new_out,
        new_up,
        new_down,
    )


f32 = jnp.float32
bf16 = jnp.bfloat16
NT = (((1,), (1,)), ((), ()))
LOG2E = 1.4426950408889634
SCORE = 0.125 * LOG2E
BIG = 16384.0
VMEM_BYTES = 63 * 1024 * 1024
TK_B, TQ_B, T_SIDE = 512, 512, 256
LANE_LOG = 41
LANE_PAD = 44


def kernel_params(flops, bytes_accessed, transcendentals=0, order=("arbitrary",)):
    return dict(
        compiler_params=pltpu.CompilerParams(
            vmem_limit_bytes=VMEM_BYTES, dimension_semantics=order
        ),
        cost_estimate=pl.CostEstimate(
            flops=int(flops), bytes_accessed=int(bytes_accessed), transcendentals=int(transcendentals)
        ),
    )


def standardise(value):
    middle = jnp.mean(value, axis=-1, keepdims=True)
    centred = value - middle
    spread = jnp.mean(centred * centred, axis=-1, keepdims=True)
    rstd = lax.rsqrt(spread + 1e-06)
    return centred * rstd, rstd


def norm_pull(grad_normed, gain, xhat, rstd):
    scaled = grad_normed * gain
    first = jnp.mean(scaled, axis=-1, keepdims=True)
    second = jnp.mean(scaled * xhat, axis=-1, keepdims=True)
    return rstd * (scaled - first - xhat * second)


def gelu_pair(x):
    size = jnp.abs(x)
    base = 1.0 + 0.23164189 * size
    t = 1.0 / base
    bell = jnp.exp2(x * x * (-0.5 * LOG2E))
    poly = t * (0.127414796 + t * (-0.142248368 + t * (0.7107068705 + t * (-0.7265760135 + t * 0.5307027145))))
    tail = poly * bell
    phi = jnp.where(x >= 0.0, 1.0 - tail, tail)
    return x * phi, phi + x * bell * 0.3989422804014327


def lane_masks():
    lane = lax.broadcasted_iota(jnp.int32, (1, 128), 1)
    low = jnp.where(lane < HEAD_DIM, 1.0, 0.0)
    return low.astype(bf16), (1.0 - low).astype(bf16)


def prepare_kernel(share, side_ref, w_ref, up_ref, out_ref, down_ref, *refs):
    vectors, (mine_ref, give_ref, second_ref) = refs[:-3], refs[-3:]
    width = down_ref.shape[1]
    blocks = up_ref.shape[1] // width
    for block in range(blocks):
        second_ref[block * share : (block + 1) * share] = up_ref[:, block * width : (block + 1) * width]
    second_ref[blocks * share : (blocks + 1) * share] = out_ref[...]
    second_ref[(blocks + 1) * share :] = down_ref[...]
    wide = w_ref.shape[1] // 6
    pairs = wide // 128
    for target, side in ((mine_ref, side_ref[0]), (give_ref, 1 - side_ref[0])):
        for pair in range(pairs):
            for kind in range(3):
                start = pl.multiple_of(kind * 2 * wide + side * wide + pair * 128, 128)
                at = 384 * pair + 128 * kind
                target[:, at : at + 128] = w_ref[:, pl.ds(start, 128)]
    lane = lax.broadcasted_iota(jnp.int32, (share, 128), 1)
    small = jnp.zeros((share, 128), f32)
    column = 0
    for ref in vectors:
        row = jnp.broadcast_to(ref[...].astype(f32), (8, ref.shape[1])).T
        for start in range(0, ref.shape[1], share):
            small = jnp.where(lane == column, row[start : start + share, 0:1], small)
            column += 1
    small = small.astype(bf16)
    mine_ref[:, 3 * wide :] = small
    give_ref[:, 3 * wide :] = small


def project_kernel(
    share, side_ref, own_ref, other_ref, w_ref, small_ref, normed_ref, mixed_ref, pack_ref, shift_s
):
    which, turn = pl.program_id(0), pl.program_id(1)
    wide = shift_s.shape[1] // 3
    pairs = wide // 128

    @pl.when((which == 0) & (turn == 0))
    def _():
        small = small_ref[...].astype(f32).T
        pack_ref[...] = small[0:16]
        shift_s[...] = jnp.zeros_like(shift_s)
        spot = lax.broadcasted_iota(jnp.int32, (wide, wide), 0)
        target = lax.broadcasted_iota(jnp.int32, (wide, wide), 1) + side_ref[0] * wide
        sums = [jnp.zeros((16, wide), f32), jnp.zeros((16, wide), f32)]
        for part in range(2):
            wanted = lax.div(spot, share) * (2 * share) + part * share + lax.rem(spot, share)
            chosen = jnp.where(wanted == target, 1.0, 0.0).astype(bf16)
            for kind in range(2):
                values = small[6 + part : 7 + part, kind * wide : (kind + 1) * wide]
                values = jnp.broadcast_to(values, (16, wide)).astype(bf16)
                sums[kind] += jnp.dot(values, chosen, preferred_element_type=f32)
        for pair in range(pairs):
            lanes = slice(128 * pair, 128 * pair + 128)
            shift_s[:, 384 * pair : 384 * pair + 128] = sums[0][0:1, lanes]
            shift_s[:, 384 * pair + 256 : 384 * pair + 384] = sums[1][0:1, lanes]

    tiles = 2
    size = normed_ref.shape[2] // tiles

    def normed_tile(i):
        rows = slice(i * size, (i + 1) * size)
        value = jnp.where(which == 0, own_ref[0, rows], other_ref[0, rows]).astype(f32)
        xhat, _ = standardise(value)
        normed = (xhat * pack_ref[0:1, :] + pack_ref[1:2, :]).astype(bf16)
        normed_ref[0, 0, rows] = normed
        return normed

    normed = normed_tile(0)
    for i in range(tiles):
        mixed = jnp.dot(normed, w_ref[...], preferred_element_type=f32) + shift_s[...]
        mixed = mixed.astype(bf16)
        if i + 1 < tiles:
            normed = normed_tile(i + 1)
        for pair in range(pairs):
            lanes = slice(384 * pair, 384 * pair + 384)
            mixed_ref[pair, 0, 0, i * size : (i + 1) * size] = mixed[:, lanes]


def attend_kernel(base, flag_ref, mixed_ref, qx_ref, kx_ref, *rest):
    own_ref, other_ref, ext_ref, q_s, k_s, v_s, acc_s = rest[-7:]
    row = base + pl.program_id(0)
    length = q_s.shape[1]
    heads = q_s.shape[0]
    half = length // 2
    low, high = lane_masks()
    qx, kx = qx_ref[0], kx_ref[0]
    q_low, q_high, k_low, k_high = qx * low, qx * high, kx * low, kx * high
    for pair in range(heads // 2):
        q = mixed_ref[pair, :, 0, :, 0:128].reshape(length, 128)
        k = mixed_ref[pair, :, 0, :, 128:256].reshape(length, 128)
        v = mixed_ref[pair, :, 0, :, 256:384].reshape(length, 128)
        q_s[2 * pair] = q * low + q_high
        q_s[2 * pair + 1] = q * high + q_low
        k_s[2 * pair] = k * low + k_high
        k_s[2 * pair + 1] = k * high + k_low
        v_s[2 * pair] = v * low + high
        v_s[2 * pair + 1] = v * high + low

    def block(q_start, k_start, size, fresh):
        q_at, k_at = slice(q_start, q_start + size), slice(k_start, k_start + size)
        for head in range(heads):
            score = lax.dot_general(q_s[head, q_at, :], k_s[head, k_at, :], NT, preferred_element_type=f32)
            expo = jnp.exp2(score * SCORE).astype(bf16)
            part = jnp.dot(expo, v_s[head, k_at, :], preferred_element_type=f32)
            if fresh:
                acc_s[head, q_at, :] = part
            else:
                acc_s[head, q_at, :] += part

    for start in range(0, length, half):
        block(start, start, half, True)
    pieces = length // T_SIDE
    for qi in range(pieces):
        for ki in range(pieces):
            if qi * T_SIDE // half != ki * T_SIDE // half:

                @pl.when(flag_ref[row, qi * pieces + ki] != 0)
                def _(qi=qi, ki=ki):
                    block(qi * T_SIDE, ki * T_SIDE, T_SIDE, False)

    lane = lax.broadcasted_iota(jnp.int32, (half, 128), 1)
    first_half = lane < HEAD_DIM
    spot = lane % HEAD_DIM
    for pair in range(heads // 2):
        for side in range(2):
            rows = slice(side * half, (side + 1) * half)
            first, second = acc_s[2 * pair, rows], acc_s[2 * pair + 1, rows]
            top = jnp.where(first_half, first, second)
            crossed = jnp.where(first_half, second, first)
            totals = pltpu.roll(crossed, HEAD_DIM, 1)
            target = own_ref if side == 0 else other_ref
            target[pair, 0] = (top / totals).astype(bf16)
            lse = -8.0 * jnp.log(crossed)
            lse_a = lse.astype(bf16).astype(f32)
            lse_b = (lse - lse_a).astype(bf16).astype(f32)
            ext = jnp.where(
                spot == LANE_LOG,
                lse_a,
                jnp.where(
                    spot == LANE_LOG + 1,
                    lse_b,
                    jnp.where(spot == LANE_LOG + 2, lse - lse_a - lse_b, qx[rows].astype(f32)),
                ),
            )
            ext_ref[pair, side, 0] = ext.astype(bf16)


def join_lanes(ref):
    return jnp.concatenate([ref[i, 0] for i in range(ref.shape[0])], axis=1)


def mlp_kernel(
    planes, share, spot_ref, x_ref, mine_ref, recv_ref, wo_ref, up_ref, near_own, far_own, near_other, far_other,
    grad_ref, pack_ref, upb_ref,
    out_ref, glow_ref, gdown_own, gdown_other, gup_own, gup_other, gbias_ref, gvec_ref,
    down_s, up_s, wo_v, up_v, down_v, gd_own, gd_other, gu_own, gu_other, load_sem, store_sem,
):
    turn = pl.program_id(0)
    side, x_at = spot_ref[0], spot_ref[2]
    chunks, size = down_s.shape[0], down_s.shape[2]
    load_out = pltpu.make_async_copy(wo_ref, wo_v, load_sem.at[0])
    load_up = pltpu.make_async_copy(up_ref, up_v, load_sem.at[1])
    load_down = []
    for index, piece in enumerate((near_own, far_own, near_other, far_other)):
        at_side = 1 - side if index // 2 else side
        column = 1 - x_at if index % 2 else x_at
        for i in range(2):
            target = down_v.at[at_side, :, i, column]
            load_down.append(pltpu.make_async_copy(piece.at[i], target, load_sem.at[2 + 2 * index + i]))

    @pl.when(turn == 0)
    def _():
        load_out.start()
        load_up.start()
        for load in load_down:
            load.start()
        down_s[...] = jnp.zeros_like(down_s)
        up_s[...] = jnp.zeros_like(up_s)
        gbias_ref[...] = jnp.zeros_like(gbias_ref)
        gvec_ref[...] = jnp.zeros_like(gvec_ref)
        load_out.wait()

    middle = (
        x_ref[0].astype(f32)
        + jnp.dot(join_lanes(mine_ref), wo_v[side], preferred_element_type=f32)
        + jnp.dot(join_lanes(recv_ref), wo_v[1 - side], preferred_element_type=f32)
        + pack_ref[2:3, :]
    )
    xhat, rstd = standardise(middle)
    normed = (xhat * pack_ref[3:4, :] + pack_ref[4:5, :]).astype(bf16)
    normed_t = normed.T
    grad = grad_ref[0]
    grad_t = grad.T
    total = middle + pack_ref[5:6, :]

    @pl.when(turn == 0)
    def _():
        load_up.wait()
        for load in load_down:
            load.wait()

    half_lines = down_v.shape[1] // (chunks // 2)

    def down_chunk(f):
        line = (f % (chunks // 2)) * half_lines
        return down_v[f // (chunks // 2), line : line + half_lines].reshape(size, down_v.shape[-1])

    def first_layer(f):
        at = slice(f * size, (f + 1) * size)
        return jnp.dot(normed, up_v[:, at], preferred_element_type=f32) + upb_ref[f : f + 1, :]

    gnormed = None
    pre = first_layer(0)
    for f in range(chunks):
        at = slice(f * size, (f + 1) * size)
        hidden, slope = gelu_pair(pre)
        ghidden = lax.dot_general(grad, down_chunk(f), NT, preferred_element_type=f32)
        if f + 1 < chunks:
            pre = first_layer(f + 1)
        hidden = hidden.astype(bf16)
        gpre = (ghidden * slope).astype(bf16)
        total = total + jnp.dot(hidden, down_chunk(f), preferred_element_type=f32)
        part = lax.dot_general(gpre, up_v[:, at], NT, preferred_element_type=f32)
        gnormed = part if gnormed is None else gnormed + part
        down_s[f] += jnp.dot(grad_t, hidden, preferred_element_type=f32)
        up_s[f] += jnp.dot(normed_t, gpre, preferred_element_type=f32)
        gbias_ref[f] += jnp.sum(gpre.astype(f32), axis=0, keepdims=True)
    out_ref[0] = total.astype(bf16)
    gmid = grad.astype(f32) + norm_pull(gnormed, pack_ref[3:4, :], xhat, rstd)
    low = gmid.astype(bf16)
    glow_ref[0] = low
    gvec_ref[0:1, :] += jnp.sum(gnormed * xhat, axis=0, keepdims=True)
    gvec_ref[1:2, :] += jnp.sum(gnormed, axis=0, keepdims=True)
    gvec_ref[2:3, :] += jnp.sum(low.astype(f32), axis=0, keepdims=True)
    gvec_ref[3:4, :] += jnp.sum(grad.astype(f32), axis=0, keepdims=True)

    @pl.when(turn == pl.num_programs(0) - 1)
    def _():
        half = chunks // 2
        rows = chunks * share
        per_chunk = size // rows
        lines_chunk = per_chunk // planes
        for f in range(chunks):
            whole = down_s[f].astype(bf16).T
            at_line = (f % half) * lines_chunk
            span = slice(at_line, at_line + lines_chunk)
            for target, result, wanted in ((gd_own, gdown_own, f // half), (gd_other, gdown_other, 1 - f // half)):

                @pl.when(side == wanted)
                def _(target=target, result=result, whole=whole, f=f, at_line=at_line, span=span):
                    for i in range(per_chunk):
                        target[i % planes, at_line + i // planes] = whole[i * rows : (i + 1) * rows]
                    pltpu.make_async_copy(target.at[:, span], result.at[:, span], store_sem.at[f]).start()

        wide = up_s.shape[1] // 2
        ups = ((gu_own, gup_own, side * wide), (gu_other, gup_other, (1 - side) * wide))
        for which, (target, result, base) in enumerate(ups):
            for f in range(chunks):
                for at in range(wide // share):
                    start = pl.multiple_of(base + at * share, 8)
                    target[at % planes, at // planes, f] = up_s[f, pl.ds(start, share), :].astype(bf16)
                pltpu.make_async_copy(
                    target.at[:, :, f], result.at[:, :, f], store_sem.at[chunks * (1 + which) + f]
                ).start()
        for f in range(chunks):
            span = slice(0, lines_chunk)
            pltpu.make_async_copy(gd_own.at[:, span], gdown_own.at[:, span], store_sem.at[f]).wait()
        for which, (target, result, base) in enumerate(ups):
            for f in range(chunks):
                pltpu.make_async_copy(
                    target.at[:, :, f], result.at[:, :, f], store_sem.at[chunks * (1 + which) + f]
                ).wait()


def attend_back_kernel(
    flag_ref, side_ref, mixed_ref, ext_ref, att_own, att_other, own_ref, other_ref, wo_ref, kx_ref,
    gmixed_ref, gbias_ref,
    q_s, d_s, k_s, v_s, kt_s, gq_s, gk_s, gv_s,
):
    row = pl.program_id(0)
    length = k_s.shape[0]
    half = length // 2
    low, high = lane_masks()
    lane = lax.broadcasted_iota(jnp.int32, (1, 128), 1)
    spot = lane % HEAD_DIM
    square_row = lax.broadcasted_iota(jnp.int32, (128, 128), 0) < HEAD_DIM
    square_col = lax.broadcasted_iota(jnp.int32, (128, 128), 1) < HEAD_DIM
    crossing = jnp.where(square_row == square_col, 0.0, -1.0).astype(bf16)
    one_hot_a = jnp.where(spot == 0, 1.0, 0.0)
    one_hot_b = jnp.where(spot == 1, 1.0, 0.0)
    v_ext = (one_hot_a + one_hot_b).astype(bf16)

    @pl.when(row == 0)
    def _():
        gbias_ref[...] = jnp.zeros_like(gbias_ref)

    mixed_at = lambda lanes: mixed_ref[0, :, 0, :, lanes].reshape(length, 128)
    q, k = mixed_at(slice(0, 128)), mixed_at(slice(128, 256))
    ext = ext_ref[0, :, 0].reshape(length, 128)
    k_s[:, 0:128] = k
    k_s[:, 128:256] = kx_ref[0]
    v_s[:, 0:128] = mixed_at(slice(256, 384))
    v_s[:, 128:256] = jnp.broadcast_to(v_ext, (length, 128))
    for head, (mine, other) in enumerate(((low, high), (high, low))):
        q_part, ext_part = q * mine, ext * other
        for i in range(length // TQ_B):
            at = slice(i * TQ_B, (i + 1) * TQ_B)
            rows = slice(head * TQ_B, (head + 1) * TQ_B)
            q_s[i, rows, 0:128] = q_part[at]
            q_s[i, rows, 128:256] = ext_part[at]
    for side in range(2):
        gates = own_ref[0] if side == 0 else other_ref[0]
        d = lax.dot_general(gates, wo_ref[...], NT, preferred_element_type=f32)
        moved = d * (att_own if side == 0 else att_other)[0, 0].astype(f32)
        moved_a = moved.astype(bf16)
        moved_b = (moved - moved_a.astype(f32)).astype(bf16)
        shift = jnp.dot(moved_a, crossing, preferred_element_type=f32) + jnp.dot(
            moved_b, crossing, preferred_element_type=f32
        )
        shift_a = shift.astype(bf16).astype(f32)
        dx = (shift_a * one_hot_a + (shift - shift_a) * one_hot_b).astype(bf16)
        d = d.astype(bf16)
        tile = min(TQ_B, half)
        for head, (mine, other) in enumerate(((low, high), (high, low))):
            d_part, dx_part = d * mine, dx * other
            for i in range(half // tile):
                at = slice(i * tile, (i + 1) * tile)
                start = side * half + i * tile
                rows = slice(head * TQ_B + start % TQ_B, head * TQ_B + start % TQ_B + tile)
                d_s[start // TQ_B, rows, 0:128] = d_part[at]
                d_s[start // TQ_B, rows, 128:256] = dx_part[at]
    for i in range(length // TK_B):
        kt_s[i] = k[i * TK_B : (i + 1) * TK_B].T
    query_blocks = length // TQ_B

    def block(k_start, q_start, size, fresh):
        k_at = slice(k_start, k_start + size)
        tile, inside = q_start // TQ_B, q_start % TQ_B
        key_tile, key_inside = k_start // TK_B, k_start % TK_B
        q_rows = [slice(head * TQ_B + inside, head * TQ_B + inside + size) for head in range(2)]
        probs, grads = [], []
        for rows in q_rows:
            score = lax.dot_general(k_s[k_at, :], q_s[tile, rows, :], NT, preferred_element_type=f32)
            inner = lax.dot_general(v_s[k_at, :], d_s[tile, rows, :], NT, preferred_element_type=f32)
            prob = jnp.exp2(score * SCORE)
            probs.append(prob.astype(bf16))
            grads.append((prob * inner).astype(bf16))
        for head in range(2):
            at = slice(head * HEAD_DIM, (head + 1) * HEAD_DIM)
            keys = kt_s[key_tile, at, key_inside : key_inside + size]
            part = jnp.dot(keys, grads[head], preferred_element_type=f32)
            if fresh:
                gq_s[tile, at, inside : inside + size] = part
            else:
                gq_s[tile, at, inside : inside + size] += part
        for target, left, right in ((gv_s, probs, d_s), (gk_s, grads, q_s)):
            if size == TQ_B:
                part = jnp.dot(jnp.concatenate(left, axis=1), right[tile, :, 0:128], preferred_element_type=f32)
            else:
                part = jnp.dot(left[0], right[tile, q_rows[0], 0:128], preferred_element_type=f32)
                part = part + jnp.dot(left[1], right[tile, q_rows[1], 0:128], preferred_element_type=f32)
            if fresh:
                target[k_at, :] = part
            else:
                target[k_at, :] += part

    for i in range(query_blocks):
        block(i * TQ_B, i * TQ_B, TQ_B, True)
    pieces = length // T_SIDE
    for ki in range(pieces):
        for qi in range(pieces):
            if ki * T_SIDE // TK_B != qi * T_SIDE // TQ_B:

                @pl.when(flag_ref[row, ki * pieces + qi] != 0)
                def _(ki=ki, qi=qi):
                    block(ki * T_SIDE, qi * T_SIDE, T_SIDE, False)

    for i in range(query_blocks):
        gq = (0.125 * gq_s[i].T).astype(bf16)
        for start in range(0, TQ_B, min(TQ_B, half)):
            at = i * TQ_B + start
            size = min(TQ_B, half)
            gmixed_ref[at // half, 0, at % half : at % half + size, 0:128] = gq[start : start + size]
        gbias_ref[0:1, 0:128] += jnp.sum(gq.astype(f32), axis=0, keepdims=True)
    gk = (0.125 * gk_s[...]).astype(bf16)
    gv = gv_s[...].astype(bf16)
    gbias_ref[0:1, 128:256] += jnp.sum(gk.astype(f32), axis=0, keepdims=True)
    gbias_ref[0:1, 256:384] += jnp.sum(gv.astype(f32), axis=0, keepdims=True)
    for side in range(2):
        gmixed_ref[side, 0, :, 128:256] = gk[side * half : (side + 1) * half]
        gmixed_ref[side, 0, :, 256:384] = gv[side * half : (side + 1) * half]


def weight_dot(normed_ref, *piece_refs):
    normed_t = jnp.concatenate([normed_ref[0, 0], normed_ref[1, 0]], axis=0).T
    sides = []
    for side in range(2):
        sides.append(jnp.concatenate([ref[side, 0] for ref in piece_refs], axis=1))
    return jnp.dot(normed_t, jnp.concatenate(sides, axis=0), preferred_element_type=f32)


def fold_lanes(value):
    total = value[:, 0:128]
    for at in range(128, value.shape[1], 128):
        total = total + value[:, at : at + 128]
    return total


def early_kernel(
    planes, share, normed_ref, g0_ref, g1_ref, b0_ref, b1_ref, mine_ref, other_ref, low_ref, low_other_ref, w_ref,
    unit_ref, first_ref, second_ref, acc_s, out_s,
):
    turn = pl.program_id(0)

    @pl.when(turn == 0)
    def _():
        acc_s[...] = jnp.zeros_like(acc_s)
        out_s[...] = jnp.zeros_like(out_s)

    acc_s[...] += weight_dot(normed_ref, g0_ref, g1_ref)
    across = (((0,), (0,)), ((), ()))
    out_s[...] += lax.dot_general(
        join_lanes(mine_ref), low_ref[0], across, preferred_element_type=f32
    ) + lax.dot_general(join_lanes(other_ref), low_other_ref[0], across, preferred_element_type=f32)

    @pl.when(turn == pl.num_programs(0) - 1)
    def _():
        weights = w_ref[...].astype(f32)
        sums = jnp.concatenate([b0_ref[0:1, :], b1_ref[0:1, :]], axis=1)
        first_ref[...] = fold_lanes(weights * acc_s[...])
        second_ref[...] = fold_lanes(weights * sums)
        count = out_s.shape[0] // share
        for at in range(count):
            spot = (at % planes, at // planes)
            for half in range(2):
                lanes = slice(384 * half, 384 * half + 384)
                for side in range(2):
                    start = (side * count + at) * share
                    unit_ref[spot + (2 * side + half,)] = acc_s[start : start + share, lanes].astype(bf16)
                unit_ref[spot + (4 + half,)] = out_s[at * share : (at + 1) * share, lanes].astype(bf16)


def scatter_rows(vector, step, offset, owners):
    n = vector.shape[1]
    owner = lax.broadcasted_iota(jnp.int32, (owners, n), 0) - offset
    mask = lax.div(lax.broadcasted_iota(jnp.int32, (owners, n), 1), step) == owner
    spread = jnp.where(mask, jnp.broadcast_to(vector, (owners, n)), 0.0).astype(bf16)
    lane = lax.rem(lax.broadcasted_iota(jnp.int32, (128, n), 1), step)
    chosen = jnp.where(lane == lax.broadcasted_iota(jnp.int32, (128, n), 0), 1.0, 0.0).astype(bf16)
    return lax.dot_general(spread, chosen, NT, preferred_element_type=f32)


def late_kernel(
    planes, share, side_ref, normed_ref, g_ref, w_ref, first_ref, second_ref, b0_ref, b1_ref, b2_ref, pack_ref,
    gvec_ref, gup_ref, unit_ref, acc_s,
):
    turn = pl.program_id(0)

    @pl.when(turn == 0)
    def _():
        acc_s[...] = jnp.zeros_like(acc_s)

    acc_s[...] += weight_dot(normed_ref, g_ref)

    @pl.when(turn == pl.num_programs(0) - 1)
    def _():
        side = side_ref[0]
        weights = w_ref[...].astype(f32)
        width = weights.shape[0]
        owners = width // share
        count = owners // 2
        inner = first_ref[...] + fold_lanes(weights * acc_s[...])
        plain = second_ref[...] + fold_lanes(weights * b2_ref[0:1, :])
        inner = jnp.sum(inner.T, axis=0, keepdims=True)
        plain = jnp.sum(plain.T, axis=0, keepdims=True)
        gain, bias = pack_ref[0:1, :], pack_ref[1:2, :]
        g_gain = (inner - bias * plain) / gain
        biases = (b0_ref, b1_ref, b2_ref)
        query = jnp.concatenate([b[0:1, 0:128] for b in biases], axis=1)
        value = jnp.concatenate([b[0:1, 256:384] for b in biases], axis=1)
        chunks = gup_ref.shape[0]
        rows_up = chunks * share
        up_bias = None
        for f in range(chunks):
            part = scatter_rows(gup_ref[f], rows_up, f * (width // rows_up), owners)
            up_bias = part if up_bias is None else up_bias + part
        wide = width // 2
        first_owner = side * (wide // (2 * share))
        qv_bias = scatter_rows(query, 2 * share, first_owner, owners) + scatter_rows(
            value, 2 * share, first_owner + count, owners
        )
        plain_rows = lambda vec: scatter_rows(vec, share, 0, owners)
        slots = [
            plain_rows(g_gain),
            plain_rows(plain),
            plain_rows(gvec_ref[2:3, :]),
            plain_rows(gvec_ref[0:1, :]),
            plain_rows(gvec_ref[1:2, :]),
            plain_rows(gvec_ref[3:4, :]),
            qv_bias,
            up_bias,
            jnp.zeros((owners, 128), f32),
        ]
        lines_of = [jnp.concatenate(slots[3 * i : 3 * i + 3], axis=1) for i in range(3)]
        blank = jnp.zeros((5, 384), f32)
        for at in range(count):
            spot = (at % planes, at // planes)
            small = []
            for half in range(2):
                owner = half * count + at
                start = owner * share
                unit_ref[spot + (half,)] = acc_s[start : start + share, :].astype(bf16)
                small += [line[owner : owner + 1, :] for line in lines_of] + [blank]
            small.append(jnp.zeros((share - 16, 384), f32))
            unit_ref[spot + (2,)] = jnp.concatenate(small, axis=0).astype(bf16)


def finish_kernel(side_ref, line_ref, got_ref, qkv_ref, out_ref, *vec_refs):
    side = side_ref[0]
    wide = qkv_ref.shape[1] // 6
    for pair in range(wide // 128):
        own = line_ref[2 * side + pair] if pair < 2 else line_ref[6 + side]
        other = got_ref[pair]
        for kind in range(3):
            lanes = slice(128 * kind, 128 * kind + 128)
            for half in range(2):
                at = kind * 2 * wide + half * wide + 128 * pair
                qkv_ref[:, at : at + 128] = jnp.where(side == half, own[:, lanes], other[:, lanes])
    out_ref[:, 0:384] = line_ref[4]
    out_ref[:, 384:768] = line_ref[5]
    start = pl.multiple_of(8 * side, 8)
    small = line_ref[8, pl.ds(start, 8), :] + got_ref[3, pl.ds(start, 8), :]
    for slot, ref in enumerate(vec_refs):
        at = 128 * (slot % 3)
        ref[...] = small[slot // 3 : slot // 3 + 1, at : at + ref.shape[1]]


def back_through(pieces, w_ref, side):
    total = None
    for i, piece in enumerate(pieces):
        part = lax.dot_general(
            piece[side, 0], w_ref[:, 384 * i : 384 * i + 384], NT, preferred_element_type=f32
        )
        total = part if total is None else total + part
    return total


def give_kernel(*refs):
    pieces, (w_ref, out_ref) = refs[:-2], refs[-2:]
    out_ref[0] = back_through(pieces, w_ref, 0).astype(bf16)


def input_kernel(*refs):
    pieces, (w_ref, recv_ref, x_ref, gmid_ref, pack_ref, ginput_ref) = refs[:-6], refs[-6:]
    gnormed = back_through(pieces, w_ref, 0) + recv_ref[0].astype(f32)
    xhat, rstd = standardise(x_ref[0].astype(f32))
    ginput_ref[0] = gmid_ref[0].astype(f32) + norm_pull(gnormed, pack_ref[0:1, :], xhat, rstd)


def partner(value):
    return lax.ppermute(value, "seq", [(0, 1), (1, 0)])


def exchange(value, axis):
    return lax.all_to_all(value, axis, 0, 0, tiled=True)


def spread_line(value, lines):
    return exchange(jnp.broadcast_to(value[None], (lines,) + value.shape), "line")


def flip(value, axis):
    return lax.ppermute(value, axis, [(0, 1), (1, 0)])


def in_order(index, own, received):
    return jnp.where(index == 0, jnp.stack([own, received]), jnp.stack([received, own]))


def spread_first(one, two):
    return lax.optimization_barrier((flip(one, "x"), flip(two, "y")))


def spread_second(one, two, got_one, got_two):
    near_one = in_order(lax.axis_index("x"), one, got_one)
    near_two = in_order(lax.axis_index("y"), two, got_two)
    near_one, near_two = lax.optimization_barrier((near_one, near_two))
    return (near_one, flip(near_one, "y")), (near_two, flip(near_two, "x"))


def spread_plane(one, two):
    return spread_second(one, two, *spread_first(one, two))


def after(value, *others):
    return lax.optimization_barrier((value,) + others)[0]


def assemble_kernel(far_plane, spot_ref, *refs):
    pieces, targets, scratch, (in_sem, out_sem) = refs[:2], refs[-6:-4], refs[-4:-2], refs[-2:]
    up_ref, out_ref = targets
    side, y = spot_ref[0], spot_ref[1]
    width = out_ref.shape[-1]
    blocks = up_ref.shape[-1] // width
    loads = [pltpu.make_async_copy(pieces[i], scratch[i], in_sem.at[i]) for i in range(2)]
    for load in loads:
        load.start()
    stores = []

    def send(source, target):
        stores.append(pltpu.make_async_copy(source, target, out_sem.at[len(stores)]))
        stores[-1].start()

    row = 1 - y if far_plane else y
    for index in range(2):
        loads[index].wait()
        at_side = 1 - side if index else side
        held = scratch[index]
        for i in range(2):
            for block in range(blocks):
                lanes = slice(block * width, (block + 1) * width)
                send(held.at[i, :, block], up_ref.at[at_side, :, row, i, :, lanes])
            send(held.at[i, :, blocks], out_ref.at[at_side, :, row, i])
    for copy in stores:
        copy.wait()


def assemble(spot, far_plane, pieces, targets, shapes):
    anywhere = pl.BlockSpec(memory_space=pl.ANY)
    blocks = pieces[0].shape[2]
    return pl.pallas_call(
        functools.partial(assemble_kernel, far_plane),
        grid_spec=pltpu.PrefetchScalarGridSpec(
            num_scalar_prefetch=1,
            grid=(1,),
            in_specs=[anywhere] * (2 + len(targets)),
            out_specs=[anywhere] * 2,
            scratch_shapes=[pltpu.VMEM(p.shape, bf16) for p in pieces]
            + [pltpu.SemaphoreType.DMA((2,)), pltpu.SemaphoreType.DMA((4 * blocks,))],
        ),
        out_shape=shapes,
        input_output_aliases={3 + i: i for i in range(len(targets))},
        name="assemble",
        **kernel_params(1e6, 12e6),
    )(spot, *pieces, *targets)


def sum_plane(value, *waits):
    received = exchange(value, ("y", "x"))
    if waits:
        received = after(received, *waits)
    return jnp.sum(received.astype(f32), axis=0)


def send_line(value, lines):
    here = lax.axis_index("line")
    pieces = []
    for shift in range(1, lines):
        piece = lax.dynamic_index_in_dim(value, (here + shift) % lines, 0, keepdims=False).astype(bf16)
        pieces.append(lax.ppermute(piece, "line", [(i, (i + shift) % lines) for i in range(lines)]))
    return pieces


def sum_line(value, lines, *waits):
    total = lax.dynamic_index_in_dim(value, lax.axis_index("line"), 0, keepdims=False)
    pieces = send_line(value, lines)
    if waits:
        pieces = lax.optimization_barrier(tuple(pieces) + waits)[: len(pieces)]
    for piece in pieces:
        total = total + piece.astype(f32)
    return total


def masks(seg, pos):
    pad = seg == CLIPS - 1
    lane = jnp.arange(128, dtype=jnp.int32) % HEAD_DIM
    seg, pos, pad = seg[..., None], pos[..., None], pad[..., None]
    clip_lane = lane < CLIPS - 1
    digit = jnp.where(lane < 9, pos // 256, jnp.where(lane < 25, (pos // 16) % 16, pos % 16))
    digit_base = jnp.where(lane < 9, 5, jnp.where(lane < 25, 9, 25))
    digit_lane = (lane >= 5) & (lane < LANE_LOG)
    hit_clip = lane == seg
    hit_digit = lane - digit_base == digit
    log_lane = (lane >= LANE_LOG) & (lane < LANE_PAD)
    pad_lane = lane == LANE_PAD
    bad = (clip_lane & ~hit_clip) | (digit_lane & pad & ~hit_digit) | (pad_lane & ~pad)
    qx = jnp.where(bad, -BIG, 0.0).astype(bf16)
    on = (clip_lane & hit_clip) | (digit_lane & pad & hit_digit) | log_lane | (pad_lane & pad)
    kx = jnp.where(on, 1.0, 0.0).astype(bf16)
    return qx, kx


def block_flags(ident, rows_block, cols_block):
    count, length = ident.shape
    by_row = ident.reshape(count, length // rows_block, rows_block)
    by_col = ident.reshape(count, length // cols_block, cols_block)
    low_row, high_row = jnp.min(by_row, axis=2)[:, :, None], jnp.max(by_row, axis=2)[:, :, None]
    low_col, high_col = jnp.min(by_col, axis=2)[:, None, :], jnp.max(by_col, axis=2)[:, None, :]
    meets = (low_row <= high_col) & (low_col <= high_row)
    return meets.astype(jnp.int32).reshape(count, -1)


def pair_device(
    lines, planes,
    tokens, segment_ids, cotangent, ln1_gain, ln1_bias, qkv_weight, qv_bias, out_weight, out_bias,
    ln2_gain, ln2_bias, up_weight, up_bias, down_weight, down_bias, avg_qkv, avg_out, avg_up, avg_down,
):
    count, part, width = tokens.shape
    length = 2 * part
    wide = width // 2
    heads = HEADS // 2
    hidden_width = up_weight.shape[1]
    chunks = hidden_width // width
    share = qkv_weight.shape[0]
    side = lax.axis_index("seq").astype(jnp.int32)
    first = side == 0
    side_arr = side.reshape(1)
    const = lambda *shape: pl.BlockSpec(shape, lambda *_: (0,) * len(shape), pipeline_mode=pl.Buffered(1))
    row_block = lambda *shape: pl.BlockSpec((1,) + shape, lambda j, *_: (j,) + (0,) * len(shape))
    both_block = lambda lanes: pl.BlockSpec((2, 1, part, lanes), lambda j, *_: (0, j, 0, 0))
    own_block = lambda lanes: pl.BlockSpec((1, 1, part, lanes), lambda j, *_: (0, j, 0, 0))

    pairs = heads // 2
    sds = jax.ShapeDtypeStruct
    small_vectors = [ln1_gain, ln1_bias, out_bias, ln2_gain, ln2_bias, down_bias, qv_bias, up_bias]
    mine, give, second = pl.pallas_call(
        functools.partial(prepare_kernel, share),
        grid_spec=pltpu.PrefetchScalarGridSpec(
            num_scalar_prefetch=1,
            grid=(1,),
            in_specs=[
                pl.BlockSpec((share, 6 * wide), lambda *_: (0, 0)),
                pl.BlockSpec((share, hidden_width), lambda *_: (0, 0)),
                pl.BlockSpec((share, width), lambda *_: (0, 0)),
                pl.BlockSpec((chunks * share, width), lambda *_: (0, 0)),
            ]
            + [pl.BlockSpec((1, v.shape[0]), lambda *_: (0, 0)) for v in small_vectors],
            out_specs=[pl.BlockSpec((share, 3 * wide + 128), lambda *_: (0, 0))] * 2
            + [pl.BlockSpec(((2 * chunks + 1) * share, width), lambda *_: (0, 0))],
        ),
        out_shape=[sds((share, 3 * wide + 128), bf16)] * 2 + [sds(((2 * chunks + 1) * share, width), bf16)],
        name="prepare",
        **kernel_params(1e6, 1e6),
    )(side_arr, qkv_weight, up_weight, out_weight, down_weight, *[v[None] for v in small_vectors])
    take = partner(give)
    tokens_other = partner(tokens)
    seg_other = partner(segment_ids)
    seg = jnp.concatenate([segment_ids, seg_other], axis=1)
    spots = jnp.arange(part, dtype=jnp.int32)
    pos = jnp.concatenate([side * part + spots, (1 - side) * part + spots])
    qx, kx = masks(seg, jnp.broadcast_to(pos, seg.shape))
    ident = jnp.where(seg == CLIPS - 1, CLIPS + pos, seg)
    flags_f = flags_b = block_flags(ident, T_SIDE, T_SIDE)

    start = jnp.where(first, jnp.stack([mine, take]), jnp.stack([take, mine]))
    x_at, y_at = lax.axis_index("x"), lax.axis_index("y")
    first_line = after(spread_line(start, lines), qx, kx, flags_f, flags_b)
    (one_m, one_r), (two_m, two_r) = spread_plane(first_line[:, 0], first_line[:, 1])
    one = in_order(y_at, one_m, one_r).transpose(2, 0, 1, 3, 4)
    two = in_order(x_at, two_m, two_r).transpose(2, 1, 0, 3, 4)
    w_first = jnp.stack([one, two]).reshape(width, 3 * wide + 128)

    own_rows = chunks * share
    second = after(second, first_line)
    up_rows = own_rows + share
    second_line = spread_line(second, lines)

    small_at = 3 * wide // 128
    normed, mixed, pack = pl.pallas_call(
        functools.partial(project_kernel, share),
        grid_spec=pltpu.PrefetchScalarGridSpec(
            num_scalar_prefetch=1,
            grid=(2, count),
            in_specs=[
                pl.BlockSpec((1, part, width), lambda h, j, *_: (jnp.where(h == 0, j, count - 1), 0, 0)),
                pl.BlockSpec((1, part, width), lambda h, j, *_: (jnp.where(h == 0, 0, j), 0, 0)),
                const(width, 3 * wide),
                pl.BlockSpec((width, 128), lambda *_: (0, small_at), pipeline_mode=pl.Buffered(1)),
            ],
            out_specs=[
                pl.BlockSpec((1, 1, part, width), lambda h, j, *_: (h, j, 0, 0)),
                pl.BlockSpec((pairs, 1, 1, part, 384), lambda h, j, *_: (0, h, j, 0, 0)),
                pl.BlockSpec((16, width), lambda *_: (0, 0)),
            ],
            scratch_shapes=[pltpu.VMEM((1, 3 * wide), f32)],
        ),
        out_shape=[
            sds((2, count, part, width), bf16),
            sds((pairs, 2, count, part, 384), bf16),
            sds((16, width), f32),
        ],
        name="project",
        **kernel_params(
            2 * 2 * count * part * width * 3 * wide, 20e6, order=("arbitrary", "arbitrary")
        ),
    )(side_arr, tokens, tokens_other, w_first, w_first)
    up_bias_all = pack[8 : 8 + chunks].reshape(chunks, -1, share).transpose(1, 0, 2).reshape(chunks, width)

    second_line = after(second_line, one_r, two_r, pack)
    halves = (second_line[:, :up_rows].reshape(lines, chunks + 1, share, width), second_line[:, up_rows:])
    halves_got = spread_first(*halves)
    same, row_mixed = (), mixed
    for base, rows_now in ((0, 1), (1, count - 1)):
        if base == 1:
            halves_got = lax.optimization_barrier(halves_got + (same[0],))[:2]
            up_pair, down_pair = spread_second(*halves, *halves_got)
            row_mixed = after(mixed, up_pair[0], down_pair[0])
        row_both = lambda lanes, base=base: pl.BlockSpec(
            (pairs, 2, 1, part, lanes), lambda j, *_: (0, 0, base + j, 0, 0)
        )
        row_one = pl.BlockSpec((pairs, 1, part, 128), lambda j, *_, base=base: (0, base + j, 0, 0))
        row_flat = pl.BlockSpec((1, length, 128), lambda j, *_, base=base: (base + j, 0, 0))
        same = pl.pallas_call(
            functools.partial(attend_kernel, base),
            grid_spec=pltpu.PrefetchScalarGridSpec(
                num_scalar_prefetch=1,
                grid=(rows_now,),
                in_specs=[row_both(384), row_flat, row_flat] + [pl.BlockSpec(memory_space=pl.ANY)] * len(same),
                out_specs=[row_one, row_one, row_both(128)],
                scratch_shapes=[pltpu.VMEM((heads, length, 128), bf16)] * 3
                + [pltpu.VMEM((heads, length, 128), f32)],
            ),
            out_shape=[sds((pairs, count, part, 128), bf16)] * 2 + [sds((pairs, 2, count, part, 128), bf16)],
            input_output_aliases={4 + i: i for i in range(len(same))},
            name="attend",
            **kernel_params(8e9, 7e6, 4e6),
        )(flags_f, row_mixed, qx, kx, *same)
    att_own, att_other, ext = same
    spot = jnp.stack([side, y_at.astype(jnp.int32), x_at.astype(jnp.int32)])
    near = [up_pair[0], down_pair[0]]
    near += [partner(piece) for piece in near]
    far = list(lax.optimization_barrier((up_pair[1], down_pair[1], att_own))[:2])
    near = list(lax.optimization_barrier(tuple(near) + tuple(far))[:4])
    far += [partner(piece) for piece in far]
    shapes = [
        sds((2, lines, 2, 2, share, hidden_width), bf16),
        sds((2, lines, 2, 2, share, width), bf16),
    ]
    targets = assemble(spot, False, near[::2], (), shapes)
    w_up, w_out = assemble(spot, True, far[::2], targets, shapes)
    w_up = w_up.reshape(width, hidden_width)
    down_pieces = [near[1], far[1], near[3], far[3]]
    w_out = w_out.reshape(2, wide, width)
    w_out_flat = w_out.reshape(2 * wide, width)

    att_recv = partner(att_other)

    head_block = pl.BlockSpec((pairs, 1, part, 128), lambda j, *_: (0, j, 0, 0))
    out_tokens, glow, gdown_own, gdown_other, gup_own, gup_other, gup_bias, gvec = pl.pallas_call(
        functools.partial(mlp_kernel, planes, share),
        grid_spec=pltpu.PrefetchScalarGridSpec(
            num_scalar_prefetch=1,
            grid=(count,),
            in_specs=[
                row_block(part, width),
                head_block,
                head_block,
            ]
            + [pl.BlockSpec(memory_space=pl.ANY)] * 6
            + [
                row_block(part, width),
                const(16, width),
                const(chunks, width),
            ],
            out_specs=[row_block(part, width)] * 2
            + [pl.BlockSpec(memory_space=pl.ANY)] * 4
            + [const(chunks, 1, width), const(8, width)],
            scratch_shapes=[pltpu.VMEM((chunks, width, width), f32)] * 2
            + [
                pltpu.VMEM((2, wide, width), bf16),
                pltpu.VMEM((width, hidden_width), bf16),
                pltpu.VMEM((2, lines, 2, 2, own_rows, width), bf16),
            ]
            + [pltpu.VMEM((planes, lines, own_rows, width), bf16)] * 2
            + [pltpu.VMEM((planes, lines, chunks, share, width), bf16)] * 2
            + [pltpu.SemaphoreType.DMA((10,)), pltpu.SemaphoreType.DMA((3 * chunks,))],
        ),
        out_shape=[
            sds((count, part, width), bf16),
            sds((count, part, width), bf16),
        ]
        + [sds((planes, lines, own_rows, width), bf16)] * 2
        + [sds((planes, lines, chunks, share, width), bf16)] * 2
        + [sds((chunks, 1, width), f32), sds((8, width), f32)],
        name="mlp",
        **kernel_params(2 * count * part * width * (width + 6 * hidden_width), 36e6, 4.7e6),
    )(spot, tokens, att_own, att_recv, w_out, w_up, *down_pieces, cotangent, pack, up_bias_all)

    glow_other = partner(glow)
    avg_qkv, avg_out, avg_up, avg_down, _ = lax.optimization_barrier((avg_qkv, avg_out, avg_up, avg_down, glow))
    new_qkv = 0.9 * avg_qkv + 0.1 * qkv_weight.astype(f32)
    new_out = 0.9 * avg_out + 0.1 * out_weight.astype(f32)
    new_up = 0.9 * avg_up + 0.1 * up_weight.astype(f32)
    new_down = 0.9 * avg_down + 0.1 * down_weight.astype(f32)
    add = lambda one, two: (one.astype(f32) + two.astype(f32)).astype(bf16)
    gdown_plane = sum_plane(add(gdown_own, partner(gdown_other)))
    gup_sum = add(gup_own, partner(gup_other))

    gmixed, gmixed_bias = [], []
    ties = ()
    for pair in range(pairs):
        lane_block = lambda lanes, pair=pair: pl.BlockSpec((1, 2, 1, part, lanes), lambda j, *_: (pair, 0, j, 0, 0))
        att_block = pl.BlockSpec((1, 1, part, 128), lambda j, *_, pair=pair: (pair, j, 0, 0))
        piece, piece_bias = pl.pallas_call(
            attend_back_kernel,
            grid_spec=pltpu.PrefetchScalarGridSpec(
                num_scalar_prefetch=2,
                grid=(count,),
                in_specs=[
                    lane_block(384),
                    lane_block(128),
                    att_block,
                    att_block,
                    row_block(part, width),
                    row_block(part, width),
                    pl.BlockSpec((128, width), lambda j, flags, where, pair=pair: (where[0] * pairs + pair, 0)),
                    row_block(length, 128),
                ],
                out_specs=[both_block(384), const(8, 384)],
                scratch_shapes=[pltpu.VMEM((length // TQ_B, 2 * TQ_B, 256), bf16)] * 2
                + [pltpu.VMEM((length, 256), bf16)] * 2
                + [
                    pltpu.VMEM((length // TK_B, 128, TK_B), bf16),
                    pltpu.VMEM((length // TQ_B, 128, TQ_B), f32),
                    pltpu.VMEM((length, 128), f32),
                    pltpu.VMEM((length, 128), f32),
                ],
            ),
            out_shape=[sds((2, count, part, 384), bf16), sds((8, 384), f32)],
            name="attend_back",
            **kernel_params(25e9, 20e6, 4e6),
        )(flags_b, side_arr, after(mixed, *ties), ext, att_own, att_other, glow, glow_other, w_out_flat, kx)
        gmixed.append(piece)
        gmixed_bias.append(piece_bias)
        if pair == 0:
            gup_plane = sum_plane(after(gup_sum, gdown_plane))
            grad_down = sum_line(gdown_plane, lines)
            ties = (gdown_plane,)
        if pair == 1:
            early, inner_sum, plain_sum = pl.pallas_call(
                functools.partial(early_kernel, planes, share),
                grid=(count,),
                in_specs=[both_block(width), both_block(384), both_block(384), const(8, 384), const(8, 384)]
                + [head_block, head_block, row_block(part, width), row_block(part, width), const(width, 768)],
                out_specs=[const(planes, lines, 6, share, 384), const(width, 128), const(width, 128)],
                out_shape=[
                    sds((planes, lines, 6, share, 384), bf16),
                    sds((width, 128), f32),
                    sds((width, 128), f32),
                ],
                scratch_shapes=[pltpu.VMEM((width, 768), f32), pltpu.VMEM((wide, width), f32)],
                name="early",
                **kernel_params(9e9, 25e6),
            )(normed, *gmixed, *gmixed_bias, att_own, att_other, glow, glow_other, w_first)
            early_plane = sum_plane(after(early, gup_plane))
            gup_line = sum_line(gup_plane, lines)
            ties = (gup_plane, grad_down, early)
    grad_up = gup_line.transpose(1, 0, 2).reshape(share, hidden_width)

    late = pl.pallas_call(
        functools.partial(late_kernel, planes, share),
        grid_spec=pltpu.PrefetchScalarGridSpec(
            num_scalar_prefetch=1,
            grid=(count,),
            in_specs=[
                both_block(width),
                both_block(384),
                pl.BlockSpec((width, 384), lambda *_: (0, 2), pipeline_mode=pl.Buffered(1)),
                const(width, 128),
                const(width, 128),
                const(8, 384),
                const(8, 384),
                const(8, 384),
                const(16, width),
                const(8, width),
                const(chunks, 1, width),
            ],
            out_specs=const(planes, lines, 3, share, 384),
            scratch_shapes=[pltpu.VMEM((width, 384), f32)],
        ),
        out_shape=sds((planes, lines, 3, share, 384), bf16),
        name="late",
        **kernel_params(4e9, 10e6),
    )(side_arr, normed, after(gmixed[2], early_plane, gup_line), w_first, inner_sum, plain_sum, *gmixed_bias, pack, gvec, gup_bias)

    piece_spec = lambda side: pl.BlockSpec((1, 1, part, 384), lambda j, *_: (side, j, 0, 0))
    give_back = pl.pallas_call(
        give_kernel,
        grid=(count,),
        in_specs=[piece_spec(1)] * pairs + [const(width, 3 * wide)],
        out_specs=row_block(part, width),
        out_shape=sds((count, part, width), bf16),
        name="give_back",
        **kernel_params(2 * count * part * width * 3 * wide, 12e6),
    )(*gmixed[:2], after(gmixed[2], late), w_first)
    recv_back = partner(give_back)

    grad_input = pl.pallas_call(
        input_kernel,
        grid=(count,),
        in_specs=[piece_spec(0)] * pairs
        + [
            const(width, 3 * wide),
            row_block(part, width),
            row_block(part, width),
            row_block(part, width),
            const(16, width),
        ],
        out_specs=row_block(part, width),
        out_shape=sds((count, part, width), f32),
        name="input_grad",
        **kernel_params(2 * count * part * width * 3 * wide, 25e6),
    )(*gmixed, w_first, recv_back, tokens, glow, pack)

    late_plane = sum_plane(late, grad_input)
    unit_line = sum_line(jnp.concatenate([early_plane, late_plane], axis=1), lines)
    theirs = lax.dynamic_slice_in_dim(unit_line, 2 * (1 - side), 2, 0)
    theirs_late = lax.dynamic_slice_in_dim(unit_line, 7 - side, 1, 0)
    got = partner(jnp.concatenate([theirs, theirs_late, unit_line[8:]], axis=0))
    sizes = [share] * 6 + [2 * share, chunks * share]
    grad_qkv, grad_out, *vecs = pl.pallas_call(
        finish_kernel,
        grid_spec=pltpu.PrefetchScalarGridSpec(
            num_scalar_prefetch=1,
            grid=(1,),
            in_specs=[
                pl.BlockSpec((9, share, 384), lambda *_: (0, 0, 0)),
                pl.BlockSpec((4, share, 384), lambda *_: (0, 0, 0)),
            ],
            out_specs=[
                pl.BlockSpec((share, 6 * wide), lambda *_: (0, 0)),
                pl.BlockSpec((share, width), lambda *_: (0, 0)),
            ]
            + [pl.BlockSpec((1, size), lambda *_: (0, 0)) for size in sizes],
        ),
        out_shape=[sds((share, 6 * wide), f32), sds((share, width), f32)] + [sds((1, size), f32) for size in sizes],
        name="finish",
        **kernel_params(1e6, 1e6),
    )(side_arr, unit_line, got)
    vec = lambda slot, size: vecs[slot].reshape(size)

    return (
        out_tokens,
        grad_input,
        vec(0, share),
        vec(1, share),
        grad_qkv,
        vec(6, 2 * share),
        grad_out,
        vec(2, share),
        vec(3, share),
        vec(4, share),
        grad_up,
        vec(7, chunks * share),
        grad_down,
        vec(5, share),
        new_qkv,
        new_out,
        new_up,
        new_down,
    )


def specs_for(rows):
    flat = ("seq",) + (rows if isinstance(rows, tuple) else (rows,))
    grid, ids, vec, mat = P(rows, "seq", None), P(rows, "seq"), P(flat), P(flat, None)
    ins = (grid, ids, grid, vec, vec, mat, vec, mat, vec, vec, vec, mat, vec, mat, vec, mat, mat, mat, mat)
    outs = (grid, grid, vec, vec, mat, vec, mat, vec, vec, vec, mat, vec, mat, vec, mat, mat, mat, mat)
    return ins, outs


def solution(mesh):
    parts, rows = mesh.shape["seq"], mesh.shape["rows"]
    planes = 4
    if parts != 2 or rows % planes:
        ins, outs = specs_for("rows")
        return jax.shard_map(on_device, mesh=mesh, in_specs=ins, out_specs=outs, check_vma=False)
    lines = rows // planes
    finer = Mesh(mesh.devices.reshape(parts, lines, 2, 2), ("seq", "line", "y", "x"))
    ins, outs = specs_for(("line", "y", "x"))
    return jax.shard_map(
        functools.partial(pair_device, lines, planes), mesh=finer, in_specs=ins, out_specs=outs, check_vma=False
    )
```

```python
import functools

import jax
import jax.numpy as jnp
from jax import lax
from jax.experimental import pallas as pl
from jax.experimental.pallas import tpu as pltpu
from jax.sharding import Mesh
from jax.sharding import PartitionSpec as P

HEADS = 12
HEAD_DIM = 64
CLIPS = 6


def layer_norm(value, gain, bias):
    middle = jnp.mean(value, axis=-1, keepdims=True)
    centred = value - middle
    spread = jnp.mean(centred * centred, axis=-1, keepdims=True)
    return centred * lax.rsqrt(spread + 1e-06) * gain + bias


def exact_gelu(value):
    return jax.nn.gelu(value, approximate=False)


def permitted(seg_query, seg_key, pos_query, pos_key):
    same_clip = seg_query[:, :, None] == seg_key[:, None, :]
    open_key = (seg_key != CLIPS - 1)[:, None, :]
    diagonal = (pos_query[:, None] == pos_key[None, :])[None]
    return (same_clip & (open_key | diagonal))[:, :, None, :]


def scores(query_part, key_part):
    return 0.125 * jnp.einsum(
        "rqhe,rkhe->rqhk", query_part, key_part, preferred_element_type=jnp.float32
    )


def exponent(score_vals, allowed):
    return jnp.where(allowed, jnp.exp(jnp.where(allowed, score_vals, 0.0)), 0.0)


def on_device(
    tokens,
    segment_ids,
    cotangent,
    ln1_gain,
    ln1_bias,
    qkv_weight,
    qv_bias,
    out_weight,
    out_bias,
    ln2_gain,
    ln2_bias,
    up_weight,
    up_bias,
    down_weight,
    down_bias,
    avg_qkv,
    avg_out,
    avg_up,
    avg_down,
):
    f32 = jnp.float32
    bf16 = jnp.bfloat16
    rows_here, shard_len, width = tokens.shape
    count_rows = rows_here * shard_len
    own_pos = lax.axis_index("seq") * shard_len + jnp.arange(shard_len, dtype=jnp.int32)
    head_shape = (rows_here, shard_len, HEADS, HEAD_DIM)
    gain_one, bias_one, w_qkv, b_qv, w_out, b_out = (
        lax.all_gather(ln1_gain, ("seq", "rows"), axis=0, tiled=True),
        lax.all_gather(ln1_bias, ("seq", "rows"), axis=0, tiled=True),
        lax.all_gather(qkv_weight, ("seq", "rows"), axis=0, tiled=True),
        lax.all_gather(qv_bias, ("seq", "rows"), axis=0, tiled=True),
        lax.all_gather(out_weight, ("seq", "rows"), axis=0, tiled=True),
        lax.all_gather(out_bias, ("seq", "rows"), axis=0, tiled=True),
    )
    residual = tokens.astype(f32).reshape(count_rows, width)
    normed, norm_one_pull = jax.vjp(
        layer_norm, residual, gain_one.astype(f32), bias_one.astype(f32)
    )
    normed_low = normed.astype(bf16)
    mixed = jnp.dot(normed_low, w_qkv, preferred_element_type=f32)
    bias_qv = b_qv.astype(f32)
    query_heads = (mixed[:, :width] + bias_qv[:width]).astype(bf16).reshape(head_shape)
    key_heads = mixed[:, width : 2 * width].astype(bf16).reshape(head_shape)
    value_heads = (mixed[:, 2 * width :] + bias_qv[width:]).astype(bf16).reshape(head_shape)
    start_state = (jnp.zeros((rows_here, shard_len, HEADS), f32), jnp.zeros(head_shape, f32))
    piece_keys = lax.all_gather(key_heads, "seq", axis=1, tiled=True)
    piece_values = lax.all_gather(value_heads, "seq", axis=1, tiled=True)
    piece_seg = lax.all_gather(segment_ids, "seq", axis=1, tiled=True)
    piece_len = piece_keys.shape[1]
    block_len = min(piece_len, shard_len)

    def forward_advance(turn, state):
        totals, weighted = state
        offset = turn * block_len
        key_block = lax.dynamic_slice_in_dim(piece_keys, offset, block_len, 1)
        value_block = lax.dynamic_slice_in_dim(piece_values, offset, block_len, 1)
        seg_block = lax.dynamic_slice_in_dim(piece_seg, offset, block_len, 1)
        key_pos = offset + jnp.arange(block_len, dtype=jnp.int32)
        allowed = permitted(segment_ids, seg_block, own_pos, key_pos)
        expo = exponent(scores(query_heads, key_block), allowed)
        totals = totals + jnp.sum(expo, axis=-1)
        weighted = weighted + jnp.einsum(
            "rqhk,rkhe->rqhe", expo.astype(bf16), value_block, preferred_element_type=f32
        )
        return (totals, weighted)

    totals, weighted = lax.fori_loop(0, piece_len // block_len, forward_advance, start_state)
    attended = weighted / totals[..., None]
    attn_in = attended.reshape(count_rows, width).astype(bf16)
    middle = residual + jnp.dot(attn_in, w_out, preferred_element_type=f32) + b_out.astype(f32)
    gain_two, bias_two, w_up, b_up, w_down, b_down = (
        lax.all_gather(ln2_gain, ("seq", "rows"), axis=0, tiled=True),
        lax.all_gather(ln2_bias, ("seq", "rows"), axis=0, tiled=True),
        lax.all_gather(up_weight, ("seq", "rows"), axis=0, tiled=True),
        lax.all_gather(up_bias, ("seq", "rows"), axis=0, tiled=True),
        lax.all_gather(down_weight, ("seq", "rows"), axis=0, tiled=True),
        lax.all_gather(down_bias, ("seq", "rows"), axis=0, tiled=True),
    )
    normed_two, norm_two_pull = jax.vjp(
        layer_norm, middle, gain_two.astype(f32), bias_two.astype(f32)
    )
    normed_two_low = normed_two.astype(bf16)
    hidden_pre = jnp.dot(normed_two_low, w_up, preferred_element_type=f32) + b_up.astype(f32)
    hidden, gelu_pull = jax.vjp(exact_gelu, hidden_pre)
    hidden_low = hidden.astype(bf16)
    final = middle + jnp.dot(hidden_low, w_down, preferred_element_type=f32) + b_down.astype(f32)
    out_tokens = final.astype(bf16).reshape(tokens.shape)
    w_up_back, w_down_back = (
        lax.all_gather(up_weight, ("seq", "rows"), axis=0, tiled=True),
        lax.all_gather(down_weight, ("seq", "rows"), axis=0, tiled=True),
    )
    grad_out = cotangent.astype(f32).reshape(count_rows, width)
    grad_low = grad_out.astype(bf16)
    grad_down = jnp.einsum("nf,nd->fd", hidden_low, grad_low, preferred_element_type=f32)
    grad_down_b = jnp.sum(grad_low, axis=0, dtype=f32)
    grad_hidden = jnp.einsum("nd,fd->nf", grad_low, w_down_back, preferred_element_type=f32)
    (grad_pre,) = gelu_pull(grad_hidden)
    grad_pre_low = grad_pre.astype(bf16)
    grad_up = jnp.einsum("nd,nf->df", normed_two_low, grad_pre_low, preferred_element_type=f32)
    grad_up_b = jnp.sum(grad_pre_low, axis=0, dtype=f32)
    grad_normed_two = jnp.einsum("nf,df->nd", grad_pre_low, w_up_back, preferred_element_type=f32)
    grad_mid_norm, grad_gain_two, grad_bias_two = norm_two_pull(grad_normed_two)
    grad_mid = grad_out + grad_mid_norm
    mlp_sums = (
        lax.psum_scatter(grad_gain_two, ("seq", "rows"), scatter_dimension=0, tiled=True),
        lax.psum_scatter(grad_bias_two, ("seq", "rows"), scatter_dimension=0, tiled=True),
        lax.psum_scatter(grad_up, ("seq", "rows"), scatter_dimension=0, tiled=True),
        lax.psum_scatter(grad_up_b, ("seq", "rows"), scatter_dimension=0, tiled=True),
        lax.psum_scatter(grad_down, ("seq", "rows"), scatter_dimension=0, tiled=True),
        lax.psum_scatter(grad_down_b, ("seq", "rows"), scatter_dimension=0, tiled=True),
    )
    w_qkv_back, w_out_back = (
        lax.all_gather(qkv_weight, ("seq", "rows"), axis=0, tiled=True),
        lax.all_gather(out_weight, ("seq", "rows"), axis=0, tiled=True),
    )
    grad_mid_low = grad_mid.astype(bf16)
    grad_wout = jnp.einsum("nd,ne->de", attn_in, grad_mid_low, preferred_element_type=f32)
    grad_bout = jnp.sum(grad_mid_low, axis=0, dtype=f32)
    grad_att = jnp.einsum(
        "ne,de->nd", grad_mid_low, w_out_back, preferred_element_type=f32
    ).reshape(head_shape)
    grad_acc = (grad_att / totals[..., None]).astype(bf16)
    shift_low = (jnp.sum(grad_att * attended, axis=-1) / totals).astype(bf16)
    shift_wide = shift_low.astype(f32)
    query_piece_keys = lax.all_gather(key_heads, "seq", axis=1, tiled=True)
    query_piece_values = lax.all_gather(value_heads, "seq", axis=1, tiled=True)
    query_piece_seg = lax.all_gather(segment_ids, "seq", axis=1, tiled=True)
    piece_len = query_piece_keys.shape[1]
    query_block_len = min(piece_len, shard_len)

    def query_advance(turn, grad_query):
        offset = turn * query_block_len
        key_block = lax.dynamic_slice_in_dim(query_piece_keys, offset, query_block_len, 1)
        value_block = lax.dynamic_slice_in_dim(query_piece_values, offset, query_block_len, 1)
        seg_block = lax.dynamic_slice_in_dim(query_piece_seg, offset, query_block_len, 1)
        key_pos = offset + jnp.arange(query_block_len, dtype=jnp.int32)
        allowed = permitted(segment_ids, seg_block, own_pos, key_pos)
        expo = exponent(scores(query_heads, key_block), allowed)
        inner = jnp.einsum("rqhe,rkhe->rqhk", grad_acc, value_block, preferred_element_type=f32)
        grad_score = (expo * (inner - shift_wide[..., None])).astype(bf16)
        return grad_query + jnp.einsum(
            "rqhk,rkhe->rqhe", grad_score, key_block, preferred_element_type=f32
        )

    grad_query = lax.fori_loop(
        0, piece_len // query_block_len, query_advance, jnp.zeros(head_shape, f32)
    )
    key_start = (jnp.zeros(head_shape, f32), jnp.zeros(head_shape, f32))
    piece_queries = lax.all_gather(query_heads, "seq", axis=1, tiled=True)
    piece_grads = lax.all_gather(grad_acc, "seq", axis=1, tiled=True)
    key_piece_seg = lax.all_gather(segment_ids, "seq", axis=1, tiled=True)
    piece_shift = lax.all_gather(shift_low, "seq", axis=1, tiled=True)
    piece_len = piece_queries.shape[1]
    key_block_len = min(piece_len, shard_len)

    def key_advance(turn, state):
        grad_key, grad_value = state
        offset = turn * key_block_len
        query_block = lax.dynamic_slice_in_dim(piece_queries, offset, key_block_len, 1)
        grad_block = lax.dynamic_slice_in_dim(piece_grads, offset, key_block_len, 1)
        seg_block = lax.dynamic_slice_in_dim(key_piece_seg, offset, key_block_len, 1)
        shift_block = lax.dynamic_slice_in_dim(piece_shift, offset, key_block_len, 1).astype(f32)
        query_pos = offset + jnp.arange(key_block_len, dtype=jnp.int32)
        allowed = permitted(seg_block, segment_ids, query_pos, own_pos)
        expo = exponent(scores(query_block, key_heads), allowed)
        inner = jnp.einsum("rqhe,rkhe->rqhk", grad_block, value_heads, preferred_element_type=f32)
        grad_score = (expo * (inner - shift_block[..., None])).astype(bf16)
        grad_key = grad_key + jnp.einsum(
            "rqhk,rqhe->rkhe", grad_score, query_block, preferred_element_type=f32
        )
        grad_value = grad_value + jnp.einsum(
            "rqhk,rqhe->rkhe", expo.astype(bf16), grad_block, preferred_element_type=f32
        )
        return (grad_key, grad_value)

    grad_key, grad_value = lax.fori_loop(0, piece_len // key_block_len, key_advance, key_start)
    grad_q_low = (0.125 * grad_query).astype(bf16).reshape(count_rows, width)
    grad_k_low = (0.125 * grad_key).astype(bf16).reshape(count_rows, width)
    grad_v_low = grad_value.astype(bf16).reshape(count_rows, width)
    grad_mixed = jnp.concatenate([grad_q_low, grad_k_low, grad_v_low], axis=1)
    grad_wqkv = jnp.einsum("nd,ne->de", normed_low, grad_mixed, preferred_element_type=f32)
    grad_bqv = jnp.concatenate(
        [jnp.sum(grad_q_low, axis=0, dtype=f32), jnp.sum(grad_v_low, axis=0, dtype=f32)], axis=0
    )
    grad_normed = jnp.einsum("ne,de->nd", grad_mixed, w_qkv_back, preferred_element_type=f32)
    grad_res_norm, grad_gain_one, grad_bias_one = norm_one_pull(grad_normed)
    grad_input = (grad_mid + grad_res_norm).reshape(tokens.shape)
    attn_sums = (
        lax.psum_scatter(grad_gain_one, ("seq", "rows"), scatter_dimension=0, tiled=True),
        lax.psum_scatter(grad_bias_one, ("seq", "rows"), scatter_dimension=0, tiled=True),
        lax.psum_scatter(grad_wqkv, ("seq", "rows"), scatter_dimension=0, tiled=True),
        lax.psum_scatter(grad_bqv, ("seq", "rows"), scatter_dimension=0, tiled=True),
        lax.psum_scatter(grad_wout, ("seq", "rows"), scatter_dimension=0, tiled=True),
        lax.psum_scatter(grad_bout, ("seq", "rows"), scatter_dimension=0, tiled=True),
    )
    new_qkv = 0.9 * avg_qkv + 0.1 * qkv_weight.astype(f32)
    new_out = 0.9 * avg_out + 0.1 * out_weight.astype(f32)
    new_up = 0.9 * avg_up + 0.1 * up_weight.astype(f32)
    new_down = 0.9 * avg_down + 0.1 * down_weight.astype(f32)
    return (
        out_tokens,
        grad_input,
        attn_sums[0],
        attn_sums[1],
        attn_sums[2],
        attn_sums[3],
        attn_sums[4],
        attn_sums[5],
        mlp_sums[0],
        mlp_sums[1],
        mlp_sums[2],
        mlp_sums[3],
        mlp_sums[4],
        mlp_sums[5],
        new_qkv,
        new_out,
        new_up,
        new_down,
    )


f32 = jnp.float32
bf16 = jnp.bfloat16
NT = (((1,), (1,)), ((), ()))
LOG2E = 1.4426950408889634
SCORE = 0.125 * LOG2E
BIG = 16384.0
VMEM_BYTES = 63 * 1024 * 1024
TK_B, TQ_B, T_SIDE = 512, 512, 256
LANE_LOG = 41
LANE_PAD = 44


def kernel_params(flops, bytes_accessed, transcendentals=0, order=("arbitrary",)):
    return dict(
        compiler_params=pltpu.CompilerParams(
            vmem_limit_bytes=VMEM_BYTES, dimension_semantics=order
        ),
        cost_estimate=pl.CostEstimate(
            flops=int(flops), bytes_accessed=int(bytes_accessed), transcendentals=int(transcendentals)
        ),
    )


def standardise(value):
    middle = jnp.mean(value, axis=-1, keepdims=True)
    centred = value - middle
    spread = jnp.mean(centred * centred, axis=-1, keepdims=True)
    rstd = lax.rsqrt(spread + 1e-06)
    return centred * rstd, rstd


def norm_pull(grad_normed, gain, xhat, rstd):
    scaled = grad_normed * gain
    first = jnp.mean(scaled, axis=-1, keepdims=True)
    second = jnp.mean(scaled * xhat, axis=-1, keepdims=True)
    return rstd * (scaled - first - xhat * second)


def gelu_pair(x):
    size = jnp.abs(x)
    base = 1.0 + 0.23164189 * size
    t = 1.0 / base
    bell = jnp.exp2(x * x * (-0.5 * LOG2E))
    poly = t * (0.127414796 + t * (-0.142248368 + t * (0.7107068705 + t * (-0.7265760135 + t * 0.5307027145))))
    tail = poly * bell
    phi = jnp.where(x >= 0.0, 1.0 - tail, tail)
    return x * phi, phi + x * bell * 0.3989422804014327


def lane_masks():
    lane = lax.broadcasted_iota(jnp.int32, (1, 128), 1)
    low = jnp.where(lane < HEAD_DIM, 1.0, 0.0)
    return low.astype(bf16), (1.0 - low).astype(bf16)


def prepare_kernel(share, side_ref, w_ref, up_ref, out_ref, down_ref, *refs):
    vectors, (mine_ref, give_ref, second_ref) = refs[:-3], refs[-3:]
    width = down_ref.shape[1]
    blocks = up_ref.shape[1] // width
    for block in range(blocks):
        second_ref[block * share : (block + 1) * share] = up_ref[:, block * width : (block + 1) * width]
    second_ref[blocks * share : (blocks + 1) * share] = out_ref[...]
    second_ref[(blocks + 1) * share :] = down_ref[...]
    wide = w_ref.shape[1] // 6
    pairs = wide // 128
    for target, side in ((mine_ref, side_ref[0]), (give_ref, 1 - side_ref[0])):
        for pair in range(pairs):
            for kind in range(3):
                start = pl.multiple_of(kind * 2 * wide + side * wide + pair * 128, 128)
                at = 384 * pair + 128 * kind
                target[:, at : at + 128] = w_ref[:, pl.ds(start, 128)]
    lane = lax.broadcasted_iota(jnp.int32, (share, 128), 1)
    small = jnp.zeros((share, 128), f32)
    column = 0
    for ref in vectors:
        row = jnp.broadcast_to(ref[...].astype(f32), (8, ref.shape[1])).T
        for start in range(0, ref.shape[1], share):
            small = jnp.where(lane == column, row[start : start + share, 0:1], small)
            column += 1
    small = small.astype(bf16)
    mine_ref[:, 3 * wide :] = small
    give_ref[:, 3 * wide :] = small


def project_kernel(
    share, side_ref, own_ref, other_ref, w_ref, small_ref, normed_ref, mixed_ref, pack_ref, shift_s
):
    which, turn = pl.program_id(0), pl.program_id(1)
    wide = shift_s.shape[1] // 3
    pairs = wide // 128

    @pl.when((which == 0) & (turn == 0))
    def _():
        small = small_ref[...].astype(f32).T
        pack_ref[...] = small[0:16]
        shift_s[...] = jnp.zeros_like(shift_s)
        spot = lax.broadcasted_iota(jnp.int32, (wide, wide), 0)
        target = lax.broadcasted_iota(jnp.int32, (wide, wide), 1) + side_ref[0] * wide
        sums = [jnp.zeros((16, wide), f32), jnp.zeros((16, wide), f32)]
        for part in range(2):
            wanted = lax.div(spot, share) * (2 * share) + part * share + lax.rem(spot, share)
            chosen = jnp.where(wanted == target, 1.0, 0.0).astype(bf16)
            for kind in range(2):
                values = small[6 + part : 7 + part, kind * wide : (kind + 1) * wide]
                values = jnp.broadcast_to(values, (16, wide)).astype(bf16)
                sums[kind] += jnp.dot(values, chosen, preferred_element_type=f32)
        for pair in range(pairs):
            lanes = slice(128 * pair, 128 * pair + 128)
            shift_s[:, 384 * pair : 384 * pair + 128] = sums[0][0:1, lanes]
            shift_s[:, 384 * pair + 256 : 384 * pair + 384] = sums[1][0:1, lanes]

    tiles = 2
    size = normed_ref.shape[2] // tiles

    def normed_tile(i):
        rows = slice(i * size, (i + 1) * size)
        value = jnp.where(which == 0, own_ref[0, rows], other_ref[0, rows]).astype(f32)
        xhat, _ = standardise(value)
        normed = (xhat * pack_ref[0:1, :] + pack_ref[1:2, :]).astype(bf16)
        normed_ref[0, 0, rows] = normed
        return normed

    normed = normed_tile(0)
    for i in range(tiles):
        mixed = jnp.dot(normed, w_ref[...], preferred_element_type=f32) + shift_s[...]
        mixed = mixed.astype(bf16)
        if i + 1 < tiles:
            normed = normed_tile(i + 1)
        for pair in range(pairs):
            lanes = slice(384 * pair, 384 * pair + 384)
            mixed_ref[pair, 0, 0, i * size : (i + 1) * size] = mixed[:, lanes]


def attend_kernel(base, flag_ref, mixed_ref, qx_ref, kx_ref, *rest):
    own_ref, other_ref, ext_ref, q_s, k_s, v_s, acc_s = rest[-7:]
    row = base + pl.program_id(0)
    length = q_s.shape[1]
    heads = q_s.shape[0]
    half = length // 2
    low, high = lane_masks()
    qx, kx = qx_ref[0], kx_ref[0]
    q_low, q_high, k_low, k_high = qx * low, qx * high, kx * low, kx * high
    for pair in range(heads // 2):
        q = mixed_ref[pair, :, 0, :, 0:128].reshape(length, 128)
        k = mixed_ref[pair, :, 0, :, 128:256].reshape(length, 128)
        v = mixed_ref[pair, :, 0, :, 256:384].reshape(length, 128)
        q_s[2 * pair] = q * low + q_high
        q_s[2 * pair + 1] = q * high + q_low
        k_s[2 * pair] = k * low + k_high
        k_s[2 * pair + 1] = k * high + k_low
        v_s[2 * pair] = v * low + high
        v_s[2 * pair + 1] = v * high + low

    def block(q_start, k_start, size, fresh):
        q_at, k_at = pl.ds(q_start, size), pl.ds(k_start, size)
        for head in range(heads):
            score = lax.dot_general(q_s[head, q_at, :], k_s[head, k_at, :], NT, preferred_element_type=f32)
            expo = jnp.exp2(score * SCORE).astype(bf16)
            part = jnp.dot(expo, v_s[head, k_at, :], preferred_element_type=f32)
            if fresh:
                acc_s[head, q_at, :] = part
            else:
                acc_s[head, q_at, :] += part

    for start in range(0, length, half):
        block(start, start, half, True)
    pieces = length // T_SIDE

    def step(index, carry):
        qi, ki = index // pieces, index % pieces
        apart = qi // (half // T_SIDE) != ki // (half // T_SIDE)

        @pl.when(apart & (flag_ref[row, index] != 0))
        def _():
            block(pl.multiple_of(qi * T_SIDE, T_SIDE), pl.multiple_of(ki * T_SIDE, T_SIDE), T_SIDE, False)

        return carry

    lax.fori_loop(0, pieces * pieces, step, 0)
    lane = lax.broadcasted_iota(jnp.int32, (half, 128), 1)
    first_half = lane < HEAD_DIM
    spot = lane % HEAD_DIM
    for pair in range(heads // 2):
        for side in range(2):
            rows = slice(side * half, (side + 1) * half)
            first, second = acc_s[2 * pair, rows], acc_s[2 * pair + 1, rows]
            top = jnp.where(first_half, first, second)
            crossed = jnp.where(first_half, second, first)
            totals = pltpu.roll(crossed, HEAD_DIM, 1)
            target = own_ref if side == 0 else other_ref
            target[pair, 0] = (top / totals).astype(bf16)
            lse = -8.0 * jnp.log(crossed)
            lse_a = lse.astype(bf16).astype(f32)
            lse_b = (lse - lse_a).astype(bf16).astype(f32)
            ext = jnp.where(
                spot == LANE_LOG,
                lse_a,
                jnp.where(
                    spot == LANE_LOG + 1,
                    lse_b,
                    jnp.where(spot == LANE_LOG + 2, lse - lse_a - lse_b, qx[rows].astype(f32)),
                ),
            )
            ext_ref[pair, side, 0] = ext.astype(bf16)


def join_lanes(ref):
    return jnp.concatenate([ref[i, 0] for i in range(ref.shape[0])], axis=1)


def mlp_kernel(
    planes, share, spot_ref, x_ref, mine_ref, recv_ref, wo_ref, up_ref, near_own, far_own, near_other, far_other,
    grad_ref, pack_ref, upb_ref,
    out_ref, glow_ref, gdown_own, gdown_other, gup_own, gup_other, gbias_ref, gvec_ref,
    down_s, up_s, wo_v, up_v, down_v, gd_own, gd_other, gu_own, gu_other, load_sem, store_sem,
):
    turn = pl.program_id(0)
    side, x_at = spot_ref[0], spot_ref[2]
    chunks, size = down_s.shape[0], down_s.shape[2]
    load_out = pltpu.make_async_copy(wo_ref, wo_v, load_sem.at[0])
    load_up = pltpu.make_async_copy(up_ref, up_v, load_sem.at[1])
    load_down = []
    for index, piece in enumerate((near_own, far_own, near_other, far_other)):
        at_side = 1 - side if index // 2 else side
        column = 1 - x_at if index % 2 else x_at
        for i in range(2):
            target = down_v.at[at_side, :, i, column]
            load_down.append(pltpu.make_async_copy(piece.at[i], target, load_sem.at[2 + 2 * index + i]))

    @pl.when(turn == 0)
    def _():
        load_out.start()
        load_up.start()
        for load in load_down:
            load.start()
        down_s[...] = jnp.zeros_like(down_s)
        up_s[...] = jnp.zeros_like(up_s)
        gbias_ref[...] = jnp.zeros_like(gbias_ref)
        gvec_ref[...] = jnp.zeros_like(gvec_ref)
        load_out.wait()

    middle = (
        x_ref[0].astype(f32)
        + jnp.dot(join_lanes(mine_ref), wo_v[side], preferred_element_type=f32)
        + jnp.dot(join_lanes(recv_ref), wo_v[1 - side], preferred_element_type=f32)
        + pack_ref[2:3, :]
    )
    xhat, rstd = standardise(middle)
    normed = (xhat * pack_ref[3:4, :] + pack_ref[4:5, :]).astype(bf16)
    normed_t = normed.T
    grad = grad_ref[0]
    grad_t = grad.T
    total = middle + pack_ref[5:6, :]

    @pl.when(turn == 0)
    def _():
        load_up.wait()
        for load in load_down:
            load.wait()

    half_lines = down_v.shape[1] // (chunks // 2)

    def down_chunk(f):
        line = (f % (chunks // 2)) * half_lines
        return down_v[f // (chunks // 2), line : line + half_lines].reshape(size, down_v.shape[-1])

    def first_layer(f):
        at = slice(f * size, (f + 1) * size)
        return jnp.dot(normed, up_v[:, at], preferred_element_type=f32) + upb_ref[f : f + 1, :]

    gnormed = None
    pre = first_layer(0)
    for f in range(chunks):
        at = slice(f * size, (f + 1) * size)
        hidden, slope = gelu_pair(pre)
        ghidden = lax.dot_general(grad, down_chunk(f), NT, preferred_element_type=f32)
        if f + 1 < chunks:
            pre = first_layer(f + 1)
        hidden = hidden.astype(bf16)
        gpre = (ghidden * slope).astype(bf16)
        total = total + jnp.dot(hidden, down_chunk(f), preferred_element_type=f32)
        part = lax.dot_general(gpre, up_v[:, at], NT, preferred_element_type=f32)
        gnormed = part if gnormed is None else gnormed + part
        down_s[f] += jnp.dot(grad_t, hidden, preferred_element_type=f32)
        up_s[f] += jnp.dot(normed_t, gpre, preferred_element_type=f32)
        gbias_ref[f] += jnp.sum(gpre.astype(f32), axis=0, keepdims=True)
    out_ref[0] = total.astype(bf16)
    gmid = grad.astype(f32) + norm_pull(gnormed, pack_ref[3:4, :], xhat, rstd)
    low = gmid.astype(bf16)
    glow_ref[0] = low
    gvec_ref[0:1, :] += jnp.sum(gnormed * xhat, axis=0, keepdims=True)
    gvec_ref[1:2, :] += jnp.sum(gnormed, axis=0, keepdims=True)
    gvec_ref[2:3, :] += jnp.sum(low.astype(f32), axis=0, keepdims=True)
    gvec_ref[3:4, :] += jnp.sum(grad.astype(f32), axis=0, keepdims=True)

    @pl.when(turn == pl.num_programs(0) - 1)
    def _():
        half = chunks // 2
        rows = chunks * share
        per_chunk = size // rows
        lines_chunk = per_chunk // planes
        for f in range(chunks):
            whole = down_s[f].astype(bf16).T
            at_line = (f % half) * lines_chunk
            span = slice(at_line, at_line + lines_chunk)
            for target, result, wanted in ((gd_own, gdown_own, f // half), (gd_other, gdown_other, 1 - f // half)):

                @pl.when(side == wanted)
                def _(target=target, result=result, whole=whole, f=f, at_line=at_line, span=span):
                    for i in range(per_chunk):
                        target[i % planes, at_line + i // planes] = whole[i * rows : (i + 1) * rows]
                    pltpu.make_async_copy(target.at[:, span], result.at[:, span], store_sem.at[f]).start()

        wide = up_s.shape[1] // 2
        ups = ((gu_own, gup_own, side * wide), (gu_other, gup_other, (1 - side) * wide))
        for which, (target, result, base) in enumerate(ups):
            for f in range(chunks):
                for at in range(wide // share):
                    start = pl.multiple_of(base + at * share, 8)
                    target[at % planes, at // planes, f] = up_s[f, pl.ds(start, share), :].astype(bf16)
                pltpu.make_async_copy(
                    target.at[:, :, f], result.at[:, :, f], store_sem.at[chunks * (1 + which) + f]
                ).start()
        for f in range(chunks):
            span = slice(0, lines_chunk)
            pltpu.make_async_copy(gd_own.at[:, span], gdown_own.at[:, span], store_sem.at[f]).wait()
        for which, (target, result, base) in enumerate(ups):
            for f in range(chunks):
                pltpu.make_async_copy(
                    target.at[:, :, f], result.at[:, :, f], store_sem.at[chunks * (1 + which) + f]
                ).wait()


def attend_back_kernel(
    flag_ref, side_ref, mixed_ref, ext_ref, att_own, att_other, own_ref, other_ref, wo_ref, kx_ref,
    gmixed_ref, gbias_ref,
    q_s, d_s, k_s, v_s, kt_s, gq_s, gk_s, gv_s,
):
    row = pl.program_id(0)
    length = k_s.shape[0]
    half = length // 2
    low, high = lane_masks()
    lane = lax.broadcasted_iota(jnp.int32, (1, 128), 1)
    spot = lane % HEAD_DIM
    square_row = lax.broadcasted_iota(jnp.int32, (128, 128), 0) < HEAD_DIM
    square_col = lax.broadcasted_iota(jnp.int32, (128, 128), 1) < HEAD_DIM
    crossing = jnp.where(square_row == square_col, 0.0, -1.0).astype(bf16)
    one_hot_a = jnp.where(spot == 0, 1.0, 0.0)
    one_hot_b = jnp.where(spot == 1, 1.0, 0.0)
    v_ext = (one_hot_a + one_hot_b).astype(bf16)

    @pl.when(row == 0)
    def _():
        gbias_ref[...] = jnp.zeros_like(gbias_ref)

    mixed_at = lambda lanes: mixed_ref[0, :, 0, :, lanes].reshape(length, 128)
    q, k = mixed_at(slice(0, 128)), mixed_at(slice(128, 256))
    ext = ext_ref[0, :, 0].reshape(length, 128)
    k_s[:, 0:128] = k
    k_s[:, 128:256] = kx_ref[0]
    v_s[:, 0:128] = mixed_at(slice(256, 384))
    v_s[:, 128:256] = jnp.broadcast_to(v_ext, (length, 128))
    for head, (mine, other) in enumerate(((low, high), (high, low))):
        q_part, ext_part = q * mine, ext * other
        for i in range(length // TQ_B):
            at = slice(i * TQ_B, (i + 1) * TQ_B)
            rows = slice(head * TQ_B, (head + 1) * TQ_B)
            q_s[i, rows, 0:128] = q_part[at]
            q_s[i, rows, 128:256] = ext_part[at]
    for side in range(2):
        gates = own_ref[0] if side == 0 else other_ref[0]
        d = lax.dot_general(gates, wo_ref[...], NT, preferred_element_type=f32)
        moved = d * (att_own if side == 0 else att_other)[0, 0].astype(f32)
        moved_a = moved.astype(bf16)
        moved_b = (moved - moved_a.astype(f32)).astype(bf16)
        shift = jnp.dot(moved_a, crossing, preferred_element_type=f32) + jnp.dot(
            moved_b, crossing, preferred_element_type=f32
        )
        shift_a = shift.astype(bf16).astype(f32)
        dx = (shift_a * one_hot_a + (shift - shift_a) * one_hot_b).astype(bf16)
        d = d.astype(bf16)
        tile = min(TQ_B, half)
        for head, (mine, other) in enumerate(((low, high), (high, low))):
            d_part, dx_part = d * mine, dx * other
            for i in range(half // tile):
                at = slice(i * tile, (i + 1) * tile)
                start = side * half + i * tile
                rows = slice(head * TQ_B + start % TQ_B, head * TQ_B + start % TQ_B + tile)
                d_s[start // TQ_B, rows, 0:128] = d_part[at]
                d_s[start // TQ_B, rows, 128:256] = dx_part[at]
    for i in range(length // TK_B):
        kt_s[i] = k[i * TK_B : (i + 1) * TK_B].T
    query_blocks = length // TQ_B

    def block(k_start, q_start, size, fresh):
        k_at = slice(k_start, k_start + size)
        tile, inside = q_start // TQ_B, q_start % TQ_B
        key_tile, key_inside = k_start // TK_B, k_start % TK_B
        q_rows = [slice(head * TQ_B + inside, head * TQ_B + inside + size) for head in range(2)]
        probs, grads = [], []
        for rows in q_rows:
            score = lax.dot_general(k_s[k_at, :], q_s[tile, rows, :], NT, preferred_element_type=f32)
            inner = lax.dot_general(v_s[k_at, :], d_s[tile, rows, :], NT, preferred_element_type=f32)
            prob = jnp.exp2(score * SCORE)
            probs.append(prob.astype(bf16))
            grads.append((prob * inner).astype(bf16))
        for head in range(2):
            at = slice(head * HEAD_DIM, (head + 1) * HEAD_DIM)
            keys = kt_s[key_tile, at, key_inside : key_inside + size]
            part = jnp.dot(keys, grads[head], preferred_element_type=f32)
            if fresh:
                gq_s[tile, at, inside : inside + size] = part
            else:
                gq_s[tile, at, inside : inside + size] += part
        for target, left, right in ((gv_s, probs, d_s), (gk_s, grads, q_s)):
            if size == TQ_B:
                part = jnp.dot(jnp.concatenate(left, axis=1), right[tile, :, 0:128], preferred_element_type=f32)
            else:
                part = jnp.dot(left[0], right[tile, q_rows[0], 0:128], preferred_element_type=f32)
                part = part + jnp.dot(left[1], right[tile, q_rows[1], 0:128], preferred_element_type=f32)
            if fresh:
                target[k_at, :] = part
            else:
                target[k_at, :] += part

    for i in range(query_blocks):
        block(i * TQ_B, i * TQ_B, TQ_B, True)
    pieces = length // T_SIDE
    for ki in range(pieces):
        for qi in range(pieces):
            if ki * T_SIDE // TK_B != qi * T_SIDE // TQ_B:

                @pl.when(flag_ref[row, ki * pieces + qi] != 0)
                def _(ki=ki, qi=qi):
                    block(ki * T_SIDE, qi * T_SIDE, T_SIDE, False)

    for i in range(query_blocks):
        gq = (0.125 * gq_s[i].T).astype(bf16)
        for start in range(0, TQ_B, min(TQ_B, half)):
            at = i * TQ_B + start
            size = min(TQ_B, half)
            gmixed_ref[at // half, 0, at % half : at % half + size, 0:128] = gq[start : start + size]
        gbias_ref[0:1, 0:128] += jnp.sum(gq.astype(f32), axis=0, keepdims=True)
    gk = (0.125 * gk_s[...]).astype(bf16)
    gv = gv_s[...].astype(bf16)
    gbias_ref[0:1, 128:256] += jnp.sum(gk.astype(f32), axis=0, keepdims=True)
    gbias_ref[0:1, 256:384] += jnp.sum(gv.astype(f32), axis=0, keepdims=True)
    for side in range(2):
        gmixed_ref[side, 0, :, 128:256] = gk[side * half : (side + 1) * half]
        gmixed_ref[side, 0, :, 256:384] = gv[side * half : (side + 1) * half]


def weight_dot(normed_ref, *piece_refs):
    normed_t = jnp.concatenate([normed_ref[0, 0], normed_ref[1, 0]], axis=0).T
    sides = []
    for side in range(2):
        sides.append(jnp.concatenate([ref[side, 0] for ref in piece_refs], axis=1))
    return jnp.dot(normed_t, jnp.concatenate(sides, axis=0), preferred_element_type=f32)


def fold_lanes(value):
    total = value[:, 0:128]
    for at in range(128, value.shape[1], 128):
        total = total + value[:, at : at + 128]
    return total


def early_kernel(
    planes, share, normed_ref, g0_ref, g1_ref, b0_ref, b1_ref, mine_ref, other_ref, low_ref, low_other_ref, w_ref,
    unit_ref, first_ref, second_ref, acc_s, out_s,
):
    turn = pl.program_id(0)

    @pl.when(turn == 0)
    def _():
        acc_s[...] = jnp.zeros_like(acc_s)
        out_s[...] = jnp.zeros_like(out_s)

    acc_s[...] += weight_dot(normed_ref, g0_ref, g1_ref)
    across = (((0,), (0,)), ((), ()))
    out_s[...] += lax.dot_general(
        join_lanes(mine_ref), low_ref[0], across, preferred_element_type=f32
    ) + lax.dot_general(join_lanes(other_ref), low_other_ref[0], across, preferred_element_type=f32)

    @pl.when(turn == pl.num_programs(0) - 1)
    def _():
        weights = w_ref[...].astype(f32)
        sums = jnp.concatenate([b0_ref[0:1, :], b1_ref[0:1, :]], axis=1)
        first_ref[...] = fold_lanes(weights * acc_s[...])
        second_ref[...] = fold_lanes(weights * sums)
        count = out_s.shape[0] // share
        for at in range(count):
            spot = (at % planes, at // planes)
            for half in range(2):
                lanes = slice(384 * half, 384 * half + 384)
                for side in range(2):
                    start = (side * count + at) * share
                    unit_ref[spot + (2 * side + half,)] = acc_s[start : start + share, lanes].astype(bf16)
                unit_ref[spot + (4 + half,)] = out_s[at * share : (at + 1) * share, lanes].astype(bf16)


def scatter_rows(vector, step, offset, owners):
    n = vector.shape[1]
    owner = lax.broadcasted_iota(jnp.int32, (owners, n), 0) - offset
    mask = lax.div(lax.broadcasted_iota(jnp.int32, (owners, n), 1), step) == owner
    spread = jnp.where(mask, jnp.broadcast_to(vector, (owners, n)), 0.0).astype(bf16)
    lane = lax.rem(lax.broadcasted_iota(jnp.int32, (128, n), 1), step)
    chosen = jnp.where(lane == lax.broadcasted_iota(jnp.int32, (128, n), 0), 1.0, 0.0).astype(bf16)
    return lax.dot_general(spread, chosen, NT, preferred_element_type=f32)


def late_kernel(
    planes, share, side_ref, normed_ref, g_ref, w_ref, first_ref, second_ref, b0_ref, b1_ref, b2_ref, pack_ref,
    gvec_ref, gup_ref, unit_ref, acc_s,
):
    turn = pl.program_id(0)

    @pl.when(turn == 0)
    def _():
        acc_s[...] = jnp.zeros_like(acc_s)

    acc_s[...] += weight_dot(normed_ref, g_ref)

    @pl.when(turn == pl.num_programs(0) - 1)
    def _():
        side = side_ref[0]
        weights = w_ref[...].astype(f32)
        width = weights.shape[0]
        owners = width // share
        count = owners // 2
        inner = first_ref[...] + fold_lanes(weights * acc_s[...])
        plain = second_ref[...] + fold_lanes(weights * b2_ref[0:1, :])
        inner = jnp.sum(inner.T, axis=0, keepdims=True)
        plain = jnp.sum(plain.T, axis=0, keepdims=True)
        gain, bias = pack_ref[0:1, :], pack_ref[1:2, :]
        g_gain = (inner - bias * plain) / gain
        biases = (b0_ref, b1_ref, b2_ref)
        query = jnp.concatenate([b[0:1, 0:128] for b in biases], axis=1)
        value = jnp.concatenate([b[0:1, 256:384] for b in biases], axis=1)
        chunks = gup_ref.shape[0]
        rows_up = chunks * share
        up_bias = None
        for f in range(chunks):
            part = scatter_rows(gup_ref[f], rows_up, f * (width // rows_up), owners)
            up_bias = part if up_bias is None else up_bias + part
        wide = width // 2
        first_owner = side * (wide // (2 * share))
        qv_bias = scatter_rows(query, 2 * share, first_owner, owners) + scatter_rows(
            value, 2 * share, first_owner + count, owners
        )
        plain_rows = lambda vec: scatter_rows(vec, share, 0, owners)
        slots = [
            plain_rows(g_gain),
            plain_rows(plain),
            plain_rows(gvec_ref[2:3, :]),
            plain_rows(gvec_ref[0:1, :]),
            plain_rows(gvec_ref[1:2, :]),
            plain_rows(gvec_ref[3:4, :]),
            qv_bias,
            up_bias,
            jnp.zeros((owners, 128), f32),
        ]
        lines_of = [jnp.concatenate(slots[3 * i : 3 * i + 3], axis=1) for i in range(3)]
        blank = jnp.zeros((5, 384), f32)
        for at in range(count):
            spot = (at % planes, at // planes)
            small = []
            for half in range(2):
                owner = half * count + at
                start = owner * share
                unit_ref[spot + (half,)] = acc_s[start : start + share, :].astype(bf16)
                small += [line[owner : owner + 1, :] for line in lines_of] + [blank]
            small.append(jnp.zeros((share - 16, 384), f32))
            unit_ref[spot + (2,)] = jnp.concatenate(small, axis=0).astype(bf16)


def finish_kernel(side_ref, line_ref, got_ref, qkv_ref, out_ref, *vec_refs):
    side = side_ref[0]
    wide = qkv_ref.shape[1] // 6
    for pair in range(wide // 128):
        own = line_ref[2 * side + pair] if pair < 2 else line_ref[6 + side]
        other = got_ref[pair]
        for kind in range(3):
            lanes = slice(128 * kind, 128 * kind + 128)
            for half in range(2):
                at = kind * 2 * wide + half * wide + 128 * pair
                qkv_ref[:, at : at + 128] = jnp.where(side == half, own[:, lanes], other[:, lanes])
    out_ref[:, 0:384] = line_ref[4]
    out_ref[:, 384:768] = line_ref[5]
    start = pl.multiple_of(8 * side, 8)
    small = line_ref[8, pl.ds(start, 8), :] + got_ref[3, pl.ds(start, 8), :]
    for slot, ref in enumerate(vec_refs):
        at = 128 * (slot % 3)
        ref[...] = small[slot // 3 : slot // 3 + 1, at : at + ref.shape[1]]


def back_through(pieces, w_ref, side):
    total = None
    for i, piece in enumerate(pieces):
        part = lax.dot_general(
            piece[side, 0], w_ref[:, 384 * i : 384 * i + 384], NT, preferred_element_type=f32
        )
        total = part if total is None else total + part
    return total


def give_kernel(*refs):
    pieces, (w_ref, out_ref) = refs[:-2], refs[-2:]
    out_ref[0] = back_through(pieces, w_ref, 0).astype(bf16)


def input_kernel(*refs):
    pieces, (w_ref, recv_ref, x_ref, gmid_ref, pack_ref, ginput_ref) = refs[:-6], refs[-6:]
    gnormed = back_through(pieces, w_ref, 0) + recv_ref[0].astype(f32)
    xhat, rstd = standardise(x_ref[0].astype(f32))
    ginput_ref[0] = gmid_ref[0].astype(f32) + norm_pull(gnormed, pack_ref[0:1, :], xhat, rstd)


def partner(value):
    return lax.ppermute(value, "seq", [(0, 1), (1, 0)])


def exchange(value, axis):
    return lax.all_to_all(value, axis, 0, 0, tiled=True)


def spread_line(value, lines):
    return exchange(jnp.broadcast_to(value[None], (lines,) + value.shape), "line")


def flip(value, axis):
    return lax.ppermute(value, axis, [(0, 1), (1, 0)])


def in_order(index, own, received):
    return jnp.where(index == 0, jnp.stack([own, received]), jnp.stack([received, own]))


def spread_first(one, two):
    return lax.optimization_barrier((flip(one, "x"), flip(two, "y")))


def spread_second(one, two, got_one, got_two):
    near_one = in_order(lax.axis_index("x"), one, got_one)
    near_two = in_order(lax.axis_index("y"), two, got_two)
    near_one, near_two = lax.optimization_barrier((near_one, near_two))
    return (near_one, flip(near_one, "y")), (near_two, flip(near_two, "x"))


def spread_plane(one, two):
    return spread_second(one, two, *spread_first(one, two))


def after(value, *others):
    return lax.optimization_barrier((value,) + others)[0]


def assemble_kernel(far_plane, spot_ref, *refs):
    pieces, targets, scratch, (in_sem, out_sem) = refs[:2], refs[-6:-4], refs[-4:-2], refs[-2:]
    up_ref, out_ref = targets
    side, y = spot_ref[0], spot_ref[1]
    width = out_ref.shape[-1]
    blocks = up_ref.shape[-1] // width
    loads = [pltpu.make_async_copy(pieces[i], scratch[i], in_sem.at[i]) for i in range(2)]
    for load in loads:
        load.start()
    stores = []

    def send(source, target):
        stores.append(pltpu.make_async_copy(source, target, out_sem.at[len(stores)]))
        stores[-1].start()

    row = 1 - y if far_plane else y
    for index in range(2):
        loads[index].wait()
        at_side = 1 - side if index else side
        held = scratch[index]
        for i in range(2):
            for block in range(blocks):
                lanes = slice(block * width, (block + 1) * width)
                send(held.at[i, :, block], up_ref.at[at_side, :, row, i, :, lanes])
            send(held.at[i, :, blocks], out_ref.at[at_side, :, row, i])
    for copy in stores:
        copy.wait()


def assemble(spot, far_plane, pieces, targets, shapes):
    anywhere = pl.BlockSpec(memory_space=pl.ANY)
    blocks = pieces[0].shape[2]
    return pl.pallas_call(
        functools.partial(assemble_kernel, far_plane),
        grid_spec=pltpu.PrefetchScalarGridSpec(
            num_scalar_prefetch=1,
            grid=(1,),
            in_specs=[anywhere] * (2 + len(targets)),
            out_specs=[anywhere] * 2,
            scratch_shapes=[pltpu.VMEM(p.shape, bf16) for p in pieces]
            + [pltpu.SemaphoreType.DMA((2,)), pltpu.SemaphoreType.DMA((4 * blocks,))],
        ),
        out_shape=shapes,
        input_output_aliases={3 + i: i for i in range(len(targets))},
        name="assemble",
        **kernel_params(1e6, 12e6),
    )(spot, *pieces, *targets)


def sum_plane(value, *waits):
    received = exchange(value, ("y", "x"))
    if waits:
        received = after(received, *waits)
    return jnp.sum(received.astype(f32), axis=0)


def send_line(value, lines):
    here = lax.axis_index("line")
    pieces = []
    for shift in range(1, lines):
        piece = lax.dynamic_index_in_dim(value, (here + shift) % lines, 0, keepdims=False).astype(bf16)
        pieces.append(lax.ppermute(piece, "line", [(i, (i + shift) % lines) for i in range(lines)]))
    return pieces


def sum_line(value, lines, *waits):
    total = lax.dynamic_index_in_dim(value, lax.axis_index("line"), 0, keepdims=False)
    pieces = send_line(value, lines)
    if waits:
        pieces = lax.optimization_barrier(tuple(pieces) + waits)[: len(pieces)]
    for piece in pieces:
        total = total + piece.astype(f32)
    return total


def masks(seg, pos):
    pad = seg == CLIPS - 1
    lane = jnp.arange(128, dtype=jnp.int32) % HEAD_DIM
    seg, pos, pad = seg[..., None], pos[..., None], pad[..., None]
    clip_lane = lane < CLIPS - 1
    digit = jnp.where(lane < 9, pos // 256, jnp.where(lane < 25, (pos // 16) % 16, pos % 16))
    digit_base = jnp.where(lane < 9, 5, jnp.where(lane < 25, 9, 25))
    digit_lane = (lane >= 5) & (lane < LANE_LOG)
    hit_clip = lane == seg
    hit_digit = lane - digit_base == digit
    log_lane = (lane >= LANE_LOG) & (lane < LANE_PAD)
    pad_lane = lane == LANE_PAD
    bad = (clip_lane & ~hit_clip) | (digit_lane & pad & ~hit_digit) | (pad_lane & ~pad)
    qx = jnp.where(bad, -BIG, 0.0).astype(bf16)
    on = (clip_lane & hit_clip) | (digit_lane & pad & hit_digit) | log_lane | (pad_lane & pad)
    kx = jnp.where(on, 1.0, 0.0).astype(bf16)
    return qx, kx


def block_flags(ident, rows_block, cols_block):
    count, length = ident.shape
    by_row = ident.reshape(count, length // rows_block, rows_block)
    by_col = ident.reshape(count, length // cols_block, cols_block)
    low_row, high_row = jnp.min(by_row, axis=2)[:, :, None], jnp.max(by_row, axis=2)[:, :, None]
    low_col, high_col = jnp.min(by_col, axis=2)[:, None, :], jnp.max(by_col, axis=2)[:, None, :]
    meets = (low_row <= high_col) & (low_col <= high_row)
    return meets.astype(jnp.int32).reshape(count, -1)


def pair_device(
    lines, planes,
    tokens, segment_ids, cotangent, ln1_gain, ln1_bias, qkv_weight, qv_bias, out_weight, out_bias,
    ln2_gain, ln2_bias, up_weight, up_bias, down_weight, down_bias, avg_qkv, avg_out, avg_up, avg_down,
):
    count, part, width = tokens.shape
    length = 2 * part
    wide = width // 2
    heads = HEADS // 2
    hidden_width = up_weight.shape[1]
    chunks = hidden_width // width
    share = qkv_weight.shape[0]
    side = lax.axis_index("seq").astype(jnp.int32)
    first = side == 0
    side_arr = side.reshape(1)
    const = lambda *shape: pl.BlockSpec(shape, lambda *_: (0,) * len(shape), pipeline_mode=pl.Buffered(1))
    row_block = lambda *shape: pl.BlockSpec((1,) + shape, lambda j, *_: (j,) + (0,) * len(shape))
    both_block = lambda lanes: pl.BlockSpec((2, 1, part, lanes), lambda j, *_: (0, j, 0, 0))
    own_block = lambda lanes: pl.BlockSpec((1, 1, part, lanes), lambda j, *_: (0, j, 0, 0))

    pairs = heads // 2
    sds = jax.ShapeDtypeStruct
    small_vectors = [ln1_gain, ln1_bias, out_bias, ln2_gain, ln2_bias, down_bias, qv_bias, up_bias]
    mine, give, second = pl.pallas_call(
        functools.partial(prepare_kernel, share),
        grid_spec=pltpu.PrefetchScalarGridSpec(
            num_scalar_prefetch=1,
            grid=(1,),
            in_specs=[
                pl.BlockSpec((share, 6 * wide), lambda *_: (0, 0)),
                pl.BlockSpec((share, hidden_width), lambda *_: (0, 0)),
                pl.BlockSpec((share, width), lambda *_: (0, 0)),
                pl.BlockSpec((chunks * share, width), lambda *_: (0, 0)),
            ]
            + [pl.BlockSpec((1, v.shape[0]), lambda *_: (0, 0)) for v in small_vectors],
            out_specs=[pl.BlockSpec((share, 3 * wide + 128), lambda *_: (0, 0))] * 2
            + [pl.BlockSpec(((2 * chunks + 1) * share, width), lambda *_: (0, 0))],
        ),
        out_shape=[sds((share, 3 * wide + 128), bf16)] * 2 + [sds(((2 * chunks + 1) * share, width), bf16)],
        name="prepare",
        **kernel_params(1e6, 1e6),
    )(side_arr, qkv_weight, up_weight, out_weight, down_weight, *[v[None] for v in small_vectors])
    take = partner(give)
    tokens_other = partner(tokens)
    seg_other = partner(segment_ids)
    seg = jnp.concatenate([segment_ids, seg_other], axis=1)
    spots = jnp.arange(part, dtype=jnp.int32)
    pos = jnp.concatenate([side * part + spots, (1 - side) * part + spots])
    qx, kx = masks(seg, jnp.broadcast_to(pos, seg.shape))
    ident = jnp.where(seg == CLIPS - 1, CLIPS + pos, seg)
    flags_f = flags_b = block_flags(ident, T_SIDE, T_SIDE)

    start = jnp.where(first, jnp.stack([mine, take]), jnp.stack([take, mine]))
    x_at, y_at = lax.axis_index("x"), lax.axis_index("y")
    first_line = after(spread_line(start, lines), qx, kx, flags_f, flags_b)
    (one_m, one_r), (two_m, two_r) = spread_plane(first_line[:, 0], first_line[:, 1])
    one = in_order(y_at, one_m, one_r).transpose(2, 0, 1, 3, 4)
    two = in_order(x_at, two_m, two_r).transpose(2, 1, 0, 3, 4)
    w_first = jnp.stack([one, two]).reshape(width, 3 * wide + 128)

    own_rows = chunks * share
    second = after(second, first_line)
    up_rows = own_rows + share
    second_line = spread_line(second, lines)

    small_at = 3 * wide // 128
    normed, mixed, pack = pl.pallas_call(
        functools.partial(project_kernel, share),
        grid_spec=pltpu.PrefetchScalarGridSpec(
            num_scalar_prefetch=1,
            grid=(2, count),
            in_specs=[
                pl.BlockSpec((1, part, width), lambda h, j, *_: (jnp.where(h == 0, j, count - 1), 0, 0)),
                pl.BlockSpec((1, part, width), lambda h, j, *_: (jnp.where(h == 0, 0, j), 0, 0)),
                const(width, 3 * wide),
                pl.BlockSpec((width, 128), lambda *_: (0, small_at), pipeline_mode=pl.Buffered(1)),
            ],
            out_specs=[
                pl.BlockSpec((1, 1, part, width), lambda h, j, *_: (h, j, 0, 0)),
                pl.BlockSpec((pairs, 1, 1, part, 384), lambda h, j, *_: (0, h, j, 0, 0)),
                pl.BlockSpec((16, width), lambda *_: (0, 0)),
            ],
            scratch_shapes=[pltpu.VMEM((1, 3 * wide), f32)],
        ),
        out_shape=[
            sds((2, count, part, width), bf16),
            sds((pairs, 2, count, part, 384), bf16),
            sds((16, width), f32),
        ],
        name="project",
        **kernel_params(
            2 * 2 * count * part * width * 3 * wide, 20e6, order=("arbitrary", "arbitrary")
        ),
    )(side_arr, tokens, tokens_other, w_first, w_first)
    up_bias_all = pack[8 : 8 + chunks].reshape(chunks, -1, share).transpose(1, 0, 2).reshape(chunks, width)

    second_line = after(second_line, one_r, two_r, pack)
    halves = (second_line[:, :up_rows].reshape(lines, chunks + 1, share, width), second_line[:, up_rows:])
    halves_got = spread_first(*halves)
    same, row_mixed = (), mixed
    for base, rows_now in ((0, 1), (1, count - 1)):
        if base == 1:
            halves_got = lax.optimization_barrier(halves_got + (same[0],))[:2]
            up_pair, down_pair = spread_second(*halves, *halves_got)
            row_mixed = after(mixed, up_pair[0], down_pair[0])
        row_both = lambda lanes, base=base: pl.BlockSpec(
            (pairs, 2, 1, part, lanes), lambda j, *_: (0, 0, base + j, 0, 0)
        )
        row_one = pl.BlockSpec((pairs, 1, part, 128), lambda j, *_, base=base: (0, base + j, 0, 0))
        row_flat = pl.BlockSpec((1, length, 128), lambda j, *_, base=base: (base + j, 0, 0))
        same = pl.pallas_call(
            functools.partial(attend_kernel, base),
            grid_spec=pltpu.PrefetchScalarGridSpec(
                num_scalar_prefetch=1,
                grid=(rows_now,),
                in_specs=[row_both(384), row_flat, row_flat] + [pl.BlockSpec(memory_space=pl.ANY)] * len(same),
                out_specs=[row_one, row_one, row_both(128)],
                scratch_shapes=[pltpu.VMEM((heads, length, 128), bf16)] * 3
                + [pltpu.VMEM((heads, length, 128), f32)],
            ),
            out_shape=[sds((pairs, count, part, 128), bf16)] * 2 + [sds((pairs, 2, count, part, 128), bf16)],
            input_output_aliases={4 + i: i for i in range(len(same))},
            name="attend",
            **kernel_params(8e9, 7e6, 4e6),
        )(flags_f, row_mixed, qx, kx, *same)
    att_own, att_other, ext = same
    spot = jnp.stack([side, y_at.astype(jnp.int32), x_at.astype(jnp.int32)])
    near = [up_pair[0], down_pair[0]]
    near += [partner(piece) for piece in near]
    far = list(lax.optimization_barrier((up_pair[1], down_pair[1], att_own))[:2])
    near = list(lax.optimization_barrier(tuple(near) + tuple(far))[:4])
    far += [partner(piece) for piece in far]
    shapes = [
        sds((2, lines, 2, 2, share, hidden_width), bf16),
        sds((2, lines, 2, 2, share, width), bf16),
    ]
    targets = assemble(spot, False, near[::2], (), shapes)
    w_up, w_out = assemble(spot, True, far[::2], targets, shapes)
    w_up = w_up.reshape(width, hidden_width)
    down_pieces = [near[1], far[1], near[3], far[3]]
    w_out = w_out.reshape(2, wide, width)
    w_out_flat = w_out.reshape(2 * wide, width)

    att_recv = partner(att_other)

    head_block = pl.BlockSpec((pairs, 1, part, 128), lambda j, *_: (0, j, 0, 0))
    out_tokens, glow, gdown_own, gdown_other, gup_own, gup_other, gup_bias, gvec = pl.pallas_call(
        functools.partial(mlp_kernel, planes, share),
        grid_spec=pltpu.PrefetchScalarGridSpec(
            num_scalar_prefetch=1,
            grid=(count,),
            in_specs=[
                row_block(part, width),
                head_block,
                head_block,
            ]
            + [pl.BlockSpec(memory_space=pl.ANY)] * 6
            + [
                row_block(part, width),
                const(16, width),
                const(chunks, width),
            ],
            out_specs=[row_block(part, width)] * 2
            + [pl.BlockSpec(memory_space=pl.ANY)] * 4
            + [const(chunks, 1, width), const(8, width)],
            scratch_shapes=[pltpu.VMEM((chunks, width, width), f32)] * 2
            + [
                pltpu.VMEM((2, wide, width), bf16),
                pltpu.VMEM((width, hidden_width), bf16),
                pltpu.VMEM((2, lines, 2, 2, own_rows, width), bf16),
            ]
            + [pltpu.VMEM((planes, lines, own_rows, width), bf16)] * 2
            + [pltpu.VMEM((planes, lines, chunks, share, width), bf16)] * 2
            + [pltpu.SemaphoreType.DMA((10,)), pltpu.SemaphoreType.DMA((3 * chunks,))],
        ),
        out_shape=[
            sds((count, part, width), bf16),
            sds((count, part, width), bf16),
        ]
        + [sds((planes, lines, own_rows, width), bf16)] * 2
        + [sds((planes, lines, chunks, share, width), bf16)] * 2
        + [sds((chunks, 1, width), f32), sds((8, width), f32)],
        name="mlp",
        **kernel_params(2 * count * part * width * (width + 6 * hidden_width), 36e6, 4.7e6),
    )(spot, tokens, att_own, att_recv, w_out, w_up, *down_pieces, cotangent, pack, up_bias_all)

    glow_other = partner(glow)
    avg_qkv, avg_out, avg_up, avg_down, _ = lax.optimization_barrier((avg_qkv, avg_out, avg_up, avg_down, glow))
    new_qkv = 0.9 * avg_qkv + 0.1 * qkv_weight.astype(f32)
    new_out = 0.9 * avg_out + 0.1 * out_weight.astype(f32)
    new_up = 0.9 * avg_up + 0.1 * up_weight.astype(f32)
    new_down = 0.9 * avg_down + 0.1 * down_weight.astype(f32)
    add = lambda one, two: (one.astype(f32) + two.astype(f32)).astype(bf16)
    gdown_plane = sum_plane(add(gdown_own, partner(gdown_other)))
    gup_sum = add(gup_own, partner(gup_other))

    gmixed, gmixed_bias = [], []
    ties = ()
    for pair in range(pairs):
        lane_block = lambda lanes, pair=pair: pl.BlockSpec((1, 2, 1, part, lanes), lambda j, *_: (pair, 0, j, 0, 0))
        att_block = pl.BlockSpec((1, 1, part, 128), lambda j, *_, pair=pair: (pair, j, 0, 0))
        piece, piece_bias = pl.pallas_call(
            attend_back_kernel,
            grid_spec=pltpu.PrefetchScalarGridSpec(
                num_scalar_prefetch=2,
                grid=(count,),
                in_specs=[
                    lane_block(384),
                    lane_block(128),
                    att_block,
                    att_block,
                    row_block(part, width),
                    row_block(part, width),
                    pl.BlockSpec((128, width), lambda j, flags, where, pair=pair: (where[0] * pairs + pair, 0)),
                    row_block(length, 128),
                ],
                out_specs=[both_block(384), const(8, 384)],
                scratch_shapes=[pltpu.VMEM((length // TQ_B, 2 * TQ_B, 256), bf16)] * 2
                + [pltpu.VMEM((length, 256), bf16)] * 2
                + [
                    pltpu.VMEM((length // TK_B, 128, TK_B), bf16),
                    pltpu.VMEM((length // TQ_B, 128, TQ_B), f32),
                    pltpu.VMEM((length, 128), f32),
                    pltpu.VMEM((length, 128), f32),
                ],
            ),
            out_shape=[sds((2, count, part, 384), bf16), sds((8, 384), f32)],
            name="attend_back",
            **kernel_params(25e9, 20e6, 4e6),
        )(flags_b, side_arr, after(mixed, *ties), ext, att_own, att_other, glow, glow_other, w_out_flat, kx)
        gmixed.append(piece)
        gmixed_bias.append(piece_bias)
        if pair == 0:
            gup_plane = sum_plane(after(gup_sum, gdown_plane))
            grad_down = sum_line(gdown_plane, lines)
            ties = (gdown_plane,)
        if pair == 1:
            early, inner_sum, plain_sum = pl.pallas_call(
                functools.partial(early_kernel, planes, share),
                grid=(count,),
                in_specs=[both_block(width), both_block(384), both_block(384), const(8, 384), const(8, 384)]
                + [head_block, head_block, row_block(part, width), row_block(part, width), const(width, 768)],
                out_specs=[const(planes, lines, 6, share, 384), const(width, 128), const(width, 128)],
                out_shape=[
                    sds((planes, lines, 6, share, 384), bf16),
                    sds((width, 128), f32),
                    sds((width, 128), f32),
                ],
                scratch_shapes=[pltpu.VMEM((width, 768), f32), pltpu.VMEM((wide, width), f32)],
                name="early",
                **kernel_params(9e9, 25e6),
            )(normed, *gmixed, *gmixed_bias, att_own, att_other, glow, glow_other, w_first)
            early_plane = sum_plane(after(early, gup_plane))
            gup_line = sum_line(gup_plane, lines)
            ties = (gup_plane, grad_down, early)
    grad_up = gup_line.transpose(1, 0, 2).reshape(share, hidden_width)

    late = pl.pallas_call(
        functools.partial(late_kernel, planes, share),
        grid_spec=pltpu.PrefetchScalarGridSpec(
            num_scalar_prefetch=1,
            grid=(count,),
            in_specs=[
                both_block(width),
                both_block(384),
                pl.BlockSpec((width, 384), lambda *_: (0, 2), pipeline_mode=pl.Buffered(1)),
                const(width, 128),
                const(width, 128),
                const(8, 384),
                const(8, 384),
                const(8, 384),
                const(16, width),
                const(8, width),
                const(chunks, 1, width),
            ],
            out_specs=const(planes, lines, 3, share, 384),
            scratch_shapes=[pltpu.VMEM((width, 384), f32)],
        ),
        out_shape=sds((planes, lines, 3, share, 384), bf16),
        name="late",
        **kernel_params(4e9, 10e6),
    )(side_arr, normed, after(gmixed[2], early_plane, gup_line), w_first, inner_sum, plain_sum, *gmixed_bias, pack, gvec, gup_bias)

    piece_spec = lambda side: pl.BlockSpec((1, 1, part, 384), lambda j, *_: (side, j, 0, 0))
    give_back = pl.pallas_call(
        give_kernel,
        grid=(count,),
        in_specs=[piece_spec(1)] * pairs + [const(width, 3 * wide)],
        out_specs=row_block(part, width),
        out_shape=sds((count, part, width), bf16),
        name="give_back",
        **kernel_params(2 * count * part * width * 3 * wide, 12e6),
    )(*gmixed[:2], after(gmixed[2], late), w_first)
    recv_back = partner(give_back)

    grad_input = pl.pallas_call(
        input_kernel,
        grid=(count,),
        in_specs=[piece_spec(0)] * pairs
        + [
            const(width, 3 * wide),
            row_block(part, width),
            row_block(part, width),
            row_block(part, width),
            const(16, width),
        ],
        out_specs=row_block(part, width),
        out_shape=sds((count, part, width), f32),
        name="input_grad",
        **kernel_params(2 * count * part * width * 3 * wide, 25e6),
    )(*gmixed, w_first, recv_back, tokens, glow, pack)

    late_plane = sum_plane(late, grad_input)
    unit_line = sum_line(jnp.concatenate([early_plane, late_plane], axis=1), lines)
    theirs = lax.dynamic_slice_in_dim(unit_line, 2 * (1 - side), 2, 0)
    theirs_late = lax.dynamic_slice_in_dim(unit_line, 7 - side, 1, 0)
    got = partner(jnp.concatenate([theirs, theirs_late, unit_line[8:]], axis=0))
    sizes = [share] * 6 + [2 * share, chunks * share]
    grad_qkv, grad_out, *vecs = pl.pallas_call(
        finish_kernel,
        grid_spec=pltpu.PrefetchScalarGridSpec(
            num_scalar_prefetch=1,
            grid=(1,),
            in_specs=[
                pl.BlockSpec((9, share, 384), lambda *_: (0, 0, 0)),
                pl.BlockSpec((4, share, 384), lambda *_: (0, 0, 0)),
            ],
            out_specs=[
                pl.BlockSpec((share, 6 * wide), lambda *_: (0, 0)),
                pl.BlockSpec((share, width), lambda *_: (0, 0)),
            ]
            + [pl.BlockSpec((1, size), lambda *_: (0, 0)) for size in sizes],
        ),
        out_shape=[sds((share, 6 * wide), f32), sds((share, width), f32)] + [sds((1, size), f32) for size in sizes],
        name="finish",
        **kernel_params(1e6, 1e6),
    )(side_arr, unit_line, got)
    vec = lambda slot, size: vecs[slot].reshape(size)

    return (
        out_tokens,
        grad_input,
        vec(0, share),
        vec(1, share),
        grad_qkv,
        vec(6, 2 * share),
        grad_out,
        vec(2, share),
        vec(3, share),
        vec(4, share),
        grad_up,
        vec(7, chunks * share),
        grad_down,
        vec(5, share),
        new_qkv,
        new_out,
        new_up,
        new_down,
    )


def specs_for(rows):
    flat = ("seq",) + (rows if isinstance(rows, tuple) else (rows,))
    grid, ids, vec, mat = P(rows, "seq", None), P(rows, "seq"), P(flat), P(flat, None)
    ins = (grid, ids, grid, vec, vec, mat, vec, mat, vec, vec, vec, mat, vec, mat, vec, mat, mat, mat, mat)
    outs = (grid, grid, vec, vec, mat, vec, mat, vec, vec, vec, mat, vec, mat, vec, mat, mat, mat, mat)
    return ins, outs


def solution(mesh):
    parts, rows = mesh.shape["seq"], mesh.shape["rows"]
    planes = 4
    if parts != 2 or rows % planes:
        ins, outs = specs_for("rows")
        return jax.shard_map(on_device, mesh=mesh, in_specs=ins, out_specs=outs, check_vma=False)
    lines = rows // planes
    finer = Mesh(mesh.devices.reshape(parts, lines, 2, 2), ("seq", "line", "y", "x"))
    ins, outs = specs_for(("line", "y", "x"))
    return jax.shard_map(
        functools.partial(pair_device, lines, planes), mesh=finer, in_specs=ins, out_specs=outs, check_vma=False
    )
```
